32 devices in a mesh: expert: 4 (over y, core), fsdp: 8 (over z, x).
Axes of the slice: x: 2, y: 2, z: 4, core: 2. Of those that a mesh axis runs over, the one named last changes fastest.
Arguments:
- hidden_in: bfloat16 [4096, 2048], P(('expert', 'fsdp')), may hold values from -6 to 6
- segment_ids: int32 [32, 128], P(('expert', 'fsdp')), may hold values from 0 to 3, never falling along the last dimension, each value on 1 to 64 neighbouring positions
- att_route: int32 [4096, 2], P(('expert', 'fsdp')), may hold values from 0 to 3, all different within a row; in each aligned block of 128 rows (0 to 127, 128 to 255, ...) at most 96 rows name the same one
- mlp_route: int32 [4096, 2], P(('expert', 'fsdp')), may hold values from 0 to 3, all different within a row; in each aligned block of 128 rows (0 to 127, 128 to 255, ...) at most 96 rows name the same one
- norm_gain1: float32 [2048], replicated, may hold values from 0.5 to 1.5
- norm_gain2: float32 [2048], replicated, may hold values from 0.5 to 1.5
- att_router: float32 [2048, 4], replicated, may hold values from -0.09375 to 0.09375
- mlp_router: float32 [2048, 4], replicated, may hold values from -0.09375 to 0.09375
- kv_weight: bfloat16 [2048, 4096], P(('expert', 'fsdp')), may hold values from -0.125 to 0.125
- query_weight: bfloat16 [4, 2048, 2048], P('expert', 'fsdp'), may hold values from -0.125 to 0.125
- out_weight: bfloat16 [4, 2048, 2048], P('expert', 'fsdp'), may hold values from -0.5 to 0.5
- att_bias: float32 [2048], replicated, may hold values from -0.6 to 0.6
- up_weight: bfloat16 [4, 2, 5632, 2048], P('expert', None, 'fsdp'), may hold values from -0.125 to 0.125
- down_weight: bfloat16 [4, 5632, 2048], P('expert', 'fsdp'), may hold values from -0.078125 to 0.078125
- mlp_bias: float32 [2048], replicated, may hold values from -0.6 to 0.6
- cotangent: float32 [4096, 2048], P(('expert', 'fsdp')), may hold values from -6 to 6
Outputs:
- layer_out: float32 [4096, 2048], P(('expert', 'fsdp'))
- grad_input: float32 [4096, 2048], P(('expert', 'fsdp'))
- grad_gain1: float32 [2048], replicated
- grad_gain2: float32 [2048], replicated
- grad_att_router: float32 [2048, 4], replicated
- grad_mlp_router: float32 [2048, 4], replicated
- grad_kv: float32 [2048, 4096], P(('expert', 'fsdp'))
- grad_query: float32 [4, 2048, 2048], P('expert', 'fsdp')
- grad_out: float32 [4, 2048, 2048], P('expert', 'fsdp')
- grad_att_bias: float32 [2048], replicated
- grad_up: float32 [4, 2, 5632, 2048], P('expert', None, 'fsdp')
- grad_down: float32 [4, 5632, 2048], P('expert', 'fsdp')
- grad_mlp_bias: float32 [2048], replicated
The draws below stay inside these ranges and needn't reach their ends.
Inputs may be any that keep to these rules, and one draw needn't show every extreme that they name: `att_route`: the 128 rows of one device name one expert at most 96 times, and this bound is reached; no row names one expert twice. `mlp_route`: the 128 rows of one device name one expert at most 96 times, and this bound is reached; no row names one expert twice. `segment_ids`: along a sequence segment ids never fall; a document holds at most 64 positions.
All inputs are finite; a program needn't handle non-finite values.
Results may differ from the reference program's by a relative error of at most 0.018.
Values may be sent and summed in bfloat16 or wider, within the bound.
No kernel may reach another device: no remote copies, remote signals or barrier semaphores. Data moves between devices by JAX's collectives and lax.ppermute only.
A program may use at most 512 MiB of HBM per device.

```python
import math
import jax
import jax.numpy as jnp
import numpy as np
from jax import lax

D = 2048
HEADS = 16
HD = 128
FF = 5632
TOP = 2
TOK_DEV = 128
EXPERTS = 4
SEQS = 32
TOKENS = 4096
HQ = 2048
CAP = 96


def levels(rng, extent, cuts, smallest, top_value):
    def one(dim, blocks):
        draws = jax.random.uniform(jax.random.fold_in(jax.random.fold_in(rng, 6), dim), (blocks,), jnp.float32, smallest / len(cuts), top_value / len(cuts))
        return jnp.repeat(jnp.exp(draws), extent[dim] // blocks).reshape((-1,) + (1,) * (len(extent) - dim - 1))

    loudness = one(*cuts[0])
    for cut in cuts[1:]:
        loudness = loudness * one(*cut)
    return loudness


def profile(count, total, most, skew):
    weights = [(1 << 20) // math.isqrt(grade ** skew) + 1 for grade in range(2, count + 1)]
    spare, holding = total - most - (count - 1), [1] * (count - 1)
    while spare > 0:
        movable = [i for i in range(count - 1) if holding[i] < most]
        whole, remaining = sum([weights[i] for i in movable]), spare
        for i in movable:
            more = min(most - holding[i], max(1, remaining * weights[i] // whole), spare)
            holding[i] = holding[i] + more
            spare = spare - more
    return np.array([most] + holding)


def uneven_parts(key, amount, total, most, skew):
    if amount == 2:
        one = jax.random.randint(key, (), max(1, total - most), min(most, total - 1) + 1)
        return jnp.stack([one, total - one])
    sizes = jnp.asarray(profile(amount, total, most, skew), jnp.int32)
    couples = (amount - 1) // 2
    giver, receiver = sizes[1:1 + 2 * couples:2], sizes[2:2 + 2 * couples:2]
    slack = jnp.minimum(giver - 1, most - receiver)
    passed = jax.random.randint(jax.random.fold_in(key, 1), (couples,), 0, 1 << 20) % (slack + 1)
    sizes = sizes.at[1:1 + 2 * couples:2].set(giver - passed).at[2:2 + 2 * couples:2].set(receiver + passed)
    return sizes[jax.random.permutation(jax.random.fold_in(key, 2), amount)]


def deal_out(stream_key, own, number, rows, count, top, limit, skew):
    sequence = jax.random.permutation(stream_key, count)
    crowded, ordinary = shares(count, rows * top, limit, skew, True), shares(count, rows * top, limit, skew, False)
    places = jnp.arange(count)

    def named(sizes, offset_by):
        used = int((sizes > 0).sum())
        fixed = max(1, used // 4)
        moved = fixed + (places - fixed + offset_by * (used - fixed)) % max(1, count - fixed)
        return jnp.zeros((count,), jnp.int32).at[sequence[jnp.where(places < fixed, places, moved)]].set(jnp.asarray(sizes, jnp.int32))

    sizes = jnp.where(number % 4 == 0, named(crowded, number // 4), named(ordinary, number - number // 4 - 1))
    mixed = jax.random.permutation(jax.random.fold_in(own, 3), count)
    source_of, sink = mixed[0:count // 2 * 2:2], mixed[1:count // 2 * 2:2]
    margin = jnp.minimum(sizes[source_of] - 1, limit - sizes[sink]) // 2
    margin = jnp.where((source_of == sequence[0]) | (sink == sequence[0]) | (sizes[sink] == 0), 0, jnp.maximum(margin, 0))
    moved = jax.random.randint(jax.random.fold_in(own, 4), (count // 2,), 0, 1 << 20) % (margin + 1)
    sizes = sizes.at[source_of].add(-moved).at[sink].add(moved)
    members = jnp.searchsorted(jnp.cumsum(sizes), jnp.arange(rows * top), side="right").astype(jnp.int32)
    table = members.reshape(top, rows).T
    table = table[jax.random.permutation(jax.random.fold_in(own, 1), rows)]
    offset_by = jax.random.randint(jax.random.fold_in(own, 2), (rows, 1), 0, top)
    return jnp.take_along_axis(table, (jnp.arange(top)[None, :] + offset_by) % top, axis=1)


def shares(number_of, total, bound, skew, full):
    weights = [(1 << 20) // math.isqrt(rank ** skew) + 1 for rank in range(1, number_of + 1)]
    largest = bound if full else min(bound, max(-(-total // number_of), total * weights[0] // sum(weights)))
    least = 1 if total - largest >= number_of - 1 else 0
    given, rest = [largest] + [least] * (number_of - 1), total - largest - least * (number_of - 1)
    while rest > 0:
        free = [i for i in range(1, number_of) if given[i] < largest] or [i for i in range(1, number_of) if given[i] < bound]
        mass, budget = sum([weights[i] for i in free]), rest
        for i in free:
            extra = min(bound - given[i], max(1, budget * weights[i] // mass), rest)
            given[i] = given[i] + extra
            rest = rest - extra
    return np.array(given)


def centred(rng, shape, spread, limit, split=(), kind=jnp.bfloat16):
    values = jax.random.normal(rng, shape, jnp.float32) * spread
    if len(split) > 0:
        values = levels(rng, shape, split, -0.22, 0.18) * values
    return jnp.clip(values, min=-limit, max=limit).astype(kind)


def setup_inputs(seed: int = 0) -> dict:
    arg_keys = jax.random.split(jax.random.key(seed), 17)
    hidden_in = centred(arg_keys[0], (TOKENS, D), 1.0, 6.0, ((0, 32),))
    segment_ids = jax.vmap(lambda own: jnp.searchsorted(jnp.cumsum(uneven_parts(own, 4, TOK_DEV, TOK_DEV // 2, 2)), jnp.arange(TOK_DEV), side="right"))(jax.random.split(arg_keys[1], SEQS)).reshape((SEQS, TOK_DEV)).astype(jnp.int32)
    att_route_keys = jax.random.split(jax.random.fold_in(arg_keys[2], 1), TOKENS // TOK_DEV)
    att_route_turns = jax.random.permutation(jax.random.fold_in(arg_keys[2], 3), TOKENS // TOK_DEV)
    att_route = jax.vmap(lambda own, number: deal_out(jax.random.fold_in(arg_keys[2], 2), own, number, TOK_DEV, EXPERTS, TOP, CAP, 2))(att_route_keys, att_route_turns).reshape((TOKENS, TOP))
    mlp_route_keys = jax.random.split(jax.random.fold_in(arg_keys[3], 1), TOKENS // TOK_DEV)
    mlp_route_turns = jax.random.permutation(jax.random.fold_in(arg_keys[3], 3), TOKENS // TOK_DEV)
    mlp_route = jax.vmap(lambda own, number: deal_out(jax.random.fold_in(arg_keys[3], 2), own, number, TOK_DEV, EXPERTS, TOP, CAP, 2))(mlp_route_keys, mlp_route_turns).reshape((TOKENS, TOP))
    norm_gain1 = jnp.clip(1.0 + 0.1 * jax.random.normal(arg_keys[4], (D,), jnp.float32), 0.5, 1.5)
    norm_gain2 = jnp.clip(1.0 + 0.1 * jax.random.normal(arg_keys[5], (D,), jnp.float32), 0.5, 1.5)
    att_router = centred(arg_keys[6], (D, EXPERTS), (2 * D) ** -0.5, 0.09375, (), jnp.float32)
    mlp_router = centred(arg_keys[7], (D, EXPERTS), (2 * D) ** -0.5, 0.09375, (), jnp.float32)
    kv_weight = centred(arg_keys[8], (D, 2 * HQ), D ** -0.5, 0.125, ((0, 32),))
    query_weight = centred(arg_keys[9], (EXPERTS, D, HQ), D ** -0.5, 0.125, ((0, 4), (1, 8)))
    out_weight = centred(arg_keys[10], (EXPERTS, HQ, D), (HQ // 16) ** -0.5, 0.5, ((0, 4), (1, 8)))
    att_bias = centred(arg_keys[11], (D,), 0.1, 0.6, (), jnp.float32)
    up_weight = centred(arg_keys[12], (EXPERTS, 2, FF, D), D ** -0.5, 0.125, ((0, 4), (2, 8)))
    down_weight = centred(arg_keys[13], (EXPERTS, FF, D), FF ** -0.5, 0.078125, ((0, 4), (1, 8)))
    mlp_bias = centred(arg_keys[14], (D,), 0.1, 0.6, (), jnp.float32)
    cotangent = centred(arg_keys[15], (TOKENS, D), 1.0, 6.0, ((0, 32),), jnp.float32)
    return dict(hidden_in=hidden_in, segment_ids=segment_ids, att_route=att_route, mlp_route=mlp_route, norm_gain1=norm_gain1, norm_gain2=norm_gain2, att_router=att_router, mlp_router=mlp_router, kv_weight=kv_weight, query_weight=query_weight, out_weight=out_weight, att_bias=att_bias, up_weight=up_weight, down_weight=down_weight, mlp_bias=mlp_bias, cotangent=cotangent)


@jax.custom_vjp
def low(v):
    return lax.optimization_barrier(v.astype(jnp.bfloat16)).astype(jnp.float32)

@jax.custom_vjp
def low_back(v):
    return v

def low_keep(v):
    return (low(v), None)

def low_pass(kept, grad):
    return (grad,)

def back_keep(v):
    return (v, None)

def back_low(kept, grad):
    return (low(grad),)
low.defvjp(low_keep, low_pass)
low_back.defvjp(back_keep, back_low)
HIGHEST = lax.Precision.HIGHEST
EPSILON = 1e-06
MASKED = -1e+30

def product(form, first, second):
    return jnp.einsum(form, first, second, precision=HIGHEST)

def norm_rows(stream, gain):
    return stream * lax.rsqrt(lax.optimization_barrier(jnp.mean(stream * stream, axis=-1, keepdims=True)) + EPSILON) * gain

def rope_tables():
    half_dim = HD // 2
    frequency = jnp.exp(jnp.arange(half_dim, dtype=jnp.float32) * (-2.0 * math.log(10000.0) / HD))
    angles = jnp.arange(TOK_DEV, dtype=jnp.float32)[:, None] * frequency[None, :]
    return (jnp.cos(angles), jnp.sin(angles))

def rotate(tensor, cosine, sine_table):
    half_dim = tensor.shape[-1] // 2
    first_half = tensor[..., :half_dim]
    second_half = tensor[..., half_dim:]
    return jnp.concatenate([first_half * cosine - second_half * sine_table, second_half * cosine + first_half * sine_table], axis=-1)

def slot_index(route):
    blocks = route.shape[0] // TOK_DEV
    flat_route = route.reshape(blocks, TOK_DEV * TOP)
    onehot = (flat_route[:, :, None] == jnp.arange(EXPERTS, dtype=jnp.int32)[None, None, :]).astype(jnp.int32)
    earlier = jnp.cumsum(onehot, axis=1) - onehot
    rank = lax.optimization_barrier(jnp.sum(earlier * onehot, axis=2))
    block_ids = jnp.arange(blocks, dtype=jnp.int32)[:, None]
    return (flat_route * (blocks * CAP) + block_ids * CAP + rank).reshape(-1).astype(jnp.int32)

def onehot_of(route):
    return (route[:, :, None] == jnp.arange(EXPERTS, dtype=jnp.int32)[None, None, :]).astype(jnp.float32)

def dispatch(rows, dest):
    buffer = jnp.zeros((EXPERTS * SEQS * CAP, rows.shape[1]), rows.dtype).at[dest].set(rows)
    return buffer.reshape(EXPERTS, SEQS * CAP, rows.shape[1])

def spread_rows(rows):
    return jnp.broadcast_to(rows[:, None, :], (rows.shape[0], TOP, rows.shape[1])).reshape(-1, rows.shape[1])

def pair_gates(normed, router, onehot):
    logits = product('td,de->te', normed, router)
    picked = lax.optimization_barrier(jnp.sum(logits[:, None, :] * onehot, axis=-1))
    return jax.nn.softmax(picked, axis=-1)

def attend_group(block):
    group_queries, group_keys, group_values, group_mask = block
    scores = low_back(product('gchqd,ghkd->gchqk', group_queries, group_keys) * (1.0 / math.sqrt(HD)))
    scores = jnp.where(group_mask[:, None, None], scores, MASKED)
    att_probs = jax.nn.softmax(scores, axis=-1)
    return product('gchqk,ghkd->gchqd', low(att_probs), group_values)

def reference(hidden_in, segment_ids, att_route, mlp_route, norm_gain1, norm_gain2, att_router, mlp_router, kv_weight, query_weight, out_weight, att_bias, up_weight, down_weight, mlp_bias, cotangent):
    att_dest = slot_index(att_route)
    mlp_dest = slot_index(mlp_route)
    att_onehot = onehot_of(att_route)
    mlp_onehot = onehot_of(mlp_route)
    position = jnp.arange(TOK_DEV, dtype=jnp.int32)
    allowed = (segment_ids[:, :, None] == segment_ids[:, None, :]) & (position[None, None, :] <= position[None, :, None])
    cosine, sine_table = rope_tables()
    group = min(SEQS, 32)

    def forward(hidden, gain_one, gain_two, router_att, router_mlp, kv_mat, query_mat, out_mat, bias_att, up_mat, down_mat, bias_mlp):
        tokens = hidden.shape[0]
        attn_input = low(norm_rows(hidden, gain_one))
        kv_raw = low_back(product('td,df->tf', attn_input, kv_mat))
        key_rows = kv_raw[:, :HQ].reshape(SEQS, TOK_DEV, HEADS, HD).transpose(0, 2, 1, 3)
        key_rows = low(rotate(key_rows, cosine, sine_table))
        value_rows = low(kv_raw[:, HQ:].reshape(SEQS, TOK_DEV, HEADS, HD).transpose(0, 2, 1, 3))
        att_gate = pair_gates(attn_input, router_att, att_onehot)
        sent = low_back(dispatch(spread_rows(attn_input), att_dest))
        query_buffer = low_back(low(product('erd,edf->erf', sent, query_mat)))
        query_rows = query_buffer.reshape(-1, HQ)[att_dest].reshape(SEQS, TOK_DEV, TOP, HEADS, HD).transpose(0, 2, 3, 1, 4)
        queries = low(rotate(query_rows, cosine, sine_table))
        shaped = (queries.reshape((SEQS // group, group) + queries.shape[1:]), key_rows.reshape((SEQS // group, group) + key_rows.shape[1:]), value_rows.reshape((SEQS // group, group) + value_rows.shape[1:]), allowed.reshape((SEQS // group, group) + allowed.shape[1:]))
        attended = lax.map(jax.checkpoint(attend_group), shaped).reshape(queries.shape)
        attended = low_back(low(attended))
        attended_rows = attended.transpose(0, 3, 1, 2, 4).reshape(tokens * TOP, HQ)
        branch_buffer = low_back(low(product('erf,efd->erd', dispatch(attended_rows, att_dest), out_mat)))
        branch_rows = branch_buffer.reshape(-1, D)[att_dest].reshape(tokens, TOP, D)
        middle = hidden + lax.optimization_barrier(jnp.sum(att_gate[:, :, None] * branch_rows, axis=1)) + bias_att
        mlp_input = low(norm_rows(middle, gain_two))
        mlp_gate = pair_gates(mlp_input, router_mlp, mlp_onehot)
        sent_mlp = low_back(dispatch(spread_rows(mlp_input), mlp_dest))
        gate_in = low_back(product('erd,efd->erf', sent_mlp, up_mat[:, 0]))
        up_in = low_back(product('erd,efd->erf', sent_mlp, up_mat[:, 1]))
        hidden_units = low(jax.nn.silu(gate_in) * up_in)
        mlp_buffer = low_back(low(product('erf,efd->erd', hidden_units, down_mat)))
        mlp_rows = mlp_buffer.reshape(-1, D)[mlp_dest].reshape(tokens, TOP, D)
        return middle + lax.optimization_barrier(jnp.sum(mlp_gate[:, :, None] * mlp_rows, axis=1)) + bias_mlp
    floats = (hidden_in.astype(jnp.float32), norm_gain1, norm_gain2, att_router, mlp_router, kv_weight.astype(jnp.float32), query_weight.astype(jnp.float32), out_weight.astype(jnp.float32), att_bias, up_weight.astype(jnp.float32), down_weight.astype(jnp.float32), mlp_bias)
    layer_out, pull = jax.vjp(forward, *floats)
    grads = pull(cotangent.astype(jnp.float32))
    return (layer_out, grads[0], grads[1], grads[2], grads[3], grads[4], grads[5], grads[6], grads[7], grads[8], grads[9], grads[10], grads[11])
```

```python
import math

import jax
import jax.numpy as jnp
from jax import lax
from jax.sharding import Mesh, PartitionSpec as P

HEADS = 16
HD = 128
TOP = 2


EPSILON = 1e-06
HIGHEST = lax.Precision.HIGHEST
MASKED = -1e30

GROUP = ("y", "c", "o")
EXPERT = ("y", "c")
ALL = ("y", "c", "o", "i")
OUTER = 4
F32 = jnp.float32
BF16 = jnp.bfloat16


def rope_tables(length):
    half_dim = HD // 2
    frequency = jnp.exp(jnp.arange(half_dim, dtype=F32) * (-2.0 * math.log(10000.0) / HD))
    angles = jnp.arange(length, dtype=F32)[:, None] * frequency[None, :]
    return (jnp.cos(angles), jnp.sin(angles))


def rotate(tensor, cosine, sine_table):
    half_dim = tensor.shape[-1] // 2
    first_half = tensor[..., :half_dim]
    second_half = tensor[..., half_dim:]
    return jnp.concatenate(
        [
            first_half * cosine - second_half * sine_table,
            second_half * cosine + first_half * sine_table,
        ],
        axis=-1,
    )


def rotate_back(tensor, cosine, sine_table):
    return rotate(tensor, cosine, -sine_table)


def norm_rows(stream, gain):
    inverse = lax.rsqrt(jnp.mean(stream * stream, axis=-1, keepdims=True) + EPSILON)
    return (stream * inverse * gain, inverse)


def norm_back(stream, inverse, gain, upstream):
    scaled = upstream * gain
    d_stream = inverse * scaled - stream * inverse**3 * jnp.mean(
        scaled * stream, axis=-1, keepdims=True
    )
    d_gain = jnp.sum(upstream * stream * inverse, axis=0)
    return (d_stream, d_gain)


def shift(value, axis):
    size = lax.axis_size(axis)
    return lax.ppermute(value, axis, [((k + 1) % size, k) for k in range(size)])


def ring_gather(value, axis):
    parts = [value]
    for _ in range(lax.axis_size(axis) - 1):
        parts.append(shift(parts[-1], axis))
    return parts


def ring_scatter(blocks, axis):
    size = lax.axis_size(axis)
    travelling = blocks[1].astype(BF16)
    for j in range(2, size):
        travelling = (shift(travelling, axis).astype(F32) + blocks[j]).astype(BF16)
    return shift(travelling, axis).astype(F32) + blocks[0]


def in_order(parts, axis):
    return jnp.roll(jnp.stack(parts), lax.axis_index(axis), axis=0)


def from_order(stacked, axis):
    return jnp.roll(stacked, -lax.axis_index(axis), axis=0)


def sum_all(value):
    for axis in ALL:
        size = lax.axis_size(axis)
        step = 1
        while step < size:
            value = value + lax.ppermute(value, axis, [(k, k ^ step) for k in range(size)])
            step *= 2
    return value


def pair_gates(normed, router, route, experts):
    logits = jnp.dot(normed.astype(F32), router, precision=HIGHEST)
    onehot = (route[:, :, None] == jnp.arange(experts, dtype=jnp.int32)[None, None, :]).astype(F32)
    picked = jnp.sum(logits[:, None, :] * onehot, axis=-1)
    return (jax.nn.softmax(picked, axis=-1), onehot)


def gates_back(gates, onehot, d_gates, normed, router):
    d_picked = gates * (d_gates - jnp.sum(gates * d_gates, axis=-1, keepdims=True))
    d_logits = jnp.sum(d_picked[:, :, None] * onehot, axis=1)
    d_router = jnp.dot(d_logits.T, normed.astype(F32), precision=HIGHEST)
    d_normed = jnp.dot(d_logits, router.T, precision=HIGHEST)
    return (d_router, d_normed)


def to_experts(gates, onehot, extra):
    by_expert = jnp.sum(gates[:, :, None] * onehot, axis=1).T
    rows = jnp.repeat(by_expert, OUTER, axis=0)[:, None, :]
    if extra is not None:
        rows = jnp.concatenate(
            [rows, jnp.broadcast_to(extra[None, None, :], rows.shape)], axis=1
        )
    return lax.all_to_all(rows, GROUP, split_axis=0, concat_axis=0, tiled=True)


def from_experts(d_gates, onehot, experts):
    rows = lax.all_to_all(d_gates, GROUP, split_axis=0, concat_axis=0, tiled=True)
    by_expert = jnp.sum(rows.reshape(experts, OUTER, -1), axis=1)
    return jnp.einsum("tce,et->tc", onehot, by_expert, precision=HIGHEST)


def meet(rows):
    return lax.all_gather(rows, GROUP, axis=0, tiled=True)


def part(rows):
    return lax.psum_scatter(rows, GROUP, scatter_dimension=0, tiled=True)


def mm(form, first, second):
    return jnp.einsum(form, first, second, preferred_element_type=F32)


def gather_query(weight):
    rows, columns = weight.shape
    mine = lax.all_to_all(
        weight.reshape(rows, OUTER, columns // OUTER), "o", split_axis=1, concat_axis=0
    )
    whole = in_order(ring_gather(mine, "i"), "i")
    return whole.transpose(1, 0, 2, 3).reshape(-1, columns // OUTER)


def scatter_query(grad):
    inner = lax.axis_size("i")
    wide = grad.shape[1]
    blocks = grad.reshape(OUTER, inner, -1, wide).transpose(1, 0, 2, 3)
    mine = ring_scatter(from_order(blocks, "i"), "i").astype(BF16)
    back = lax.all_to_all(mine, "o", split_axis=0, concat_axis=0, tiled=True)
    return back.transpose(1, 0, 2).reshape(back.shape[1], -1).astype(F32)


def gather_kv(weight):
    rows, columns = weight.shape
    wide = columns // (2 * OUTER)
    mine = lax.all_to_all(
        weight.reshape(rows, 2, OUTER, wide), "o", split_axis=2, concat_axis=0
    )
    whole = in_order(ring_gather(mine, "y"), "y")
    whole = in_order(ring_gather(whole, "i"), "i")
    whole = in_order(ring_gather(whole, "c"), "c")
    return whole.transpose(2, 0, 3, 1, 4, 5, 6).reshape(-1, 2 * wide)


def scatter_kv(grad):
    high, inner = lax.axis_size("y"), lax.axis_size("i")
    wide = grad.shape[1]
    blocks = grad.reshape(high, 2, OUTER, inner, -1, wide).transpose(1, 0, 3, 2, 4, 5)
    mine = ring_scatter(from_order(blocks, "c"), "c")
    mine = ring_scatter(from_order(mine, "y"), "y")
    mine = ring_scatter(from_order(mine, "i"), "i").astype(BF16)
    back = lax.all_to_all(mine, "o", split_axis=0, concat_axis=0, tiled=True)
    rows = back.shape[1]
    back = back.reshape(OUTER, rows, 2, wide // 2).transpose(1, 2, 0, 3)
    return back.reshape(rows, -1).astype(F32)


def shards(
    hidden_in,
    segment_ids,
    att_route,
    mlp_route,
    norm_gain1,
    norm_gain2,
    att_router,
    mlp_router,
    kv_weight,
    query_weight,
    out_weight,
    att_bias,
    up_weight,
    down_weight,
    mlp_bias,
    cotangent,
):
    experts = lax.axis_size(EXPERT)
    blocks = lax.axis_size(GROUP)
    inner = lax.axis_size("i")
    tokens, width = hidden_in.shape
    heads = HEADS // OUTER
    span = heads * HD
    score_scale = 1.0 / math.sqrt(HD)
    cosine, sine_table = rope_tables(tokens)
    position = jnp.arange(tokens)

    up_parts = ring_gather(up_weight[0], "i")
    down_parts = ring_gather(down_weight[0], "i")
    query_mat = gather_query(query_weight[0])
    kv_mat = gather_kv(kv_weight)
    slab = jnp.concatenate([query_mat, kv_mat], axis=1)
    out_mat = in_order(ring_gather(out_weight[0], "i"), "i").reshape(span, width)

    residual = hidden_in.astype(F32)
    normed_one, inverse_one = norm_rows(residual, norm_gain1)
    attn_input = normed_one.astype(BF16)
    att_gate, att_onehot = pair_gates(attn_input, att_router, att_route, experts)
    received = to_experts(att_gate, att_onehot, segment_ids[0].astype(F32))
    gate_a = received[:, 0, :]
    segment = received[:, 1, :]
    allowed = (segment[:, :, None] == segment[:, None, :]) & (
        position[None, None, :] <= position[None, :, None]
    )
    all_attn = meet(attn_input)
    cot_low = cotangent.astype(BF16)
    all_cot = meet(cot_low)
    qkv = mm("td,df->tf", all_attn, slab)

    def split_heads(columns):
        return columns.reshape(blocks, tokens, heads, HD).transpose(0, 2, 1, 3)

    queries = rotate(
        split_heads(qkv[:, :span].astype(BF16)).astype(F32), cosine, sine_table
    ).astype(BF16)
    key_rows = rotate(split_heads(qkv[:, span : 2 * span]), cosine, sine_table).astype(BF16)
    value_rows = split_heads(qkv[:, 2 * span :].astype(BF16))

    def probs():
        scores = mm("ghqd,ghkd->ghqk", queries, key_rows) * score_scale
        return jax.nn.softmax(jnp.where(allowed[:, None], scores, MASKED), axis=-1)

    attended = mm("ghqk,ghkd->ghqd", probs().astype(BF16), value_rows)
    gated = (attended * gate_a[:, None, :, None]).astype(BF16)
    gated = gated.transpose(0, 2, 1, 3).reshape(blocks * tokens, span)
    branch = part(mm("tf,fd->td", gated, out_mat).astype(BF16))

    middle = residual + branch.astype(F32) + att_bias
    normed_two, inverse_two = norm_rows(middle, norm_gain2)
    mlp_input = normed_two.astype(BF16)
    mlp_gate, mlp_onehot = pair_gates(mlp_input, mlp_router, mlp_route, experts)
    gate_m = to_experts(mlp_gate, mlp_onehot, None).reshape(-1, 1)
    all_mlp = meet(mlp_input)
    rows_out = None
    rows_back = None
    d_gate_m = None
    grad_up_parts = []
    grad_down_parts = []
    for up, down in zip(up_parts, down_parts):
        units = down.shape[0]
        flat_up = up.reshape(2 * units, width)
        d_units = mm("td,fd->tf", all_cot, down)
        both = mm("td,fd->tf", all_mlp, flat_up)
        gate_in, up_in = both[:, :units], both[:, units:]
        sigma = jax.nn.sigmoid(gate_in)
        hidden_units = gate_in * sigma * up_in
        d_here = jnp.sum(hidden_units * d_units, axis=-1)
        d_gate_m = d_here if d_gate_m is None else d_gate_m + d_here
        gated_units = (hidden_units * gate_m).astype(BF16)
        d_units = d_units * gate_m
        d_both = jnp.concatenate(
            [
                (d_units * up_in * sigma * (1.0 + gate_in * (1.0 - sigma))).astype(BF16),
                (d_units * gate_in * sigma).astype(BF16),
            ],
            axis=1,
        )
        back = mm("tf,fd->td", d_both, flat_up)
        rows_back = back if rows_back is None else rows_back + back
        ahead = mm("tf,fd->td", gated_units, down)
        rows_out = ahead if rows_out is None else rows_out + ahead
        grad_up_parts.append(mm("tf,td->fd", d_both, all_mlp).reshape(2, units, width))
        grad_down_parts.append(mm("tf,td->fd", gated_units, all_cot))
    d_mlp_input = part(rows_back.astype(BF16)).astype(F32)
    d_mlp_gate = from_experts(d_gate_m.reshape(blocks, tokens), mlp_onehot, experts)
    layer_out = middle + part(rows_out.astype(BF16)).astype(F32) + mlp_bias
    d_upper = ring_scatter(grad_up_parts, "i")[None]
    d_lower = ring_scatter(grad_down_parts, "i")[None]
    d_mlp_router, d_mlp_from_router = gates_back(
        mlp_gate, mlp_onehot, d_mlp_gate, mlp_input, mlp_router
    )
    d_norm_two, d_gain_two = norm_back(
        middle, inverse_two, norm_gain2, d_mlp_input + d_mlp_from_router
    )
    d_middle = cotangent + d_norm_two
    summed_one = sum_all(
        jnp.concatenate(
            [
                jnp.stack([d_gain_two, jnp.sum(d_middle, axis=0), jnp.sum(cotangent, axis=0)]),
                d_mlp_router,
            ]
        )
    )

    all_mid = meet(d_middle.astype(BF16))
    d_out = mm("tf,td->fd", gated, all_mid).reshape(inner, -1, width)
    d_output = ring_scatter(from_order(d_out, "i"), "i")[None]
    d_rows = split_heads(mm("td,fd->tf", all_mid, out_mat))
    probs_full = probs()
    gate_b = gate_a[:, None, :, None]
    d_att = (d_rows * gate_b).astype(BF16)
    d_probs = mm("ghqd,ghkd->ghqk", d_rows.astype(BF16), value_rows)
    inner_sum = jnp.sum(probs_full * d_probs, axis=-1, keepdims=True)
    d_scores = (probs_full * (d_probs - inner_sum) * gate_b).astype(BF16)
    d_att_gate = from_experts(jnp.sum(inner_sum[..., 0], axis=1), att_onehot, experts)
    d_queries = mm("ghqk,ghkd->ghqd", d_scores, key_rows) * score_scale
    d_keys = mm("ghqk,ghqd->ghkd", d_scores, queries) * score_scale
    d_values = mm("ghqk,ghqd->ghkd", probs_full.astype(BF16), d_att)

    def join_heads(tensor):
        return tensor.astype(BF16).transpose(0, 2, 1, 3).reshape(blocks * tokens, span)

    d_qkv = jnp.concatenate(
        [
            join_heads(rotate_back(d_queries, cosine, sine_table)),
            join_heads(rotate_back(d_keys, cosine, sine_table)),
            join_heads(d_values),
        ],
        axis=1,
    )
    d_attn_input = part(mm("tf,df->td", d_qkv, slab).astype(BF16)).astype(F32)
    d_slab = mm("td,tf->df", all_attn, d_qkv)
    d_query = scatter_query(d_slab[:, :span])[None]
    d_kv_weight = scatter_kv(d_slab[:, span:])
    d_att_router, d_att_from_router = gates_back(
        att_gate, att_onehot, d_att_gate, attn_input, att_router
    )
    d_norm_one, d_gain_one = norm_back(
        residual, inverse_one, norm_gain1, d_attn_input + d_att_from_router
    )
    d_input = d_middle + d_norm_one
    summed_two = sum_all(jnp.concatenate([d_gain_one[None], d_att_router]))
    return (
        layer_out,
        d_input,
        summed_two[0],
        summed_one[0],
        summed_two[1:].T,
        summed_one[3:].T,
        d_kv_weight,
        d_query,
        d_output,
        summed_one[1],
        d_upper,
        d_lower,
        summed_one[2],
    )


def solution(mesh):
    experts, fsdp = mesh.shape["expert"], mesh.shape["fsdp"]
    fine = Mesh(mesh.devices.reshape(experts // 2, 2, OUTER, fsdp // OUTER), ALL)
    shard = ("o", "i")
    rows = P(ALL, None)
    placed = (
        rows,
        rows,
        rows,
        rows,
        P(),
        P(),
        P(),
        P(),
        rows,
        P(EXPERT, shard, None),
        P(EXPERT, shard, None),
        P(),
        P(EXPERT, None, shard, None),
        P(EXPERT, shard, None),
        P(),
        rows,
    )
    return jax.shard_map(
        shards,
        mesh=fine,
        in_specs=placed,
        out_specs=(
            rows,
            rows,
            P(),
            P(),
            P(),
            P(),
            rows,
            P(EXPERT, shard, None),
            P(EXPERT, shard, None),
            P(),
            P(EXPERT, None, shard, None),
            P(EXPERT, shard, None),
            P(),
        ),
        check_vma=False,
    )
```

```python
import functools
import math

import jax
import jax.numpy as jnp
from jax import lax
from jax.experimental import pallas as pl
from jax.experimental.pallas import tpu as pltpu
from jax.sharding import Mesh, PartitionSpec as P

HEADS = 16
HD = 128
TOP = 2


EPSILON = 1e-06
HIGHEST = lax.Precision.HIGHEST
MASKED = -1e30

GROUP = ("y", "c", "o")
EXPERT = ("y", "c")
ALL = ("y", "c", "o", "i")
OUTER = 4
F32 = jnp.float32
BF16 = jnp.bfloat16


def rope_tables(length):
    half_dim = HD // 2
    frequency = jnp.exp(jnp.arange(half_dim, dtype=F32) * (-2.0 * math.log(10000.0) / HD))
    angles = jnp.arange(length, dtype=F32)[:, None] * frequency[None, :]
    cosine, sine = jnp.cos(angles), jnp.sin(angles)
    return (
        jnp.concatenate([cosine, cosine], axis=1),
        jnp.concatenate([-sine, sine], axis=1),
    )


def norm_rows(stream, gain):
    inverse = lax.rsqrt(jnp.mean(stream * stream, axis=-1, keepdims=True) + EPSILON)
    return (stream * inverse * gain, inverse)


def norm_back(stream, inverse, gain, upstream):
    scaled = upstream * gain
    d_stream = inverse * scaled - stream * inverse**3 * jnp.mean(
        scaled * stream, axis=-1, keepdims=True
    )
    d_gain = jnp.sum(upstream * stream * inverse, axis=0)
    return (d_stream, d_gain)


def shift(value, axis):
    size = lax.axis_size(axis)
    return lax.ppermute(value, axis, [((k + 1) % size, k) for k in range(size)])


def ring_gather(value, axis):
    parts = [value]
    for _ in range(lax.axis_size(axis) - 1):
        parts.append(shift(parts[-1], axis))
    return parts


def ring_scatter(blocks, axis):
    size = lax.axis_size(axis)
    travelling = blocks[1].astype(BF16)
    for j in range(2, size):
        travelling = (shift(travelling, axis).astype(F32) + blocks[j]).astype(BF16)
    return shift(travelling, axis).astype(F32) + blocks[0]


def in_order(parts, axis):
    if len(parts) == 2:
        first = lax.axis_index(axis) == 0
        return jnp.stack([jnp.where(first, *parts), jnp.where(first, *parts[::-1])])
    return jnp.roll(jnp.stack(parts), lax.axis_index(axis), axis=0)


def from_order(parts, axis):
    if len(parts) == 2:
        first = lax.axis_index(axis) == 0
        return [jnp.where(first, *parts), jnp.where(first, *parts[::-1])]
    return list(jnp.roll(jnp.stack(parts), -lax.axis_index(axis), axis=0))


def sum_all(value):
    for axis in ALL:
        size = lax.axis_size(axis)
        step = 1
        while step < size:
            value = value + lax.ppermute(value, axis, [(k, k ^ step) for k in range(size)])
            step *= 2
    return value


def pair_gates(normed, router, route, experts):
    logits = jnp.dot(normed.astype(F32), router, precision=HIGHEST)
    onehot = (route[:, :, None] == jnp.arange(experts, dtype=jnp.int32)[None, None, :]).astype(F32)
    picked = jnp.sum(logits[:, None, :] * onehot, axis=-1)
    return (jax.nn.softmax(picked, axis=-1), onehot)


def gates_back(gates, onehot, d_gates, normed, router):
    d_picked = gates * (d_gates - jnp.sum(gates * d_gates, axis=-1, keepdims=True))
    d_logits = jnp.sum(d_picked[:, :, None] * onehot, axis=1)
    d_router = jnp.dot(d_logits.T, normed.astype(F32), precision=HIGHEST)
    d_normed = jnp.dot(d_logits, router.T, precision=HIGHEST)
    return (d_router, d_normed)


def to_experts(gates, onehot, extra):
    by_expert = jnp.sum(gates[:, :, None] * onehot, axis=1).T
    rows = jnp.repeat(by_expert, OUTER, axis=0)[:, None, :]
    if extra is not None:
        rows = jnp.concatenate(
            [rows, jnp.broadcast_to(extra[None, None, :], rows.shape)], axis=1
        )
    return lax.all_to_all(rows, GROUP, split_axis=0, concat_axis=0, tiled=True)


def from_experts(d_gates, onehot, experts):
    rows = lax.all_to_all(d_gates, GROUP, split_axis=0, concat_axis=0, tiled=True)
    by_expert = jnp.sum(rows.reshape(experts, OUTER, -1), axis=1)
    return jnp.einsum("tce,et->tc", onehot, by_expert, precision=HIGHEST)


def meet(rows):
    return lax.all_gather(rows, GROUP, axis=0, tiled=True)


def part(rows):
    return lax.psum_scatter(rows, GROUP, scatter_dimension=0, tiled=True)


def mm(form, first, second):
    return jnp.einsum(form, first, second, preferred_element_type=F32)


def head_columns(matrix):
    span = HEADS // OUTER * HD
    whole = HEADS * HD
    return [
        jnp.concatenate(
            [
                matrix[:, start + k * span : start + (k + 1) * span]
                for start in range(0, matrix.shape[1], whole)
            ],
            axis=1,
        )
        for k in range(OUTER)
    ]


def gather_rows(weight):
    inner = lax.axis_size("i")
    sent = jnp.stack([block for block in head_columns(weight) for _ in range(inner)])
    here = lax.all_to_all(sent, ("o", "i"), split_axis=0, concat_axis=0, tiled=True)
    return here.reshape(-1, here.shape[2])


def scatter_rows(grad):
    inner = lax.axis_size("i")
    sent = grad.astype(BF16).reshape(OUTER * inner, -1, grad.shape[1])
    here = lax.all_to_all(sent, ("o", "i"), split_axis=0, concat_axis=0, tiled=True)
    total = jnp.sum(here.reshape((OUTER, inner) + here.shape[1:]).astype(F32), axis=1)
    span = HEADS // OUTER * HD
    return jnp.concatenate(
        [
            total[k, :, start : start + span]
            for start in range(0, grad.shape[1], span)
            for k in range(OUTER)
        ],
        axis=1,
    )


def gather_kv(weight):
    here = gather_rows(weight)
    wide = here.shape[1]
    here = in_order(ring_gather(here, "y"), "y")
    whole = in_order(ring_gather(here, "c"), "c")
    return whole.transpose(1, 0, 2, 3).reshape(-1, wide)


def scatter_kv(grad):
    high = lax.axis_size("y")
    blocks = grad.reshape(high, 2, -1, grad.shape[1])
    mine = ring_scatter(from_order([blocks[:, 0], blocks[:, 1]], "c"), "c")
    mine = ring_scatter(from_order([mine[k] for k in range(high)], "y"), "y")
    return scatter_rows(mine)


VMEM = 56 * 1024 * 1024
SEQ_STEP = 4
ROW_STEP = 256


def nn(first, second):
    return jnp.dot(first, second, preferred_element_type=F32)


def nt(first, second):
    return lax.dot_general(first, second, (((1,), (1,)), ((), ())), preferred_element_type=F32)


def tn(first, second):
    return lax.dot_general(first, second, (((0,), (0,)), ((), ())), preferred_element_type=F32)


def as_column(row, rows):
    return jnp.broadcast_to(row, (rows, rows)).T[:, :1]


def turn(head, cosine, sine):
    return head * cosine + pltpu.roll(head, HD // 2, 1) * sine


def turn_back(head, cosine, sine):
    return head * cosine - pltpu.roll(head, HD // 2, 1) * sine


def allowed_keys(segment, length):
    keys = jnp.broadcast_to(segment, (length, length))
    row = lax.broadcasted_iota(jnp.int32, (length, length), 0)
    column = lax.broadcasted_iota(jnp.int32, (length, length), 1)
    return (keys == keys.T) & (column <= row)


def softmax_rows(queries, keys, allowed):
    scores = jnp.where(allowed, nt(queries, keys) * (1.0 / math.sqrt(HD)), MASKED)
    exponent = jnp.exp(scores - jnp.max(scores, axis=-1, keepdims=True))
    return exponent / jnp.sum(exponent, axis=-1, keepdims=True)


def attend_kernel(x_ref, info_ref, cos_ref, sin_ref, slab_ref, out_ref, qkv_ref, gated_ref, part_ref):
    length = cos_ref.shape[0]
    span = out_ref.shape[0]
    raw = nn(x_ref[...], slab_ref[...])
    cosine, sine = cos_ref[...], sin_ref[...]
    for seq in range(info_ref.shape[0]):
        rows = slice(seq * length, (seq + 1) * length)
        gate = as_column(info_ref[seq, 0:1, :], length)
        allowed = allowed_keys(info_ref[seq, 1:2, :], length)
        for start in range(0, span, HD):
            cols = slice(start, start + HD)
            key_cols = slice(span + start, span + start + HD)
            value_cols = slice(2 * span + start, 2 * span + start + HD)
            queries = turn(raw[rows, cols].astype(BF16).astype(F32), cosine, sine).astype(BF16)
            keys = turn(raw[rows, key_cols], cosine, sine).astype(BF16)
            values = raw[rows, value_cols].astype(BF16)
            qkv_ref[rows, cols] = queries
            qkv_ref[rows, key_cols] = keys
            qkv_ref[rows, value_cols] = values
            probs = softmax_rows(queries, keys, allowed)
            gated_ref[rows, cols] = (nn(probs.astype(BF16), values) * gate).astype(BF16)
    part_ref[...] = nn(gated_ref[...], out_ref[...]).astype(BF16)


def attend_back_kernel(
    mid_ref, info_ref, cos_ref, sin_ref, qkv_ref, slab_ref, out_ref, d_qkv_ref, part_ref, d_gate_ref
):
    length = cos_ref.shape[0]
    span = out_ref.shape[0]
    scale = 1.0 / math.sqrt(HD)
    d_rows = nt(mid_ref[...], out_ref[...])
    cosine, sine = cos_ref[...], sin_ref[...]
    for seq in range(info_ref.shape[0]):
        rows = slice(seq * length, (seq + 1) * length)
        gate = as_column(info_ref[seq, 0:1, :], length)
        allowed = allowed_keys(info_ref[seq, 1:2, :], length)
        d_gate = jnp.zeros((length, length), F32)
        for start in range(0, span, HD):
            cols = slice(start, start + HD)
            key_cols = slice(span + start, span + start + HD)
            value_cols = slice(2 * span + start, 2 * span + start + HD)
            queries, keys, values = qkv_ref[rows, cols], qkv_ref[rows, key_cols], qkv_ref[rows, value_cols]
            probs = softmax_rows(queries, keys, allowed)
            d_head = d_rows[rows, cols]
            weighted = probs * nt(d_head.astype(BF16), values)
            d_gate = d_gate + weighted
            d_scores = (
                (weighted - probs * jnp.sum(weighted, axis=-1, keepdims=True)) * gate
            ).astype(BF16)
            d_qkv_ref[rows, cols] = turn_back(nn(d_scores, keys) * scale, cosine, sine).astype(BF16)
            d_qkv_ref[rows, key_cols] = turn_back(
                tn(d_scores, queries) * scale, cosine, sine
            ).astype(BF16)
            d_qkv_ref[rows, value_cols] = tn(
                probs.astype(BF16), (d_head * gate).astype(BF16)
            ).astype(BF16)
        d_gate_ref[seq] = jnp.sum(d_gate.T, axis=0, keepdims=True)
    part_ref[...] = nt(d_qkv_ref[...], slab_ref[...]).astype(BF16)


def fixed(shape):
    return pl.BlockSpec(shape, lambda step: (0,) * len(shape))


def rows_spec(rows, columns):
    return pl.BlockSpec((rows, columns), lambda step: (step, 0))


def info_spec(seqs, kinds, length):
    return pl.BlockSpec((seqs, kinds, length), lambda step: (step, 0, 0))


def shape(dims, dtype=BF16):
    return jax.ShapeDtypeStruct(dims, dtype)


def attend(rows, info, cosine, sine, slab, out_mat):
    count, width = rows.shape
    length = cosine.shape[0]
    step = SEQ_STEP * length
    span = out_mat.shape[0]
    flops = 2 * count * width * 4 * span + 4 * count * length * span
    return pl.pallas_call(
        attend_kernel,
        grid=(count // step,),
        in_specs=[
            rows_spec(step, width),
            info_spec(SEQ_STEP, 2, length),
            fixed(cosine.shape),
            fixed(sine.shape),
            fixed(slab.shape),
            fixed(out_mat.shape),
        ],
        out_specs=[rows_spec(step, 3 * span), rows_spec(step, span), rows_spec(step, width)],
        out_shape=[shape((count, 3 * span)), shape((count, span)), shape((count, width))],
        compiler_params=pltpu.CompilerParams(vmem_limit_bytes=VMEM),
        cost_estimate=pl.CostEstimate(
            flops=flops, bytes_accessed=4 * count * (width + 2 * span), transcendentals=0
        ),
        name="attend",
    )(rows, info, cosine, sine, slab, out_mat)


def attend_back(d_middle, info, cosine, sine, qkv, slab, out_mat):
    count, width = d_middle.shape
    length = cosine.shape[0]
    step = SEQ_STEP * length
    span = out_mat.shape[0]
    flops = 2 * count * width * 4 * span + 10 * count * length * span
    return pl.pallas_call(
        attend_back_kernel,
        grid=(count // step,),
        in_specs=[
            rows_spec(step, width),
            info_spec(SEQ_STEP, 2, length),
            fixed(cosine.shape),
            fixed(sine.shape),
            rows_spec(step, 3 * span),
            fixed(slab.shape),
            fixed(out_mat.shape),
        ],
        out_specs=[rows_spec(step, 3 * span), rows_spec(step, width), info_spec(SEQ_STEP, 1, length)],
        out_shape=[
            shape((count, 3 * span)),
            shape((count, width)),
            shape((count // length, 1, length), F32),
        ],
        compiler_params=pltpu.CompilerParams(vmem_limit_bytes=VMEM),
        cost_estimate=pl.CostEstimate(
            flops=flops, bytes_accessed=4 * count * (width + 3 * span), transcendentals=0
        ),
        name="attend_back",
    )(d_middle, info, cosine, sine, qkv, slab, out_mat)


def units_kernel(parts, x_ref, info_ref, *refs):
    d_units_refs, up_refs = refs[:parts], refs[parts : 2 * parts]
    d_both_refs, gated_refs = refs[2 * parts : 3 * parts], refs[3 * parts : 4 * parts]
    back_ref, d_gate_ref = refs[4 * parts :]
    length = info_ref.shape[2]
    rows = x_ref[...]
    gate = jnp.concatenate(
        [as_column(info_ref[seq], length) for seq in range(info_ref.shape[0])], axis=0
    )
    back = jnp.zeros(back_ref.shape, F32)
    d_gate = jnp.zeros((rows.shape[0], 1), F32)
    for part in range(parts):
        up_ref = up_refs[part]
        units = up_ref.shape[0] // 2
        gate_in = nt(rows, up_ref[:units])
        up_in = nt(rows, up_ref[units:])
        sigma = jax.nn.sigmoid(gate_in)
        active = gate_in * sigma
        hidden_units = active * up_in
        d_units = d_units_refs[part][...].astype(F32)
        d_gate = d_gate + jnp.sum(hidden_units * d_units, axis=-1, keepdims=True)
        gated_refs[part][...] = (hidden_units * gate).astype(BF16)
        d_units = d_units * gate
        d_first = (d_units * up_in * (sigma + active * (1.0 - sigma))).astype(BF16)
        d_second = (d_units * active).astype(BF16)
        d_both_refs[part][:, :units] = d_first
        d_both_refs[part][:, units:] = d_second
        back = back + nn(d_first, up_ref[:units]) + nn(d_second, up_ref[units:])
    back_ref[...] = back.astype(BF16)
    for seq in range(info_ref.shape[0]):
        column = jnp.broadcast_to(d_gate[seq * length : (seq + 1) * length], (length, length))
        d_gate_ref[seq] = column.T[:1]


def run_units(rows, info, d_units, up_parts):
    count, width = rows.shape
    length = info.shape[2]
    parts = len(up_parts)
    units = d_units[0].shape[1]
    seqs = ROW_STEP // length
    return pl.pallas_call(
        functools.partial(units_kernel, parts),
        grid=(count // ROW_STEP,),
        in_specs=[rows_spec(ROW_STEP, width), info_spec(seqs, 1, length)]
        + [rows_spec(ROW_STEP, units)] * parts
        + [fixed(up.shape) for up in up_parts],
        out_specs=[rows_spec(ROW_STEP, 2 * units)] * parts
        + [rows_spec(ROW_STEP, units)] * parts
        + [rows_spec(ROW_STEP, width), info_spec(seqs, 1, length)],
        out_shape=[shape((count, 2 * units))] * parts
        + [shape((count, units))] * parts
        + [shape((count, width)), shape((count // length, 1, length), F32)],
        compiler_params=pltpu.CompilerParams(vmem_limit_bytes=VMEM),
        cost_estimate=pl.CostEstimate(
            flops=8 * count * width * units * parts,
            bytes_accessed=4 * count * (width + 2 * units * parts),
            transcendentals=0,
        ),
        name="units",
    )(rows, info, *d_units, *up_parts)


def shards(
    hidden_in,
    segment_ids,
    att_route,
    mlp_route,
    norm_gain1,
    norm_gain2,
    att_router,
    mlp_router,
    kv_weight,
    query_weight,
    out_weight,
    att_bias,
    up_weight,
    down_weight,
    mlp_bias,
    cotangent,
):
    experts = lax.axis_size(EXPERT)
    inner = lax.axis_size("i")
    tokens, width = hidden_in.shape
    span = HEADS // OUTER * HD
    cosine, sine_table = rope_tables(tokens)

    kv_mat = gather_kv(kv_weight)
    query_mat = gather_rows(query_weight[0])
    slab = jnp.concatenate([query_mat, kv_mat], axis=1)
    out_mat = in_order(ring_gather(out_weight[0], "i"), "i").reshape(span, width)
    down_parts = ring_gather(down_weight[0], "i")
    up_parts = ring_gather(up_weight[0].reshape(-1, width), "i")

    residual = hidden_in.astype(F32)
    normed_one, inverse_one = norm_rows(residual, norm_gain1)
    attn_input = normed_one.astype(BF16)
    att_gate, att_onehot = pair_gates(attn_input, att_router, att_route, experts)
    info = to_experts(att_gate, att_onehot, segment_ids[0].astype(F32))
    all_attn = meet(attn_input)
    cot_low, all_attn_seen = lax.optimization_barrier((cotangent.astype(BF16), all_attn[:8, :128]))
    all_cot = meet(cot_low)
    qkv, gated, branch = attend(all_attn, info, cosine, sine_table, slab, out_mat)
    branch, all_cot = lax.optimization_barrier((branch, all_cot))
    branch = part(branch)

    middle = residual + branch.astype(F32) + att_bias
    normed_two, inverse_two = norm_rows(middle, norm_gain2)
    mlp_input = normed_two.astype(BF16)
    mlp_gate, mlp_onehot = pair_gates(mlp_input, mlp_router, mlp_route, experts)
    gate_m = to_experts(mlp_gate, mlp_onehot, None)
    all_mlp = meet(mlp_input)
    d_units = [mm("td,fd->tf", all_cot, down).astype(BF16) for down in down_parts]
    found = run_units(all_mlp, gate_m, d_units, up_parts)
    d_both, gated_units = found[:inner], found[inner : 2 * inner]
    rows_back, d_gate_m = found[2 * inner :]
    d_mlp_input = part(rows_back)
    gated_units, d_both, d_mlp_input = lax.optimization_barrier((gated_units, d_both, d_mlp_input))
    d_mlp_input = d_mlp_input.astype(F32)
    d_mlp_gate = from_experts(d_gate_m[:, 0], mlp_onehot, experts)
    d_mlp_router, d_mlp_from_router = gates_back(
        mlp_gate, mlp_onehot, d_mlp_gate, mlp_input, mlp_router
    )
    d_norm_two, d_gain_two = norm_back(
        middle, inverse_two, norm_gain2, d_mlp_input + d_mlp_from_router
    )
    d_middle = cotangent + d_norm_two
    summed_one = sum_all(
        jnp.concatenate(
            [
                jnp.stack([d_gain_two, jnp.sum(d_middle, axis=0), jnp.sum(cotangent, axis=0)]),
                d_mlp_router,
            ]
        )
    )

    all_mid = meet(d_middle.astype(BF16))
    d_qkv, rows_one, d_gate_a = attend_back(
        all_mid, info, cosine, sine_table, qkv, slab, out_mat
    )
    d_attn_input = part(rows_one).astype(F32)
    d_att_gate = from_experts(d_gate_a[:, 0], att_onehot, experts)
    rows_out = None
    for units_here, down in zip(gated_units, down_parts):
        ahead = mm("tf,fd->td", units_here, down)
        rows_out = ahead if rows_out is None else rows_out + ahead
    layer_out = middle + part(rows_out.astype(BF16)).astype(F32) + mlp_bias
    d_upper = ring_scatter([mm("tf,td->fd", d_here, all_mlp) for d_here in d_both], "i")
    d_upper = d_upper.reshape(up_weight.shape)
    d_lower = ring_scatter([mm("tf,td->fd", here, all_cot) for here in gated_units], "i")[None]
    d_out = mm("tf,td->fd", gated, all_mid).reshape(inner, -1, width)
    d_output = ring_scatter(from_order([d_out[k] for k in range(inner)], "i"), "i")[None]
    d_slab = mm("td,tf->df", all_attn, d_qkv)
    d_query = scatter_rows(d_slab[:, :span])[None]
    d_kv_weight = scatter_kv(d_slab[:, span:])
    d_att_router, d_att_from_router = gates_back(
        att_gate, att_onehot, d_att_gate, attn_input, att_router
    )
    d_norm_one, d_gain_one = norm_back(
        residual, inverse_one, norm_gain1, d_attn_input + d_att_from_router
    )
    d_input = d_middle + d_norm_one
    summed_two = sum_all(jnp.concatenate([d_gain_one[None], d_att_router]))
    return (
        layer_out,
        d_input,
        summed_two[0],
        summed_one[0],
        summed_two[1:].T,
        summed_one[3:].T,
        d_kv_weight,
        d_query,
        d_output,
        summed_one[1],
        d_upper,
        d_lower,
        summed_one[2],
    )


def solution(mesh):
    experts, fsdp = mesh.shape["expert"], mesh.shape["fsdp"]
    fine = Mesh(mesh.devices.reshape(experts // 2, 2, OUTER, fsdp // OUTER), ALL)
    shard = ("o", "i")
    rows = P(ALL, None)
    placed = (
        rows,
        rows,
        rows,
        rows,
        P(),
        P(),
        P(),
        P(),
        rows,
        P(EXPERT, shard, None),
        P(EXPERT, shard, None),
        P(),
        P(EXPERT, None, shard, None),
        P(EXPERT, shard, None),
        P(),
        rows,
    )
    return jax.shard_map(
        shards,
        mesh=fine,
        in_specs=placed,
        out_specs=(
            rows,
            rows,
            P(),
            P(),
            P(),
            P(),
            rows,
            P(EXPERT, shard, None),
            P(EXPERT, shard, None),
            P(),
            P(EXPERT, None, shard, None),
            P(EXPERT, shard, None),
            P(),
        ),
        check_vma=False,
    )
```

```python
import functools
import math

import jax
import jax.numpy as jnp
from jax import lax
from jax.experimental import pallas as pl
from jax.experimental.pallas import tpu as pltpu
from jax.sharding import Mesh, PartitionSpec as P

HEADS = 16
HD = 128
TOP = 2


EPSILON = 1e-06
HIGHEST = lax.Precision.HIGHEST
MASKED = -1e30

GROUP = ("y", "c", "o")
EXPERT = ("y", "c")
ALL = ("y", "c", "o", "i")
OUTER = 4
F32 = jnp.float32
BF16 = jnp.bfloat16


def rope_tables(length):
    half_dim = HD // 2
    frequency = jnp.exp(jnp.arange(half_dim, dtype=F32) * (-2.0 * math.log(10000.0) / HD))
    angles = jnp.arange(length, dtype=F32)[:, None] * frequency[None, :]
    cosine, sine = jnp.cos(angles), jnp.sin(angles)
    return (
        jnp.concatenate([cosine, cosine], axis=1),
        jnp.concatenate([-sine, sine], axis=1),
    )


def norm_rows(stream, gain):
    inverse = lax.rsqrt(jnp.mean(stream * stream, axis=-1, keepdims=True) + EPSILON)
    return (stream * inverse * gain, inverse)


def norm_back(stream, inverse, gain, upstream):
    scaled = upstream * gain
    d_stream = inverse * scaled - stream * inverse**3 * jnp.mean(
        scaled * stream, axis=-1, keepdims=True
    )
    d_gain = jnp.sum(upstream * stream * inverse, axis=0)
    return (d_stream, d_gain)


def shift(value, axis):
    size = lax.axis_size(axis)
    return lax.ppermute(value, axis, [((k + 1) % size, k) for k in range(size)])


def ring_gather(value, axis):
    parts = [value]
    for _ in range(lax.axis_size(axis) - 1):
        parts.append(shift(parts[-1], axis))
    return parts


def ring_scatter(blocks, axis):
    size = lax.axis_size(axis)
    travelling = blocks[1].astype(BF16)
    for j in range(2, size):
        travelling = (shift(travelling, axis).astype(F32) + blocks[j]).astype(BF16)
    return shift(travelling, axis).astype(F32) + blocks[0]


def in_order(parts, axis, place=0):
    if len(parts) == 2:
        first = lax.axis_index(axis) == 0
        return jnp.stack([jnp.where(first, *parts), jnp.where(first, *parts[::-1])], axis=place)
    return jnp.roll(jnp.stack(parts, axis=place), lax.axis_index(axis), axis=place)


def from_order(parts, axis):
    if len(parts) == 2:
        first = lax.axis_index(axis) == 0
        return [jnp.where(first, *parts), jnp.where(first, *parts[::-1])]
    return list(jnp.roll(jnp.stack(parts), -lax.axis_index(axis), axis=0))


def sum_all(value):
    for axis in ALL:
        size = lax.axis_size(axis)
        step = 1
        while step < size:
            value = value + lax.ppermute(value, axis, [(k, k ^ step) for k in range(size)])
            step *= 2
    return value


def pair_gates(normed, router, route, experts):
    logits = jnp.dot(normed.astype(F32), router, precision=HIGHEST)
    onehot = (route[:, :, None] == jnp.arange(experts, dtype=jnp.int32)[None, None, :]).astype(F32)
    picked = jnp.sum(logits[:, None, :] * onehot, axis=-1)
    return (jax.nn.softmax(picked, axis=-1), onehot)


def gates_back(gates, onehot, d_gates, normed, router):
    d_picked = gates * (d_gates - jnp.sum(gates * d_gates, axis=-1, keepdims=True))
    d_logits = jnp.sum(d_picked[:, :, None] * onehot, axis=1)
    d_router = jnp.dot(d_logits.T, normed.astype(F32), precision=HIGHEST)
    d_normed = jnp.dot(d_logits, router.T, precision=HIGHEST)
    return (d_router, d_normed)


def to_experts(gates, onehot, extra):
    by_expert = jnp.sum(gates[:, :, None] * onehot, axis=1).T
    rows = jnp.repeat(by_expert, OUTER, axis=0)[:, None, :]
    if extra is not None:
        rows = jnp.concatenate(
            [rows, jnp.broadcast_to(extra[None, None, :], rows.shape)], axis=1
        )
    return lax.all_to_all(rows, GROUP, split_axis=0, concat_axis=0, tiled=True)


def from_experts(d_gates, onehot, experts):
    rows = lax.all_to_all(d_gates, GROUP, split_axis=0, concat_axis=0, tiled=True)
    by_expert = jnp.sum(rows.reshape(experts, OUTER, -1), axis=1)
    return jnp.einsum("tce,et->tc", onehot, by_expert, precision=HIGHEST)


def meet(rows):
    return lax.all_gather(rows, GROUP, axis=0, tiled=True)


def part(rows):
    return lax.psum_scatter(rows, GROUP, scatter_dimension=0, tiled=True)


def mm(form, first, second):
    return jnp.einsum(form, first, second, preferred_element_type=F32)


def head_columns(matrix):
    span = HEADS // OUTER * HD
    whole = HEADS * HD
    return [
        jnp.concatenate(
            [
                matrix[:, start + k * span : start + (k + 1) * span]
                for start in range(0, matrix.shape[1], whole)
            ],
            axis=1,
        )
        for k in range(OUTER)
    ]


def gather_heads(weight):
    return lax.all_to_all(
        jnp.stack(head_columns(weight)), "o", split_axis=0, concat_axis=0, tiled=True
    )


def gather_query(weight):
    parts = ring_gather(gather_heads(weight), "i")
    return in_order(parts, "i", 1).reshape(-1, parts[0].shape[2])


def scatter_rows(grad):
    inner = lax.axis_size("i")
    blocks = grad.reshape(OUTER, inner, -1, grad.shape[1])
    blocks = from_order([blocks[:, k] for k in range(inner)], "i")
    mine = ring_scatter(blocks, "i").astype(BF16)
    here = lax.all_to_all(mine, "o", split_axis=0, concat_axis=0, tiled=True).astype(F32)
    span = HEADS // OUTER * HD
    return jnp.concatenate(
        [
            here[k, :, start : start + span]
            for start in range(0, grad.shape[1], span)
            for k in range(OUTER)
        ],
        axis=1,
    )


def gather_kv(weight):
    here = ring_gather(gather_heads(weight), "y")
    here = ring_gather(jnp.stack(here), "i")
    here = ring_gather(jnp.stack(here), "c")
    whole = in_order([in_order([in_order(list(one), "y", 0) for one in two], "i", 2) for two in here], "c", 1)
    return whole.reshape(-1, whole.shape[-1])


def scatter_kv(grad):
    high = lax.axis_size("y")
    blocks = grad.reshape(high, 2, -1, grad.shape[1])
    mine = ring_scatter(from_order([blocks[:, 0], blocks[:, 1]], "c"), "c")
    mine = ring_scatter(from_order([mine[k] for k in range(high)], "y"), "y")
    return scatter_rows(mine)


def own_places():
    return jnp.stack([lax.axis_index(axis) for axis in GROUP]).astype(jnp.int32)


def add_low(first, second):
    return (first.astype(F32) + second.astype(F32)).astype(BF16)


def ring_low(blocks, axis):
    travelling = blocks[1]
    for j in range(2, lax.axis_size(axis)):
        travelling = add_low(shift(travelling, axis), blocks[j])
    return add_low(shift(travelling, axis), blocks[0])


def part_by_rings(rows):
    rows = ring_low([rows[k] for k in range(rows.shape[0])], "c")
    half = rows.shape[2] // 2
    first, second = rows[:, :, :half], rows[:, :, half:]
    first = ring_low([first[k] for k in range(first.shape[0])], "y")
    first = ring_low([first[k] for k in range(first.shape[0])], "o")
    second = ring_low([second[:, k] for k in range(second.shape[1])], "o")
    second = ring_low([second[k] for k in range(second.shape[0])], "y")
    return jnp.concatenate([first, second])


VMEM = 56 * 1024 * 1024
ROW_STEP = 256


def nn(first, second):
    return jnp.dot(first, second, preferred_element_type=F32)


def nt(first, second):
    return lax.dot_general(first, second, (((1,), (1,)), ((), ())), preferred_element_type=F32)


def tn(first, second):
    return lax.dot_general(first, second, (((0,), (0,)), ((), ())), preferred_element_type=F32)


def as_column(row, rows):
    return jnp.broadcast_to(row, (rows, rows)).T[:, :1]


def turn(head, cosine, sine):
    return head * cosine + pltpu.roll(head, HD // 2, 1) * sine


def turn_back(head, cosine, sine):
    return head * cosine - pltpu.roll(head, HD // 2, 1) * sine


def allowed_keys(segment, length):
    keys = jnp.broadcast_to(segment, (length, length))
    row = lax.broadcasted_iota(jnp.int32, (length, length), 0)
    column = lax.broadcasted_iota(jnp.int32, (length, length), 1)
    return (keys == keys.T) & (column <= row)


def heads_nt(first, second):
    return lax.dot_general(first, second, (((2,), (2,)), ((0,), (0,))), preferred_element_type=F32)


def heads_nn(first, second):
    return lax.dot_general(first, second, (((2,), (1,)), ((0,), (0,))), preferred_element_type=F32)


def heads_tn(first, second):
    return lax.dot_general(first, second, (((1,), (1,)), ((0,), (0,))), preferred_element_type=F32)


def softmax_rows(queries, keys, allowed):
    scores = jnp.where(allowed[None], heads_nt(queries, keys) * (1.0 / math.sqrt(HD)), MASKED)
    exponent = jnp.exp(scores - jnp.max(scores, axis=-1, keepdims=True))
    return exponent / jnp.sum(exponent, axis=-1, keepdims=True)


def place_rows(places_ref, part_ref, value, first, length):
    count = part_ref.shape[2]
    for seq in range(value.shape[0] // length):
        slot = lax.rem(first + seq - places_ref[2] + count, count)
        part_ref[0, 0, slot] = value[seq * length : (seq + 1) * length]


def attend_kernel(
    places_ref, x_ref, info_ref, cos_ref, sin_ref, slab_ref, out_ref, qkv_ref, gated_ref, part_ref
):
    length = cos_ref.shape[0]
    span = out_ref.shape[0]
    raw = nn(x_ref[...], slab_ref[...])
    cosine, sine = cos_ref[...], sin_ref[...]
    starts = range(0, span, HD)
    for seq in range(info_ref.shape[0]):
        rows = slice(seq * length, (seq + 1) * length)
        gate = as_column(info_ref[seq, 0:1, :], length)
        allowed = allowed_keys(info_ref[seq, 1:2, :], length)
        queries, keys, values = [], [], []
        for at in starts:
            head = raw[rows, at : at + HD].astype(BF16).astype(F32)
            queries.append(turn(head, cosine, sine).astype(BF16))
            keys.append(turn(raw[rows, span + at : span + at + HD], cosine, sine).astype(BF16))
            values.append(raw[rows, 2 * span + at : 2 * span + at + HD].astype(BF16))
            qkv_ref[rows, at : at + HD] = queries[-1]
            qkv_ref[rows, span + at : span + at + HD] = keys[-1]
            qkv_ref[rows, 2 * span + at : 2 * span + at + HD] = values[-1]
        probs = softmax_rows(jnp.stack(queries), jnp.stack(keys), allowed)
        gated = (heads_nn(probs.astype(BF16), jnp.stack(values)) * gate[None]).astype(BF16)
        for number, at in enumerate(starts):
            gated_ref[rows, at : at + HD] = gated[number]
    place_rows(places_ref, part_ref, nn(gated_ref[...], out_ref[...]).astype(BF16), 0, length)


def attend_back_kernel(
    places_ref,
    mid_ref,
    info_ref,
    cos_ref,
    sin_ref,
    qkv_ref,
    x_ref,
    slab_ref,
    out_ref,
    d_qkv_ref,
    part_ref,
    d_gate_ref,
    d_gain_ref,
):
    length = cos_ref.shape[0]
    span = out_ref.shape[0]
    scale = 1.0 / math.sqrt(HD)
    d_rows = nt(mid_ref[...], out_ref[...])
    cosine, sine = cos_ref[...], sin_ref[...]
    starts = range(0, span, HD)
    for seq in range(info_ref.shape[0]):
        rows = slice(seq * length, (seq + 1) * length)
        gate = as_column(info_ref[seq, 0:1, :], length)[None]
        allowed = allowed_keys(info_ref[seq, 1:2, :], length)
        queries = jnp.stack([qkv_ref[rows, at : at + HD] for at in starts])
        keys = jnp.stack([qkv_ref[rows, span + at : span + at + HD] for at in starts])
        values = jnp.stack([qkv_ref[rows, 2 * span + at : 2 * span + at + HD] for at in starts])
        d_heads = jnp.stack([d_rows[rows, at : at + HD] for at in starts])
        probs = softmax_rows(queries, keys, allowed)
        weighted = probs * heads_nt(d_heads.astype(BF16), values)
        sums = jnp.sum(weighted, axis=-1, keepdims=True)
        d_scores = ((weighted - probs * sums) * gate).astype(BF16)
        d_queries = heads_nn(d_scores, keys) * scale
        d_keys = heads_tn(d_scores, queries) * scale
        d_values = heads_tn(probs.astype(BF16), (d_heads * gate).astype(BF16))
        for number, at in enumerate(starts):
            d_qkv_ref[rows, at : at + HD] = turn_back(d_queries[number], cosine, sine).astype(BF16)
            d_qkv_ref[rows, span + at : span + at + HD] = turn_back(
                d_keys[number], cosine, sine
            ).astype(BF16)
            d_qkv_ref[rows, 2 * span + at : 2 * span + at + HD] = d_values[number].astype(BF16)
        total = jnp.broadcast_to(jnp.sum(sums, axis=0), (length, length))
        d_gate_ref[seq] = total.T[:1]
    d_input = nt(d_qkv_ref[...], slab_ref[...])

    @pl.when(pl.program_id(0) == 0)
    def _():
        d_gain_ref[...] = jnp.zeros_like(d_gain_ref)

    d_gain_ref[...] += jnp.sum(d_input * x_ref[...].astype(F32), axis=0, keepdims=True)
    place_rows(places_ref, part_ref, d_input.astype(BF16), 0, length)


def fixed(shape):
    return pl.BlockSpec(shape, lambda step, places: (0,) * len(shape))


def rows_spec(rows, columns):
    return pl.BlockSpec((rows, columns), lambda step, places: (step, 0))


def info_spec(seqs, kinds, length):
    return pl.BlockSpec((seqs, kinds, length), lambda step, places: (step, 0, 0))


def place_spec(high, length, width, steps):
    def index(step, places):
        pair = lax.div(step, steps)
        low = lax.rem(lax.rem(pair, 2) - places[1] + 2, 2)
        return (low, lax.rem(lax.div(pair, 2) - places[0] + high, high), 0, 0, 0)

    return pl.BlockSpec((1, 1, OUTER, length, width), index)


def shape(dims, dtype=BF16):
    return jax.ShapeDtypeStruct(dims, dtype)


def call(kernel, name, steps, in_specs, out_specs, out_shape, flops, moved, operands):
    return pl.pallas_call(
        kernel,
        grid_spec=pltpu.PrefetchScalarGridSpec(
            num_scalar_prefetch=1, grid=(steps,), in_specs=in_specs, out_specs=out_specs
        ),
        out_shape=out_shape,
        compiler_params=pltpu.CompilerParams(vmem_limit_bytes=VMEM),
        cost_estimate=pl.CostEstimate(flops=flops, bytes_accessed=moved, transcendentals=0),
        name=name,
    )(*operands)


def attend(places, rows, info, cosine, sine, slab, out_mat):
    count, width = rows.shape
    length = cosine.shape[0]
    step = OUTER * length
    span = out_mat.shape[0]
    high = count // (2 * step)
    return call(
        attend_kernel,
        "attend",
        count // step,
        [
            rows_spec(step, width),
            info_spec(OUTER, 2, length),
            fixed(cosine.shape),
            fixed(sine.shape),
            fixed(slab.shape),
            fixed(out_mat.shape),
        ],
        [rows_spec(step, 3 * span), rows_spec(step, span), place_spec(high, length, width, 1)],
        [shape((count, 3 * span)), shape((count, span)), shape((2, high, OUTER, length, width))],
        2 * count * width * 4 * span + 4 * count * length * span,
        4 * count * (width + 2 * span),
        (places, rows, info, cosine, sine, slab, out_mat),
    )


def attend_back(places, d_middle, info, cosine, sine, qkv, rows, slab, out_mat):
    count, width = d_middle.shape
    length = cosine.shape[0]
    step = OUTER * length
    span = out_mat.shape[0]
    high = count // (2 * step)
    return call(
        attend_back_kernel,
        "attend_back",
        count // step,
        [
            rows_spec(step, width),
            info_spec(OUTER, 2, length),
            fixed(cosine.shape),
            fixed(sine.shape),
            rows_spec(step, 3 * span),
            rows_spec(step, width),
            fixed(slab.shape),
            fixed(out_mat.shape),
        ],
        [
            rows_spec(step, 3 * span),
            place_spec(high, length, width, 1),
            info_spec(OUTER, 1, length),
            fixed((1, width)),
        ],
        [
            shape((count, 3 * span)),
            shape((2, high, OUTER, length, width)),
            shape((count // length, 1, length), F32),
            shape((1, width), F32),
        ],
        2 * count * width * 4 * span + 10 * count * length * span,
        4 * count * (2 * width + 3 * span),
        (places, d_middle, info, cosine, sine, qkv, rows, slab, out_mat),
    )


def units_kernel(parts, places_ref, x_ref, info_ref, *refs):
    d_units_refs, up_refs = refs[:parts], refs[parts : 3 * parts]
    d_both_refs, gated_refs = refs[3 * parts : 4 * parts], refs[4 * parts : 5 * parts]
    back_ref, d_gate_ref = refs[5 * parts :]
    length = info_ref.shape[2]
    seqs = info_ref.shape[0]
    rows = x_ref[...]
    gate = jnp.concatenate([as_column(info_ref[seq], length) for seq in range(seqs)], axis=0)
    back = jnp.zeros((seqs * length, back_ref.shape[-1]), F32)
    d_gate = jnp.zeros((seqs * length, 1), F32)
    for part in range(parts):
        first_ref, second_ref = up_refs[2 * part : 2 * part + 2]
        units = first_ref.shape[0]
        gate_in = nt(rows, first_ref[...])
        up_in = nt(rows, second_ref[...])
        sigma = jax.nn.sigmoid(gate_in)
        active = gate_in * sigma
        hidden_units = active * up_in
        d_units = d_units_refs[part][...].astype(F32)
        d_gate = d_gate + jnp.sum(hidden_units * d_units, axis=-1, keepdims=True)
        gated_refs[part][...] = (hidden_units * gate).astype(BF16)
        d_units = d_units * gate
        d_first = (d_units * up_in * (sigma + active * (1.0 - sigma))).astype(BF16)
        d_second = (d_units * active).astype(BF16)
        d_both_refs[part][:, :units] = d_first
        d_both_refs[part][:, units:] = d_second
        back = back + nn(d_first, first_ref[...]) + nn(d_second, second_ref[...])
    first = lax.rem(pl.program_id(0), OUTER // seqs) * seqs
    place_rows(places_ref, back_ref, back.astype(BF16), first, length)
    for seq in range(seqs):
        column = jnp.broadcast_to(d_gate[seq * length : (seq + 1) * length], (length, length))
        d_gate_ref[seq] = column.T[:1]


def run_units(places, rows, info, d_units, own_up, other_up):
    count, width = rows.shape
    length = info.shape[2]
    parts = 1 + len(other_up) // 2
    units = d_units[0].shape[1]
    seqs = ROW_STEP // length
    high = count // (2 * OUTER * length)
    own_specs = [
        pl.BlockSpec((units, width), lambda step, places, half=half: (half, 0)) for half in range(2)
    ]
    return call(
        functools.partial(units_kernel, parts),
        "units",
        count // ROW_STEP,
        [rows_spec(ROW_STEP, width), info_spec(seqs, 1, length)]
        + [rows_spec(ROW_STEP, units)] * parts
        + own_specs
        + [fixed(one.shape) for one in other_up],
        [rows_spec(ROW_STEP, 2 * units)] * parts
        + [rows_spec(ROW_STEP, units)] * parts
        + [place_spec(high, length, width, OUTER // seqs), info_spec(seqs, 1, length)],
        [shape((count, 2 * units))] * parts
        + [shape((count, units))] * parts
        + [
            shape((2, high, OUTER, length, width)),
            shape((count // length, 1, length), F32),
        ],
        8 * count * width * units * parts,
        4 * count * (width + 2 * units * parts),
        (places, rows, info, *d_units, own_up, own_up, *other_up),
    )


def shards(
    hidden_in,
    segment_ids,
    att_route,
    mlp_route,
    norm_gain1,
    norm_gain2,
    att_router,
    mlp_router,
    kv_weight,
    query_weight,
    out_weight,
    att_bias,
    up_weight,
    down_weight,
    mlp_bias,
    cotangent,
):
    experts = lax.axis_size(EXPERT)
    inner = lax.axis_size("i")
    tokens, width = hidden_in.shape
    span = HEADS // OUTER * HD
    cosine, sine_table = rope_tables(tokens)

    places = own_places()
    tie = lax.optimization_barrier

    kv_mat = gather_kv(kv_weight)
    query_mat = gather_query(query_weight[0])
    slab = jnp.concatenate([query_mat, kv_mat], axis=1)
    out_mat = in_order(ring_gather(out_weight[0], "i"), "i").reshape(span, width)
    own_up = up_weight[0].reshape(-1, width)
    down_source, _ = tie((down_weight[0], slab))
    down_parts = ring_gather(down_source, "i")

    residual = hidden_in.astype(F32)
    normed_one, inverse_one = norm_rows(residual, norm_gain1)
    attn_input = normed_one.astype(BF16)
    att_gate, att_onehot = pair_gates(attn_input, att_router, att_route, experts)
    info = to_experts(att_gate, att_onehot, segment_ids[0].astype(F32))
    all_attn = meet(attn_input)
    cot_low, all_attn = tie((cotangent.astype(BF16), all_attn))
    all_cot = meet(cot_low)
    qkv, gated, branch = attend(places, all_attn, info, cosine, sine_table, slab, out_mat)
    branch = part_by_rings(branch)

    branch, down_parts, all_cot = tie((branch, down_parts, all_cot))
    first_source, _ = tie((up_weight[0, 0], down_parts[-1]))
    first_parts = ring_gather(first_source, "i")
    middle = residual + branch.astype(F32) + att_bias
    normed_two, inverse_two = norm_rows(middle, norm_gain2)
    mlp_input = normed_two.astype(BF16)
    mlp_gate, mlp_onehot = pair_gates(mlp_input, mlp_router, mlp_route, experts)
    mlp_input, first_parts = tie((mlp_input, first_parts))
    second_source, _ = tie((up_weight[0, 1], first_parts[-1]))
    second_parts = ring_gather(second_source, "i")
    gate_m = to_experts(mlp_gate, mlp_onehot, None)
    all_mlp = meet(mlp_input)
    d_units = [mm("td,fd->tf", all_cot, down).astype(BF16) for down in down_parts]
    other_up = [one for pair in zip(first_parts[1:], second_parts[1:]) for one in pair]
    found = run_units(places, all_mlp, gate_m, d_units, own_up, other_up)
    d_both, gated_units = found[:inner], found[inner : 2 * inner]
    rows_back, d_gate_m = found[2 * inner :]
    d_mlp_gate = from_experts(d_gate_m[:, 0], mlp_onehot, experts)
    d_mlp_input = part_by_rings(rows_back).astype(F32)
    d_mlp_router, d_mlp_from_router = gates_back(
        mlp_gate, mlp_onehot, d_mlp_gate, mlp_input, mlp_router
    )
    d_norm_two, d_gain_two = norm_back(
        middle, inverse_two, norm_gain2, d_mlp_input + d_mlp_from_router
    )
    d_middle = cotangent + d_norm_two
    summed_one = sum_all(
        jnp.concatenate(
            [
                jnp.stack([d_gain_two, jnp.sum(d_middle, axis=0), jnp.sum(cotangent, axis=0)]),
                d_mlp_router,
            ]
        )
    )
    d_upper = ring_scatter([mm("tf,td->fd", d_here, all_mlp) for d_here in d_both], "i")
    d_upper = d_upper.reshape(up_weight.shape)
    d_lower = ring_scatter([mm("tf,td->fd", here, all_cot) for here in gated_units], "i")[None]
    rows_out = None
    for units_here, down in zip(gated_units, down_parts):
        ahead = mm("tf,fd->td", units_here, down)
        rows_out = ahead if rows_out is None else rows_out + ahead
    rows_out = rows_out.astype(BF16)

    all_mid = meet(d_middle.astype(BF16))
    rows_out, all_mid = tie((rows_out, all_mid))
    layer_out = middle + part(rows_out).astype(F32) + mlp_bias
    d_qkv, rows_one, d_gate_a, d_gain_a = attend_back(
        places, all_mid, info, cosine, sine_table, qkv, all_attn, slab, out_mat
    )
    d_att_gate = from_experts(d_gate_a[:, 0], att_onehot, experts)
    d_attn_input = part_by_rings(rows_one).astype(F32)
    d_out = mm("tf,td->fd", gated, all_mid).reshape(inner, -1, width)
    d_output = ring_scatter(from_order([d_out[k] for k in range(inner)], "i"), "i")[None]
    d_slab = mm("td,tf->df", all_attn, d_qkv)
    d_query = scatter_rows(d_slab[:, :span])[None]
    d_kv_weight = scatter_kv(d_slab[:, span:])
    d_att_router, d_att_from_router = gates_back(
        att_gate, att_onehot, d_att_gate, attn_input, att_router
    )
    d_norm_one, _ = norm_back(
        residual, inverse_one, norm_gain1, d_attn_input + d_att_from_router
    )
    d_gain_one = d_gain_a / norm_gain1 + jnp.sum(
        d_att_from_router * residual * inverse_one, axis=0, keepdims=True
    )
    d_input = d_middle + d_norm_one
    summed_two = sum_all(jnp.concatenate([d_gain_one, d_att_router]))
    return (
        layer_out,
        d_input,
        summed_two[0],
        summed_one[0],
        summed_two[1:].T,
        summed_one[3:].T,
        d_kv_weight,
        d_query,
        d_output,
        summed_one[1],
        d_upper,
        d_lower,
        summed_one[2],
    )


def solution(mesh):
    experts, fsdp = mesh.shape["expert"], mesh.shape["fsdp"]
    fine = Mesh(mesh.devices.reshape(experts // 2, 2, OUTER, fsdp // OUTER), ALL)
    shard = ("o", "i")
    rows = P(ALL, None)
    placed = (
        rows,
        rows,
        rows,
        rows,
        P(),
        P(),
        P(),
        P(),
        rows,
        P(EXPERT, shard, None),
        P(EXPERT, shard, None),
        P(),
        P(EXPERT, None, shard, None),
        P(EXPERT, shard, None),
        P(),
        rows,
    )
    return jax.shard_map(
        shards,
        mesh=fine,
        in_specs=placed,
        out_specs=(
            rows,
            rows,
            P(),
            P(),
            P(),
            P(),
            rows,
            P(EXPERT, shard, None),
            P(EXPERT, shard, None),
            P(),
            P(EXPERT, None, shard, None),
            P(EXPERT, shard, None),
            P(),
        ),
        check_vma=False,
    )
```

```python
import functools
import math

import jax
import jax.numpy as jnp
from jax import lax
from jax.experimental import pallas as pl
from jax.experimental.pallas import tpu as pltpu
from jax.sharding import Mesh, PartitionSpec as P

HEADS = 16
HD = 128
TOP = 2


EPSILON = 1e-06
HIGHEST = lax.Precision.HIGHEST
MASKED = -1e30

GROUP = ("y", "c", "o")
EXPERT = ("y", "c")
ALL = ("y", "c", "o", "i")
OUTER = 4
F32 = jnp.float32
BF16 = jnp.bfloat16


def rope_tables(length):
    half_dim = HD // 2
    frequency = jnp.exp(jnp.arange(half_dim, dtype=F32) * (-2.0 * math.log(10000.0) / HD))
    angles = jnp.arange(length, dtype=F32)[:, None] * frequency[None, :]
    cosine, sine = jnp.cos(angles), jnp.sin(angles)
    return (
        jnp.concatenate([cosine, cosine], axis=1),
        jnp.concatenate([-sine, sine], axis=1),
    )


def norm_rows(stream, gain):
    inverse = lax.rsqrt(jnp.mean(stream * stream, axis=-1, keepdims=True) + EPSILON)
    return (stream * inverse * gain, inverse)


def norm_back(stream, inverse, gain, upstream):
    scaled = upstream * gain
    d_stream = inverse * scaled - stream * inverse**3 * jnp.mean(
        scaled * stream, axis=-1, keepdims=True
    )
    d_gain = jnp.sum(upstream * stream * inverse, axis=0)
    return (d_stream, d_gain)


def shift(value, axis):
    size = lax.axis_size(axis)
    return lax.ppermute(value, axis, [((k + 1) % size, k) for k in range(size)])


def ring_gather(value, axis):
    parts = [value]
    for _ in range(lax.axis_size(axis) - 1):
        parts.append(shift(parts[-1], axis))
    return parts


def ring_scatter(blocks, axis, after=None):
    size = lax.axis_size(axis)
    travelling = blocks[1].astype(BF16)
    for j in range(2, size):
        travelling = (shift(travelling, axis).astype(F32) + blocks[j]).astype(BF16)
    arrived = shift(travelling, axis)
    if after is not None:
        arrived, _ = lax.optimization_barrier((arrived, after))
    return arrived.astype(F32) + blocks[0]


def in_order(parts, axis, place=0):
    if len(parts) == 2:
        first = lax.axis_index(axis) == 0
        return jnp.stack([jnp.where(first, *parts), jnp.where(first, *parts[::-1])], axis=place)
    return jnp.roll(jnp.stack(parts, axis=place), lax.axis_index(axis), axis=place)


def from_order(parts, axis):
    if len(parts) == 2:
        first = lax.axis_index(axis) == 0
        return [jnp.where(first, *parts), jnp.where(first, *parts[::-1])]
    return list(jnp.roll(jnp.stack(parts), -lax.axis_index(axis), axis=0))


def sum_all(value):
    for axis in ALL:
        size = lax.axis_size(axis)
        step = 1
        while step < size:
            value = value + lax.ppermute(value, axis, [(k, k ^ step) for k in range(size)])
            step *= 2
    return value


def pair_gates(normed, router, route, experts):
    logits = jnp.dot(normed.astype(F32), router, precision=HIGHEST)
    onehot = (route[:, :, None] == jnp.arange(experts, dtype=jnp.int32)[None, None, :]).astype(F32)
    picked = jnp.sum(logits[:, None, :] * onehot, axis=-1)
    return (jax.nn.softmax(picked, axis=-1), onehot)


def gates_back(gates, onehot, d_gates, normed, router):
    d_picked = gates * (d_gates - jnp.sum(gates * d_gates, axis=-1, keepdims=True))
    d_logits = jnp.sum(d_picked[:, :, None] * onehot, axis=1)
    d_router = jnp.dot(d_logits.T, normed.astype(F32), precision=HIGHEST)
    d_normed = jnp.dot(d_logits, router.T, precision=HIGHEST)
    return (d_router, d_normed)


def to_experts(gates, onehot, extra):
    by_expert = jnp.sum(gates[:, :, None] * onehot, axis=1).T
    rows = jnp.repeat(by_expert, OUTER, axis=0)[:, None, :]
    if extra is not None:
        rows = jnp.concatenate(
            [rows, jnp.broadcast_to(extra[None, None, :], rows.shape)], axis=1
        )
    return lax.all_to_all(rows, GROUP, split_axis=0, concat_axis=0, tiled=True)


def from_experts(d_gates, onehot, experts):
    rows = lax.all_to_all(d_gates, GROUP, split_axis=0, concat_axis=0, tiled=True)
    by_expert = jnp.sum(rows.reshape(experts, OUTER, -1), axis=1)
    return jnp.einsum("tce,et->tc", onehot, by_expert, precision=HIGHEST)


def meet(rows):
    return lax.all_gather(rows, GROUP, axis=0, tiled=True)


def part(rows):
    return lax.psum_scatter(rows, GROUP, scatter_dimension=0, tiled=True)


def mm(form, first, second):
    return jnp.einsum(form, first, second, preferred_element_type=F32)


def head_columns(matrix):
    span = HEADS // OUTER * HD
    whole = HEADS * HD
    return [
        jnp.concatenate(
            [
                matrix[:, start + k * span : start + (k + 1) * span]
                for start in range(0, matrix.shape[1], whole)
            ],
            axis=1,
        )
        for k in range(OUTER)
    ]


def gather_heads(weight):
    parts = ring_gather(weight, "i")
    sent = in_order([jnp.stack(head_columns(one)) for one in parts], "i", 1)
    here = lax.all_to_all(sent, "o", split_axis=0, concat_axis=0, tiled=True)
    return here.reshape(-1, here.shape[-1])


def scatter_rows(grad):
    inner = lax.axis_size("i")
    blocks = grad.reshape(OUTER, inner, -1, grad.shape[1])
    blocks = from_order([blocks[:, k] for k in range(inner)], "i")
    mine = ring_scatter(blocks, "i").astype(BF16)
    here = lax.all_to_all(mine, "o", split_axis=0, concat_axis=0, tiled=True).astype(F32)
    span = HEADS // OUTER * HD
    return jnp.concatenate(
        [
            here[k, :, start : start + span]
            for start in range(0, grad.shape[1], span)
            for k in range(OUTER)
        ],
        axis=1,
    )


def gather_kv(rows):
    here = ring_gather(jnp.stack(ring_gather(rows, "y")), "c")
    whole = in_order([in_order(list(one), "y", 0) for one in here], "c", 1)
    return whole.reshape(-1, whole.shape[-1])


def scatter_kv(grad):
    high = lax.axis_size("y")
    blocks = grad.reshape(high, 2, -1, grad.shape[1])
    mine = ring_scatter(from_order([blocks[:, 0], blocks[:, 1]], "c"), "c")
    mine = ring_scatter(from_order([mine[k] for k in range(high)], "y"), "y")
    return scatter_rows(mine)


def own_places():
    return jnp.stack([lax.axis_index(axis) for axis in GROUP]).astype(jnp.int32)


def add_low(first, second):
    return (first.astype(F32) + second.astype(F32)).astype(BF16)


def ring_low(blocks, axis):
    travelling = blocks[1]
    for j in range(2, lax.axis_size(axis)):
        travelling = add_low(shift(travelling, axis), blocks[j])
    return add_low(shift(travelling, axis), blocks[0])


def part_by_rings(rows):
    half = rows.shape[2] // 2
    first, second = rows[:, :, :half], rows[:, :, half:]
    first = ring_low([first[k] for k in range(first.shape[0])], "y")
    first = ring_low([first[k] for k in range(first.shape[0])], "o")
    second = ring_low([second[:, k] for k in range(second.shape[1])], "o")
    second = ring_low([second[k] for k in range(second.shape[0])], "y")
    return jnp.concatenate([first, second])


VMEM = 56 * 1024 * 1024
ROW_STEP = 256


def nn(first, second):
    return jnp.dot(first, second, preferred_element_type=F32)


def nt(first, second):
    return lax.dot_general(first, second, (((1,), (1,)), ((), ())), preferred_element_type=F32)


def tn(first, second):
    return lax.dot_general(first, second, (((0,), (0,)), ((), ())), preferred_element_type=F32)


def as_column(row, rows):
    return jnp.broadcast_to(row, (rows, rows)).T[:, :1]


def turn(head, cosine, sine):
    return head * cosine + pltpu.roll(head, HD // 2, 1) * sine


def turn_back(head, cosine, sine):
    return head * cosine - pltpu.roll(head, HD // 2, 1) * sine


def allowed_keys(segment, length):
    keys = jnp.broadcast_to(segment, (length, length))
    row = lax.broadcasted_iota(jnp.int32, (length, length), 0)
    column = lax.broadcasted_iota(jnp.int32, (length, length), 1)
    return (keys == keys.T) & (column <= row)


def heads_nt(first, second):
    return lax.dot_general(first, second, (((2,), (2,)), ((0,), (0,))), preferred_element_type=F32)


def heads_nn(first, second):
    return lax.dot_general(first, second, (((2,), (1,)), ((0,), (0,))), preferred_element_type=F32)


def heads_tn(first, second):
    return lax.dot_general(first, second, (((1,), (1,)), ((0,), (0,))), preferred_element_type=F32)


def softmax_rows(queries, keys, allowed):
    scores = jnp.where(allowed[None], heads_nt(queries, keys) * (1.0 / math.sqrt(HD)), MASKED)
    exponent = jnp.exp(scores - jnp.max(scores, axis=-1, keepdims=True))
    return exponent / jnp.sum(exponent, axis=-1, keepdims=True)


def place_rows(places_ref, part_ref, value, length):
    count = part_ref.shape[2]
    for seq in range(count):
        slot = lax.rem(seq - places_ref[2] + count, count)
        part_ref[0, 0, slot] = value[seq * length : (seq + 1) * length]


def attend_kernel(
    places_ref, x_ref, info_ref, cos_ref, sin_ref, slab_ref, out_ref, qkv_ref, gated_ref, part_ref
):
    del places_ref
    length = cos_ref.shape[0]
    span = out_ref.shape[0]
    raw = nn(x_ref[...], slab_ref[...])
    cosine, sine = cos_ref[...], sin_ref[...]
    starts = range(0, span, HD)
    for seq in range(info_ref.shape[0]):
        rows = slice(seq * length, (seq + 1) * length)
        gate = as_column(info_ref[seq, 0:1, :], length)
        allowed = allowed_keys(info_ref[seq, 1:2, :], length)
        queries, keys, values = [], [], []
        for at in starts:
            head = raw[rows, at : at + HD].astype(BF16).astype(F32)
            queries.append(turn(head, cosine, sine).astype(BF16))
            keys.append(turn(raw[rows, span + at : span + at + HD], cosine, sine).astype(BF16))
            values.append(raw[rows, 2 * span + at : 2 * span + at + HD].astype(BF16))
            qkv_ref[rows, at : at + HD] = queries[-1]
            qkv_ref[rows, span + at : span + at + HD] = keys[-1]
            qkv_ref[rows, 2 * span + at : 2 * span + at + HD] = values[-1]
        probs = softmax_rows(jnp.stack(queries), jnp.stack(keys), allowed)
        gated = (heads_nn(probs.astype(BF16), jnp.stack(values)) * gate[None]).astype(BF16)
        for number, at in enumerate(starts):
            gated_ref[rows, at : at + HD] = gated[number]
    part_ref[...] = nn(gated_ref[...], out_ref[...]).astype(BF16)


def attend_back_kernel(
    places_ref,
    mid_ref,
    info_ref,
    cos_ref,
    sin_ref,
    qkv_ref,
    x_ref,
    slab_ref,
    out_ref,
    d_qkv_ref,
    part_ref,
    d_gate_ref,
    d_gain_ref,
):
    length = cos_ref.shape[0]
    span = out_ref.shape[0]
    scale = 1.0 / math.sqrt(HD)
    d_rows = nt(mid_ref[...], out_ref[...])
    cosine, sine = cos_ref[...], sin_ref[...]
    starts = range(0, span, HD)
    for seq in range(info_ref.shape[0]):
        rows = slice(seq * length, (seq + 1) * length)
        gate = as_column(info_ref[seq, 0:1, :], length)[None]
        allowed = allowed_keys(info_ref[seq, 1:2, :], length)
        queries = jnp.stack([qkv_ref[rows, at : at + HD] for at in starts])
        keys = jnp.stack([qkv_ref[rows, span + at : span + at + HD] for at in starts])
        values = jnp.stack([qkv_ref[rows, 2 * span + at : 2 * span + at + HD] for at in starts])
        d_heads = jnp.stack([d_rows[rows, at : at + HD] for at in starts])
        probs = softmax_rows(queries, keys, allowed)
        weighted = probs * heads_nt(d_heads.astype(BF16), values)
        sums = jnp.sum(weighted, axis=-1, keepdims=True)
        d_scores = ((weighted - probs * sums) * gate).astype(BF16)
        d_queries = heads_nn(d_scores, keys) * scale
        d_keys = heads_tn(d_scores, queries) * scale
        d_values = heads_tn(probs.astype(BF16), (d_heads * gate).astype(BF16))
        for number, at in enumerate(starts):
            d_qkv_ref[rows, at : at + HD] = turn_back(d_queries[number], cosine, sine).astype(BF16)
            d_qkv_ref[rows, span + at : span + at + HD] = turn_back(
                d_keys[number], cosine, sine
            ).astype(BF16)
            d_qkv_ref[rows, 2 * span + at : 2 * span + at + HD] = d_values[number].astype(BF16)
        total = jnp.broadcast_to(jnp.sum(sums, axis=0), (length, length))
        d_gate_ref[seq] = total.T[:1]
    d_input = nt(d_qkv_ref[...], slab_ref[...])

    @pl.when(pl.program_id(0) == 0)
    def _():
        d_gain_ref[...] = jnp.zeros_like(d_gain_ref)

    d_gain_ref[...] += jnp.sum(d_input * x_ref[...].astype(F32), axis=0, keepdims=True)
    place_rows(places_ref, part_ref, d_input.astype(BF16), length)


def fixed(shape):
    return pl.BlockSpec(shape, lambda step, places: (0,) * len(shape))


def rows_spec(rows, columns):
    return pl.BlockSpec((rows, columns), lambda step, places: (step, 0))


def info_spec(seqs, kinds, length):
    return pl.BlockSpec((seqs, kinds, length), lambda step, places: (step, 0, 0))


def place_spec(high, length, width):
    def index(step, places):
        low = lax.rem(lax.rem(step, 2) - places[1] + 2, 2)
        return (low, lax.rem(lax.div(step, 2) - places[0] + high, high), 0, 0, 0)

    return pl.BlockSpec((1, 1, OUTER, length, width), index)


def shape(dims, dtype=BF16):
    return jax.ShapeDtypeStruct(dims, dtype)


def call(kernel, name, steps, in_specs, out_specs, out_shape, flops, moved, operands):
    return pl.pallas_call(
        kernel,
        grid_spec=pltpu.PrefetchScalarGridSpec(
            num_scalar_prefetch=1, grid=(steps,), in_specs=in_specs, out_specs=out_specs
        ),
        out_shape=out_shape,
        compiler_params=pltpu.CompilerParams(vmem_limit_bytes=VMEM),
        cost_estimate=pl.CostEstimate(flops=flops, bytes_accessed=moved, transcendentals=0),
        name=name,
    )(*operands)


def attend(places, rows, info, cosine, sine, slab, out_mat):
    count, width = rows.shape
    length = cosine.shape[0]
    step = OUTER * length
    span = out_mat.shape[0]
    return call(
        attend_kernel,
        "attend",
        count // step,
        [
            rows_spec(step, width),
            info_spec(OUTER, 2, length),
            fixed(cosine.shape),
            fixed(sine.shape),
            fixed(slab.shape),
            fixed(out_mat.shape),
        ],
        [rows_spec(step, 3 * span), rows_spec(step, span), rows_spec(step, width)],
        [shape((count, 3 * span)), shape((count, span)), shape((count, width))],
        2 * count * width * 4 * span + 4 * count * length * span,
        4 * count * (width + 2 * span),
        (places, rows, info, cosine, sine, slab, out_mat),
    )


def attend_back(places, d_middle, info, cosine, sine, qkv, rows, slab, out_mat):
    count, width = d_middle.shape
    length = cosine.shape[0]
    step = OUTER * length
    span = out_mat.shape[0]
    high = count // (2 * step)
    return call(
        attend_back_kernel,
        "attend_back",
        count // step,
        [
            rows_spec(step, width),
            info_spec(OUTER, 2, length),
            fixed(cosine.shape),
            fixed(sine.shape),
            rows_spec(step, 3 * span),
            rows_spec(step, width),
            fixed(slab.shape),
            fixed(out_mat.shape),
        ],
        [
            rows_spec(step, 3 * span),
            place_spec(high, length, width),
            info_spec(OUTER, 1, length),
            fixed((1, width)),
        ],
        [
            shape((count, 3 * span)),
            shape((2, high, OUTER, length, width)),
            shape((count // length, 1, length), F32),
            shape((1, width), F32),
        ],
        2 * count * width * 4 * span + 10 * count * length * span,
        4 * count * (2 * width + 3 * span),
        (places, d_middle, info, cosine, sine, qkv, rows, slab, out_mat),
    )


def units_kernel(parts, places_ref, x_ref, info_ref, *refs):
    del places_ref
    d_units_refs, up_refs = refs[:parts], refs[parts : 3 * parts]
    d_both_refs, gated_refs = refs[3 * parts : 4 * parts], refs[4 * parts : 5 * parts]
    back_ref, d_gate_ref = refs[5 * parts :]
    length = info_ref.shape[2]
    seqs = info_ref.shape[0]
    rows = x_ref[...]
    gate = jnp.concatenate([as_column(info_ref[seq], length) for seq in range(seqs)], axis=0)
    back = jnp.zeros((seqs * length, back_ref.shape[-1]), F32)
    d_gate = jnp.zeros((seqs * length, 1), F32)
    for part in range(parts):
        first_ref, second_ref = up_refs[2 * part : 2 * part + 2]
        units = first_ref.shape[0]
        gate_in = nt(rows, first_ref[...])
        up_in = nt(rows, second_ref[...])
        sigma = jax.nn.sigmoid(gate_in)
        active = gate_in * sigma
        hidden_units = active * up_in
        d_units = d_units_refs[part][...].astype(F32)
        d_gate = d_gate + jnp.sum(hidden_units * d_units, axis=-1, keepdims=True)
        gated_refs[part][...] = (hidden_units * gate).astype(BF16)
        d_units = d_units * gate
        d_first = (d_units * up_in * (sigma + active * (1.0 - sigma))).astype(BF16)
        d_second = (d_units * active).astype(BF16)
        d_both_refs[part][:, :units] = d_first
        d_both_refs[part][:, units:] = d_second
        back = back + nn(d_first, first_ref[...]) + nn(d_second, second_ref[...])
    back_ref[...] = back.astype(BF16)
    for seq in range(seqs):
        column = jnp.broadcast_to(d_gate[seq * length : (seq + 1) * length], (length, length))
        d_gate_ref[seq] = column.T[:1]


def run_units(places, rows, info, d_units, own_up, other_up):
    count, width = rows.shape
    length = info.shape[2]
    parts = 1 + len(other_up) // 2
    units = d_units[0].shape[1]
    seqs = ROW_STEP // length
    own_specs = [
        pl.BlockSpec((units, width), lambda step, places, half=half: (half, 0)) for half in range(2)
    ]
    return call(
        functools.partial(units_kernel, parts),
        "units",
        count // ROW_STEP,
        [rows_spec(ROW_STEP, width), info_spec(seqs, 1, length)]
        + [rows_spec(ROW_STEP, units)] * parts
        + own_specs
        + [fixed(one.shape) for one in other_up],
        [rows_spec(ROW_STEP, 2 * units)] * parts
        + [rows_spec(ROW_STEP, units)] * parts
        + [rows_spec(ROW_STEP, width), info_spec(seqs, 1, length)],
        [shape((count, 2 * units))] * parts
        + [shape((count, units))] * parts
        + [shape((count, width)), shape((count // length, 1, length), F32)],
        8 * count * width * units * parts,
        4 * count * (width + 2 * units * parts),
        (places, rows, info, *d_units, own_up, own_up, *other_up),
    )


def shards(
    hidden_in,
    segment_ids,
    att_route,
    mlp_route,
    norm_gain1,
    norm_gain2,
    att_router,
    mlp_router,
    kv_weight,
    query_weight,
    out_weight,
    att_bias,
    up_weight,
    down_weight,
    mlp_bias,
    cotangent,
):
    experts = lax.axis_size(EXPERT)
    inner = lax.axis_size("i")
    tokens, width = hidden_in.shape
    span = HEADS // OUTER * HD
    cosine, sine_table = rope_tables(tokens)

    places = own_places()
    tie = lax.optimization_barrier

    kv_rows = gather_heads(kv_weight)
    kv_mat = gather_kv(kv_rows)
    query_mat = gather_heads(query_weight[0])
    slab = jnp.concatenate([query_mat, kv_mat], axis=1)
    out_source, _ = tie((out_weight[0], kv_rows))
    out_parts = ring_gather(out_source, "i")
    out_mat = in_order(out_parts, "i").reshape(span, width)
    own_up = up_weight[0].reshape(-1, width)
    down_source, _ = tie((down_weight[0], out_parts[-1]))
    down_parts = ring_gather(down_source, "i")

    residual = hidden_in.astype(F32)
    normed_one, inverse_one = norm_rows(residual, norm_gain1)
    attn_input = normed_one.astype(BF16)
    att_gate, att_onehot = pair_gates(attn_input, att_router, att_route, experts)
    info = to_experts(att_gate, att_onehot, segment_ids[0].astype(F32))
    all_attn = meet(attn_input)
    cot_low, _ = tie((cotangent.astype(BF16), kv_rows))
    all_cot = meet(cot_low)
    slab, down_parts = tie((slab, down_parts))
    qkv, gated, branch = attend(places, all_attn, info, cosine, sine_table, slab, out_mat)
    first_source, branch = tie((up_weight[0, 0], branch))
    first_parts = ring_gather(first_source, "i")
    branch = part(branch)

    all_cot, first_parts = tie((all_cot, first_parts))
    d_units = [mm("td,fd->tf", all_cot, down).astype(BF16) for down in down_parts]
    branch, d_units = tie((branch, d_units))
    middle = residual + branch.astype(F32) + att_bias
    normed_two, inverse_two = norm_rows(middle, norm_gain2)
    mlp_input = normed_two.astype(BF16)
    mlp_gate, mlp_onehot = pair_gates(mlp_input, mlp_router, mlp_route, experts)
    second_source, mlp_input = tie((up_weight[0, 1], mlp_input))
    second_parts = ring_gather(second_source, "i")
    all_mlp = meet(mlp_input)
    gate_m = to_experts(mlp_gate, mlp_onehot, None)
    gate_m, second_parts = tie((gate_m, second_parts))
    other_up = [one for pair in zip(first_parts[1:], second_parts[1:]) for one in pair]
    found = run_units(places, all_mlp, gate_m, d_units, own_up, other_up)
    d_both, gated_units = found[:inner], found[inner : 2 * inner]
    rows_back, d_gate_m = found[2 * inner :]
    d_mlp_input = part(rows_back)
    d_mlp_gate = from_experts(d_gate_m[:, 0], mlp_onehot, experts)
    grad_up = [mm("tf,td->fd", d_here, all_mlp) for d_here in d_both]
    grad_down = [mm("tf,td->fd", here, all_cot) for here in gated_units]
    rows_out = None
    for units_here, down in zip(gated_units, down_parts):
        ahead = mm("tf,fd->td", units_here, down)
        rows_out = ahead if rows_out is None else rows_out + ahead
    rows_out = rows_out.astype(BF16)
    d_mlp_router, d_mlp_from_router = gates_back(
        mlp_gate, mlp_onehot, d_mlp_gate, mlp_input, mlp_router
    )
    d_norm_two, d_gain_two = norm_back(
        middle, inverse_two, norm_gain2, d_mlp_input.astype(F32) + d_mlp_from_router
    )
    d_middle = cotangent + d_norm_two
    summed_one = sum_all(
        jnp.concatenate(
            [
                jnp.stack([d_gain_two, jnp.sum(d_middle, axis=0), jnp.sum(cotangent, axis=0)]),
                d_mlp_router,
            ]
        )
    )

    all_mid = meet(d_middle.astype(BF16))
    rows_out, all_mid = tie((rows_out, all_mid))
    d_qkv, rows_one, d_gate_a, d_gain_a = attend_back(
        places, all_mid, info, cosine, sine_table, qkv, all_attn, slab, out_mat
    )
    rows_one = ring_low([rows_one[0], rows_one[1]], "c")
    d_qkv, rows_one = tie((d_qkv, rows_one))
    d_attn_input = part_by_rings(rows_one).astype(F32)
    d_att_gate = from_experts(d_gate_a[:, 0], att_onehot, experts)
    d_slab = mm("td,tf->df", all_attn, d_qkv)
    d_query = scatter_rows(d_slab[:, :span])[None]
    d_kv_weight = scatter_kv(d_slab[:, span:])
    d_out = mm("tf,td->fd", gated, all_mid).reshape(inner, -1, width)
    d_output = ring_scatter(from_order([d_out[k] for k in range(inner)], "i"), "i")[None]
    layer_out = middle + part(rows_out).astype(F32) + mlp_bias
    d_upper = ring_scatter(grad_up, "i", d_attn_input)
    d_upper = d_upper.reshape(up_weight.shape)
    d_lower = ring_scatter(grad_down, "i", d_attn_input)[None]
    d_att_router, d_att_from_router = gates_back(
        att_gate, att_onehot, d_att_gate, attn_input, att_router
    )
    d_norm_one, _ = norm_back(
        residual, inverse_one, norm_gain1, d_attn_input + d_att_from_router
    )
    d_gain_one = d_gain_a / norm_gain1 + jnp.sum(
        d_att_from_router * residual * inverse_one, axis=0, keepdims=True
    )
    d_input = d_middle + d_norm_one
    summed_two = sum_all(jnp.concatenate([d_gain_one, d_att_router]))
    return (
        layer_out,
        d_input,
        summed_two[0],
        summed_one[0],
        summed_two[1:].T,
        summed_one[3:].T,
        d_kv_weight,
        d_query,
        d_output,
        summed_one[1],
        d_upper,
        d_lower,
        summed_one[2],
    )


def solution(mesh):
    experts, fsdp = mesh.shape["expert"], mesh.shape["fsdp"]
    fine = Mesh(mesh.devices.reshape(experts // 2, 2, OUTER, fsdp // OUTER), ALL)
    shard = ("o", "i")
    rows = P(ALL, None)
    placed = (
        rows,
        rows,
        rows,
        rows,
        P(),
        P(),
        P(),
        P(),
        rows,
        P(EXPERT, shard, None),
        P(EXPERT, shard, None),
        P(),
        P(EXPERT, None, shard, None),
        P(EXPERT, shard, None),
        P(),
        rows,
    )
    return jax.shard_map(
        shards,
        mesh=fine,
        in_specs=placed,
        out_specs=(
            rows,
            rows,
            P(),
            P(),
            P(),
            P(),
            rows,
            P(EXPERT, shard, None),
            P(EXPERT, shard, None),
            P(),
            P(EXPERT, None, shard, None),
            P(EXPERT, shard, None),
            P(),
        ),
        check_vma=False,
    )
```

```python
import functools
import math

import jax
import jax.numpy as jnp
from jax import lax
from jax.experimental import pallas as pl
from jax.experimental.pallas import tpu as pltpu
from jax.sharding import Mesh, PartitionSpec as P

HEADS = 16
HD = 128
TOP = 2


EPSILON = 1e-06
HIGHEST = lax.Precision.HIGHEST
MASKED = -1e30

GROUP = ("y", "c", "o")
EXPERT = ("y", "c")
ALL = ("y", "c", "o", "i")
OUTER = 4
F32 = jnp.float32
BF16 = jnp.bfloat16


def rope_tables(length):
    half_dim = HD // 2
    frequency = jnp.exp(jnp.arange(half_dim, dtype=F32) * (-2.0 * math.log(10000.0) / HD))
    angles = jnp.arange(length, dtype=F32)[:, None] * frequency[None, :]
    cosine, sine = jnp.cos(angles), jnp.sin(angles)
    return (
        jnp.concatenate([cosine, cosine], axis=1),
        jnp.concatenate([-sine, sine], axis=1),
    )


def norm_rows(stream, gain):
    inverse = lax.rsqrt(jnp.mean(stream * stream, axis=-1, keepdims=True) + EPSILON)
    return (stream * inverse * gain, inverse)


def norm_back(stream, inverse, gain, upstream):
    scaled = upstream * gain
    d_stream = inverse * scaled - stream * inverse**3 * jnp.mean(
        scaled * stream, axis=-1, keepdims=True
    )
    d_gain = jnp.sum(upstream * stream * inverse, axis=0)
    return (d_stream, d_gain)


def shift(value, axis):
    size = lax.axis_size(axis)
    return lax.ppermute(value, axis, [((k + 1) % size, k) for k in range(size)])


def ring_gather(value, axis):
    parts = [value]
    for _ in range(lax.axis_size(axis) - 1):
        parts.append(shift(parts[-1], axis))
    return parts


def ring_scatter(blocks, axis, after=None):
    size = lax.axis_size(axis)
    travelling = blocks[1].astype(BF16)
    for j in range(2, size):
        travelling = (shift(travelling, axis).astype(F32) + blocks[j]).astype(BF16)
    arrived = shift(travelling, axis)
    if after is not None:
        arrived, _ = lax.optimization_barrier((arrived, after))
    return arrived.astype(F32) + blocks[0]


def in_order(parts, axis, place=0):
    if len(parts) == 2:
        first = lax.axis_index(axis) == 0
        return jnp.stack([jnp.where(first, *parts), jnp.where(first, *parts[::-1])], axis=place)
    return jnp.roll(jnp.stack(parts, axis=place), lax.axis_index(axis), axis=place)


def from_order(parts, axis):
    if len(parts) == 2:
        first = lax.axis_index(axis) == 0
        return [jnp.where(first, *parts), jnp.where(first, *parts[::-1])]
    return list(jnp.roll(jnp.stack(parts), -lax.axis_index(axis), axis=0))


def sum_all(value):
    for axis in ALL:
        size = lax.axis_size(axis)
        step = 1
        while step < size:
            value = value + lax.ppermute(value, axis, [(k, k ^ step) for k in range(size)])
            step *= 2
    return value


def pair_gates(normed, router, route, experts):
    logits = jnp.dot(normed.astype(F32), router, precision=HIGHEST)
    onehot = (route[:, :, None] == jnp.arange(experts, dtype=jnp.int32)[None, None, :]).astype(F32)
    picked = jnp.sum(logits[:, None, :] * onehot, axis=-1)
    return (jax.nn.softmax(picked, axis=-1), onehot)


def gates_back(gates, onehot, d_gates, normed, router):
    d_picked = gates * (d_gates - jnp.sum(gates * d_gates, axis=-1, keepdims=True))
    d_logits = jnp.sum(d_picked[:, :, None] * onehot, axis=1)
    d_router = jnp.dot(d_logits.T, normed.astype(F32), precision=HIGHEST)
    d_normed = jnp.dot(d_logits, router.T, precision=HIGHEST)
    return (d_router, d_normed)


def to_experts(gates, onehot, extra):
    by_expert = jnp.sum(gates[:, :, None] * onehot, axis=1).T
    rows = jnp.repeat(by_expert, OUTER, axis=0)[:, None, :]
    if extra is not None:
        rows = jnp.concatenate(
            [rows, jnp.broadcast_to(extra[None, None, :], rows.shape)], axis=1
        )
    return lax.all_to_all(rows, GROUP, split_axis=0, concat_axis=0, tiled=True)


def from_experts(d_gates, onehot, experts):
    rows = lax.all_to_all(d_gates, GROUP, split_axis=0, concat_axis=0, tiled=True)
    by_expert = jnp.sum(rows.reshape(experts, OUTER, -1), axis=1)
    return jnp.einsum("tce,et->tc", onehot, by_expert, precision=HIGHEST)


def meet(rows):
    return lax.all_gather(rows, GROUP, axis=0, tiled=True)


def part(rows):
    return lax.psum_scatter(rows, GROUP, scatter_dimension=0, tiled=True)


def mm(form, first, second):
    return jnp.einsum(form, first, second, preferred_element_type=F32)


def head_blocks(matrix):
    span = HEADS // OUTER * HD
    return jnp.stack([matrix[:, k * span : (k + 1) * span] for k in range(OUTER)])


def join_blocks(blocks):
    return jnp.concatenate([blocks[k] for k in range(OUTER)], axis=1)


def exchange(blocks):
    return lax.all_to_all(blocks, "o", split_axis=0, concat_axis=0, tiled=True)


def gather_heads(places, query_weight, kv_weight):
    whole = HEADS * HD
    rows = query_weight.shape[0]
    here = exchange(
        jnp.concatenate(
            [
                head_blocks(query_weight),
                head_blocks(kv_weight[:, :whole]),
                head_blocks(kv_weight[:, whole:]),
            ],
            axis=1,
        )
    )
    span = here.shape[2]
    kv = ring_gather(here[:, rows:].reshape(OUTER, 2, -1, span), "i")
    query_source, _ = lax.optimization_barrier((here[:, :rows], kv[-1]))
    query = in_order(ring_gather(query_source, "i"), "i", 1).reshape(-1, span)
    kv = jnp.stack(ring_gather(jnp.stack(kv), "y"))
    kv = jnp.stack(ring_gather(kv, "c"))
    return query, arrange(places, kv)


def scatter_query(grad):
    inner = lax.axis_size("i")
    blocks = grad.reshape(OUTER, inner, -1, grad.shape[1])
    blocks = from_order([blocks[:, k] for k in range(inner)], "i")
    mine = ring_scatter(blocks, "i").astype(BF16)
    return join_blocks(exchange(mine)).astype(F32)


def scatter_kv(grad):
    high, inner = lax.axis_size("y"), lax.axis_size("i")
    wide = grad.shape[1]
    blocks = grad.reshape(high, 2, OUTER, inner, -1, wide)
    mine = ring_scatter(from_order([blocks[:, 0], blocks[:, 1]], "c"), "c")
    mine = ring_scatter(from_order([mine[k] for k in range(high)], "y"), "y")
    mine = ring_scatter(from_order([mine[:, k] for k in range(inner)], "i"), "i").astype(BF16)
    here = exchange(mine)
    half = wide // 2
    return jnp.concatenate(
        [join_blocks(here[:, :, :half]), join_blocks(here[:, :, half:])], axis=1
    ).astype(F32)


def own_places():
    return jnp.stack([lax.axis_index(axis) for axis in ALL]).astype(jnp.int32)


def add_low(first, second):
    return (first.astype(F32) + second.astype(F32)).astype(BF16)


def ring_low(blocks, axis):
    travelling = blocks[1]
    for j in range(2, lax.axis_size(axis)):
        travelling = add_low(shift(travelling, axis), blocks[j])
    return add_low(shift(travelling, axis), blocks[0])


def part_by_rings(rows):
    rows = ring_low([rows[k] for k in range(rows.shape[0])], "c")
    half = rows.shape[2] // 2
    first, second = rows[:, :, :half], rows[:, :, half:]
    first = ring_low([first[k] for k in range(first.shape[0])], "y")
    first = ring_low([first[k] for k in range(first.shape[0])], "o")
    second = ring_low([second[:, k] for k in range(second.shape[1])], "o")
    second = ring_low([second[k] for k in range(second.shape[0])], "y")
    return jnp.concatenate([first, second])


VMEM = 56 * 1024 * 1024
ROW_STEP = 256


def nn(first, second):
    return jnp.dot(first, second, preferred_element_type=F32)


def nt(first, second):
    return lax.dot_general(first, second, (((1,), (1,)), ((), ())), preferred_element_type=F32)


def tn(first, second):
    return lax.dot_general(first, second, (((0,), (0,)), ((), ())), preferred_element_type=F32)


def as_column(row, rows):
    return jnp.broadcast_to(row, (rows, rows)).T[:, :1]


def turn(head, cosine, sine):
    return head * cosine + pltpu.roll(head, HD // 2, 1) * sine


def turn_back(head, cosine, sine):
    return head * cosine - pltpu.roll(head, HD // 2, 1) * sine


def allowed_keys(segment, length):
    keys = jnp.broadcast_to(segment, (length, length))
    row = lax.broadcasted_iota(jnp.int32, (length, length), 0)
    column = lax.broadcasted_iota(jnp.int32, (length, length), 1)
    return (keys == keys.T) & (column <= row)


def heads_nt(first, second):
    return lax.dot_general(first, second, (((2,), (2,)), ((0,), (0,))), preferred_element_type=F32)


def heads_nn(first, second):
    return lax.dot_general(first, second, (((2,), (1,)), ((0,), (0,))), preferred_element_type=F32)


def heads_tn(first, second):
    return lax.dot_general(first, second, (((1,), (1,)), ((0,), (0,))), preferred_element_type=F32)


def softmax_rows(queries, keys, allowed):
    scores = jnp.where(allowed[None], heads_nt(queries, keys) * (1.0 / math.sqrt(HD)), MASKED)
    exponent = jnp.exp(scores - jnp.max(scores, axis=-1, keepdims=True))
    return exponent / jnp.sum(exponent, axis=-1, keepdims=True)


def place_rows(places_ref, part_ref, value, length):
    count = part_ref.shape[2]
    for seq in range(count):
        slot = lax.rem(seq - places_ref[2] + count, count)
        part_ref[0, 0, slot] = value[seq * length : (seq + 1) * length]


def arrange_kernel(places_ref, in_ref, out_ref):
    del places_ref
    half = in_ref.shape[-1]
    for outer in range(OUTER):
        out_ref[0, 0, outer, 0, :, :half] = in_ref[0, 0, 0, outer, 0]
        out_ref[0, 0, outer, 0, :, half:] = in_ref[0, 0, 0, outer, 1]


def attend_kernel(
    places_ref,
    x_ref,
    info_ref,
    cos_ref,
    sin_ref,
    query_ref,
    kv_ref,
    out_ref,
    qkv_ref,
    gated_ref,
    part_ref,
):
    del places_ref
    length = cos_ref.shape[0]
    span = out_ref.shape[0]
    raw_query = nn(x_ref[...], query_ref[...])
    raw = nn(x_ref[...], kv_ref[...])
    cosine, sine = cos_ref[...], sin_ref[...]
    starts = range(0, span, HD)
    for seq in range(info_ref.shape[0]):
        rows = slice(seq * length, (seq + 1) * length)
        gate = as_column(info_ref[seq, 0:1, :], length)
        allowed = allowed_keys(info_ref[seq, 1:2, :], length)
        queries, keys, values = [], [], []
        for at in starts:
            head = raw_query[rows, at : at + HD].astype(BF16).astype(F32)
            queries.append(turn(head, cosine, sine).astype(BF16))
            keys.append(turn(raw[rows, at : at + HD], cosine, sine).astype(BF16))
            values.append(raw[rows, span + at : span + at + HD].astype(BF16))
            qkv_ref[rows, at : at + HD] = queries[-1]
            qkv_ref[rows, span + at : span + at + HD] = keys[-1]
            qkv_ref[rows, 2 * span + at : 2 * span + at + HD] = values[-1]
        probs = softmax_rows(jnp.stack(queries), jnp.stack(keys), allowed)
        gated = (heads_nn(probs.astype(BF16), jnp.stack(values)) * gate[None]).astype(BF16)
        for number, at in enumerate(starts):
            gated_ref[rows, at : at + HD] = gated[number]
    part_ref[...] = nn(gated_ref[...], out_ref[...]).astype(BF16)


def attend_back_kernel(
    places_ref,
    mid_ref,
    info_ref,
    cos_ref,
    sin_ref,
    qkv_ref,
    x_ref,
    query_ref,
    kv_ref,
    out_ref,
    d_query_ref,
    d_kv_ref,
    part_ref,
    d_gate_ref,
    d_gain_ref,
):
    del places_ref
    length = cos_ref.shape[0]
    span = out_ref.shape[0]
    scale = 1.0 / math.sqrt(HD)
    d_rows = nt(mid_ref[...], out_ref[...])
    cosine, sine = cos_ref[...], sin_ref[...]
    starts = range(0, span, HD)
    for seq in range(info_ref.shape[0]):
        rows = slice(seq * length, (seq + 1) * length)
        gate = as_column(info_ref[seq, 0:1, :], length)[None]
        allowed = allowed_keys(info_ref[seq, 1:2, :], length)
        queries = jnp.stack([qkv_ref[rows, at : at + HD] for at in starts])
        keys = jnp.stack([qkv_ref[rows, span + at : span + at + HD] for at in starts])
        values = jnp.stack([qkv_ref[rows, 2 * span + at : 2 * span + at + HD] for at in starts])
        d_heads = jnp.stack([d_rows[rows, at : at + HD] for at in starts])
        probs = softmax_rows(queries, keys, allowed)
        weighted = probs * heads_nt(d_heads.astype(BF16), values)
        sums = jnp.sum(weighted, axis=-1, keepdims=True)
        d_scores = ((weighted - probs * sums) * gate).astype(BF16)
        d_queries = heads_nn(d_scores, keys) * scale
        d_keys = heads_tn(d_scores, queries) * scale
        d_values = heads_tn(probs.astype(BF16), (d_heads * gate).astype(BF16))
        for number, at in enumerate(starts):
            cols = slice(at, at + HD)
            d_query_ref[rows, cols] = turn_back(d_queries[number], cosine, sine).astype(BF16)
            d_kv_ref[rows, cols] = turn_back(d_keys[number], cosine, sine).astype(BF16)
            d_kv_ref[rows, span + at : span + at + HD] = d_values[number].astype(BF16)
        total = jnp.broadcast_to(jnp.sum(sums, axis=0), (length, length))
        d_gate_ref[seq] = total.T[:1]
    d_input = nt(d_query_ref[...], query_ref[...]) + nt(d_kv_ref[...], kv_ref[...])

    @pl.when(pl.program_id(0) == 0)
    def _():
        d_gain_ref[...] = jnp.zeros_like(d_gain_ref)

    d_gain_ref[...] += jnp.sum(d_input * x_ref[...].astype(F32), axis=0, keepdims=True)
    part_ref[...] = d_input.astype(BF16)


def layer_rows_kernel(parts, places_ref, *refs):
    gated_refs, down_refs, part_ref = refs[:parts], refs[parts : 2 * parts], refs[2 * parts]
    length = part_ref.shape[3]
    value = nn(gated_refs[0][...], down_refs[0][...])
    for part in range(1, parts):
        value = value + nn(gated_refs[part][...], down_refs[part][...])
    place_rows(places_ref, part_ref, value.astype(BF16), length)


def fixed(shape):
    return pl.BlockSpec(shape, lambda step, places: (0,) * len(shape))


def rows_spec(rows, columns):
    return pl.BlockSpec((rows, columns), lambda step, places: (step, 0))


def info_spec(seqs, kinds, length):
    return pl.BlockSpec((seqs, kinds, length), lambda step, places: (step, 0, 0))


def place_spec(high, length, width):
    def index(step, places):
        low = lax.rem(lax.rem(step, 2) - places[1] + 2, 2)
        return (low, lax.rem(lax.div(step, 2) - places[0] + high, high), 0, 0, 0)

    return pl.BlockSpec((1, 1, OUTER, length, width), index)


def shape(dims, dtype=BF16):
    return jax.ShapeDtypeStruct(dims, dtype)


def call(kernel, name, steps, in_specs, out_specs, out_shape, flops, moved, operands):
    return pl.pallas_call(
        kernel,
        grid_spec=pltpu.PrefetchScalarGridSpec(
            num_scalar_prefetch=1, grid=(steps,), in_specs=in_specs, out_specs=out_specs
        ),
        out_shape=out_shape,
        compiler_params=pltpu.CompilerParams(vmem_limit_bytes=VMEM),
        cost_estimate=pl.CostEstimate(flops=flops, bytes_accessed=moved, transcendentals=0),
        name=name,
    )(*operands)


def arrange(places, value):
    low, high, inner, outer, kinds, rows, span = value.shape

    def index(step, places):
        y = lax.div(step, 2 * inner)
        c = lax.rem(lax.div(step, inner), 2)
        i = lax.rem(step, inner)
        return (
            lax.rem(c - places[1] + 2, 2),
            lax.rem(y - places[0] + high, high),
            lax.rem(i - places[3] + inner, inner),
            0,
            0,
            0,
            0,
        )

    def out_index(step, places):
        return (
            lax.div(step, 2 * inner),
            lax.rem(lax.div(step, inner), 2),
            0,
            lax.rem(step, inner),
            0,
            0,
        )

    dims = (high, low, outer, inner, rows, kinds * span)
    found = call(
        arrange_kernel,
        "arrange",
        high * low * inner,
        [pl.BlockSpec((1, 1, 1, outer, kinds, rows, span), index)],
        pl.BlockSpec((1, 1, outer, 1, rows, kinds * span), out_index),
        shape(dims),
        0,
        4 * value.size,
        (places, value),
    )
    return found.reshape(-1, kinds * span)


def attend(places, both, info, cosine, sine, query_mat, kv_mat, out_mat):
    count = both.shape[0]
    span, width = out_mat.shape
    length = cosine.shape[0]
    step = OUTER * length
    return call(
        attend_kernel,
        "attend",
        count // step,
        [
            rows_spec(step, width),
            info_spec(OUTER, 2, length),
            fixed(cosine.shape),
            fixed(sine.shape),
            fixed(query_mat.shape),
            fixed(kv_mat.shape),
            fixed(out_mat.shape),
        ],
        [rows_spec(step, 3 * span), rows_spec(step, span), rows_spec(step, width)],
        [shape((count, 3 * span)), shape((count, span)), shape((count, width))],
        2 * count * width * 4 * span + 4 * count * length * span,
        4 * count * (width + 2 * span),
        (places, both, info, cosine, sine, query_mat, kv_mat, out_mat),
    )


def attend_back(places, d_middle, info, cosine, sine, qkv, both, query_mat, kv_mat, out_mat):
    count, width = d_middle.shape
    length = cosine.shape[0]
    step = OUTER * length
    span = out_mat.shape[0]
    return call(
        attend_back_kernel,
        "attend_back",
        count // step,
        [
            rows_spec(step, width),
            info_spec(OUTER, 2, length),
            fixed(cosine.shape),
            fixed(sine.shape),
            rows_spec(step, 3 * span),
            rows_spec(step, width),
            fixed(query_mat.shape),
            fixed(kv_mat.shape),
            fixed(out_mat.shape),
        ],
        [
            rows_spec(step, span),
            rows_spec(step, 2 * span),
            rows_spec(step, width),
            info_spec(OUTER, 1, length),
            fixed((1, width)),
        ],
        [
            shape((count, span)),
            shape((count, 2 * span)),
            shape((count, width)),
            shape((count // length, 1, length), F32),
            shape((1, width), F32),
        ],
        2 * count * width * 4 * span + 10 * count * length * span,
        4 * count * (2 * width + 3 * span),
        (places, d_middle, info, cosine, sine, qkv, both, query_mat, kv_mat, out_mat),
    )


def layer_rows(places, gated_units, down_parts, length):
    count, units = gated_units[0].shape
    width = down_parts[0].shape[1]
    parts = len(down_parts)
    step = OUTER * length
    high = count // (2 * step)
    return call(
        functools.partial(layer_rows_kernel, parts),
        "layer_rows",
        count // step,
        [rows_spec(step, units)] * parts + [fixed(down.shape) for down in down_parts],
        place_spec(high, length, width),
        shape((2, high, OUTER, length, width)),
        2 * count * width * units * parts,
        4 * count * (width + units * parts),
        (places, *gated_units, *down_parts),
    )


def units_kernel(parts, places_ref, x_ref, info_ref, *refs):
    del places_ref
    d_units_refs, up_refs = refs[:parts], refs[parts : 3 * parts]
    d_both_refs, gated_refs = refs[3 * parts : 4 * parts], refs[4 * parts : 5 * parts]
    back_ref, d_gate_ref = refs[5 * parts :]
    length = info_ref.shape[2]
    seqs = info_ref.shape[0]
    rows = x_ref[...]
    gate = jnp.concatenate([as_column(info_ref[seq], length) for seq in range(seqs)], axis=0)
    back = jnp.zeros((seqs * length, back_ref.shape[-1]), F32)
    d_gate = jnp.zeros((seqs * length, 1), F32)
    for part in range(parts):
        first_ref, second_ref = up_refs[2 * part : 2 * part + 2]
        units = first_ref.shape[0]
        gate_in = nt(rows, first_ref[...])
        up_in = nt(rows, second_ref[...])
        sigma = jax.nn.sigmoid(gate_in)
        active = gate_in * sigma
        hidden_units = active * up_in
        d_units = d_units_refs[part][...].astype(F32)
        d_gate = d_gate + jnp.sum(hidden_units * d_units, axis=-1, keepdims=True)
        gated_refs[part][...] = (hidden_units * gate).astype(BF16)
        d_units = d_units * gate
        d_first = (d_units * up_in * (sigma + active * (1.0 - sigma))).astype(BF16)
        d_second = (d_units * active).astype(BF16)
        d_both_refs[part][:, :units] = d_first
        d_both_refs[part][:, units:] = d_second
        back = back + nn(d_first, first_ref[...]) + nn(d_second, second_ref[...])
    back_ref[...] = back.astype(BF16)
    for seq in range(seqs):
        column = jnp.broadcast_to(d_gate[seq * length : (seq + 1) * length], (length, length))
        d_gate_ref[seq] = column.T[:1]


def run_units(places, rows, info, d_units, own_up, other_up):
    count, width = rows.shape
    length = info.shape[2]
    parts = 1 + len(other_up) // 2
    units = d_units[0].shape[1]
    seqs = ROW_STEP // length
    own_specs = [
        pl.BlockSpec((units, width), lambda step, places, half=half: (half, 0)) for half in range(2)
    ]
    return call(
        functools.partial(units_kernel, parts),
        "units",
        count // ROW_STEP,
        [rows_spec(ROW_STEP, width), info_spec(seqs, 1, length)]
        + [rows_spec(ROW_STEP, units)] * parts
        + own_specs
        + [fixed(one.shape) for one in other_up],
        [rows_spec(ROW_STEP, 2 * units)] * parts
        + [rows_spec(ROW_STEP, units)] * parts
        + [rows_spec(ROW_STEP, width), info_spec(seqs, 1, length)],
        [shape((count, 2 * units))] * parts
        + [shape((count, units))] * parts
        + [shape((count, width)), shape((count // length, 1, length), F32)],
        8 * count * width * units * parts,
        4 * count * (width + 2 * units * parts),
        (places, rows, info, *d_units, own_up, own_up, *other_up),
    )


def shards(
    hidden_in,
    segment_ids,
    att_route,
    mlp_route,
    norm_gain1,
    norm_gain2,
    att_router,
    mlp_router,
    kv_weight,
    query_weight,
    out_weight,
    att_bias,
    up_weight,
    down_weight,
    mlp_bias,
    cotangent,
):
    experts = lax.axis_size(EXPERT)
    inner = lax.axis_size("i")
    tokens, width = hidden_in.shape
    span = HEADS // OUTER * HD
    cosine, sine_table = rope_tables(tokens)

    places = own_places()
    tie = lax.optimization_barrier

    query_mat, kv_mat = gather_heads(places, query_weight[0], kv_weight)
    out_source, _ = tie((out_weight[0], query_mat[:16, :128]))
    out_parts = ring_gather(out_source, "i")
    out_mat = in_order(out_parts, "i").reshape(span, width)
    own_up = up_weight[0].reshape(-1, width)
    down_source, _ = tie((down_weight[0], out_parts[-1]))
    down_parts = ring_gather(down_source, "i")

    residual = hidden_in.astype(F32)
    normed_one, inverse_one = norm_rows(residual, norm_gain1)
    attn_input = normed_one.astype(BF16)
    att_gate, att_onehot = pair_gates(attn_input, att_router, att_route, experts)
    info = to_experts(att_gate, att_onehot, segment_ids[0].astype(F32))
    both = meet(jnp.concatenate([attn_input, cotangent.astype(BF16)], axis=1))
    qkv, gated, branch = attend(
        places, both, info, cosine, sine_table, query_mat, kv_mat, out_mat
    )
    first_source, branch, both = tie((up_weight[0, 0], branch, both))
    first_parts = ring_gather(first_source, "i")
    all_attn, all_cot = both[:, :width], both[:, width:]
    branch = part(branch)

    all_cot, first_parts, down_parts = tie((all_cot, first_parts, down_parts))
    d_units = [mm("td,fd->tf", all_cot, down).astype(BF16) for down in down_parts]
    branch, d_units = tie((branch, d_units))
    middle = residual + branch.astype(F32) + att_bias
    normed_two, inverse_two = norm_rows(middle, norm_gain2)
    mlp_input = normed_two.astype(BF16)
    mlp_gate, mlp_onehot = pair_gates(mlp_input, mlp_router, mlp_route, experts)
    second_source, mlp_input = tie((up_weight[0, 1], mlp_input))
    second_parts = ring_gather(second_source, "i")
    all_mlp = meet(mlp_input)
    gate_m = to_experts(mlp_gate, mlp_onehot, None)
    gate_m, second_parts = tie((gate_m, second_parts))
    other_up = [one for pair in zip(first_parts[1:], second_parts[1:]) for one in pair]
    found = run_units(places, all_mlp, gate_m, d_units, own_up, other_up)
    d_both, gated_units = found[:inner], found[inner : 2 * inner]
    rows_back, d_gate_m = found[2 * inner :]
    d_mlp_input = part(rows_back)
    d_mlp_gate = from_experts(d_gate_m[:, 0], mlp_onehot, experts)
    grad_up = [mm("tf,td->fd", d_here, all_mlp) for d_here in d_both]
    grad_down = [mm("tf,td->fd", here, all_cot) for here in gated_units]
    rows_out = layer_rows(places, gated_units, down_parts, tokens)
    low_up = [one.astype(BF16) for one in grad_up[1:]]
    low_down = [one.astype(BF16) for one in grad_down[1:]]
    d_mlp_input, low_up, low_down, rows_out = tie((d_mlp_input, low_up, low_down, rows_out))
    grad_up, grad_down = grad_up[:1] + low_up, grad_down[:1] + low_down
    d_mlp_router, d_mlp_from_router = gates_back(
        mlp_gate, mlp_onehot, d_mlp_gate, mlp_input, mlp_router
    )
    d_norm_two, d_gain_two = norm_back(
        middle, inverse_two, norm_gain2, d_mlp_input.astype(F32) + d_mlp_from_router
    )
    d_middle = cotangent + d_norm_two
    sums = jnp.concatenate(
        [
            jnp.stack([d_gain_two, jnp.sum(d_middle, axis=0), jnp.sum(cotangent, axis=0)]),
            d_mlp_router,
        ]
    )

    all_mid = meet(d_middle.astype(BF16))
    rows_out = part_by_rings(rows_out)
    all_mid, rows_out = tie((all_mid, rows_out))
    layer_out = middle + rows_out.astype(F32) + mlp_bias
    d_heads, d_kv, rows_one, d_gate_a, d_gain_a = attend_back(
        places, all_mid, info, cosine, sine_table, qkv, both, query_mat, kv_mat, out_mat
    )
    d_attn_input = part(rows_one)
    d_att_gate = from_experts(d_gate_a[:, 0], att_onehot, experts)
    d_kv_weight = scatter_kv(mm("td,tf->df", all_attn, d_kv))
    d_query = scatter_query(mm("td,tf->df", all_attn, d_heads))[None]
    d_out = mm("tf,td->fd", gated, all_mid).reshape(inner, -1, width)
    d_output = ring_scatter(from_order([d_out[k] for k in range(inner)], "i"), "i")[None]
    d_upper = ring_scatter(grad_up, "i", rows_one)
    d_upper = d_upper.reshape(up_weight.shape)
    d_lower = ring_scatter(grad_down, "i", rows_one)[None]
    d_att_router, d_att_from_router = gates_back(
        att_gate, att_onehot, d_att_gate, attn_input, att_router
    )
    d_gain_one = d_gain_a / norm_gain1 + jnp.sum(
        d_att_from_router * residual * inverse_one, axis=0, keepdims=True
    )
    summed = sum_all(jnp.concatenate([d_gain_one, sums, d_att_router]))
    d_attn_input, summed = tie((d_attn_input, summed))
    d_norm_one, _ = norm_back(
        residual, inverse_one, norm_gain1, d_attn_input.astype(F32) + d_att_from_router
    )
    d_input = d_middle + d_norm_one
    return (
        layer_out,
        d_input,
        summed[0],
        summed[1],
        summed[4 + experts :].T,
        summed[4 : 4 + experts].T,
        d_kv_weight,
        d_query,
        d_output,
        summed[2],
        d_upper,
        d_lower,
        summed[3],
    )


def solution(mesh):
    experts, fsdp = mesh.shape["expert"], mesh.shape["fsdp"]
    fine = Mesh(mesh.devices.reshape(experts // 2, 2, OUTER, fsdp // OUTER), ALL)
    shard = ("o", "i")
    rows = P(ALL, None)
    placed = (
        rows,
        rows,
        rows,
        rows,
        P(),
        P(),
        P(),
        P(),
        rows,
        P(EXPERT, shard, None),
        P(EXPERT, shard, None),
        P(),
        P(EXPERT, None, shard, None),
        P(EXPERT, shard, None),
        P(),
        rows,
    )
    return jax.shard_map(
        shards,
        mesh=fine,
        in_specs=placed,
        out_specs=(
            rows,
            rows,
            P(),
            P(),
            P(),
            P(),
            rows,
            P(EXPERT, shard, None),
            P(EXPERT, shard, None),
            P(),
            P(EXPERT, None, shard, None),
            P(EXPERT, shard, None),
            P(),
        ),
        check_vma=False,
    )
```

```python
import functools
import math

import jax
import jax.numpy as jnp
from jax import lax
from jax.experimental import pallas as pl
from jax.experimental.pallas import tpu as pltpu
from jax.sharding import Mesh, PartitionSpec as P

HEADS = 16
HD = 128
TOP = 2


EPSILON = 1e-06
HIGHEST = lax.Precision.HIGHEST
MASKED = -1e30

GROUP = ("y", "c", "o")
EXPERT = ("y", "c")
ALL = ("y", "c", "o", "i")
OUTER = 4
F32 = jnp.float32
BF16 = jnp.bfloat16


def rope_tables(length):
    half_dim = HD // 2
    frequency = jnp.exp(jnp.arange(half_dim, dtype=F32) * (-2.0 * math.log(10000.0) / HD))
    angles = jnp.arange(length, dtype=F32)[:, None] * frequency[None, :]
    cosine, sine = jnp.cos(angles), jnp.sin(angles)
    return (
        jnp.concatenate([cosine, cosine], axis=1),
        jnp.concatenate([-sine, sine], axis=1),
    )


def norm_rows(stream, gain):
    inverse = lax.rsqrt(jnp.mean(stream * stream, axis=-1, keepdims=True) + EPSILON)
    return (stream * inverse * gain, inverse)


def norm_back(stream, inverse, gain, upstream):
    scaled = upstream * gain
    d_stream = inverse * scaled - stream * inverse**3 * jnp.mean(
        scaled * stream, axis=-1, keepdims=True
    )
    d_gain = jnp.sum(upstream * stream * inverse, axis=0)
    return (d_stream, d_gain)


def shift(value, axis):
    size = lax.axis_size(axis)
    return lax.ppermute(value, axis, [((k + 1) % size, k) for k in range(size)])


def ring_gather(value, axis):
    parts = [value]
    for _ in range(lax.axis_size(axis) - 1):
        parts.append(shift(parts[-1], axis))
    return parts


def ring_scatter(blocks, axis, after=None):
    size = lax.axis_size(axis)
    travelling = blocks[1].astype(BF16)
    for j in range(2, size):
        travelling = (shift(travelling, axis).astype(F32) + blocks[j]).astype(BF16)
    arrived = shift(travelling, axis)
    if after is not None:
        arrived, _ = lax.optimization_barrier((arrived, after))
    return arrived.astype(F32) + blocks[0]


def in_order(parts, axis, place=0):
    if len(parts) == 2:
        first = lax.axis_index(axis) == 0
        return jnp.stack([jnp.where(first, *parts), jnp.where(first, *parts[::-1])], axis=place)
    return jnp.roll(jnp.stack(parts, axis=place), lax.axis_index(axis), axis=place)


def from_order(parts, axis):
    if len(parts) == 2:
        first = lax.axis_index(axis) == 0
        return [jnp.where(first, *parts), jnp.where(first, *parts[::-1])]
    return list(jnp.roll(jnp.stack(parts), -lax.axis_index(axis), axis=0))


def sum_all(value):
    for axis in ALL:
        size = lax.axis_size(axis)
        step = 1
        while step < size:
            value = value + lax.ppermute(value, axis, [(k, k ^ step) for k in range(size)])
            step *= 2
    return value


def pair_gates(normed, router, route, experts):
    logits = jnp.dot(normed.astype(F32), router, precision=HIGHEST)
    onehot = (route[:, :, None] == jnp.arange(experts, dtype=jnp.int32)[None, None, :]).astype(F32)
    picked = jnp.sum(logits[:, None, :] * onehot, axis=-1)
    return (jax.nn.softmax(picked, axis=-1), onehot)


def gates_back(gates, onehot, d_gates, normed, router):
    d_picked = gates * (d_gates - jnp.sum(gates * d_gates, axis=-1, keepdims=True))
    d_logits = jnp.sum(d_picked[:, :, None] * onehot, axis=1)
    d_router = jnp.dot(d_logits.T, normed.astype(F32), precision=HIGHEST)
    d_normed = jnp.dot(d_logits, router.T, precision=HIGHEST)
    return (d_router, d_normed)


def to_experts(gates, onehot, extra):
    by_expert = jnp.sum(gates[:, :, None] * onehot, axis=1).T
    rows = jnp.repeat(by_expert, OUTER, axis=0)[:, None, :]
    if extra is not None:
        rows = jnp.concatenate(
            [rows, jnp.broadcast_to(extra[None, None, :], rows.shape)], axis=1
        )
    return lax.all_to_all(rows, GROUP, split_axis=0, concat_axis=0, tiled=True)


def from_experts(d_gates, onehot, experts):
    rows = lax.all_to_all(d_gates, GROUP, split_axis=0, concat_axis=0, tiled=True)
    by_expert = jnp.sum(rows.reshape(experts, OUTER, -1), axis=1)
    return jnp.einsum("tce,et->tc", onehot, by_expert, precision=HIGHEST)


def meet(rows):
    return lax.all_gather(rows, GROUP, axis=0, tiled=True)


def part(rows):
    return lax.psum_scatter(rows, GROUP, scatter_dimension=0, tiled=True)


def mm(form, first, second):
    return jnp.einsum(form, first, second, preferred_element_type=F32)


def head_blocks(matrix):
    span = HEADS // OUTER * HD
    return jnp.stack([matrix[:, k * span : (k + 1) * span] for k in range(OUTER)])


def join_blocks(blocks):
    return jnp.concatenate([blocks[k] for k in range(OUTER)], axis=1)


def exchange(blocks):
    return lax.all_to_all(blocks, "o", split_axis=0, concat_axis=0, tiled=True)


def gather_heads(places, query_weight, kv_weight, beside):
    whole = HEADS * HD
    rows = query_weight.shape[0]
    here = exchange(
        jnp.concatenate(
            [
                head_blocks(query_weight),
                head_blocks(kv_weight[:, :whole]),
                head_blocks(kv_weight[:, whole:]),
            ],
            axis=1,
        )
    )
    here, beside = lax.optimization_barrier((here, beside()))
    span = here.shape[2]
    kv = ring_gather(here[:, rows:].reshape(OUTER, 2, -1, span), "i")
    query_source, _ = lax.optimization_barrier((here[:, :rows], kv[-1]))
    query = in_order(ring_gather(query_source, "i"), "i", 1).reshape(-1, span)
    kv = ring_gather(jnp.stack(kv), "y")
    seen = kv[-1][0, 0, 0, 0]
    kv = jnp.stack(ring_gather(jnp.stack(kv), "c"))
    return query, arrange(places, kv), beside, seen


def scatter_query(grad):
    inner = lax.axis_size("i")
    blocks = grad.reshape(OUTER, inner, -1, grad.shape[1])
    blocks = from_order([blocks[:, k] for k in range(inner)], "i")
    mine = ring_scatter(blocks, "i").astype(BF16)
    return join_blocks(exchange(mine)).astype(F32)


def scatter_kv(grad):
    high, inner = lax.axis_size("y"), lax.axis_size("i")
    wide = grad.shape[1]
    blocks = grad.reshape(high, 2, OUTER, inner, -1, wide)
    mine = ring_scatter(from_order([blocks[:, 0], blocks[:, 1]], "c"), "c")
    mine = ring_scatter(from_order([mine[k] for k in range(high)], "y"), "y")
    mine = ring_scatter(from_order([mine[:, k] for k in range(inner)], "i"), "i").astype(BF16)
    here = exchange(mine)
    half = wide // 2
    return jnp.concatenate(
        [join_blocks(here[:, :, :half]), join_blocks(here[:, :, half:])], axis=1
    ).astype(F32)


def own_places():
    return jnp.stack([lax.axis_index(axis) for axis in ALL]).astype(jnp.int32)


def add_low(first, second):
    return (first.astype(F32) + second.astype(F32)).astype(BF16)


def ring_low(blocks, axis):
    travelling = blocks[1]
    for j in range(2, lax.axis_size(axis)):
        travelling = add_low(shift(travelling, axis), blocks[j])
    return add_low(shift(travelling, axis), blocks[0])


def part_low(rows):
    return ring_low([rows[k] for k in range(rows.shape[0])], "c")


def part_first(rows):
    half = rows.shape[2] // 2
    first, second = rows[:, :, :half], rows[:, :, half:]
    first = ring_low([first[k] for k in range(first.shape[0])], "y")
    second = ring_low([second[:, k] for k in range(second.shape[1])], "o")
    return first, second


def part_second(first, second):
    first = ring_low([first[k] for k in range(first.shape[0])], "o")
    second = ring_low([second[k] for k in range(second.shape[0])], "y")
    return jnp.concatenate([first, second])


VMEM = 56 * 1024 * 1024
ROW_STEP = 256


def nn(first, second):
    return jnp.dot(first, second, preferred_element_type=F32)


def nt(first, second):
    return lax.dot_general(first, second, (((1,), (1,)), ((), ())), preferred_element_type=F32)


def tn(first, second):
    return lax.dot_general(first, second, (((0,), (0,)), ((), ())), preferred_element_type=F32)


def as_column(row, rows):
    return jnp.broadcast_to(row, (rows, rows)).T[:, :1]


def turn(head, cosine, sine):
    return head * cosine + pltpu.roll(head, HD // 2, 1) * sine


def turn_back(head, cosine, sine):
    return head * cosine - pltpu.roll(head, HD // 2, 1) * sine


def allowed_keys(segment, length):
    keys = jnp.broadcast_to(segment, (length, length))
    row = lax.broadcasted_iota(jnp.int32, (length, length), 0)
    column = lax.broadcasted_iota(jnp.int32, (length, length), 1)
    return (keys == keys.T) & (column <= row)


def heads_nt(first, second):
    return lax.dot_general(first, second, (((2,), (2,)), ((0,), (0,))), preferred_element_type=F32)


def heads_nn(first, second):
    return lax.dot_general(first, second, (((2,), (1,)), ((0,), (0,))), preferred_element_type=F32)


def heads_tn(first, second):
    return lax.dot_general(first, second, (((1,), (1,)), ((0,), (0,))), preferred_element_type=F32)


def softmax_rows(queries, keys, allowed):
    scores = jnp.where(allowed[None], heads_nt(queries, keys) * (1.0 / math.sqrt(HD)), MASKED)
    exponent = jnp.exp(scores - jnp.max(scores, axis=-1, keepdims=True))
    return exponent / jnp.sum(exponent, axis=-1, keepdims=True)


def place_rows(places_ref, part_ref, value, length):
    count = part_ref.shape[2]
    for seq in range(count):
        slot = lax.rem(seq - places_ref[2] + count, count)
        part_ref[0, 0, slot] = value[seq * length : (seq + 1) * length]


def arrange_kernel(places_ref, in_ref, out_ref):
    del places_ref
    half = in_ref.shape[-1]
    for outer in range(OUTER):
        out_ref[0, 0, outer, 0, :, :half] = in_ref[0, 0, 0, outer, 0]
        out_ref[0, 0, outer, 0, :, half:] = in_ref[0, 0, 0, outer, 1]


def attend_kernel(
    places_ref,
    x_ref,
    info_ref,
    cos_ref,
    sin_ref,
    query_ref,
    kv_ref,
    out_ref,
    qkv_ref,
    gated_ref,
    part_ref,
):
    length = cos_ref.shape[0]
    span = out_ref.shape[0]
    raw_query = nn(x_ref[...], query_ref[...])
    raw = nn(x_ref[...], kv_ref[...])
    cosine, sine = cos_ref[...], sin_ref[...]
    starts = range(0, span, HD)
    for seq in range(info_ref.shape[0]):
        rows = slice(seq * length, (seq + 1) * length)
        gate = as_column(info_ref[seq, 0:1, :], length)
        allowed = allowed_keys(info_ref[seq, 1:2, :], length)
        queries, keys, values = [], [], []
        for at in starts:
            head = raw_query[rows, at : at + HD].astype(BF16).astype(F32)
            queries.append(turn(head, cosine, sine).astype(BF16))
            keys.append(turn(raw[rows, at : at + HD], cosine, sine).astype(BF16))
            values.append(raw[rows, span + at : span + at + HD].astype(BF16))
            qkv_ref[rows, at : at + HD] = queries[-1]
            qkv_ref[rows, span + at : span + at + HD] = keys[-1]
            qkv_ref[rows, 2 * span + at : 2 * span + at + HD] = values[-1]
        probs = softmax_rows(jnp.stack(queries), jnp.stack(keys), allowed)
        gated = (heads_nn(probs.astype(BF16), jnp.stack(values)) * gate[None]).astype(BF16)
        for number, at in enumerate(starts):
            gated_ref[rows, at : at + HD] = gated[number]
    place_rows(places_ref, part_ref, nn(gated_ref[...], out_ref[...]).astype(BF16), length)


def attend_back_kernel(
    places_ref,
    mid_ref,
    info_ref,
    cos_ref,
    sin_ref,
    qkv_ref,
    x_ref,
    query_ref,
    kv_ref,
    out_ref,
    d_query_ref,
    d_kv_ref,
    part_ref,
    d_gate_ref,
    d_gain_ref,
):
    del places_ref
    length = cos_ref.shape[0]
    span = out_ref.shape[0]
    scale = 1.0 / math.sqrt(HD)
    d_rows = nt(mid_ref[...], out_ref[...])
    cosine, sine = cos_ref[...], sin_ref[...]
    starts = range(0, span, HD)
    for seq in range(info_ref.shape[0]):
        rows = slice(seq * length, (seq + 1) * length)
        gate = as_column(info_ref[seq, 0:1, :], length)[None]
        allowed = allowed_keys(info_ref[seq, 1:2, :], length)
        queries = jnp.stack([qkv_ref[rows, at : at + HD] for at in starts])
        keys = jnp.stack([qkv_ref[rows, span + at : span + at + HD] for at in starts])
        values = jnp.stack([qkv_ref[rows, 2 * span + at : 2 * span + at + HD] for at in starts])
        d_heads = jnp.stack([d_rows[rows, at : at + HD] for at in starts])
        probs = softmax_rows(queries, keys, allowed)
        weighted = probs * heads_nt(d_heads.astype(BF16), values)
        sums = jnp.sum(weighted, axis=-1, keepdims=True)
        d_scores = ((weighted - probs * sums) * gate).astype(BF16)
        d_queries = heads_nn(d_scores, keys) * scale
        d_keys = heads_tn(d_scores, queries) * scale
        d_values = heads_tn(probs.astype(BF16), (d_heads * gate).astype(BF16))
        for number, at in enumerate(starts):
            cols = slice(at, at + HD)
            d_query_ref[rows, cols] = turn_back(d_queries[number], cosine, sine).astype(BF16)
            d_kv_ref[rows, cols] = turn_back(d_keys[number], cosine, sine).astype(BF16)
            d_kv_ref[rows, span + at : span + at + HD] = d_values[number].astype(BF16)
        total = jnp.broadcast_to(jnp.sum(sums, axis=0), (length, length))
        d_gate_ref[seq] = total.T[:1]
    d_input = nt(d_query_ref[...], query_ref[...]) + nt(d_kv_ref[...], kv_ref[...])

    @pl.when(pl.program_id(0) == 0)
    def _():
        d_gain_ref[...] = jnp.zeros_like(d_gain_ref)

    d_gain_ref[...] += jnp.sum(d_input * x_ref[...].astype(F32), axis=0, keepdims=True)
    part_ref[...] = d_input.astype(BF16)


def layer_rows_kernel(parts, places_ref, *refs):
    gated_refs, down_refs, part_ref = refs[:parts], refs[parts : 2 * parts], refs[2 * parts]
    length = part_ref.shape[3]
    value = nn(gated_refs[0][...], down_refs[0][...])
    for part in range(1, parts):
        value = value + nn(gated_refs[part][...], down_refs[part][...])
    place_rows(places_ref, part_ref, value.astype(BF16), length)


def fixed(shape):
    return pl.BlockSpec(shape, lambda step, places: (0,) * len(shape))


def rows_spec(rows, columns):
    return pl.BlockSpec((rows, columns), lambda step, places: (step, 0))


def info_spec(seqs, kinds, length):
    return pl.BlockSpec((seqs, kinds, length), lambda step, places: (step, 0, 0))


def place_spec(high, length, width):
    def index(step, places):
        low = lax.rem(lax.rem(step, 2) - places[1] + 2, 2)
        return (low, lax.rem(lax.div(step, 2) - places[0] + high, high), 0, 0, 0)

    return pl.BlockSpec((1, 1, OUTER, length, width), index)


def shape(dims, dtype=BF16):
    return jax.ShapeDtypeStruct(dims, dtype)


def call(kernel, name, steps, in_specs, out_specs, out_shape, flops, moved, operands):
    return pl.pallas_call(
        kernel,
        grid_spec=pltpu.PrefetchScalarGridSpec(
            num_scalar_prefetch=1, grid=(steps,), in_specs=in_specs, out_specs=out_specs
        ),
        out_shape=out_shape,
        compiler_params=pltpu.CompilerParams(vmem_limit_bytes=VMEM),
        cost_estimate=pl.CostEstimate(flops=flops, bytes_accessed=moved, transcendentals=0),
        name=name,
    )(*operands)


def arrange(places, value):
    low, high, inner, outer, kinds, rows, span = value.shape

    def index(step, places):
        y = lax.div(step, 2 * inner)
        c = lax.rem(lax.div(step, inner), 2)
        i = lax.rem(step, inner)
        return (
            lax.rem(c - places[1] + 2, 2),
            lax.rem(y - places[0] + high, high),
            lax.rem(i - places[3] + inner, inner),
            0,
            0,
            0,
            0,
        )

    def out_index(step, places):
        return (
            lax.div(step, 2 * inner),
            lax.rem(lax.div(step, inner), 2),
            0,
            lax.rem(step, inner),
            0,
            0,
        )

    dims = (high, low, outer, inner, rows, kinds * span)
    found = call(
        arrange_kernel,
        "arrange",
        high * low * inner,
        [pl.BlockSpec((1, 1, 1, outer, kinds, rows, span), index)],
        pl.BlockSpec((1, 1, outer, 1, rows, kinds * span), out_index),
        shape(dims),
        0,
        4 * value.size,
        (places, value),
    )
    return found.reshape(-1, kinds * span)


def attend(places, rows, info, cosine, sine, query_mat, kv_mat, out_mat):
    count, width = rows.shape
    span = out_mat.shape[0]
    length = cosine.shape[0]
    step = OUTER * length
    high = count // (2 * step)
    return call(
        attend_kernel,
        "attend",
        count // step,
        [
            rows_spec(step, width),
            info_spec(OUTER, 2, length),
            fixed(cosine.shape),
            fixed(sine.shape),
            fixed(query_mat.shape),
            fixed(kv_mat.shape),
            fixed(out_mat.shape),
        ],
        [rows_spec(step, 3 * span), rows_spec(step, span), place_spec(high, length, width)],
        [shape((count, 3 * span)), shape((count, span)), shape((2, high, OUTER, length, width))],
        2 * count * width * 4 * span + 4 * count * length * span,
        4 * count * (width + 2 * span),
        (places, rows, info, cosine, sine, query_mat, kv_mat, out_mat),
    )


def attend_back(places, d_middle, info, cosine, sine, qkv, rows, query_mat, kv_mat, out_mat):
    count, width = d_middle.shape
    length = cosine.shape[0]
    step = OUTER * length
    span = out_mat.shape[0]
    return call(
        attend_back_kernel,
        "attend_back",
        count // step,
        [
            rows_spec(step, width),
            info_spec(OUTER, 2, length),
            fixed(cosine.shape),
            fixed(sine.shape),
            rows_spec(step, 3 * span),
            rows_spec(step, width),
            fixed(query_mat.shape),
            fixed(kv_mat.shape),
            fixed(out_mat.shape),
        ],
        [
            rows_spec(step, span),
            rows_spec(step, 2 * span),
            rows_spec(step, width),
            info_spec(OUTER, 1, length),
            fixed((1, width)),
        ],
        [
            shape((count, span)),
            shape((count, 2 * span)),
            shape((count, width)),
            shape((count // length, 1, length), F32),
            shape((1, width), F32),
        ],
        2 * count * width * 4 * span + 10 * count * length * span,
        4 * count * (2 * width + 3 * span),
        (places, d_middle, info, cosine, sine, qkv, rows, query_mat, kv_mat, out_mat),
    )


def layer_rows(places, gated_units, down_parts, length):
    count, units = gated_units[0].shape
    width = down_parts[0].shape[1]
    parts = len(down_parts)
    step = OUTER * length
    high = count // (2 * step)
    return call(
        functools.partial(layer_rows_kernel, parts),
        "layer_rows",
        count // step,
        [rows_spec(step, units)] * parts + [fixed(down.shape) for down in down_parts],
        place_spec(high, length, width),
        shape((2, high, OUTER, length, width)),
        2 * count * width * units * parts,
        4 * count * (width + units * parts),
        (places, *gated_units, *down_parts),
    )


def units_kernel(places_ref, x_ref, info_ref, d_units_ref, first_ref, second_ref, *refs):
    del places_ref
    sums_refs, (d_both_ref, gated_ref, back_ref, d_gate_ref) = refs[:-4], refs[-4:]
    length = info_ref.shape[2]
    seqs = info_ref.shape[0]
    units = first_ref.shape[0]
    rows = x_ref[...]
    gate = jnp.concatenate([as_column(info_ref[seq], length) for seq in range(seqs)], axis=0)
    gate_in = nt(rows, first_ref[...])
    up_in = nt(rows, second_ref[...])
    sigma = jax.nn.sigmoid(gate_in)
    active = gate_in * sigma
    hidden_units = active * up_in
    d_units = d_units_ref[...].astype(F32)
    d_gate = jnp.sum(hidden_units * d_units, axis=-1, keepdims=True)
    gated_ref[...] = (hidden_units * gate).astype(BF16)
    d_units = d_units * gate
    d_first = (d_units * up_in * (sigma + active * (1.0 - sigma))).astype(BF16)
    d_second = (d_units * active).astype(BF16)
    d_both_ref[:, :units] = d_first
    d_both_ref[:, units:] = d_second
    back = nn(d_first, first_ref[...]) + nn(d_second, second_ref[...])
    if sums_refs:
        back = back + sums_refs[0][...]
    back_ref[...] = back.astype(back_ref.dtype)
    for seq in range(seqs):
        column = jnp.broadcast_to(d_gate[seq * length : (seq + 1) * length], (length, length))
        d_gate_ref[seq] = column.T[:1]


def run_units(places, rows, info, d_units, first, second, sums, last):
    count, width = rows.shape
    length = info.shape[2]
    units = d_units.shape[1]
    seqs = ROW_STEP // length

    def weight_spec(block):
        return pl.BlockSpec((units, width), lambda step, places: (block, 0))

    extra = [] if sums is None else [sums]
    return call(
        units_kernel,
        "units",
        count // ROW_STEP,
        [rows_spec(ROW_STEP, width), info_spec(seqs, 1, length), rows_spec(ROW_STEP, units)]
        + [weight_spec(first[1]), weight_spec(second[1])]
        + [rows_spec(ROW_STEP, width) for _ in extra],
        [
            rows_spec(ROW_STEP, 2 * units),
            rows_spec(ROW_STEP, units),
            rows_spec(ROW_STEP, width),
            info_spec(seqs, 1, length),
        ],
        [
            shape((count, 2 * units)),
            shape((count, units)),
            shape((count, width), BF16 if last else F32),
            shape((count // length, 1, length), F32),
        ],
        0,
        0,
        (places, rows, info, d_units, first[0], second[0], *extra),
    )


def shards(
    hidden_in,
    segment_ids,
    att_route,
    mlp_route,
    norm_gain1,
    norm_gain2,
    att_router,
    mlp_router,
    kv_weight,
    query_weight,
    out_weight,
    att_bias,
    up_weight,
    down_weight,
    mlp_bias,
    cotangent,
):
    experts = lax.axis_size(EXPERT)
    inner = lax.axis_size("i")
    tokens, width = hidden_in.shape
    span = HEADS // OUTER * HD
    cosine, sine_table = rope_tables(tokens)

    places = own_places()
    tie = lax.optimization_barrier

    query_mat, kv_mat, down_parts, seen = gather_heads(
        places, query_weight[0], kv_weight, lambda: ring_gather(down_weight[0], "i")
    )
    out_source, _ = tie((out_weight[0], seen))
    out_mat = in_order(ring_gather(out_source, "i"), "i").reshape(span, width)
    own_up = up_weight[0].reshape(-1, width)

    residual = hidden_in.astype(F32)
    normed_one, inverse_one = norm_rows(residual, norm_gain1)
    attn_input = normed_one.astype(BF16)
    att_gate, att_onehot = pair_gates(attn_input, att_router, att_route, experts)
    info = to_experts(att_gate, att_onehot, segment_ids[0].astype(F32))
    all_attn = meet(attn_input)
    cot_low, _ = tie((cotangent.astype(BF16), seen))
    all_cot = meet(cot_low)
    qkv, gated, branch = attend(
        places, all_attn, info, cosine, sine_table, query_mat, kv_mat, out_mat
    )
    up_source, branch = tie((own_up, branch))
    branch = part_second(*part_first(part_low(branch)))

    d_units = [mm("td,fd->tf", all_cot, down).astype(BF16) for down in down_parts]
    branch, d_units = tie((branch, d_units))
    middle = residual + branch.astype(F32) + att_bias
    normed_two, inverse_two = norm_rows(middle, norm_gain2)
    mlp_input = normed_two.astype(BF16)
    mlp_gate, mlp_onehot = pair_gates(mlp_input, mlp_router, mlp_route, experts)
    up_parts = ring_gather(up_source, "i")
    all_mlp = meet(mlp_input)
    gate_m = to_experts(mlp_gate, mlp_onehot, None)
    d_both, gated_units, rows_back, d_gate_m = [], [], None, None
    for number, up in enumerate(up_parts):
        source = own_up if number == 0 else up
        found = run_units(
            places,
            all_mlp,
            gate_m,
            d_units[number],
            (source, 0),
            (source, 1),
            rows_back,
            number == inner - 1,
        )
        d_both.append(found[0])
        gated_units.append(found[1])
        rows_back = found[2]
        d_gate_m = found[3] if d_gate_m is None else d_gate_m + found[3]
    d_mlp_input = part(rows_back)
    d_mlp_gate = from_experts(d_gate_m[:, 0], mlp_onehot, experts)
    grad_up = [mm("tf,td->fd", d_here, all_mlp) for d_here in d_both]
    grad_down = [mm("tf,td->fd", here, all_cot) for here in gated_units]
    rows_out = layer_rows(places, gated_units, down_parts, tokens)
    low_up = [one.astype(BF16) for one in grad_up[1:]]
    low_down = [one.astype(BF16) for one in grad_down[1:]]
    d_mlp_input, low_up, low_down, rows_out = tie((d_mlp_input, low_up, low_down, rows_out))
    grad_up, grad_down = grad_up[:1] + low_up, grad_down[:1] + low_down
    d_mlp_router, d_mlp_from_router = gates_back(
        mlp_gate, mlp_onehot, d_mlp_gate, mlp_input, mlp_router
    )
    d_norm_two, d_gain_two = norm_back(
        middle, inverse_two, norm_gain2, d_mlp_input.astype(F32) + d_mlp_from_router
    )
    d_middle = cotangent + d_norm_two
    sums = jnp.concatenate(
        [
            jnp.stack([d_gain_two, jnp.sum(d_middle, axis=0), jnp.sum(cotangent, axis=0)]),
            d_mlp_router,
        ]
    )

    all_mid = meet(d_middle.astype(BF16))
    rows_out, all_mid = tie((part_first(part_low(rows_out)), all_mid))
    rows_out = part_second(*rows_out)
    d_heads, d_kv, rows_one, d_gate_a, d_gain_a = attend_back(
        places, all_mid, info, cosine, sine_table, qkv, all_attn, query_mat, kv_mat, out_mat
    )
    layer_out = middle + rows_out.astype(F32) + mlp_bias
    d_attn_input = part(rows_one)
    d_att_gate = from_experts(d_gate_a[:, 0], att_onehot, experts)
    d_kv_weight = scatter_kv(mm("td,tf->df", all_attn, d_kv))
    d_query = scatter_query(mm("td,tf->df", all_attn, d_heads))[None]
    d_out = mm("tf,td->fd", gated, all_mid).reshape(inner, -1, width)
    d_output = ring_scatter(from_order([d_out[k] for k in range(inner)], "i"), "i")[None]
    d_upper = ring_scatter(grad_up, "i", d_attn_input)
    d_upper = d_upper.reshape(up_weight.shape)
    d_lower = ring_scatter(grad_down, "i", d_attn_input)[None]
    d_att_router, d_att_from_router = gates_back(
        att_gate, att_onehot, d_att_gate, attn_input, att_router
    )
    d_gain_one = d_gain_a / norm_gain1 + jnp.sum(
        d_att_from_router * residual * inverse_one, axis=0, keepdims=True
    )
    summed = sum_all(jnp.concatenate([d_gain_one, sums, d_att_router]))
    d_attn_input, summed = tie((d_attn_input, summed))
    d_norm_one, _ = norm_back(
        residual, inverse_one, norm_gain1, d_attn_input.astype(F32) + d_att_from_router
    )
    d_input = d_middle + d_norm_one
    return (
        layer_out,
        d_input,
        summed[0],
        summed[1],
        summed[4 + experts :].T,
        summed[4 : 4 + experts].T,
        d_kv_weight,
        d_query,
        d_output,
        summed[2],
        d_upper,
        d_lower,
        summed[3],
    )


def solution(mesh):
    experts, fsdp = mesh.shape["expert"], mesh.shape["fsdp"]
    fine = Mesh(mesh.devices.reshape(experts // 2, 2, OUTER, fsdp // OUTER), ALL)
    shard = ("o", "i")
    rows = P(ALL, None)
    placed = (
        rows,
        rows,
        rows,
        rows,
        P(),
        P(),
        P(),
        P(),
        rows,
        P(EXPERT, shard, None),
        P(EXPERT, shard, None),
        P(),
        P(EXPERT, None, shard, None),
        P(EXPERT, shard, None),
        P(),
        rows,
    )
    return jax.shard_map(
        shards,
        mesh=fine,
        in_specs=placed,
        out_specs=(
            rows,
            rows,
            P(),
            P(),
            P(),
            P(),
            rows,
            P(EXPERT, shard, None),
            P(EXPERT, shard, None),
            P(),
            P(EXPERT, None, shard, None),
            P(EXPERT, shard, None),
            P(),
        ),
        check_vma=False,
    )
```

```python
import functools
import math

import jax
import jax.numpy as jnp
from jax import lax
from jax.experimental import pallas as pl
from jax.experimental.pallas import tpu as pltpu
from jax.sharding import Mesh, PartitionSpec as P

HEADS = 16
HD = 128
TOP = 2


EPSILON = 1e-06
HIGHEST = lax.Precision.HIGHEST
MASKED = -1e30

GROUP = ("y", "c", "o")
EXPERT = ("y", "c")
ALL = ("y", "c", "o", "i")
OUTER = 4
F32 = jnp.float32
BF16 = jnp.bfloat16


def rope_tables(length):
    half_dim = HD // 2
    frequency = jnp.exp(jnp.arange(half_dim, dtype=F32) * (-2.0 * math.log(10000.0) / HD))
    angles = jnp.arange(length, dtype=F32)[:, None] * frequency[None, :]
    cosine, sine = jnp.cos(angles), jnp.sin(angles)
    return (
        jnp.concatenate([cosine, cosine], axis=1),
        jnp.concatenate([-sine, sine], axis=1),
    )


def norm_rows(stream, gain):
    inverse = lax.rsqrt(jnp.mean(stream * stream, axis=-1, keepdims=True) + EPSILON)
    return (stream * inverse * gain, inverse)


def norm_back(stream, inverse, gain, upstream):
    scaled = upstream * gain
    d_stream = inverse * scaled - stream * inverse**3 * jnp.mean(
        scaled * stream, axis=-1, keepdims=True
    )
    d_gain = jnp.sum(upstream * stream * inverse, axis=0)
    return (d_stream, d_gain)


def shift(value, axis):
    size = lax.axis_size(axis)
    return lax.ppermute(value, axis, [((k + 1) % size, k) for k in range(size)])


def shift_far(value):
    size = lax.axis_size("i")
    pairs = [
        (low * size + (k + 1) % size, (1 - low) * size + k) for k in range(size) for low in range(2)
    ]
    return shift(lax.ppermute(value, ("c", "i"), pairs), "c")


def far_gather(value):
    parts = [value]
    for _ in range(lax.axis_size("i") - 1):
        parts.append(shift_far(parts[-1]))
    return parts


def far_scatter(blocks, after):
    size = lax.axis_size("i")
    travelling = blocks[1].astype(BF16)
    for j in range(2, size):
        travelling = (shift_far(travelling).astype(F32) + blocks[j]).astype(BF16)
    arrived, _ = lax.optimization_barrier((shift_far(travelling), after))
    return arrived.astype(F32) + blocks[0]


def ring_gather(value, axis):
    parts = [value]
    for _ in range(lax.axis_size(axis) - 1):
        parts.append(shift(parts[-1], axis))
    return parts


def ring_scatter(blocks, axis):
    size = lax.axis_size(axis)
    travelling = blocks[1].astype(BF16)
    for j in range(2, size):
        travelling = (shift(travelling, axis).astype(F32) + blocks[j]).astype(BF16)
    return shift(travelling, axis).astype(F32) + blocks[0]


def in_order(parts, axis, place=0):
    if len(parts) == 2:
        first = lax.axis_index(axis) == 0
        return jnp.stack([jnp.where(first, *parts), jnp.where(first, *parts[::-1])], axis=place)
    return jnp.roll(jnp.stack(parts, axis=place), lax.axis_index(axis), axis=place)


def from_order(parts, axis):
    if len(parts) == 2:
        first = lax.axis_index(axis) == 0
        return [jnp.where(first, *parts), jnp.where(first, *parts[::-1])]
    return list(jnp.roll(jnp.stack(parts), -lax.axis_index(axis), axis=0))


def sum_all(value):
    for axis in ALL:
        size = lax.axis_size(axis)
        step = 1
        while step < size:
            value = value + lax.ppermute(value, axis, [(k, k ^ step) for k in range(size)])
            step *= 2
    return value


def pair_gates(normed, router, route, experts):
    logits = jnp.dot(normed.astype(F32), router, precision=HIGHEST)
    onehot = (route[:, :, None] == jnp.arange(experts, dtype=jnp.int32)[None, None, :]).astype(F32)
    picked = jnp.sum(logits[:, None, :] * onehot, axis=-1)
    return (jax.nn.softmax(picked, axis=-1), onehot)


def gates_back(gates, onehot, d_gates, normed, router):
    d_picked = gates * (d_gates - jnp.sum(gates * d_gates, axis=-1, keepdims=True))
    d_logits = jnp.sum(d_picked[:, :, None] * onehot, axis=1)
    d_router = jnp.dot(d_logits.T, normed.astype(F32), precision=HIGHEST)
    d_normed = jnp.dot(d_logits, router.T, precision=HIGHEST)
    return (d_router, d_normed)


def to_experts(gates, onehot, extra):
    by_expert = jnp.sum(gates[:, :, None] * onehot, axis=1).T
    rows = jnp.repeat(by_expert, OUTER, axis=0)[:, None, :]
    if extra is not None:
        rows = jnp.concatenate(
            [rows, jnp.broadcast_to(extra[None, None, :], rows.shape)], axis=1
        )
    return lax.all_to_all(rows, GROUP, split_axis=0, concat_axis=0, tiled=True)


def from_experts(d_gates, onehot, experts):
    rows = lax.all_to_all(d_gates, GROUP, split_axis=0, concat_axis=0, tiled=True)
    by_expert = jnp.sum(rows.reshape(experts, OUTER, -1), axis=1)
    return jnp.einsum("tce,et->tc", onehot, by_expert, precision=HIGHEST)


def meet(rows):
    return lax.all_gather(rows, GROUP, axis=0, tiled=True)


def part(rows):
    return lax.psum_scatter(rows, GROUP, scatter_dimension=0, tiled=True)


def mm(form, first, second):
    return jnp.einsum(form, first, second, preferred_element_type=F32)


def head_blocks(matrix):
    span = HEADS // OUTER * HD
    return jnp.stack([matrix[:, k * span : (k + 1) * span] for k in range(OUTER)])


def join_blocks(blocks):
    return jnp.concatenate([blocks[k] for k in range(OUTER)], axis=1)


def exchange(blocks):
    return lax.all_to_all(blocks, "o", split_axis=0, concat_axis=0, tiled=True)


def gather_heads(places, query_weight, kv_weight, beside):
    whole = HEADS * HD
    rows = query_weight.shape[0]
    here = exchange(
        jnp.concatenate(
            [
                head_blocks(query_weight),
                head_blocks(kv_weight[:, :whole]),
                head_blocks(kv_weight[:, whole:]),
            ],
            axis=1,
        )
    )
    here, beside = lax.optimization_barrier((here, beside()))
    span = here.shape[2]
    kv = ring_gather(here[:, rows:].reshape(OUTER, 2, -1, span), "i")
    query_source, _ = lax.optimization_barrier((here[:, :rows], kv[-1]))
    query = ring_gather(query_source, "i")
    kv = ring_gather(jnp.stack(kv), "y")
    query, kv = lax.optimization_barrier((query, kv))
    query = in_order(query, "i", 1).reshape(-1, span)
    seen = kv[-1][0, 0, 0, 0]
    kv = jnp.stack(ring_gather(jnp.stack(kv), "c"))
    return query, arrange(places, kv), beside, seen


def scatter_query(grad):
    inner = lax.axis_size("i")
    blocks = grad.reshape(OUTER, inner, -1, grad.shape[1])
    blocks = from_order([blocks[:, k] for k in range(inner)], "i")
    mine = ring_scatter(blocks, "i").astype(BF16)
    return join_blocks(exchange(mine)).astype(F32)


def scatter_kv(kept, sent):
    mine = lax.ppermute(sent, "c", [(0, 1), (1, 0)]).astype(F32) + kept
    high, inner = lax.axis_size("y"), lax.axis_size("i")
    wide = kept.shape[-1]
    mine = mine.reshape(high, OUTER, inner, -1, wide)
    mine = ring_scatter(from_order([mine[k] for k in range(high)], "y"), "y")
    mine = ring_scatter(from_order([mine[:, k] for k in range(inner)], "i"), "i").astype(BF16)
    here = exchange(mine)
    half = wide // 2
    return jnp.concatenate(
        [join_blocks(here[:, :, :half]), join_blocks(here[:, :, half:])], axis=1
    ).astype(F32)


def own_places():
    return jnp.stack([lax.axis_index(axis) for axis in ALL]).astype(jnp.int32)


def add_low(first, second):
    return (first.astype(F32) + second.astype(F32)).astype(BF16)


def ring_low(blocks, axis):
    travelling = blocks[1]
    for j in range(2, lax.axis_size(axis)):
        travelling = add_low(shift(travelling, axis), blocks[j])
    return add_low(shift(travelling, axis), blocks[0])


def part_low(rows):
    return ring_low([rows[k] for k in range(rows.shape[0])], "c")


def part_first(rows):
    half = rows.shape[2] // 2
    first, second = rows[:, :, :half], rows[:, :, half:]
    first = ring_low([first[k] for k in range(first.shape[0])], "y")
    second = ring_low([second[:, k] for k in range(second.shape[1])], "o")
    return first, second


def part_second(first, second):
    first = ring_low([first[k] for k in range(first.shape[0])], "o")
    second = ring_low([second[k] for k in range(second.shape[0])], "y")
    return jnp.concatenate([first, second])


VMEM = 56 * 1024 * 1024
ROW_STEP = 256


def nn(first, second):
    return jnp.dot(first, second, preferred_element_type=F32)


def nt(first, second):
    return lax.dot_general(first, second, (((1,), (1,)), ((), ())), preferred_element_type=F32)


def tn(first, second):
    return lax.dot_general(first, second, (((0,), (0,)), ((), ())), preferred_element_type=F32)


def as_column(row, rows):
    return jnp.broadcast_to(row, (rows, rows)).T[:, :1]


def turn(head, cosine, sine):
    return head * cosine + pltpu.roll(head, HD // 2, 1) * sine


def turn_back(head, cosine, sine):
    return head * cosine - pltpu.roll(head, HD // 2, 1) * sine


def allowed_keys(segment, length):
    keys = jnp.broadcast_to(segment, (length, length))
    row = lax.broadcasted_iota(jnp.int32, (length, length), 0)
    column = lax.broadcasted_iota(jnp.int32, (length, length), 1)
    return (keys == keys.T) & (column <= row)


def heads_nt(first, second):
    return lax.dot_general(first, second, (((2,), (2,)), ((0,), (0,))), preferred_element_type=F32)


def heads_nn(first, second):
    return lax.dot_general(first, second, (((2,), (1,)), ((0,), (0,))), preferred_element_type=F32)


def heads_tn(first, second):
    return lax.dot_general(first, second, (((1,), (1,)), ((0,), (0,))), preferred_element_type=F32)


def softmax_rows(queries, keys, allowed):
    scores = jnp.where(allowed[None], heads_nt(queries, keys) * (1.0 / math.sqrt(HD)), MASKED)
    exponent = jnp.exp(scores - jnp.max(scores, axis=-1, keepdims=True))
    return exponent / jnp.sum(exponent, axis=-1, keepdims=True)


def place_rows(places_ref, part_ref, value, length):
    count = part_ref.shape[2]
    for seq in range(count):
        slot = lax.rem(seq - places_ref[2] + count, count)
        part_ref[0, 0, slot] = value[seq * length : (seq + 1) * length]


def arrange_kernel(places_ref, in_ref, out_ref):
    del places_ref
    half = in_ref.shape[-1]
    for outer in range(OUTER):
        out_ref[0, 0, outer, 0, :, :half] = in_ref[0, 0, 0, outer, 0]
        out_ref[0, 0, outer, 0, :, half:] = in_ref[0, 0, 0, outer, 1]


def attend_kernel(
    places_ref,
    x_ref,
    info_ref,
    cos_ref,
    sin_ref,
    query_ref,
    kv_ref,
    out_ref,
    qkv_ref,
    gated_ref,
    part_ref,
):
    length = cos_ref.shape[0]
    span = out_ref.shape[0]
    raw_query = nn(x_ref[...], query_ref[...])
    raw = nn(x_ref[...], kv_ref[...])
    cosine, sine = cos_ref[...], sin_ref[...]
    starts = range(0, span, HD)
    for seq in range(info_ref.shape[0]):
        rows = slice(seq * length, (seq + 1) * length)
        gate = as_column(info_ref[seq, 0:1, :], length)
        allowed = allowed_keys(info_ref[seq, 1:2, :], length)
        queries, keys, values = [], [], []
        for at in starts:
            head = raw_query[rows, at : at + HD].astype(BF16).astype(F32)
            queries.append(turn(head, cosine, sine).astype(BF16))
            keys.append(turn(raw[rows, at : at + HD], cosine, sine).astype(BF16))
            values.append(raw[rows, span + at : span + at + HD].astype(BF16))
            qkv_ref[rows, at : at + HD] = queries[-1]
            qkv_ref[rows, span + at : span + at + HD] = keys[-1]
            qkv_ref[rows, 2 * span + at : 2 * span + at + HD] = values[-1]
        probs = softmax_rows(jnp.stack(queries), jnp.stack(keys), allowed)
        gated = (heads_nn(probs.astype(BF16), jnp.stack(values)) * gate[None]).astype(BF16)
        for number, at in enumerate(starts):
            gated_ref[rows, at : at + HD] = gated[number]
    place_rows(places_ref, part_ref, nn(gated_ref[...], out_ref[...]).astype(BF16), length)


def attend_back_kernel(
    places_ref,
    mid_ref,
    info_ref,
    cos_ref,
    sin_ref,
    qkv_ref,
    x_ref,
    query_ref,
    kv_ref,
    out_ref,
    d_query_ref,
    d_kv_ref,
    part_ref,
    d_gate_ref,
    d_gain_ref,
):
    del places_ref
    length = cos_ref.shape[0]
    span = out_ref.shape[0]
    scale = 1.0 / math.sqrt(HD)
    d_rows = nt(mid_ref[...], out_ref[...])
    cosine, sine = cos_ref[...], sin_ref[...]
    starts = range(0, span, HD)
    for seq in range(info_ref.shape[0]):
        rows = slice(seq * length, (seq + 1) * length)
        gate = as_column(info_ref[seq, 0:1, :], length)[None]
        allowed = allowed_keys(info_ref[seq, 1:2, :], length)
        queries = jnp.stack([qkv_ref[rows, at : at + HD] for at in starts])
        keys = jnp.stack([qkv_ref[rows, span + at : span + at + HD] for at in starts])
        values = jnp.stack([qkv_ref[rows, 2 * span + at : 2 * span + at + HD] for at in starts])
        d_heads = jnp.stack([d_rows[rows, at : at + HD] for at in starts])
        probs = softmax_rows(queries, keys, allowed)
        weighted = probs * heads_nt(d_heads.astype(BF16), values)
        sums = jnp.sum(weighted, axis=-1, keepdims=True)
        d_scores = ((weighted - probs * sums) * gate).astype(BF16)
        d_queries = heads_nn(d_scores, keys) * scale
        d_keys = heads_tn(d_scores, queries) * scale
        d_values = heads_tn(probs.astype(BF16), (d_heads * gate).astype(BF16))
        for number, at in enumerate(starts):
            cols = slice(at, at + HD)
            d_query_ref[rows, cols] = turn_back(d_queries[number], cosine, sine).astype(BF16)
            d_kv_ref[rows, cols] = turn_back(d_keys[number], cosine, sine).astype(BF16)
            d_kv_ref[rows, span + at : span + at + HD] = d_values[number].astype(BF16)
        total = jnp.broadcast_to(jnp.sum(sums, axis=0), (length, length))
        d_gate_ref[seq] = total.T[:1]
    d_input = nt(d_query_ref[...], query_ref[...]) + nt(d_kv_ref[...], kv_ref[...])

    @pl.when(pl.program_id(0) == 0)
    def _():
        d_gain_ref[...] = jnp.zeros_like(d_gain_ref)

    d_gain_ref[...] += jnp.sum(d_input * x_ref[...].astype(F32), axis=0, keepdims=True)
    part_ref[...] = d_input.astype(BF16)


def layer_rows_kernel(parts, places_ref, *refs):
    gated_refs, down_refs, part_ref = refs[:parts], refs[parts : 2 * parts], refs[2 * parts]
    length = part_ref.shape[3]
    value = nn(gated_refs[0][...], down_refs[0][...])
    for part in range(1, parts):
        value = value + nn(gated_refs[part][...], down_refs[part][...])
    place_rows(places_ref, part_ref, value.astype(BF16), length)


def fixed(shape):
    return pl.BlockSpec(shape, lambda step, places: (0,) * len(shape))


def rows_spec(rows, columns):
    return pl.BlockSpec((rows, columns), lambda step, places: (step, 0))


def info_spec(seqs, kinds, length):
    return pl.BlockSpec((seqs, kinds, length), lambda step, places: (step, 0, 0))


def place_spec(high, length, width):
    def index(step, places):
        low = lax.rem(lax.rem(step, 2) - places[1] + 2, 2)
        return (low, lax.rem(lax.div(step, 2) - places[0] + high, high), 0, 0, 0)

    return pl.BlockSpec((1, 1, OUTER, length, width), index)


def shape(dims, dtype=BF16):
    return jax.ShapeDtypeStruct(dims, dtype)


def call(kernel, name, steps, in_specs, out_specs, out_shape, flops, moved, operands):
    return pl.pallas_call(
        kernel,
        grid_spec=pltpu.PrefetchScalarGridSpec(
            num_scalar_prefetch=1, grid=(steps,), in_specs=in_specs, out_specs=out_specs
        ),
        out_shape=out_shape,
        compiler_params=pltpu.CompilerParams(vmem_limit_bytes=VMEM),
        cost_estimate=pl.CostEstimate(flops=flops, bytes_accessed=moved, transcendentals=0),
        name=name,
    )(*operands)


def arrange(places, value):
    low, high, inner, outer, kinds, rows, span = value.shape

    def index(step, places):
        y = lax.div(step, 2 * inner)
        c = lax.rem(lax.div(step, inner), 2)
        i = lax.rem(step, inner)
        return (
            lax.rem(c - places[1] + 2, 2),
            lax.rem(y - places[0] + high, high),
            lax.rem(i - places[3] + inner, inner),
            0,
            0,
            0,
            0,
        )

    def out_index(step, places):
        return (
            lax.div(step, 2 * inner),
            lax.rem(lax.div(step, inner), 2),
            0,
            lax.rem(step, inner),
            0,
            0,
        )

    dims = (high, low, outer, inner, rows, kinds * span)
    found = call(
        arrange_kernel,
        "arrange",
        high * low * inner,
        [pl.BlockSpec((1, 1, 1, outer, kinds, rows, span), index)],
        pl.BlockSpec((1, 1, outer, 1, rows, kinds * span), out_index),
        shape(dims),
        0,
        4 * value.size,
        (places, value),
    )
    return found.reshape(-1, kinds * span)


def attend(places, rows, info, cosine, sine, query_mat, kv_mat, out_mat):
    count, width = rows.shape
    span = out_mat.shape[0]
    length = cosine.shape[0]
    step = OUTER * length
    high = count // (2 * step)
    return call(
        attend_kernel,
        "attend",
        count // step,
        [
            rows_spec(step, width),
            info_spec(OUTER, 2, length),
            fixed(cosine.shape),
            fixed(sine.shape),
            fixed(query_mat.shape),
            fixed(kv_mat.shape),
            fixed(out_mat.shape),
        ],
        [rows_spec(step, 3 * span), rows_spec(step, span), place_spec(high, length, width)],
        [shape((count, 3 * span)), shape((count, span)), shape((2, high, OUTER, length, width))],
        2 * count * width * 4 * span + 4 * count * length * span,
        4 * count * (width + 2 * span),
        (places, rows, info, cosine, sine, query_mat, kv_mat, out_mat),
    )


def attend_back(places, d_middle, info, cosine, sine, qkv, rows, query_mat, kv_mat, out_mat):
    count, width = d_middle.shape
    length = cosine.shape[0]
    step = OUTER * length
    span = out_mat.shape[0]
    return call(
        attend_back_kernel,
        "attend_back",
        count // step,
        [
            rows_spec(step, width),
            info_spec(OUTER, 2, length),
            fixed(cosine.shape),
            fixed(sine.shape),
            rows_spec(step, 3 * span),
            rows_spec(step, width),
            fixed(query_mat.shape),
            fixed(kv_mat.shape),
            fixed(out_mat.shape),
        ],
        [
            rows_spec(step, span),
            rows_spec(step, 2 * span),
            rows_spec(step, width),
            info_spec(OUTER, 1, length),
            fixed((1, width)),
        ],
        [
            shape((count, span)),
            shape((count, 2 * span)),
            shape((count, width)),
            shape((count // length, 1, length), F32),
            shape((1, width), F32),
        ],
        2 * count * width * 4 * span + 10 * count * length * span,
        4 * count * (2 * width + 3 * span),
        (places, d_middle, info, cosine, sine, qkv, rows, query_mat, kv_mat, out_mat),
    )


def layer_rows(places, gated_units, down_parts, length):
    count, units = gated_units[0].shape
    width = down_parts[0].shape[1]
    parts = len(down_parts)
    step = OUTER * length
    high = count // (2 * step)
    return call(
        functools.partial(layer_rows_kernel, parts),
        "layer_rows",
        count // step,
        [rows_spec(step, units)] * parts + [fixed(down.shape) for down in down_parts],
        place_spec(high, length, width),
        shape((2, high, OUTER, length, width)),
        2 * count * width * units * parts,
        4 * count * (width + units * parts),
        (places, *gated_units, *down_parts),
    )


def units_kernel(places_ref, x_ref, info_ref, d_units_ref, first_ref, second_ref, *refs):
    del places_ref
    sums_refs, (d_both_ref, gated_ref, back_ref, d_gate_ref) = refs[:-4], refs[-4:]
    length = info_ref.shape[2]
    seqs = info_ref.shape[0]
    units = first_ref.shape[0]
    rows = x_ref[...]
    gate = jnp.concatenate([as_column(info_ref[seq], length) for seq in range(seqs)], axis=0)
    gate_in = nt(rows, first_ref[...])
    up_in = nt(rows, second_ref[...])
    sigma = jax.nn.sigmoid(gate_in)
    active = gate_in * sigma
    hidden_units = active * up_in
    d_units = d_units_ref[...].astype(F32)
    d_gate = jnp.sum(hidden_units * d_units, axis=-1, keepdims=True)
    gated_ref[...] = (hidden_units * gate).astype(BF16)
    d_units = d_units * gate
    d_first = (d_units * up_in * (sigma + active * (1.0 - sigma))).astype(BF16)
    d_second = (d_units * active).astype(BF16)
    d_both_ref[:, :units] = d_first
    d_both_ref[:, units:] = d_second
    back = nn(d_first, first_ref[...]) + nn(d_second, second_ref[...])
    if sums_refs:
        back = back + sums_refs[0][...]
    back_ref[...] = back.astype(back_ref.dtype)
    for seq in range(seqs):
        column = jnp.broadcast_to(d_gate[seq * length : (seq + 1) * length], (length, length))
        d_gate_ref[seq] = column.T[:1]


def run_units(places, rows, info, d_units, first, second, sums, last):
    count, width = rows.shape
    length = info.shape[2]
    units = d_units.shape[1]
    seqs = ROW_STEP // length

    def weight_spec(block):
        return pl.BlockSpec((units, width), lambda step, places: (block, 0))

    extra = [] if sums is None else [sums]
    return call(
        units_kernel,
        "units",
        count // ROW_STEP,
        [rows_spec(ROW_STEP, width), info_spec(seqs, 1, length), rows_spec(ROW_STEP, units)]
        + [weight_spec(first[1]), weight_spec(second[1])]
        + [rows_spec(ROW_STEP, width) for _ in extra],
        [
            rows_spec(ROW_STEP, 2 * units),
            rows_spec(ROW_STEP, units),
            rows_spec(ROW_STEP, width),
            info_spec(seqs, 1, length),
        ],
        [
            shape((count, 2 * units)),
            shape((count, units)),
            shape((count, width), BF16 if last else F32),
            shape((count // length, 1, length), F32),
        ],
        0,
        0,
        (places, rows, info, d_units, first[0], second[0], *extra),
    )


def shards(
    hidden_in,
    segment_ids,
    att_route,
    mlp_route,
    norm_gain1,
    norm_gain2,
    att_router,
    mlp_router,
    kv_weight,
    query_weight,
    out_weight,
    att_bias,
    up_weight,
    down_weight,
    mlp_bias,
    cotangent,
):
    experts = lax.axis_size(EXPERT)
    inner = lax.axis_size("i")
    tokens, width = hidden_in.shape
    span = HEADS // OUTER * HD
    cosine, sine_table = rope_tables(tokens)

    places = own_places()
    tie = lax.optimization_barrier

    query_mat, kv_mat, down_parts, seen = gather_heads(
        places, query_weight[0], kv_weight, lambda: ring_gather(down_weight[0], "i")
    )
    out_source, _ = tie((out_weight[0], seen))
    out_mat = in_order(ring_gather(out_source, "i"), "i").reshape(span, width)
    own_up = up_weight[0].reshape(-1, width)

    residual = hidden_in.astype(F32)
    normed_one, inverse_one = norm_rows(residual, norm_gain1)
    attn_input = normed_one.astype(BF16)
    att_gate, att_onehot = pair_gates(attn_input, att_router, att_route, experts)
    info = to_experts(att_gate, att_onehot, segment_ids[0].astype(F32))
    all_attn = meet(attn_input)
    cot_low, _ = tie((cotangent.astype(BF16), seen))
    all_cot = meet(cot_low)
    qkv, gated, branch = attend(
        places, all_attn, info, cosine, sine_table, query_mat, kv_mat, out_mat
    )
    up_source, branch = tie((own_up, branch))
    branch = part_second(*part_first(part_low(branch)))

    d_units = [mm("td,fd->tf", all_cot, down).astype(BF16) for down in down_parts]
    branch, d_units = tie((branch, d_units))
    middle = residual + branch.astype(F32) + att_bias
    normed_two, inverse_two = norm_rows(middle, norm_gain2)
    mlp_input = normed_two.astype(BF16)
    mlp_gate, mlp_onehot = pair_gates(mlp_input, mlp_router, mlp_route, experts)
    up_parts = far_gather(up_source)
    all_mlp = meet(mlp_input)
    gate_m = to_experts(mlp_gate, mlp_onehot, None)
    d_both, gated_units, rows_back, d_gate_m = [], [], None, None
    for number, up in enumerate(up_parts):
        source = own_up if number == 0 else up
        found = run_units(
            places,
            all_mlp,
            gate_m,
            d_units[number],
            (source, 0),
            (source, 1),
            rows_back,
            number == inner - 1,
        )
        d_both.append(found[0])
        gated_units.append(found[1])
        rows_back = found[2]
        d_gate_m = found[3] if d_gate_m is None else d_gate_m + found[3]
    d_mlp_input = part(rows_back)
    d_mlp_gate = from_experts(d_gate_m[:, 0], mlp_onehot, experts)
    grad_up = [mm("tf,td->fd", d_here, all_mlp) for d_here in d_both]
    grad_down = [mm("tf,td->fd", here, all_cot) for here in gated_units]
    low_up = [one.astype(BF16) for one in grad_up[1:]]
    low_down = [one.astype(BF16) for one in grad_down[1:]]
    rows_out = part_low(layer_rows(places, gated_units, down_parts, tokens))
    half = tokens // 2
    rows_first, rows_second = rows_out[:, :, :half], rows_out[:, :, half:]
    rows_first = ring_low([rows_first[k] for k in range(rows_first.shape[0])], "y")
    d_mlp_input, rows_first, low_up, low_down = tie((d_mlp_input, rows_first, low_up, low_down))
    d_mlp_router, d_mlp_from_router = gates_back(
        mlp_gate, mlp_onehot, d_mlp_gate, mlp_input, mlp_router
    )
    d_norm_two, d_gain_two = norm_back(
        middle, inverse_two, norm_gain2, d_mlp_input.astype(F32) + d_mlp_from_router
    )
    d_middle = cotangent + d_norm_two
    sums = jnp.concatenate(
        [
            jnp.stack([d_gain_two, jnp.sum(d_middle, axis=0), jnp.sum(cotangent, axis=0)]),
            d_mlp_router,
        ]
    )

    all_mid = meet(d_middle.astype(BF16))
    rows_second = ring_low([rows_second[:, k] for k in range(OUTER)], "o")
    all_mid, rows_second = tie((all_mid, rows_second))
    d_heads, d_kv, rows_one, d_gate_a, d_gain_a = attend_back(
        places, all_mid, info, cosine, sine_table, qkv, all_attn, query_mat, kv_mat, out_mat
    )
    rows_first, rows_second, d_heads = tie((rows_first, rows_second, d_heads))
    layer_out = middle + part_second(rows_first, rows_second).astype(F32) + mlp_bias
    d_attn_input = part(rows_one)
    d_att_gate = from_experts(d_gate_a[:, 0], att_onehot, experts)
    d_kv_mat = mm("td,tf->df", all_attn, d_kv).reshape(experts // 2, 2, -1, 2 * span)
    d_kv_mat = from_order([d_kv_mat[:, 0], d_kv_mat[:, 1]], "c")
    d_kv_sent, d_heads, all_mid = tie((d_kv_mat[1].astype(BF16), d_heads, all_mid))
    d_kv_weight = scatter_kv(d_kv_mat[0], d_kv_sent)
    d_query = scatter_query(mm("td,tf->df", all_attn, d_heads))[None]
    d_out = mm("tf,td->fd", gated, all_mid).reshape(inner, -1, width)
    d_output = ring_scatter(from_order([d_out[k] for k in range(inner)], "i"), "i")[None]
    d_upper = far_scatter(grad_up[:1] + low_up, d_attn_input).reshape(up_weight.shape)
    d_lower = far_scatter(grad_down[:1] + low_down, d_attn_input)[None]
    d_att_router, d_att_from_router = gates_back(
        att_gate, att_onehot, d_att_gate, attn_input, att_router
    )
    d_gain_one = d_gain_a / norm_gain1 + jnp.sum(
        d_att_from_router * residual * inverse_one, axis=0, keepdims=True
    )
    summed = sum_all(jnp.concatenate([d_gain_one, sums, d_att_router]))
    d_attn_input, summed = tie((d_attn_input, summed))
    d_norm_one, _ = norm_back(
        residual, inverse_one, norm_gain1, d_attn_input.astype(F32) + d_att_from_router
    )
    d_input = d_middle + d_norm_one
    return (
        layer_out,
        d_input,
        summed[0],
        summed[1],
        summed[4 + experts :].T,
        summed[4 : 4 + experts].T,
        d_kv_weight,
        d_query,
        d_output,
        summed[2],
        d_upper,
        d_lower,
        summed[3],
    )


def solution(mesh):
    experts, fsdp = mesh.shape["expert"], mesh.shape["fsdp"]
    fine = Mesh(mesh.devices.reshape(experts // 2, 2, OUTER, fsdp // OUTER), ALL)
    shard = ("o", "i")
    rows = P(ALL, None)
    placed = (
        rows,
        rows,
        rows,
        rows,
        P(),
        P(),
        P(),
        P(),
        rows,
        P(EXPERT, shard, None),
        P(EXPERT, shard, None),
        P(),
        P(EXPERT, None, shard, None),
        P(EXPERT, shard, None),
        P(),
        rows,
    )
    return jax.shard_map(
        shards,
        mesh=fine,
        in_specs=placed,
        out_specs=(
            rows,
            rows,
            P(),
            P(),
            P(),
            P(),
            rows,
            P(EXPERT, shard, None),
            P(EXPERT, shard, None),
            P(),
            P(EXPERT, None, shard, None),
            P(EXPERT, shard, None),
            P(),
        ),
        check_vma=False,
    )
```

```python
import functools
import math

import jax
import jax.numpy as jnp
from jax import lax
from jax.experimental import pallas as pl
from jax.experimental.pallas import tpu as pltpu
from jax.sharding import Mesh, PartitionSpec as P

HEADS = 16
HD = 128
TOP = 2


EPSILON = 1e-06
HIGHEST = lax.Precision.HIGHEST
MASKED = -1e30

GROUP = ("y", "c", "o")
EXPERT = ("y", "c")
ALL = ("y", "c", "o", "i")
OUTER = 4
F32 = jnp.float32
BF16 = jnp.bfloat16


def rope_tables(length):
    half_dim = HD // 2
    frequency = jnp.exp(jnp.arange(half_dim, dtype=F32) * (-2.0 * math.log(10000.0) / HD))
    angles = jnp.arange(length, dtype=F32)[:, None] * frequency[None, :]
    cosine, sine = jnp.cos(angles), jnp.sin(angles)
    return (
        jnp.concatenate([cosine, cosine], axis=1),
        jnp.concatenate([-sine, sine], axis=1),
    )


def norm_rows(stream, gain):
    inverse = lax.rsqrt(jnp.mean(stream * stream, axis=-1, keepdims=True) + EPSILON)
    return (stream * inverse * gain, inverse)


def norm_back(stream, inverse, gain, upstream):
    scaled = upstream * gain
    d_stream = inverse * scaled - stream * inverse**3 * jnp.mean(
        scaled * stream, axis=-1, keepdims=True
    )
    d_gain = jnp.sum(upstream * stream * inverse, axis=0)
    return (d_stream, d_gain)


def shift(value, axis):
    size = lax.axis_size(axis)
    return lax.ppermute(value, axis, [((k + 1) % size, k) for k in range(size)])


def after(value, *others):
    token, _ = lax.optimization_barrier((lax.create_token(), others))
    return lax.optimization_barrier((token, value))[1]


def ring_gather(value, axis):
    parts = [value]
    for _ in range(lax.axis_size(axis) - 1):
        parts.append(shift(parts[-1], axis))
    return parts


def ring_open(blocks, axis):
    size = lax.axis_size(axis)
    travelling = blocks[1].astype(BF16)
    for j in range(2, size):
        travelling = (shift(travelling, axis).astype(F32) + blocks[j]).astype(BF16)
    return blocks[0], shift(travelling, axis)


def ring_scatter(blocks, axis, *others):
    own, arrived = ring_open(blocks, axis)
    if others:
        arrived = after(arrived, *others)
    return arrived.astype(F32) + own


def in_order(parts, axis, place=0):
    if len(parts) == 2:
        first = lax.axis_index(axis) == 0
        return jnp.stack([jnp.where(first, *parts), jnp.where(first, *parts[::-1])], axis=place)
    return jnp.roll(jnp.stack(parts, axis=place), lax.axis_index(axis), axis=place)


def from_order(parts, axis):
    if len(parts) == 2:
        first = lax.axis_index(axis) == 0
        return [jnp.where(first, *parts), jnp.where(first, *parts[::-1])]
    return list(jnp.roll(jnp.stack(parts), -lax.axis_index(axis), axis=0))


def sum_all(value):
    for axis in ALL:
        size = lax.axis_size(axis)
        step = 1
        while step < size:
            value = value + lax.ppermute(value, axis, [(k, k ^ step) for k in range(size)])
            step *= 2
    return value


def pair_gates(normed, router, route, experts):
    logits = jnp.dot(normed.astype(F32), router, precision=HIGHEST)
    onehot = (route[:, :, None] == jnp.arange(experts, dtype=jnp.int32)[None, None, :]).astype(F32)
    picked = jnp.sum(logits[:, None, :] * onehot, axis=-1)
    return (jax.nn.softmax(picked, axis=-1), onehot)


def gates_back(gates, onehot, d_gates, normed, router):
    d_picked = gates * (d_gates - jnp.sum(gates * d_gates, axis=-1, keepdims=True))
    d_logits = jnp.sum(d_picked[:, :, None] * onehot, axis=1)
    d_router = jnp.dot(d_logits.T, normed.astype(F32), precision=HIGHEST)
    d_normed = jnp.dot(d_logits, router.T, precision=HIGHEST)
    return (d_router, d_normed)


def to_experts(gates, onehot, extra):
    by_expert = jnp.sum(gates[:, :, None] * onehot, axis=1).T
    rows = jnp.repeat(by_expert, OUTER, axis=0)[:, None, :]
    if extra is not None:
        rows = jnp.concatenate(
            [rows, jnp.broadcast_to(extra[None, None, :], rows.shape)], axis=1
        )
    return lax.all_to_all(rows, GROUP, split_axis=0, concat_axis=0, tiled=True)


def from_experts(d_gates, onehot, experts):
    rows = lax.all_to_all(d_gates, GROUP, split_axis=0, concat_axis=0, tiled=True)
    by_expert = jnp.sum(rows.reshape(experts, OUTER, -1), axis=1)
    return jnp.einsum("tce,et->tc", onehot, by_expert, precision=HIGHEST)


def meet(rows):
    return lax.all_gather(rows, GROUP, axis=0, tiled=True)


def part(rows):
    return lax.psum_scatter(rows, GROUP, scatter_dimension=0, tiled=True)


def mm(form, first, second):
    return jnp.einsum(form, first, second, preferred_element_type=F32)


def head_blocks(matrix):
    span = HEADS // OUTER * HD
    return jnp.stack([matrix[:, k * span : (k + 1) * span] for k in range(OUTER)])


def join_blocks(blocks):
    return jnp.concatenate([blocks[k] for k in range(OUTER)], axis=1)


def exchange(blocks):
    return lax.all_to_all(blocks, "o", split_axis=0, concat_axis=0, tiled=True)


def gather_heads(places, query_weight, kv_weight, beside):
    whole = HEADS * HD
    rows = query_weight.shape[0]
    here = exchange(
        jnp.concatenate(
            [
                head_blocks(query_weight),
                head_blocks(kv_weight[:, :whole]),
                head_blocks(kv_weight[:, whole:]),
            ],
            axis=1,
        )
    )
    here = after(here, *beside)
    span = here.shape[2]
    kv = ring_gather(here[:, rows:].reshape(OUTER, 2, -1, span), "i")
    query = ring_gather(after(here[:, :rows], kv[-1]), "i")
    kv = ring_gather(jnp.stack(kv), "y")
    kv = after(kv, query)
    query = in_order(query, "i", 1).reshape(-1, span)
    seen = kv[-1][0, 0, 0, 0]
    kv = jnp.stack(ring_gather(jnp.stack(kv), "c"))
    return query, arrange(places, kv), seen


def scatter_query(grad):
    inner = lax.axis_size("i")
    blocks = grad.reshape(OUTER, inner, -1, grad.shape[1])
    blocks = from_order([blocks[:, k] for k in range(inner)], "i")
    mine = ring_scatter(blocks, "i").astype(BF16)
    return join_blocks(exchange(mine)).astype(F32)


def scatter_kv(kept, sent):
    mine = lax.ppermute(sent, "c", [(0, 1), (1, 0)]).astype(F32) + kept
    high, inner = lax.axis_size("y"), lax.axis_size("i")
    wide = kept.shape[-1]
    mine = mine.reshape(high, OUTER, inner, -1, wide)
    mine = ring_scatter(from_order([mine[k] for k in range(high)], "y"), "y")
    mine = ring_scatter(from_order([mine[:, k] for k in range(inner)], "i"), "i").astype(BF16)
    here = exchange(mine)
    half = wide // 2
    return jnp.concatenate(
        [join_blocks(here[:, :, :half]), join_blocks(here[:, :, half:])], axis=1
    ).astype(F32)


def own_places():
    return jnp.stack([lax.axis_index(axis) for axis in ALL]).astype(jnp.int32)


def add_low(first, second):
    return (first.astype(F32) + second.astype(F32)).astype(BF16)


def ring_low(blocks, axis):
    travelling = blocks[1]
    for j in range(2, lax.axis_size(axis)):
        travelling = add_low(shift(travelling, axis), blocks[j])
    return add_low(shift(travelling, axis), blocks[0])


def part_low(rows):
    return ring_low([rows[k] for k in range(rows.shape[0])], "c")


def part_first(rows):
    half = rows.shape[2] // 2
    first, second = rows[:, :, :half], rows[:, :, half:]
    first = ring_low([first[k] for k in range(first.shape[0])], "y")
    second = ring_low([second[:, k] for k in range(second.shape[1])], "o")
    return first, second


def part_second(first, second):
    first = ring_low([first[k] for k in range(first.shape[0])], "o")
    second = ring_low([second[k] for k in range(second.shape[0])], "y")
    return jnp.concatenate([first, second])


VMEM = 56 * 1024 * 1024
ROW_STEP = 256


def nn(first, second):
    return jnp.dot(first, second, preferred_element_type=F32)


def nt(first, second):
    return lax.dot_general(first, second, (((1,), (1,)), ((), ())), preferred_element_type=F32)


def tn(first, second):
    return lax.dot_general(first, second, (((0,), (0,)), ((), ())), preferred_element_type=F32)


def as_column(row, rows):
    return jnp.broadcast_to(row, (rows, rows)).T[:, :1]


def turn(head, cosine, sine):
    return head * cosine + pltpu.roll(head, HD // 2, 1) * sine


def turn_back(head, cosine, sine):
    return head * cosine - pltpu.roll(head, HD // 2, 1) * sine


def allowed_keys(segment, length):
    keys = jnp.broadcast_to(segment, (length, length))
    row = lax.broadcasted_iota(jnp.int32, (length, length), 0)
    column = lax.broadcasted_iota(jnp.int32, (length, length), 1)
    return (keys == keys.T) & (column <= row)


def heads_nt(first, second):
    return lax.dot_general(first, second, (((2,), (2,)), ((0,), (0,))), preferred_element_type=F32)


def heads_nn(first, second):
    return lax.dot_general(first, second, (((2,), (1,)), ((0,), (0,))), preferred_element_type=F32)


def heads_tn(first, second):
    return lax.dot_general(first, second, (((1,), (1,)), ((0,), (0,))), preferred_element_type=F32)


def softmax_rows(queries, keys, allowed):
    scores = jnp.where(allowed[None], heads_nt(queries, keys) * (1.0 / math.sqrt(HD)), MASKED)
    exponent = jnp.exp(scores - jnp.max(scores, axis=-1, keepdims=True))
    return exponent / jnp.sum(exponent, axis=-1, keepdims=True)


def place_rows(places_ref, part_ref, value, length):
    count = part_ref.shape[2]
    for seq in range(count):
        slot = lax.rem(seq - places_ref[2] + count, count)
        part_ref[0, 0, slot] = value[seq * length : (seq + 1) * length]


def arrange_kernel(places_ref, in_ref, out_ref):
    del places_ref
    half = in_ref.shape[-1]
    for outer in range(OUTER):
        out_ref[0, 0, outer, 0, :, :half] = in_ref[0, 0, 0, outer, 0]
        out_ref[0, 0, outer, 0, :, half:] = in_ref[0, 0, 0, outer, 1]


def attend_kernel(
    places_ref,
    x_ref,
    info_ref,
    cos_ref,
    sin_ref,
    query_ref,
    kv_ref,
    qkv_ref,
    gated_ref,
):
    del places_ref
    length = cos_ref.shape[0]
    span = query_ref.shape[1]
    raw_query = nn(x_ref[...], query_ref[...])
    raw = nn(x_ref[...], kv_ref[...])
    cosine, sine = cos_ref[...], sin_ref[...]
    starts = range(0, span, HD)
    for seq in range(info_ref.shape[0]):
        rows = slice(seq * length, (seq + 1) * length)
        gate = as_column(info_ref[seq, 0:1, :], length)
        allowed = allowed_keys(info_ref[seq, 1:2, :], length)
        queries, keys, values = [], [], []
        for at in starts:
            head = raw_query[rows, at : at + HD].astype(BF16).astype(F32)
            queries.append(turn(head, cosine, sine).astype(BF16))
            keys.append(turn(raw[rows, at : at + HD], cosine, sine).astype(BF16))
            values.append(raw[rows, span + at : span + at + HD].astype(BF16))
            qkv_ref[rows, at : at + HD] = queries[-1]
            qkv_ref[rows, span + at : span + at + HD] = keys[-1]
            qkv_ref[rows, 2 * span + at : 2 * span + at + HD] = values[-1]
        probs = softmax_rows(jnp.stack(queries), jnp.stack(keys), allowed)
        gated = (heads_nn(probs.astype(BF16), jnp.stack(values)) * gate[None]).astype(BF16)
        for number, at in enumerate(starts):
            gated_ref[rows, at : at + HD] = gated[number]


def attend_back_kernel(
    places_ref,
    mid_ref,
    info_ref,
    cos_ref,
    sin_ref,
    qkv_ref,
    x_ref,
    query_ref,
    kv_ref,
    out_ref,
    d_query_ref,
    d_kv_ref,
    part_ref,
    d_gate_ref,
    d_gain_ref,
):
    del places_ref
    length = cos_ref.shape[0]
    span = out_ref.shape[0]
    scale = 1.0 / math.sqrt(HD)
    d_rows = nt(mid_ref[...], out_ref[...])
    cosine, sine = cos_ref[...], sin_ref[...]
    starts = range(0, span, HD)
    for seq in range(info_ref.shape[0]):
        rows = slice(seq * length, (seq + 1) * length)
        gate = as_column(info_ref[seq, 0:1, :], length)[None]
        allowed = allowed_keys(info_ref[seq, 1:2, :], length)
        queries = jnp.stack([qkv_ref[rows, at : at + HD] for at in starts])
        keys = jnp.stack([qkv_ref[rows, span + at : span + at + HD] for at in starts])
        values = jnp.stack([qkv_ref[rows, 2 * span + at : 2 * span + at + HD] for at in starts])
        d_heads = jnp.stack([d_rows[rows, at : at + HD] for at in starts])
        probs = softmax_rows(queries, keys, allowed)
        weighted = probs * heads_nt(d_heads.astype(BF16), values)
        sums = jnp.sum(weighted, axis=-1, keepdims=True)
        d_scores = ((weighted - probs * sums) * gate).astype(BF16)
        d_queries = heads_nn(d_scores, keys) * scale
        d_keys = heads_tn(d_scores, queries) * scale
        d_values = heads_tn(probs.astype(BF16), (d_heads * gate).astype(BF16))
        for number, at in enumerate(starts):
            cols = slice(at, at + HD)
            d_query_ref[rows, cols] = turn_back(d_queries[number], cosine, sine).astype(BF16)
            d_kv_ref[rows, cols] = turn_back(d_keys[number], cosine, sine).astype(BF16)
            d_kv_ref[rows, span + at : span + at + HD] = d_values[number].astype(BF16)
        total = jnp.broadcast_to(jnp.sum(sums, axis=0), (length, length))
        d_gate_ref[seq] = total.T[:1]
    d_input = nt(d_query_ref[...], query_ref[...]) + nt(d_kv_ref[...], kv_ref[...])

    @pl.when(pl.program_id(0) == 0)
    def _():
        d_gain_ref[...] = jnp.zeros_like(d_gain_ref)

    d_gain_ref[...] += jnp.sum(d_input * x_ref[...].astype(F32), axis=0, keepdims=True)
    part_ref[...] = d_input.astype(BF16)


def rows_kernel(parts, places_ref, *refs):
    gated_refs, down_refs, part_ref = refs[:parts], refs[parts : 2 * parts], refs[2 * parts]
    length = part_ref.shape[3]
    value = nn(gated_refs[0][...], down_refs[0][...])
    for part in range(1, parts):
        value = value + nn(gated_refs[part][...], down_refs[part][...])
    place_rows(places_ref, part_ref, value.astype(BF16), length)


def fixed(shape):
    return pl.BlockSpec(shape, lambda step, places: (0,) * len(shape))


def rows_spec(rows, columns):
    return pl.BlockSpec((rows, columns), lambda step, places: (step, 0))


def info_spec(seqs, kinds, length):
    return pl.BlockSpec((seqs, kinds, length), lambda step, places: (step, 0, 0))


def place_spec(high, length, width):
    def index(step, places):
        low = lax.rem(lax.rem(step, 2) - places[1] + 2, 2)
        return (low, lax.rem(lax.div(step, 2) - places[0] + high, high), 0, 0, 0)

    return pl.BlockSpec((1, 1, OUTER, length, width), index)


def shape(dims, dtype=BF16):
    return jax.ShapeDtypeStruct(dims, dtype)


def call(kernel, name, steps, in_specs, out_specs, out_shape, flops, moved, operands):
    return pl.pallas_call(
        kernel,
        grid_spec=pltpu.PrefetchScalarGridSpec(
            num_scalar_prefetch=1, grid=(steps,), in_specs=in_specs, out_specs=out_specs
        ),
        out_shape=out_shape,
        compiler_params=pltpu.CompilerParams(vmem_limit_bytes=VMEM),
        cost_estimate=pl.CostEstimate(flops=flops, bytes_accessed=moved, transcendentals=0),
        name=name,
    )(*operands)


def arrange(places, value):
    low, high, inner, outer, kinds, rows, span = value.shape

    def index(step, places):
        y = lax.div(step, 2 * inner)
        c = lax.rem(lax.div(step, inner), 2)
        i = lax.rem(step, inner)
        return (
            lax.rem(c - places[1] + 2, 2),
            lax.rem(y - places[0] + high, high),
            lax.rem(i - places[3] + inner, inner),
            0,
            0,
            0,
            0,
        )

    def out_index(step, places):
        return (
            lax.div(step, 2 * inner),
            lax.rem(lax.div(step, inner), 2),
            0,
            lax.rem(step, inner),
            0,
            0,
        )

    dims = (high, low, outer, inner, rows, kinds * span)
    found = call(
        arrange_kernel,
        "arrange",
        high * low * inner,
        [pl.BlockSpec((1, 1, 1, outer, kinds, rows, span), index)],
        pl.BlockSpec((1, 1, outer, 1, rows, kinds * span), out_index),
        shape(dims),
        0,
        4 * value.size,
        (places, value),
    )
    return found.reshape(-1, kinds * span)


def attend(places, rows, info, cosine, sine, query_mat, kv_mat):
    count, width = rows.shape
    span = query_mat.shape[1]
    length = cosine.shape[0]
    step = OUTER * length
    return call(
        attend_kernel,
        "attend",
        count // step,
        [
            rows_spec(step, width),
            info_spec(OUTER, 2, length),
            fixed(cosine.shape),
            fixed(sine.shape),
            fixed(query_mat.shape),
            fixed(kv_mat.shape),
        ],
        [rows_spec(step, 3 * span), rows_spec(step, span)],
        [shape((count, 3 * span)), shape((count, span))],
        2 * count * width * 3 * span + 4 * count * length * span,
        4 * count * (width + 2 * span),
        (places, rows, info, cosine, sine, query_mat, kv_mat),
    )


def attend_back(places, d_middle, info, cosine, sine, qkv, rows, query_mat, kv_mat, out_mat):
    count, width = d_middle.shape
    length = cosine.shape[0]
    step = OUTER * length
    span = out_mat.shape[0]
    return call(
        attend_back_kernel,
        "attend_back",
        count // step,
        [
            rows_spec(step, width),
            info_spec(OUTER, 2, length),
            fixed(cosine.shape),
            fixed(sine.shape),
            rows_spec(step, 3 * span),
            rows_spec(step, width),
            fixed(query_mat.shape),
            fixed(kv_mat.shape),
            fixed(out_mat.shape),
        ],
        [
            rows_spec(step, span),
            rows_spec(step, 2 * span),
            rows_spec(step, width),
            info_spec(OUTER, 1, length),
            fixed((1, width)),
        ],
        [
            shape((count, span)),
            shape((count, 2 * span)),
            shape((count, width)),
            shape((count // length, 1, length), F32),
            shape((1, width), F32),
        ],
        2 * count * width * 4 * span + 10 * count * length * span,
        4 * count * (2 * width + 3 * span),
        (places, d_middle, info, cosine, sine, qkv, rows, query_mat, kv_mat, out_mat),
    )


def ring_rows(places, gated_units, down_parts, length):
    count, units = gated_units[0].shape
    width = down_parts[0].shape[1]
    parts = len(down_parts)
    step = OUTER * length
    high = count // (2 * step)
    return call(
        functools.partial(rows_kernel, parts),
        "rows",
        count // step,
        [rows_spec(step, units)] * parts + [fixed(down.shape) for down in down_parts],
        place_spec(high, length, width),
        shape((2, high, OUTER, length, width)),
        2 * count * width * units * parts,
        4 * count * (width + units * parts),
        (places, *gated_units, *down_parts),
    )


def units_kernel(places_ref, x_ref, info_ref, d_units_ref, first_ref, second_ref, *refs):
    del places_ref
    sums_refs, (d_both_ref, gated_ref, back_ref, d_gate_ref) = refs[:-4], refs[-4:]
    length = info_ref.shape[2]
    seqs = info_ref.shape[0]
    units = first_ref.shape[0]
    rows = x_ref[...]
    gate = jnp.concatenate([as_column(info_ref[seq], length) for seq in range(seqs)], axis=0)
    gate_in = nt(rows, first_ref[...])
    up_in = nt(rows, second_ref[...])
    sigma = jax.nn.sigmoid(gate_in)
    active = gate_in * sigma
    hidden_units = active * up_in
    d_units = d_units_ref[...].astype(F32)
    d_gate = jnp.sum(hidden_units * d_units, axis=-1, keepdims=True)
    gated_ref[...] = (hidden_units * gate).astype(BF16)
    d_units = d_units * gate
    d_first = (d_units * up_in * (sigma + active * (1.0 - sigma))).astype(BF16)
    d_second = (d_units * active).astype(BF16)
    d_both_ref[:, :units] = d_first
    d_both_ref[:, units:] = d_second
    back = nn(d_first, first_ref[...]) + nn(d_second, second_ref[...])
    if sums_refs:
        back = back + sums_refs[0][...]
    back_ref[...] = back.astype(back_ref.dtype)
    for seq in range(seqs):
        column = jnp.broadcast_to(d_gate[seq * length : (seq + 1) * length], (length, length))
        d_gate_ref[seq] = column.T[:1]


def run_units(places, rows, info, d_units, first, second, sums, last):
    count, width = rows.shape
    length = info.shape[2]
    units = d_units.shape[1]
    seqs = ROW_STEP // length

    def weight_spec(block):
        return pl.BlockSpec((units, width), lambda step, places: (block, 0))

    extra = [] if sums is None else [sums]
    return call(
        units_kernel,
        "units",
        count // ROW_STEP,
        [rows_spec(ROW_STEP, width), info_spec(seqs, 1, length), rows_spec(ROW_STEP, units)]
        + [weight_spec(first[1]), weight_spec(second[1])]
        + [rows_spec(ROW_STEP, width) for _ in extra],
        [
            rows_spec(ROW_STEP, 2 * units),
            rows_spec(ROW_STEP, units),
            rows_spec(ROW_STEP, width),
            info_spec(seqs, 1, length),
        ],
        [
            shape((count, 2 * units)),
            shape((count, units)),
            shape((count, width), BF16 if last else F32),
            shape((count // length, 1, length), F32),
        ],
        0,
        0,
        (places, rows, info, d_units, first[0], second[0], *extra),
    )


def shards(
    hidden_in,
    segment_ids,
    att_route,
    mlp_route,
    norm_gain1,
    norm_gain2,
    att_router,
    mlp_router,
    kv_weight,
    query_weight,
    out_weight,
    att_bias,
    up_weight,
    down_weight,
    mlp_bias,
    cotangent,
):
    experts = lax.axis_size(EXPERT)
    inner = lax.axis_size("i")
    tokens, width = hidden_in.shape
    span = HEADS // OUTER * HD
    cosine, sine_table = rope_tables(tokens)

    places = own_places()

    down_parts = ring_gather(down_weight[0], "i")
    query_mat, kv_mat, seen = gather_heads(
        places, query_weight[0], kv_weight, down_parts[1:]
    )
    out_mat = in_order(ring_gather(after(out_weight[0], seen), "i"), "i").reshape(span, width)
    own_up = up_weight[0].reshape(-1, width)

    residual = hidden_in.astype(F32)
    normed_one, inverse_one = norm_rows(residual, norm_gain1)
    attn_input = normed_one.astype(BF16)
    att_gate, att_onehot = pair_gates(attn_input, att_router, att_route, experts)
    info = to_experts(att_gate, att_onehot, segment_ids[0].astype(F32))
    all_attn = meet(attn_input)
    all_cot = meet(after(cotangent.astype(BF16), seen))
    qkv, gated = attend(places, all_attn, info, cosine, sine_table, query_mat, kv_mat)
    branch = part_low(ring_rows(places, [gated], [out_mat], tokens))
    branch = part_second(*part_first(branch))

    d_units = [mm("td,fd->tf", all_cot, down).astype(BF16) for down in down_parts]
    branch = after(branch, d_units)
    middle = residual + branch.astype(F32) + att_bias
    normed_two, inverse_two = norm_rows(middle, norm_gain2)
    mlp_input = normed_two.astype(BF16)
    mlp_gate, mlp_onehot = pair_gates(mlp_input, mlp_router, mlp_route, experts)
    up_parts = ring_gather(after(own_up, branch), "i")
    all_mlp = meet(mlp_input)
    gate_m = to_experts(mlp_gate, mlp_onehot, None)
    d_both, gated_units, rows_back, d_gate_m = [], [], None, None
    for number, up in enumerate(up_parts):
        source = own_up if number == 0 else up
        found = run_units(
            places,
            all_mlp,
            gate_m,
            d_units[number],
            (source, 0),
            (source, 1),
            rows_back,
            number == inner - 1,
        )
        d_both.append(found[0])
        gated_units.append(found[1])
        rows_back = found[2]
        d_gate_m = found[3] if d_gate_m is None else d_gate_m + found[3]
    d_mlp_input = part(rows_back)
    d_mlp_gate = from_experts(d_gate_m[:, 0], mlp_onehot, experts)
    grad_up = [mm("tf,td->fd", d_here, all_mlp) for d_here in d_both]
    grad_down = [mm("tf,td->fd", here, all_cot) for here in gated_units]
    low_up = [one.astype(BF16) for one in grad_up[1:]]
    low_down = [one.astype(BF16) for one in grad_down[1:]]
    rows_out = part_low(ring_rows(places, gated_units, down_parts, tokens))
    half = tokens // 2
    rows_first, rows_second = rows_out[:, :, :half], rows_out[:, :, half:]
    rows_first = ring_low([rows_first[k] for k in range(rows_first.shape[0])], "y")
    d_lower, last = ring_open(grad_down[:1] + low_down, "i")
    d_mlp_input = after(d_mlp_input, rows_first, low_up, last)
    d_mlp_router, d_mlp_from_router = gates_back(
        mlp_gate, mlp_onehot, d_mlp_gate, mlp_input, mlp_router
    )
    d_norm_two, d_gain_two = norm_back(
        middle, inverse_two, norm_gain2, d_mlp_input.astype(F32) + d_mlp_from_router
    )
    d_middle = cotangent + d_norm_two
    sums = jnp.concatenate(
        [
            jnp.stack([d_gain_two, jnp.sum(d_middle, axis=0), jnp.sum(cotangent, axis=0)]),
            d_mlp_router,
        ]
    )

    all_mid = meet(d_middle.astype(BF16))
    rows_second = ring_low([rows_second[:, k] for k in range(OUTER)], "o")
    all_mid = after(all_mid, rows_second)
    d_heads, d_kv, rows_one, d_gate_a, d_gain_a = attend_back(
        places, all_mid, info, cosine, sine_table, qkv, all_attn, query_mat, kv_mat, out_mat
    )
    rows_out = part_second(after(rows_first, d_heads), after(rows_second, d_heads))
    layer_out = middle + rows_out.astype(F32) + mlp_bias
    d_attn_input = part(rows_one)
    d_att_gate = from_experts(d_gate_a[:, 0], att_onehot, experts)
    d_kv_mat = mm("td,tf->df", all_attn, d_kv).reshape(experts // 2, 2, -1, 2 * span)
    d_kv_mat = from_order([d_kv_mat[:, 0], d_kv_mat[:, 1]], "c")
    d_kv_sent = d_kv_mat[1].astype(BF16)
    d_heads, all_mid = after((d_heads, all_mid), d_kv_sent)
    d_kv_weight = scatter_kv(d_kv_mat[0], d_kv_sent)
    d_query = scatter_query(mm("td,tf->df", all_attn, d_heads))[None]
    d_out = mm("tf,td->fd", gated, all_mid).reshape(inner, -1, width)
    d_output = ring_scatter(from_order([d_out[k] for k in range(inner)], "i"), "i")[None]
    d_upper = ring_scatter(grad_up[:1] + low_up, "i", d_attn_input).reshape(up_weight.shape)
    d_lower = (after(last, d_attn_input).astype(F32) + d_lower)[None]
    d_att_router, d_att_from_router = gates_back(
        att_gate, att_onehot, d_att_gate, attn_input, att_router
    )
    d_gain_one = d_gain_a / norm_gain1 + jnp.sum(
        d_att_from_router * residual * inverse_one, axis=0, keepdims=True
    )
    summed = sum_all(jnp.concatenate([d_gain_one, sums, d_att_router]))
    d_attn_input = after(d_attn_input, summed)
    d_norm_one, _ = norm_back(
        residual, inverse_one, norm_gain1, d_attn_input.astype(F32) + d_att_from_router
    )
    d_input = d_middle + d_norm_one
    return (
        layer_out,
        d_input,
        summed[0],
        summed[1],
        summed[4 + experts :].T,
        summed[4 : 4 + experts].T,
        d_kv_weight,
        d_query,
        d_output,
        summed[2],
        d_upper,
        d_lower,
        summed[3],
    )


def solution(mesh):
    experts, fsdp = mesh.shape["expert"], mesh.shape["fsdp"]
    fine = Mesh(mesh.devices.reshape(experts // 2, 2, OUTER, fsdp // OUTER), ALL)
    shard = ("o", "i")
    rows = P(ALL, None)
    placed = (
        rows,
        rows,
        rows,
        rows,
        P(),
        P(),
        P(),
        P(),
        rows,
        P(EXPERT, shard, None),
        P(EXPERT, shard, None),
        P(),
        P(EXPERT, None, shard, None),
        P(EXPERT, shard, None),
        P(),
        rows,
    )
    return jax.shard_map(
        shards,
        mesh=fine,
        in_specs=placed,
        out_specs=(
            rows,
            rows,
            P(),
            P(),
            P(),
            P(),
            rows,
            P(EXPERT, shard, None),
            P(EXPERT, shard, None),
            P(),
            P(EXPERT, None, shard, None),
            P(EXPERT, shard, None),
            P(),
        ),
        check_vma=False,
    )
```

```python
import functools
import math

import jax
import jax.numpy as jnp
from jax import lax
from jax.experimental import pallas as pl
from jax.experimental.pallas import tpu as pltpu
from jax.sharding import Mesh, PartitionSpec as P

HEADS = 16
HD = 128
TOP = 2


EPSILON = 1e-06
HIGHEST = lax.Precision.HIGHEST
MASKED = -1e30

GROUP = ("y", "c", "o")
EXPERT = ("y", "c")
ALL = ("y", "c", "o", "i")
OUTER = 4
F32 = jnp.float32
BF16 = jnp.bfloat16


def rope_tables(length):
    half_dim = HD // 2
    frequency = jnp.exp(jnp.arange(half_dim, dtype=F32) * (-2.0 * math.log(10000.0) / HD))
    angles = jnp.arange(length, dtype=F32)[:, None] * frequency[None, :]
    cosine, sine = jnp.cos(angles), jnp.sin(angles)
    return (
        jnp.concatenate([cosine, cosine], axis=1),
        jnp.concatenate([-sine, sine], axis=1),
    )


def norm_rows(stream, gain):
    inverse = lax.rsqrt(jnp.mean(stream * stream, axis=-1, keepdims=True) + EPSILON)
    return (stream * inverse * gain, inverse)


def norm_back(stream, inverse, gain, upstream):
    scaled = upstream * gain
    d_stream = inverse * scaled - stream * inverse**3 * jnp.mean(
        scaled * stream, axis=-1, keepdims=True
    )
    d_gain = jnp.sum(upstream * stream * inverse, axis=0)
    return (d_stream, d_gain)


def shift(value, axis):
    size = lax.axis_size(axis)
    return lax.ppermute(value, axis, [((k + 1) % size, k) for k in range(size)])


def after(value, *others):
    token, _ = lax.optimization_barrier((lax.create_token(), others))
    return lax.optimization_barrier((token, value))[1]


def ring_gather(value, axis):
    parts = [value]
    for _ in range(lax.axis_size(axis) - 1):
        parts.append(shift(parts[-1], axis))
    return parts


def ring_open(blocks, axis):
    size = lax.axis_size(axis)
    travelling = blocks[1].astype(BF16)
    for j in range(2, size):
        travelling = (shift(travelling, axis).astype(F32) + blocks[j]).astype(BF16)
    return blocks[0], shift(travelling, axis)


def ring_scatter(blocks, axis, *others):
    own, arrived = ring_open(blocks, axis)
    if others:
        arrived = after(arrived, *others)
    return arrived.astype(F32) + own


def in_order(parts, axis, place=0):
    if len(parts) == 2:
        first = lax.axis_index(axis) == 0
        return jnp.stack([jnp.where(first, *parts), jnp.where(first, *parts[::-1])], axis=place)
    return jnp.roll(jnp.stack(parts, axis=place), lax.axis_index(axis), axis=place)


def from_order(parts, axis):
    if len(parts) == 2:
        first = lax.axis_index(axis) == 0
        return [jnp.where(first, *parts), jnp.where(first, *parts[::-1])]
    return list(jnp.roll(jnp.stack(parts), -lax.axis_index(axis), axis=0))


def sum_over(value, axes):
    for axis in axes:
        size = lax.axis_size(axis)
        step = 1
        while step < size:
            value = value + lax.ppermute(value, axis, [(k, k ^ step) for k in range(size)])
            step *= 2
    return value


def pair_gates(normed, router, route, experts):
    logits = jnp.dot(normed.astype(F32), router, precision=HIGHEST)
    onehot = (route[:, :, None] == jnp.arange(experts, dtype=jnp.int32)[None, None, :]).astype(F32)
    picked = jnp.sum(logits[:, None, :] * onehot, axis=-1)
    return (jax.nn.softmax(picked, axis=-1), onehot)


def gates_back(gates, onehot, d_gates, normed, router):
    d_picked = gates * (d_gates - jnp.sum(gates * d_gates, axis=-1, keepdims=True))
    d_logits = jnp.sum(d_picked[:, :, None] * onehot, axis=1)
    d_router = jnp.dot(d_logits.T, normed.astype(F32), precision=HIGHEST)
    d_normed = jnp.dot(d_logits, router.T, precision=HIGHEST)
    return (d_router, d_normed)


def to_experts(gates, onehot, extra):
    by_expert = jnp.sum(gates[:, :, None] * onehot, axis=1).T
    rows = jnp.repeat(by_expert, OUTER, axis=0)[:, None, :]
    if extra is not None:
        rows = jnp.concatenate(
            [rows, jnp.broadcast_to(extra[None, None, :], rows.shape)], axis=1
        )
    return lax.all_to_all(rows, GROUP, split_axis=0, concat_axis=0, tiled=True)


def from_experts(d_gates, onehot, experts):
    rows = lax.all_to_all(d_gates, GROUP, split_axis=0, concat_axis=0, tiled=True)
    by_expert = jnp.sum(rows.reshape(experts, OUTER, -1), axis=1)
    return jnp.einsum("tce,et->tc", onehot, by_expert, precision=HIGHEST)


def meet(rows):
    return lax.all_gather(rows, GROUP, axis=0, tiled=True)


def part(rows):
    return lax.psum_scatter(rows, GROUP, scatter_dimension=0, tiled=True)


def mm(form, first, second):
    return jnp.einsum(form, first, second, preferred_element_type=F32)


def head_blocks(matrix):
    span = HEADS // OUTER * HD
    return jnp.stack([matrix[:, k * span : (k + 1) * span] for k in range(OUTER)])


def join_blocks(blocks):
    return jnp.concatenate([blocks[k] for k in range(OUTER)], axis=1)


def exchange(blocks):
    return lax.all_to_all(blocks, "o", split_axis=0, concat_axis=0, tiled=True)


def gather_heads(places, query_weight, kv_weight, beside):
    whole = HEADS * HD
    rows = query_weight.shape[0]
    here = exchange(
        jnp.concatenate(
            [
                head_blocks(query_weight),
                head_blocks(kv_weight[:, :whole]),
                head_blocks(kv_weight[:, whole:]),
            ],
            axis=1,
        )
    )
    here = after(here, *beside)
    span = here.shape[2]
    kv = ring_gather(here[:, rows:].reshape(OUTER, 2, -1, span), "i")
    query = ring_gather(after(here[:, :rows], kv[-1]), "i")
    kv = ring_gather(jnp.stack(kv), "y")
    kv = after(kv, query)
    query = in_order(query, "i", 1).reshape(-1, span)
    seen = kv[-1][0, 0, 0, 0]
    kv = jnp.stack(ring_gather(jnp.stack(kv), "c"))
    return query, arrange(places, kv), seen


def scatter_query(grad, *others):
    inner = lax.axis_size("i")
    blocks = grad.reshape(OUTER, inner, -1, grad.shape[1])
    blocks = from_order([blocks[:, k] for k in range(inner)], "i")
    mine = ring_scatter(blocks[:1] + list(after(blocks[1:], *others)), "i").astype(BF16)
    return join_blocks(exchange(mine)).astype(F32)


def scatter_kv(kept, sent):
    mine = lax.ppermute(sent, "c", [(0, 1), (1, 0)]).astype(F32) + kept
    high, inner = lax.axis_size("y"), lax.axis_size("i")
    wide = kept.shape[-1]
    mine = mine.reshape(high, OUTER, inner, -1, wide)
    own, arrived = ring_open(from_order([mine[k] for k in range(high)], "y"), "y")
    mine = arrived.astype(F32) + own
    mine = ring_scatter(from_order([mine[:, k] for k in range(inner)], "i"), "i").astype(BF16)
    here = exchange(mine)
    half = wide // 2
    whole = jnp.concatenate(
        [join_blocks(here[:, :, :half]), join_blocks(here[:, :, half:])], axis=1
    )
    return whole.astype(F32), arrived


def own_places():
    return jnp.stack([lax.axis_index(axis) for axis in ALL]).astype(jnp.int32)


def add_low(first, second):
    return (first.astype(F32) + second.astype(F32)).astype(BF16)


def ring_low(blocks, axis, *others):
    travelling = blocks[1]
    for j in range(2, lax.axis_size(axis)):
        travelling = add_low(shift(travelling, axis), blocks[j])
    arrived = shift(travelling, axis)
    if others:
        arrived = after(arrived, *others)
    return add_low(arrived, blocks[0])


def part_low(rows):
    return ring_low([rows[k] for k in range(rows.shape[0])], "c")


def part_first(rows):
    half = rows.shape[2] // 2
    first, second = rows[:, :, :half], rows[:, :, half:]
    first = ring_low([first[k] for k in range(first.shape[0])], "y")
    second = ring_low([second[:, k] for k in range(second.shape[1])], "o")
    return first, second


def part_second(first, second):
    first = ring_low([first[k] for k in range(first.shape[0])], "o")
    second = ring_low([second[k] for k in range(second.shape[0])], "y")
    return jnp.concatenate([first, second])


VMEM = 56 * 1024 * 1024
ROW_STEP = 256


def nn(first, second):
    return jnp.dot(first, second, preferred_element_type=F32)


def nt(first, second):
    return lax.dot_general(first, second, (((1,), (1,)), ((), ())), preferred_element_type=F32)


def tn(first, second):
    return lax.dot_general(first, second, (((0,), (0,)), ((), ())), preferred_element_type=F32)


def as_column(row, rows):
    return jnp.broadcast_to(row, (rows, rows)).T[:, :1]


def turn(head, cosine, sine):
    return head * cosine + pltpu.roll(head, HD // 2, 1) * sine


def turn_back(head, cosine, sine):
    return head * cosine - pltpu.roll(head, HD // 2, 1) * sine


def allowed_keys(segment, length):
    keys = jnp.broadcast_to(segment, (length, length))
    row = lax.broadcasted_iota(jnp.int32, (length, length), 0)
    column = lax.broadcasted_iota(jnp.int32, (length, length), 1)
    return (keys == keys.T) & (column <= row)


def heads_nt(first, second):
    return lax.dot_general(first, second, (((2,), (2,)), ((0,), (0,))), preferred_element_type=F32)


def heads_nn(first, second):
    return lax.dot_general(first, second, (((2,), (1,)), ((0,), (0,))), preferred_element_type=F32)


def heads_tn(first, second):
    return lax.dot_general(first, second, (((1,), (1,)), ((0,), (0,))), preferred_element_type=F32)


def softmax_rows(queries, keys, allowed):
    scores = jnp.where(allowed[None], heads_nt(queries, keys) * (1.0 / math.sqrt(HD)), MASKED)
    exponent = jnp.exp(scores - jnp.max(scores, axis=-1, keepdims=True))
    return exponent / jnp.sum(exponent, axis=-1, keepdims=True)


def place_rows(places_ref, part_ref, value, length):
    count = part_ref.shape[2]
    for seq in range(count):
        slot = lax.rem(seq - places_ref[2] + count, count)
        part_ref[0, 0, slot] = value[seq * length : (seq + 1) * length]


def arrange_kernel(places_ref, in_ref, out_ref):
    del places_ref
    half = in_ref.shape[-1]
    for outer in range(OUTER):
        out_ref[0, 0, outer, 0, :, :half] = in_ref[0, 0, 0, outer, 0]
        out_ref[0, 0, outer, 0, :, half:] = in_ref[0, 0, 0, outer, 1]


def attend_kernel(
    places_ref,
    x_ref,
    info_ref,
    cos_ref,
    sin_ref,
    query_ref,
    kv_ref,
    qkv_ref,
    gated_ref,
):
    del places_ref
    length = cos_ref.shape[0]
    span = query_ref.shape[1]
    raw_query = nn(x_ref[...], query_ref[...])
    raw = nn(x_ref[...], kv_ref[...])
    cosine, sine = cos_ref[...], sin_ref[...]
    starts = range(0, span, HD)
    for seq in range(info_ref.shape[0]):
        rows = slice(seq * length, (seq + 1) * length)
        gate = as_column(info_ref[seq, 0:1, :], length)
        allowed = allowed_keys(info_ref[seq, 1:2, :], length)
        queries, keys, values = [], [], []
        for at in starts:
            head = raw_query[rows, at : at + HD].astype(BF16).astype(F32)
            queries.append(turn(head, cosine, sine).astype(BF16))
            keys.append(turn(raw[rows, at : at + HD], cosine, sine).astype(BF16))
            values.append(raw[rows, span + at : span + at + HD].astype(BF16))
            qkv_ref[rows, at : at + HD] = queries[-1]
            qkv_ref[rows, span + at : span + at + HD] = keys[-1]
            qkv_ref[rows, 2 * span + at : 2 * span + at + HD] = values[-1]
        probs = softmax_rows(jnp.stack(queries), jnp.stack(keys), allowed)
        gated = (heads_nn(probs.astype(BF16), jnp.stack(values)) * gate[None]).astype(BF16)
        for number, at in enumerate(starts):
            gated_ref[rows, at : at + HD] = gated[number]


def attend_back_kernel(
    places_ref,
    mid_ref,
    info_ref,
    cos_ref,
    sin_ref,
    qkv_ref,
    x_ref,
    query_ref,
    kv_ref,
    out_ref,
    d_query_ref,
    d_kv_ref,
    part_ref,
    d_gate_ref,
    d_gain_ref,
):
    del places_ref
    length = cos_ref.shape[0]
    span = out_ref.shape[0]
    scale = 1.0 / math.sqrt(HD)
    d_rows = nt(mid_ref[...], out_ref[...])
    cosine, sine = cos_ref[...], sin_ref[...]
    starts = range(0, span, HD)
    for seq in range(info_ref.shape[0]):
        rows = slice(seq * length, (seq + 1) * length)
        gate = as_column(info_ref[seq, 0:1, :], length)[None]
        allowed = allowed_keys(info_ref[seq, 1:2, :], length)
        queries = jnp.stack([qkv_ref[rows, at : at + HD] for at in starts])
        keys = jnp.stack([qkv_ref[rows, span + at : span + at + HD] for at in starts])
        values = jnp.stack([qkv_ref[rows, 2 * span + at : 2 * span + at + HD] for at in starts])
        d_heads = jnp.stack([d_rows[rows, at : at + HD] for at in starts])
        probs = softmax_rows(queries, keys, allowed)
        weighted = probs * heads_nt(d_heads.astype(BF16), values)
        sums = jnp.sum(weighted, axis=-1, keepdims=True)
        d_scores = ((weighted - probs * sums) * gate).astype(BF16)
        d_queries = heads_nn(d_scores, keys) * scale
        d_keys = heads_tn(d_scores, queries) * scale
        d_values = heads_tn(probs.astype(BF16), (d_heads * gate).astype(BF16))
        for number, at in enumerate(starts):
            cols = slice(at, at + HD)
            d_query_ref[rows, cols] = turn_back(d_queries[number], cosine, sine).astype(BF16)
            d_kv_ref[rows, cols] = turn_back(d_keys[number], cosine, sine).astype(BF16)
            d_kv_ref[rows, span + at : span + at + HD] = d_values[number].astype(BF16)
        total = jnp.broadcast_to(jnp.sum(sums, axis=0), (length, length))
        d_gate_ref[seq] = total.T[:1]
    d_input = nt(d_query_ref[...], query_ref[...]) + nt(d_kv_ref[...], kv_ref[...])

    @pl.when(pl.program_id(0) == 0)
    def _():
        d_gain_ref[...] = jnp.zeros_like(d_gain_ref)

    d_gain_ref[...] += jnp.sum(d_input * x_ref[...].astype(F32), axis=0, keepdims=True)
    part_ref[...] = d_input.astype(BF16)


def rows_kernel(parts, places_ref, *refs):
    gated_refs, down_refs, part_ref = refs[:parts], refs[parts : 2 * parts], refs[2 * parts]
    length = part_ref.shape[3]
    value = nn(gated_refs[0][...], down_refs[0][...])
    for part in range(1, parts):
        value = value + nn(gated_refs[part][...], down_refs[part][...])
    place_rows(places_ref, part_ref, value.astype(BF16), length)


def fixed(shape):
    return pl.BlockSpec(shape, lambda step, places: (0,) * len(shape))


def rows_spec(rows, columns):
    return pl.BlockSpec((rows, columns), lambda step, places: (step, 0))


def info_spec(seqs, kinds, length):
    return pl.BlockSpec((seqs, kinds, length), lambda step, places: (step, 0, 0))


def place_spec(high, length, width):
    def index(step, places):
        low = lax.rem(lax.rem(step, 2) - places[1] + 2, 2)
        return (low, lax.rem(lax.div(step, 2) - places[0] + high, high), 0, 0, 0)

    return pl.BlockSpec((1, 1, OUTER, length, width), index)


def shape(dims, dtype=BF16):
    return jax.ShapeDtypeStruct(dims, dtype)


def call(kernel, name, steps, in_specs, out_specs, out_shape, flops, moved, operands):
    return pl.pallas_call(
        kernel,
        grid_spec=pltpu.PrefetchScalarGridSpec(
            num_scalar_prefetch=1, grid=(steps,), in_specs=in_specs, out_specs=out_specs
        ),
        out_shape=out_shape,
        compiler_params=pltpu.CompilerParams(vmem_limit_bytes=VMEM),
        cost_estimate=pl.CostEstimate(flops=flops, bytes_accessed=moved, transcendentals=0),
        name=name,
    )(*operands)


def arrange(places, value):
    low, high, inner, outer, kinds, rows, span = value.shape

    def index(step, places):
        y = lax.div(step, 2 * inner)
        c = lax.rem(lax.div(step, inner), 2)
        i = lax.rem(step, inner)
        return (
            lax.rem(c - places[1] + 2, 2),
            lax.rem(y - places[0] + high, high),
            lax.rem(i - places[3] + inner, inner),
            0,
            0,
            0,
            0,
        )

    def out_index(step, places):
        return (
            lax.div(step, 2 * inner),
            lax.rem(lax.div(step, inner), 2),
            0,
            lax.rem(step, inner),
            0,
            0,
        )

    dims = (high, low, outer, inner, rows, kinds * span)
    found = call(
        arrange_kernel,
        "arrange",
        high * low * inner,
        [pl.BlockSpec((1, 1, 1, outer, kinds, rows, span), index)],
        pl.BlockSpec((1, 1, outer, 1, rows, kinds * span), out_index),
        shape(dims),
        0,
        4 * value.size,
        (places, value),
    )
    return found.reshape(-1, kinds * span)


def attend(places, rows, info, cosine, sine, query_mat, kv_mat):
    count, width = rows.shape
    span = query_mat.shape[1]
    length = cosine.shape[0]
    step = OUTER * length
    return call(
        attend_kernel,
        "attend",
        count // step,
        [
            rows_spec(step, width),
            info_spec(OUTER, 2, length),
            fixed(cosine.shape),
            fixed(sine.shape),
            fixed(query_mat.shape),
            fixed(kv_mat.shape),
        ],
        [rows_spec(step, 3 * span), rows_spec(step, span)],
        [shape((count, 3 * span)), shape((count, span))],
        2 * count * width * 3 * span + 4 * count * length * span,
        4 * count * (width + 2 * span),
        (places, rows, info, cosine, sine, query_mat, kv_mat),
    )


def attend_back(places, d_middle, info, cosine, sine, qkv, rows, query_mat, kv_mat, out_mat):
    count, width = d_middle.shape
    length = cosine.shape[0]
    step = OUTER * length
    span = out_mat.shape[0]
    return call(
        attend_back_kernel,
        "attend_back",
        count // step,
        [
            rows_spec(step, width),
            info_spec(OUTER, 2, length),
            fixed(cosine.shape),
            fixed(sine.shape),
            rows_spec(step, 3 * span),
            rows_spec(step, width),
            fixed(query_mat.shape),
            fixed(kv_mat.shape),
            fixed(out_mat.shape),
        ],
        [
            rows_spec(step, span),
            rows_spec(step, 2 * span),
            rows_spec(step, width),
            info_spec(OUTER, 1, length),
            fixed((1, width)),
        ],
        [
            shape((count, span)),
            shape((count, 2 * span)),
            shape((count, width)),
            shape((count // length, 1, length), F32),
            shape((1, width), F32),
        ],
        2 * count * width * 4 * span + 10 * count * length * span,
        4 * count * (2 * width + 3 * span),
        (places, d_middle, info, cosine, sine, qkv, rows, query_mat, kv_mat, out_mat),
    )


def ring_rows(places, gated_units, down_parts, length):
    count, units = gated_units[0].shape
    width = down_parts[0].shape[1]
    parts = len(down_parts)
    step = OUTER * length
    high = count // (2 * step)
    return call(
        functools.partial(rows_kernel, parts),
        "rows",
        count // step,
        [rows_spec(step, units)] * parts + [fixed(down.shape) for down in down_parts],
        place_spec(high, length, width),
        shape((2, high, OUTER, length, width)),
        2 * count * width * units * parts,
        4 * count * (width + units * parts),
        (places, *gated_units, *down_parts),
    )


def units_kernel(places_ref, x_ref, info_ref, d_units_ref, first_ref, second_ref, *refs):
    del places_ref
    sums_refs, (d_both_ref, gated_ref, back_ref, d_gate_ref) = refs[:-4], refs[-4:]
    length = info_ref.shape[2]
    seqs = info_ref.shape[0]
    units = first_ref.shape[0]
    rows = x_ref[...]
    gate = jnp.concatenate([as_column(info_ref[seq], length) for seq in range(seqs)], axis=0)
    gate_in = nt(rows, first_ref[...])
    up_in = nt(rows, second_ref[...])
    sigma = jax.nn.sigmoid(gate_in)
    active = gate_in * sigma
    hidden_units = active * up_in
    d_units = d_units_ref[...].astype(F32)
    d_gate = jnp.sum(hidden_units * d_units, axis=-1, keepdims=True)
    gated_ref[...] = (hidden_units * gate).astype(BF16)
    d_units = d_units * gate
    d_first = (d_units * up_in * (sigma + active * (1.0 - sigma))).astype(BF16)
    d_second = (d_units * active).astype(BF16)
    d_both_ref[:, :units] = d_first
    d_both_ref[:, units:] = d_second
    back = nn(d_first, first_ref[...]) + nn(d_second, second_ref[...])
    if sums_refs:
        back = back + sums_refs[0][...]
    back_ref[...] = back.astype(back_ref.dtype)
    for seq in range(seqs):
        column = jnp.broadcast_to(d_gate[seq * length : (seq + 1) * length], (length, length))
        d_gate_ref[seq] = column.T[:1]


def run_units(places, rows, info, d_units, first, second, sums, last):
    count, width = rows.shape
    length = info.shape[2]
    units = d_units.shape[1]
    seqs = ROW_STEP // length

    def weight_spec(block):
        return pl.BlockSpec((units, width), lambda step, places: (block, 0))

    extra = [] if sums is None else [sums]
    return call(
        units_kernel,
        "units",
        count // ROW_STEP,
        [rows_spec(ROW_STEP, width), info_spec(seqs, 1, length), rows_spec(ROW_STEP, units)]
        + [weight_spec(first[1]), weight_spec(second[1])]
        + [rows_spec(ROW_STEP, width) for _ in extra],
        [
            rows_spec(ROW_STEP, 2 * units),
            rows_spec(ROW_STEP, units),
            rows_spec(ROW_STEP, width),
            info_spec(seqs, 1, length),
        ],
        [
            shape((count, 2 * units)),
            shape((count, units)),
            shape((count, width), BF16 if last else F32),
            shape((count // length, 1, length), F32),
        ],
        0,
        0,
        (places, rows, info, d_units, first[0], second[0], *extra),
    )


def shards(
    hidden_in,
    segment_ids,
    att_route,
    mlp_route,
    norm_gain1,
    norm_gain2,
    att_router,
    mlp_router,
    kv_weight,
    query_weight,
    out_weight,
    att_bias,
    up_weight,
    down_weight,
    mlp_bias,
    cotangent,
):
    experts = lax.axis_size(EXPERT)
    inner = lax.axis_size("i")
    tokens, width = hidden_in.shape
    span = HEADS // OUTER * HD
    cosine, sine_table = rope_tables(tokens)

    places = own_places()

    down_parts = ring_gather(down_weight[0], "i")
    query_mat, kv_mat, seen = gather_heads(
        places, query_weight[0], kv_weight, down_parts[1:]
    )
    out_parts = ring_gather(after(out_weight[0], seen), "i")
    own_up = up_weight[0].reshape(-1, width)

    residual = hidden_in.astype(F32)
    normed_one, inverse_one = norm_rows(residual, norm_gain1)
    attn_input = normed_one.astype(BF16)
    att_gate, att_onehot = pair_gates(attn_input, att_router, att_route, experts)
    info = to_experts(att_gate, att_onehot, segment_ids[0].astype(F32))
    all_attn = meet(attn_input)
    all_cot = meet(after(cotangent.astype(BF16), seen))
    qkv, gated = attend(places, all_attn, info, cosine, sine_table, query_mat, kv_mat)
    out_parts = out_parts[:1] + list(after(out_parts[1:], gated))
    out_mat = in_order(out_parts, "i").reshape(span, width)
    branch = part_low(ring_rows(places, [gated], [out_mat], tokens))
    branch = part_second(*part_first(branch))

    d_units = [mm("td,fd->tf", all_cot, down).astype(BF16) for down in down_parts]
    branch = after(branch, d_units)
    middle = residual + branch.astype(F32) + att_bias
    normed_two, inverse_two = norm_rows(middle, norm_gain2)
    mlp_input = normed_two.astype(BF16)
    mlp_gate, mlp_onehot = pair_gates(mlp_input, mlp_router, mlp_route, experts)
    up_parts = ring_gather(after(own_up, branch), "i")
    all_mlp = meet(mlp_input)
    gate_m = to_experts(mlp_gate, mlp_onehot, None)
    d_both, gated_units, rows_back, d_gate_m = [], [], None, None
    for number, up in enumerate(up_parts):
        source = own_up if number == 0 else up
        found = run_units(
            places,
            all_mlp,
            gate_m,
            d_units[number],
            (source, 0),
            (source, 1),
            rows_back,
            number == inner - 1,
        )
        d_both.append(found[0])
        gated_units.append(found[1])
        rows_back = found[2]
        d_gate_m = found[3] if d_gate_m is None else d_gate_m + found[3]
    d_mlp_input = part(rows_back)
    d_mlp_gate = from_experts(d_gate_m[:, 0], mlp_onehot, experts)
    grad_up = [mm("tf,td->fd", d_here, all_mlp) for d_here in d_both]
    grad_down = [mm("tf,td->fd", here, all_cot) for here in gated_units]
    low_up = [one.astype(BF16) for one in grad_up[1:]]
    low_down = [one.astype(BF16) for one in grad_down[1:]]
    rows_out = part_low(ring_rows(places, gated_units, down_parts, tokens))
    half = tokens // 2
    rows_first, rows_second = rows_out[:, :, :half], rows_out[:, :, half:]
    lower_own, lower_last = ring_open(grad_down[:1] + low_down, "i")
    upper_own, upper_last = ring_open(grad_up[:1] + low_up, "i")
    d_mlp_input = after(d_mlp_input, rows_out, low_up, lower_last)
    d_mlp_router, d_mlp_from_router = gates_back(
        mlp_gate, mlp_onehot, d_mlp_gate, mlp_input, mlp_router
    )
    d_norm_two, d_gain_two = norm_back(
        middle, inverse_two, norm_gain2, d_mlp_input.astype(F32) + d_mlp_from_router
    )
    d_middle = cotangent + d_norm_two
    sums = jnp.concatenate(
        [
            jnp.stack([d_gain_two, jnp.sum(d_middle, axis=0), jnp.sum(cotangent, axis=0)]),
            d_mlp_router,
        ]
    )

    all_mid = meet(d_middle.astype(BF16))
    rows_second = ring_low([rows_second[:, k] for k in range(OUTER)], "o")
    all_mid = after(all_mid, rows_second)
    d_heads, d_kv, rows_one, d_gate_a, d_gain_a = attend_back(
        places, all_mid, info, cosine, sine_table, qkv, all_attn, query_mat, kv_mat, out_mat
    )
    rows_first = after(rows_first, all_mid)
    rows_first = [rows_first[k] for k in range(rows_first.shape[0])]
    rows_out = part_second(ring_low(rows_first, "y", d_heads), after(rows_second, d_heads))
    layer_out = middle + rows_out.astype(F32) + mlp_bias
    d_attn_input = part(rows_one)
    d_att_gate = from_experts(d_gate_a[:, 0], att_onehot, experts)
    d_kv_mat = mm("td,tf->df", all_attn, d_kv).reshape(experts // 2, 2, -1, 2 * span)
    d_kv_mat = from_order([d_kv_mat[:, 0], d_kv_mat[:, 1]], "c")
    d_kv_sent = d_kv_mat[1].astype(BF16)
    d_heads, all_mid = after((d_heads, all_mid), d_kv_sent)
    d_kv_weight, kv_arrived = scatter_kv(d_kv_mat[0], d_kv_sent)
    d_att_router, d_att_from_router = gates_back(
        att_gate, att_onehot, d_att_gate, attn_input, att_router
    )
    d_gain_one = d_gain_a / norm_gain1 + jnp.sum(
        d_att_from_router * residual * inverse_one, axis=0, keepdims=True
    )
    summed = sum_over(jnp.concatenate([d_gain_one, sums, d_att_router]), ("i",))
    d_query = scatter_query(mm("td,tf->df", all_attn, d_heads), summed)[None]
    d_out = mm("tf,td->fd", gated, all_mid).reshape(inner, -1, width)
    d_out = from_order([d_out[k] for k in range(inner)], "i")
    d_output = ring_scatter(d_out[:1] + list(after(d_out[1:], summed)), "i")[None]
    d_upper = (after(upper_last, d_kv_sent).astype(F32) + upper_own).reshape(up_weight.shape)
    d_lower = (lower_last.astype(F32) + lower_own)[None]
    summed = sum_over(after(summed, kv_arrived), ("c", "o", "y"))
    d_attn_input = after(d_attn_input, summed)
    d_norm_one, _ = norm_back(
        residual, inverse_one, norm_gain1, d_attn_input.astype(F32) + d_att_from_router
    )
    d_input = d_middle + d_norm_one
    return (
        layer_out,
        d_input,
        summed[0],
        summed[1],
        summed[4 + experts :].T,
        summed[4 : 4 + experts].T,
        d_kv_weight,
        d_query,
        d_output,
        summed[2],
        d_upper,
        d_lower,
        summed[3],
    )


def solution(mesh):
    experts, fsdp = mesh.shape["expert"], mesh.shape["fsdp"]
    fine = Mesh(mesh.devices.reshape(experts // 2, 2, OUTER, fsdp // OUTER), ALL)
    shard = ("o", "i")
    rows = P(ALL, None)
    placed = (
        rows,
        rows,
        rows,
        rows,
        P(),
        P(),
        P(),
        P(),
        rows,
        P(EXPERT, shard, None),
        P(EXPERT, shard, None),
        P(),
        P(EXPERT, None, shard, None),
        P(EXPERT, shard, None),
        P(),
        rows,
    )
    return jax.shard_map(
        shards,
        mesh=fine,
        in_specs=placed,
        out_specs=(
            rows,
            rows,
            P(),
            P(),
            P(),
            P(),
            rows,
            P(EXPERT, shard, None),
            P(EXPERT, shard, None),
            P(),
            P(EXPERT, None, shard, None),
            P(EXPERT, shard, None),
            P(),
        ),
        check_vma=False,
    )
```

```python
import functools
import math

import jax
import jax.numpy as jnp
from jax import lax
from jax.experimental import pallas as pl
from jax.experimental.pallas import tpu as pltpu
from jax.sharding import Mesh, PartitionSpec as P

HEADS = 16
HD = 128
TOP = 2


EPSILON = 1e-06
HIGHEST = lax.Precision.HIGHEST
MASKED = -1e30

GROUP = ("y", "c", "o")
EXPERT = ("y", "c")
ALL = ("y", "c", "o", "i")
OUTER = 4
F32 = jnp.float32
BF16 = jnp.bfloat16


def rope_tables(length):
    half_dim = HD // 2
    frequency = jnp.exp(jnp.arange(half_dim, dtype=F32) * (-2.0 * math.log(10000.0) / HD))
    angles = jnp.arange(length, dtype=F32)[:, None] * frequency[None, :]
    cosine, sine = jnp.cos(angles), jnp.sin(angles)
    return (
        jnp.concatenate([cosine, cosine], axis=1),
        jnp.concatenate([-sine, sine], axis=1),
    )


def norm_rows(stream, gain):
    inverse = lax.rsqrt(jnp.mean(stream * stream, axis=-1, keepdims=True) + EPSILON)
    return (stream * inverse * gain, inverse)


def norm_back(stream, inverse, gain, upstream):
    scaled = upstream * gain
    d_stream = inverse * scaled - stream * inverse**3 * jnp.mean(
        scaled * stream, axis=-1, keepdims=True
    )
    d_gain = jnp.sum(upstream * stream * inverse, axis=0)
    return (d_stream, d_gain)


def shift(value, axis):
    size = lax.axis_size(axis)
    return lax.ppermute(value, axis, [((k + 1) % size, k) for k in range(size)])


def after(value, *others):
    token, _ = lax.optimization_barrier((lax.create_token(), others))
    return lax.optimization_barrier((token, value))[1]


def ring_gather(value, axis):
    parts = [value]
    for _ in range(lax.axis_size(axis) - 1):
        parts.append(shift(parts[-1], axis))
    return parts


def ring_open(blocks, axis):
    size = lax.axis_size(axis)
    travelling = blocks[1].astype(BF16)
    for j in range(2, size):
        travelling = (shift(travelling, axis).astype(F32) + blocks[j].astype(F32)).astype(BF16)
    return blocks[0], shift(travelling, axis)


def ring_scatter(blocks, axis, *others):
    own, arrived = ring_open(blocks, axis)
    if others:
        arrived = after(arrived, *others)
    return arrived.astype(F32) + own


def in_order(parts, axis, place=0):
    if len(parts) == 2:
        first = lax.axis_index(axis) == 0
        return jnp.stack([jnp.where(first, *parts), jnp.where(first, *parts[::-1])], axis=place)
    return jnp.roll(jnp.stack(parts, axis=place), lax.axis_index(axis), axis=place)


def from_order(parts, axis):
    if len(parts) == 2:
        first = lax.axis_index(axis) == 0
        return [jnp.where(first, *parts), jnp.where(first, *parts[::-1])]
    return list(jnp.roll(jnp.stack(parts), -lax.axis_index(axis), axis=0))


def sum_over(value, axes):
    for axis in axes:
        size = lax.axis_size(axis)
        step = 1
        while step < size:
            value = value + lax.ppermute(value, axis, [(k, k ^ step) for k in range(size)])
            step *= 2
    return value


def pair_gates(normed, router, route, experts):
    logits = jnp.dot(normed.astype(F32), router, precision=HIGHEST)
    onehot = (route[:, :, None] == jnp.arange(experts, dtype=jnp.int32)[None, None, :]).astype(F32)
    picked = jnp.sum(logits[:, None, :] * onehot, axis=-1)
    return (jax.nn.softmax(picked, axis=-1), onehot)


def gates_back(gates, onehot, d_gates, normed, router):
    d_picked = gates * (d_gates - jnp.sum(gates * d_gates, axis=-1, keepdims=True))
    d_logits = jnp.sum(d_picked[:, :, None] * onehot, axis=1)
    d_router = jnp.dot(d_logits.T, normed.astype(F32), precision=HIGHEST)
    d_normed = jnp.dot(d_logits, router.T, precision=HIGHEST)
    return (d_router, d_normed)


def to_experts(gates, onehot, extra):
    by_expert = jnp.sum(gates[:, :, None] * onehot, axis=1).T
    rows = jnp.repeat(by_expert, OUTER, axis=0)[:, None, :]
    if extra is not None:
        rows = jnp.concatenate(
            [rows, jnp.broadcast_to(extra[None, None, :], rows.shape)], axis=1
        )
    return lax.all_to_all(rows, GROUP, split_axis=0, concat_axis=0, tiled=True)


def from_experts(d_gates, onehot, experts):
    rows = lax.all_to_all(d_gates, GROUP, split_axis=0, concat_axis=0, tiled=True)
    by_expert = jnp.sum(rows.reshape(experts, OUTER, -1), axis=1)
    return jnp.einsum("tce,et->tc", onehot, by_expert, precision=HIGHEST)


def meet(rows):
    return lax.all_gather(rows, GROUP, axis=0, tiled=True)


def part(rows):
    return lax.psum_scatter(rows, GROUP, scatter_dimension=0, tiled=True)


def mm(form, first, second):
    return jnp.einsum(form, first, second, preferred_element_type=F32)


def head_blocks(matrix):
    span = HEADS // OUTER * HD
    return jnp.stack([matrix[:, k * span : (k + 1) * span] for k in range(OUTER)])


def join_blocks(blocks):
    return jnp.concatenate([blocks[k] for k in range(OUTER)], axis=1)


def exchange(blocks):
    return lax.all_to_all(blocks, "o", split_axis=0, concat_axis=0, tiled=True)


def gather_heads(places, query_weight, kv_weight, beside):
    whole = HEADS * HD
    rows = query_weight.shape[0]
    here = exchange(
        jnp.concatenate(
            [
                head_blocks(query_weight),
                head_blocks(kv_weight[:, :whole]),
                head_blocks(kv_weight[:, whole:]),
            ],
            axis=1,
        )
    )
    here = after(here, *beside)
    span = here.shape[2]
    kv = ring_gather(here[:, rows:].reshape(OUTER, 2, -1, span), "i")
    query = ring_gather(after(here[:, :rows], kv[-1]), "i")
    kv = ring_gather(jnp.stack(kv), "y")
    kv = after(kv, query)
    query = in_order(query, "i", 1).reshape(-1, span)
    seen = kv[-1][0, 0, 0, 0]
    kv = jnp.stack(ring_gather(jnp.stack(kv), "c"))
    return query, arrange(places, kv), seen


def scatter_query(grad, *others):
    inner = lax.axis_size("i")
    blocks = grad.reshape(OUTER, inner, -1, grad.shape[1])
    blocks = from_order([blocks[:, k] for k in range(inner)], "i")
    mine = ring_scatter(blocks[:1] + list(after(blocks[1:], *others)), "i").astype(BF16)
    return join_blocks(exchange(mine)).astype(F32)


def scatter_kv(kept, sent):
    mine = lax.ppermute(sent, "c", [(0, 1), (1, 0)]).astype(F32) + kept
    high, inner = lax.axis_size("y"), lax.axis_size("i")
    wide = kept.shape[-1]
    mine = mine.reshape(high, OUTER, inner, -1, wide)
    blocks = from_order([mine[k] for k in range(high)], "y")
    sent = blocks[1].astype(BF16)
    own, arrived = ring_open([blocks[0], sent] + blocks[2:], "y")
    mine = arrived.astype(F32) + own
    mine = ring_scatter(from_order([mine[:, k] for k in range(inner)], "i"), "i").astype(BF16)
    here = exchange(mine)
    half = wide // 2
    whole = jnp.concatenate(
        [join_blocks(here[:, :, :half]), join_blocks(here[:, :, half:])], axis=1
    )
    return whole.astype(F32), sent, arrived


def own_places():
    return jnp.stack([lax.axis_index(axis) for axis in ALL]).astype(jnp.int32)


def add_low(first, second):
    return (first.astype(F32) + second.astype(F32)).astype(BF16)


def ring_low(blocks, axis):
    travelling = blocks[1]
    for j in range(2, lax.axis_size(axis)):
        travelling = add_low(shift(travelling, axis), blocks[j])
    return add_low(shift(travelling, axis), blocks[0])


def part_low(rows):
    return ring_low([rows[k] for k in range(rows.shape[0])], "c")


def part_first(rows):
    half = rows.shape[2] // 2
    first, second = rows[:, :, :half], rows[:, :, half:]
    first = ring_low([first[k] for k in range(first.shape[0])], "y")
    second = ring_low([second[:, k] for k in range(second.shape[1])], "o")
    return first, second


def part_second(first, second):
    first = ring_low([first[k] for k in range(first.shape[0])], "o")
    second = ring_low([second[k] for k in range(second.shape[0])], "y")
    return jnp.concatenate([first, second])


VMEM = 56 * 1024 * 1024
ROW_STEP = 256


def nn(first, second):
    return jnp.dot(first, second, preferred_element_type=F32)


def nt(first, second):
    return lax.dot_general(first, second, (((1,), (1,)), ((), ())), preferred_element_type=F32)


def tn(first, second):
    return lax.dot_general(first, second, (((0,), (0,)), ((), ())), preferred_element_type=F32)


def as_column(row, rows):
    return jnp.broadcast_to(row, (rows, rows)).T[:, :1]


def turn(head, cosine, sine):
    return head * cosine + pltpu.roll(head, HD // 2, 1) * sine


def turn_back(head, cosine, sine):
    return head * cosine - pltpu.roll(head, HD // 2, 1) * sine


def allowed_keys(segment, length):
    keys = jnp.broadcast_to(segment, (length, length))
    row = lax.broadcasted_iota(jnp.int32, (length, length), 0)
    column = lax.broadcasted_iota(jnp.int32, (length, length), 1)
    return (keys == keys.T) & (column <= row)


def heads_nt(first, second):
    return lax.dot_general(first, second, (((2,), (2,)), ((0,), (0,))), preferred_element_type=F32)


def heads_nn(first, second):
    return lax.dot_general(first, second, (((2,), (1,)), ((0,), (0,))), preferred_element_type=F32)


def heads_tn(first, second):
    return lax.dot_general(first, second, (((1,), (1,)), ((0,), (0,))), preferred_element_type=F32)


def softmax_rows(queries, keys, allowed):
    scores = jnp.where(allowed[None], heads_nt(queries, keys) * (1.0 / math.sqrt(HD)), MASKED)
    exponent = jnp.exp(scores - jnp.max(scores, axis=-1, keepdims=True))
    return exponent / jnp.sum(exponent, axis=-1, keepdims=True)


def place_rows(places_ref, part_ref, value, length):
    count = part_ref.shape[2]
    for seq in range(count):
        slot = lax.rem(seq - places_ref[2] + count, count)
        part_ref[0, 0, slot] = value[seq * length : (seq + 1) * length]


def arrange_kernel(places_ref, in_ref, out_ref):
    del places_ref
    half = in_ref.shape[-1]
    for outer in range(OUTER):
        out_ref[0, 0, outer, 0, :, :half] = in_ref[0, 0, 0, outer, 0]
        out_ref[0, 0, outer, 0, :, half:] = in_ref[0, 0, 0, outer, 1]


def attend_kernel(
    places_ref,
    x_ref,
    info_ref,
    cos_ref,
    sin_ref,
    query_ref,
    kv_ref,
    qkv_ref,
    gated_ref,
):
    del places_ref
    length = cos_ref.shape[0]
    span = query_ref.shape[1]
    raw_query = nn(x_ref[...], query_ref[...])
    raw = nn(x_ref[...], kv_ref[...])
    cosine, sine = cos_ref[...], sin_ref[...]
    starts = range(0, span, HD)
    for seq in range(info_ref.shape[0]):
        rows = slice(seq * length, (seq + 1) * length)
        gate = as_column(info_ref[seq, 0:1, :], length)
        allowed = allowed_keys(info_ref[seq, 1:2, :], length)
        queries, keys, values = [], [], []
        for at in starts:
            head = raw_query[rows, at : at + HD].astype(BF16).astype(F32)
            queries.append(turn(head, cosine, sine).astype(BF16))
            keys.append(turn(raw[rows, at : at + HD], cosine, sine).astype(BF16))
            values.append(raw[rows, span + at : span + at + HD].astype(BF16))
            qkv_ref[rows, at : at + HD] = queries[-1]
            qkv_ref[rows, span + at : span + at + HD] = keys[-1]
            qkv_ref[rows, 2 * span + at : 2 * span + at + HD] = values[-1]
        probs = softmax_rows(jnp.stack(queries), jnp.stack(keys), allowed)
        gated = (heads_nn(probs.astype(BF16), jnp.stack(values)) * gate[None]).astype(BF16)
        for number, at in enumerate(starts):
            gated_ref[rows, at : at + HD] = gated[number]


def attend_back_kernel(
    places_ref,
    mid_ref,
    info_ref,
    cos_ref,
    sin_ref,
    qkv_ref,
    x_ref,
    query_ref,
    kv_ref,
    out_ref,
    d_query_ref,
    d_kv_ref,
    part_ref,
    d_gate_ref,
    d_gain_ref,
):
    del places_ref
    length = cos_ref.shape[0]
    span = out_ref.shape[0]
    scale = 1.0 / math.sqrt(HD)
    d_rows = nt(mid_ref[...], out_ref[...])
    cosine, sine = cos_ref[...], sin_ref[...]
    starts = range(0, span, HD)
    for seq in range(info_ref.shape[0]):
        rows = slice(seq * length, (seq + 1) * length)
        gate = as_column(info_ref[seq, 0:1, :], length)[None]
        allowed = allowed_keys(info_ref[seq, 1:2, :], length)
        queries = jnp.stack([qkv_ref[rows, at : at + HD] for at in starts])
        keys = jnp.stack([qkv_ref[rows, span + at : span + at + HD] for at in starts])
        values = jnp.stack([qkv_ref[rows, 2 * span + at : 2 * span + at + HD] for at in starts])
        d_heads = jnp.stack([d_rows[rows, at : at + HD] for at in starts])
        probs = softmax_rows(queries, keys, allowed)
        weighted = probs * heads_nt(d_heads.astype(BF16), values)
        sums = jnp.sum(weighted, axis=-1, keepdims=True)
        d_scores = ((weighted - probs * sums) * gate).astype(BF16)
        d_queries = heads_nn(d_scores, keys) * scale
        d_keys = heads_tn(d_scores, queries) * scale
        d_values = heads_tn(probs.astype(BF16), (d_heads * gate).astype(BF16))
        for number, at in enumerate(starts):
            cols = slice(at, at + HD)
            d_query_ref[rows, cols] = turn_back(d_queries[number], cosine, sine).astype(BF16)
            d_kv_ref[rows, cols] = turn_back(d_keys[number], cosine, sine).astype(BF16)
            d_kv_ref[rows, span + at : span + at + HD] = d_values[number].astype(BF16)
        total = jnp.broadcast_to(jnp.sum(sums, axis=0), (length, length))
        d_gate_ref[seq] = total.T[:1]
    d_input = nt(d_query_ref[...], query_ref[...]) + nt(d_kv_ref[...], kv_ref[...])

    @pl.when(pl.program_id(0) == 0)
    def _():
        d_gain_ref[...] = jnp.zeros_like(d_gain_ref)

    d_gain_ref[...] += jnp.sum(d_input * x_ref[...].astype(F32), axis=0, keepdims=True)
    part_ref[...] = d_input.astype(BF16)


def rows_kernel(parts, places_ref, *refs):
    gated_refs, down_refs, part_ref = refs[:parts], refs[parts : 2 * parts], refs[2 * parts]
    length = part_ref.shape[3]
    value = nn(gated_refs[0][...], down_refs[0][...])
    for part in range(1, parts):
        value = value + nn(gated_refs[part][...], down_refs[part][...])
    place_rows(places_ref, part_ref, value.astype(BF16), length)


def fixed(shape):
    return pl.BlockSpec(shape, lambda step, places: (0,) * len(shape))


def rows_spec(rows, columns):
    return pl.BlockSpec((rows, columns), lambda step, places: (step, 0))


def info_spec(seqs, kinds, length):
    return pl.BlockSpec((seqs, kinds, length), lambda step, places: (step, 0, 0))


def place_spec(high, length, width):
    def index(step, places):
        low = lax.rem(lax.rem(step, 2) - places[1] + 2, 2)
        return (low, lax.rem(lax.div(step, 2) - places[0] + high, high), 0, 0, 0)

    return pl.BlockSpec((1, 1, OUTER, length, width), index)


def shape(dims, dtype=BF16):
    return jax.ShapeDtypeStruct(dims, dtype)


def call(kernel, name, steps, in_specs, out_specs, out_shape, flops, moved, operands):
    return pl.pallas_call(
        kernel,
        grid_spec=pltpu.PrefetchScalarGridSpec(
            num_scalar_prefetch=1, grid=(steps,), in_specs=in_specs, out_specs=out_specs
        ),
        out_shape=out_shape,
        compiler_params=pltpu.CompilerParams(vmem_limit_bytes=VMEM),
        cost_estimate=pl.CostEstimate(flops=flops, bytes_accessed=moved, transcendentals=0),
        name=name,
    )(*operands)


def arrange(places, value):
    low, high, inner, outer, kinds, rows, span = value.shape

    def index(step, places):
        y = lax.div(step, 2 * inner)
        c = lax.rem(lax.div(step, inner), 2)
        i = lax.rem(step, inner)
        return (
            lax.rem(c - places[1] + 2, 2),
            lax.rem(y - places[0] + high, high),
            lax.rem(i - places[3] + inner, inner),
            0,
            0,
            0,
            0,
        )

    def out_index(step, places):
        return (
            lax.div(step, 2 * inner),
            lax.rem(lax.div(step, inner), 2),
            0,
            lax.rem(step, inner),
            0,
            0,
        )

    dims = (high, low, outer, inner, rows, kinds * span)
    found = call(
        arrange_kernel,
        "arrange",
        high * low * inner,
        [pl.BlockSpec((1, 1, 1, outer, kinds, rows, span), index)],
        pl.BlockSpec((1, 1, outer, 1, rows, kinds * span), out_index),
        shape(dims),
        0,
        4 * value.size,
        (places, value),
    )
    return found.reshape(-1, kinds * span)


def attend(places, rows, info, cosine, sine, query_mat, kv_mat):
    count, width = rows.shape
    span = query_mat.shape[1]
    length = cosine.shape[0]
    step = OUTER * length
    return call(
        attend_kernel,
        "attend",
        count // step,
        [
            rows_spec(step, width),
            info_spec(OUTER, 2, length),
            fixed(cosine.shape),
            fixed(sine.shape),
            fixed(query_mat.shape),
            fixed(kv_mat.shape),
        ],
        [rows_spec(step, 3 * span), rows_spec(step, span)],
        [shape((count, 3 * span)), shape((count, span))],
        2 * count * width * 3 * span + 4 * count * length * span,
        4 * count * (width + 2 * span),
        (places, rows, info, cosine, sine, query_mat, kv_mat),
    )


def attend_back(places, d_middle, info, cosine, sine, qkv, rows, query_mat, kv_mat, out_mat):
    count, width = d_middle.shape
    length = cosine.shape[0]
    step = OUTER * length
    span = out_mat.shape[0]
    return call(
        attend_back_kernel,
        "attend_back",
        count // step,
        [
            rows_spec(step, width),
            info_spec(OUTER, 2, length),
            fixed(cosine.shape),
            fixed(sine.shape),
            rows_spec(step, 3 * span),
            rows_spec(step, width),
            fixed(query_mat.shape),
            fixed(kv_mat.shape),
            fixed(out_mat.shape),
        ],
        [
            rows_spec(step, span),
            rows_spec(step, 2 * span),
            rows_spec(step, width),
            info_spec(OUTER, 1, length),
            fixed((1, width)),
        ],
        [
            shape((count, span)),
            shape((count, 2 * span)),
            shape((count, width)),
            shape((count // length, 1, length), F32),
            shape((1, width), F32),
        ],
        2 * count * width * 4 * span + 10 * count * length * span,
        4 * count * (2 * width + 3 * span),
        (places, d_middle, info, cosine, sine, qkv, rows, query_mat, kv_mat, out_mat),
    )


def ring_rows(places, gated_units, down_parts, length):
    count, units = gated_units[0].shape
    width = down_parts[0].shape[1]
    parts = len(down_parts)
    step = OUTER * length
    high = count // (2 * step)
    return call(
        functools.partial(rows_kernel, parts),
        "rows",
        count // step,
        [rows_spec(step, units)] * parts + [fixed(down.shape) for down in down_parts],
        place_spec(high, length, width),
        shape((2, high, OUTER, length, width)),
        2 * count * width * units * parts,
        4 * count * (width + units * parts),
        (places, *gated_units, *down_parts),
    )


def units_kernel(places_ref, x_ref, info_ref, d_units_ref, first_ref, second_ref, *refs):
    del places_ref
    sums_refs, (d_both_ref, gated_ref, back_ref, d_gate_ref) = refs[:-4], refs[-4:]
    length = info_ref.shape[2]
    seqs = info_ref.shape[0]
    units = first_ref.shape[0]
    rows = x_ref[...]
    gate = jnp.concatenate([as_column(info_ref[seq], length) for seq in range(seqs)], axis=0)
    gate_in = nt(rows, first_ref[...])
    up_in = nt(rows, second_ref[...])
    sigma = jax.nn.sigmoid(gate_in)
    active = gate_in * sigma
    hidden_units = active * up_in
    d_units = d_units_ref[...].astype(F32)
    d_gate = jnp.sum(hidden_units * d_units, axis=-1, keepdims=True)
    gated_ref[...] = (hidden_units * gate).astype(BF16)
    d_units = d_units * gate
    d_first = (d_units * up_in * (sigma + active * (1.0 - sigma))).astype(BF16)
    d_second = (d_units * active).astype(BF16)
    d_both_ref[:, :units] = d_first
    d_both_ref[:, units:] = d_second
    back = nn(d_first, first_ref[...]) + nn(d_second, second_ref[...])
    if sums_refs:
        back = back + sums_refs[0][...]
    back_ref[...] = back.astype(back_ref.dtype)
    for seq in range(seqs):
        column = jnp.broadcast_to(d_gate[seq * length : (seq + 1) * length], (length, length))
        d_gate_ref[seq] = column.T[:1]


def run_units(places, rows, info, d_units, first, second, sums, last):
    count, width = rows.shape
    length = info.shape[2]
    units = d_units.shape[1]
    seqs = ROW_STEP // length

    def weight_spec(block):
        return pl.BlockSpec((units, width), lambda step, places: (block, 0))

    extra = [] if sums is None else [sums]
    return call(
        units_kernel,
        "units",
        count // ROW_STEP,
        [rows_spec(ROW_STEP, width), info_spec(seqs, 1, length), rows_spec(ROW_STEP, units)]
        + [weight_spec(first[1]), weight_spec(second[1])]
        + [rows_spec(ROW_STEP, width) for _ in extra],
        [
            rows_spec(ROW_STEP, 2 * units),
            rows_spec(ROW_STEP, units),
            rows_spec(ROW_STEP, width),
            info_spec(seqs, 1, length),
        ],
        [
            shape((count, 2 * units)),
            shape((count, units)),
            shape((count, width), BF16 if last else F32),
            shape((count // length, 1, length), F32),
        ],
        0,
        0,
        (places, rows, info, d_units, first[0], second[0], *extra),
    )


def shards(
    hidden_in,
    segment_ids,
    att_route,
    mlp_route,
    norm_gain1,
    norm_gain2,
    att_router,
    mlp_router,
    kv_weight,
    query_weight,
    out_weight,
    att_bias,
    up_weight,
    down_weight,
    mlp_bias,
    cotangent,
):
    experts = lax.axis_size(EXPERT)
    inner = lax.axis_size("i")
    tokens, width = hidden_in.shape
    span = HEADS // OUTER * HD
    cosine, sine_table = rope_tables(tokens)

    places = own_places()

    down_parts = ring_gather(down_weight[0], "i")
    query_mat, kv_mat, seen = gather_heads(
        places, query_weight[0], kv_weight, down_parts[1:]
    )
    out_parts = ring_gather(after(out_weight[0], seen), "i")
    own_up = up_weight[0].reshape(-1, width)

    residual = hidden_in.astype(F32)
    normed_one, inverse_one = norm_rows(residual, norm_gain1)
    attn_input = normed_one.astype(BF16)
    att_gate, att_onehot = pair_gates(attn_input, att_router, att_route, experts)
    info = to_experts(att_gate, att_onehot, segment_ids[0].astype(F32))
    all_attn = meet(attn_input)
    all_cot = meet(after(cotangent.astype(BF16), seen))
    qkv, gated = attend(places, all_attn, info, cosine, sine_table, query_mat, kv_mat)
    out_parts = out_parts[:1] + list(after(out_parts[1:], gated))
    out_mat = in_order(out_parts, "i").reshape(span, width)
    branch = part_low(ring_rows(places, [gated], [out_mat], tokens))
    branch = part_second(*part_first(branch))

    d_units = [mm("td,fd->tf", all_cot, down).astype(BF16) for down in down_parts]
    branch = after(branch, d_units)
    middle = residual + branch.astype(F32) + att_bias
    normed_two, inverse_two = norm_rows(middle, norm_gain2)
    mlp_input = normed_two.astype(BF16)
    mlp_gate, mlp_onehot = pair_gates(mlp_input, mlp_router, mlp_route, experts)
    up_parts = ring_gather(after(own_up, gated), "i")
    all_mlp = meet(mlp_input)
    gate_m = to_experts(mlp_gate, mlp_onehot, None)
    d_both, gated_units, rows_back, d_gate_m = [], [], None, None
    for number, up in enumerate(up_parts):
        source = own_up if number == 0 else up
        found = run_units(
            places,
            all_mlp,
            gate_m,
            d_units[number],
            (source, 0),
            (source, 1),
            rows_back,
            number == inner - 1,
        )
        d_both.append(found[0])
        gated_units.append(found[1])
        rows_back = found[2]
        d_gate_m = found[3] if d_gate_m is None else d_gate_m + found[3]
    d_mlp_input = part(rows_back)
    d_mlp_gate = from_experts(d_gate_m[:, 0], mlp_onehot, experts)
    grad_up = [mm("tf,td->fd", d_here, all_mlp) for d_here in d_both]
    grad_down = [mm("tf,td->fd", here, all_cot) for here in gated_units]
    low_up = [one.astype(BF16) for one in grad_up[1:]]
    low_down = [one.astype(BF16) for one in grad_down[1:]]
    rows_out = part_low(ring_rows(places, gated_units, down_parts, tokens))
    half = tokens // 2
    rows_first, rows_second = rows_out[:, :, :half], rows_out[:, :, half:]
    lower_own, lower_last = ring_open(grad_down[:1] + low_down, "i")
    upper_own, upper_last = ring_open(grad_up[:1] + low_up, "i")
    d_mlp_input = after(d_mlp_input, rows_out, low_up, lower_last)
    d_mlp_router, d_mlp_from_router = gates_back(
        mlp_gate, mlp_onehot, d_mlp_gate, mlp_input, mlp_router
    )
    d_norm_two, d_gain_two = norm_back(
        middle, inverse_two, norm_gain2, d_mlp_input.astype(F32) + d_mlp_from_router
    )
    d_middle = cotangent + d_norm_two
    sums = jnp.concatenate(
        [
            jnp.stack([d_gain_two, jnp.sum(d_middle, axis=0), jnp.sum(cotangent, axis=0)]),
            d_mlp_router,
        ]
    )

    all_mid = meet(d_middle.astype(BF16))
    rows_second = ring_low([rows_second[:, k] for k in range(OUTER)], "o")
    all_mid = after(all_mid, rows_second)
    d_heads, d_kv, rows_one, d_gate_a, d_gain_a = attend_back(
        places, all_mid, info, cosine, sine_table, qkv, all_attn, query_mat, kv_mat, out_mat
    )
    rows_first = after(rows_first, all_mid)
    rows_first = [rows_first[k] for k in range(rows_first.shape[0])]
    rows_first = ring_low(rows_first, "y")
    d_attn_input = part(after(rows_one, rows_first))
    d_att_gate = from_experts(d_gate_a[:, 0], att_onehot, experts)
    d_kv_mat = mm("td,tf->df", all_attn, d_kv).reshape(experts // 2, 2, -1, 2 * span)
    d_kv_mat = from_order([d_kv_mat[:, 0], d_kv_mat[:, 1]], "c")
    d_kv_sent = d_kv_mat[1].astype(BF16)
    d_kv_weight, kv_sent, kv_arrived = scatter_kv(d_kv_mat[0], d_kv_sent)
    d_heads, all_mid = after((d_heads, all_mid), kv_sent)
    d_att_router, d_att_from_router = gates_back(
        att_gate, att_onehot, d_att_gate, attn_input, att_router
    )
    d_gain_one = d_gain_a / norm_gain1 + jnp.sum(
        d_att_from_router * residual * inverse_one, axis=0, keepdims=True
    )
    summed = sum_over(jnp.concatenate([d_gain_one, sums, d_att_router]), ("i",))
    d_query = scatter_query(mm("td,tf->df", all_attn, d_heads), summed)[None]
    d_out = mm("tf,td->fd", gated, all_mid).reshape(inner, -1, width)
    d_out = from_order([d_out[k] for k in range(inner)], "i")
    d_output = ring_scatter(d_out[:1] + list(after(d_out[1:], kv_arrived)), "i")[None]
    rows_out = part_second(*after((rows_first, rows_second), kv_sent))
    layer_out = middle + rows_out.astype(F32) + mlp_bias
    d_upper = (after(upper_last, kv_sent).astype(F32) + upper_own).reshape(up_weight.shape)
    d_lower = (lower_last.astype(F32) + lower_own)[None]
    summed = sum_over(after(summed, kv_arrived), ("c", "o", "y"))
    d_attn_input = after(d_attn_input, summed)
    d_norm_one, _ = norm_back(
        residual, inverse_one, norm_gain1, d_attn_input.astype(F32) + d_att_from_router
    )
    d_input = d_middle + d_norm_one
    return (
        layer_out,
        d_input,
        summed[0],
        summed[1],
        summed[4 + experts :].T,
        summed[4 : 4 + experts].T,
        d_kv_weight,
        d_query,
        d_output,
        summed[2],
        d_upper,
        d_lower,
        summed[3],
    )


def solution(mesh):
    experts, fsdp = mesh.shape["expert"], mesh.shape["fsdp"]
    fine = Mesh(mesh.devices.reshape(experts // 2, 2, OUTER, fsdp // OUTER), ALL)
    shard = ("o", "i")
    rows = P(ALL, None)
    placed = (
        rows,
        rows,
        rows,
        rows,
        P(),
        P(),
        P(),
        P(),
        rows,
        P(EXPERT, shard, None),
        P(EXPERT, shard, None),
        P(),
        P(EXPERT, None, shard, None),
        P(EXPERT, shard, None),
        P(),
        rows,
    )
    return jax.shard_map(
        shards,
        mesh=fine,
        in_specs=placed,
        out_specs=(
            rows,
            rows,
            P(),
            P(),
            P(),
            P(),
            rows,
            P(EXPERT, shard, None),
            P(EXPERT, shard, None),
            P(),
            P(EXPERT, None, shard, None),
            P(EXPERT, shard, None),
            P(),
        ),
        check_vma=False,
    )
```

```python
import functools
import math

import jax
import jax.numpy as jnp
from jax import lax
from jax.experimental import pallas as pl
from jax.experimental.pallas import tpu as pltpu
from jax.sharding import Mesh, PartitionSpec as P

HEADS = 16
HD = 128
TOP = 2


EPSILON = 1e-06
HIGHEST = lax.Precision.HIGHEST
MASKED = -1e30

GROUP = ("y", "c", "o")
EXPERT = ("y", "c")
ALL = ("y", "c", "o", "i")
OUTER = 4
F32 = jnp.float32
BF16 = jnp.bfloat16


def rope_tables(length):
    half_dim = HD // 2
    frequency = jnp.exp(jnp.arange(half_dim, dtype=F32) * (-2.0 * math.log(10000.0) / HD))
    angles = jnp.arange(length, dtype=F32)[:, None] * frequency[None, :]
    cosine, sine = jnp.cos(angles), jnp.sin(angles)
    return (
        jnp.concatenate([cosine, cosine], axis=1),
        jnp.concatenate([-sine, sine], axis=1),
    )


def norm_rows(stream, gain):
    inverse = lax.rsqrt(jnp.mean(stream * stream, axis=-1, keepdims=True) + EPSILON)
    return (stream * inverse * gain, inverse)


def norm_back(stream, inverse, gain, upstream):
    scaled = upstream * gain
    d_stream = inverse * scaled - stream * inverse**3 * jnp.mean(
        scaled * stream, axis=-1, keepdims=True
    )
    d_gain = jnp.sum(upstream * stream * inverse, axis=0)
    return (d_stream, d_gain)


def shift(value, axis):
    size = lax.axis_size(axis)
    return lax.ppermute(value, axis, [((k + 1) % size, k) for k in range(size)])


def after(value, *others):
    token, _ = lax.optimization_barrier((lax.create_token(), others))
    return lax.optimization_barrier((token, value))[1]


def ring_gather(value, axis):
    parts = [value]
    for _ in range(lax.axis_size(axis) - 1):
        parts.append(shift(parts[-1], axis))
    return parts


def ring_open(blocks, axis):
    size = lax.axis_size(axis)
    travelling = blocks[1].astype(BF16)
    for j in range(2, size):
        travelling = (shift(travelling, axis).astype(F32) + blocks[j].astype(F32)).astype(BF16)
    return blocks[0], shift(travelling, axis)


def ring_scatter(blocks, axis, *others):
    own, arrived = ring_open(blocks, axis)
    if others:
        arrived = after(arrived, *others)
    return arrived.astype(F32) + own


def in_order(parts, axis, place=0):
    if len(parts) == 2:
        first = lax.axis_index(axis) == 0
        return jnp.stack([jnp.where(first, *parts), jnp.where(first, *parts[::-1])], axis=place)
    return jnp.roll(jnp.stack(parts, axis=place), lax.axis_index(axis), axis=place)


def from_order(parts, axis):
    if len(parts) == 2:
        first = lax.axis_index(axis) == 0
        return [jnp.where(first, *parts), jnp.where(first, *parts[::-1])]
    return list(jnp.roll(jnp.stack(parts), -lax.axis_index(axis), axis=0))


def sum_over(value, axes):
    for axis in axes:
        size = lax.axis_size(axis)
        step = 1
        while step < size:
            value = value + lax.ppermute(value, axis, [(k, k ^ step) for k in range(size)])
            step *= 2
    return value


def pair_gates(normed, router, route, experts):
    logits = jnp.dot(normed.astype(F32), router, precision=HIGHEST)
    onehot = (route[:, :, None] == jnp.arange(experts, dtype=jnp.int32)[None, None, :]).astype(F32)
    picked = jnp.sum(logits[:, None, :] * onehot, axis=-1)
    return (jax.nn.softmax(picked, axis=-1), onehot)


def gates_back(gates, onehot, d_gates, normed, router):
    d_picked = gates * (d_gates - jnp.sum(gates * d_gates, axis=-1, keepdims=True))
    d_logits = jnp.sum(d_picked[:, :, None] * onehot, axis=1)
    d_router = jnp.dot(d_logits.T, normed.astype(F32), precision=HIGHEST)
    d_normed = jnp.dot(d_logits, router.T, precision=HIGHEST)
    return (d_router, d_normed)


def to_experts(gates, onehot, extra):
    by_expert = jnp.sum(gates[:, :, None] * onehot, axis=1).T
    rows = jnp.repeat(by_expert, OUTER, axis=0)[:, None, :]
    if extra is not None:
        rows = jnp.concatenate(
            [rows, jnp.broadcast_to(extra[None, None, :], rows.shape)], axis=1
        )
    return lax.all_to_all(rows, GROUP, split_axis=0, concat_axis=0, tiled=True)


def from_experts(d_gates, onehot, experts):
    rows = lax.all_to_all(d_gates, GROUP, split_axis=0, concat_axis=0, tiled=True)
    by_expert = jnp.sum(rows.reshape(experts, OUTER, -1), axis=1)
    return jnp.einsum("tce,et->tc", onehot, by_expert, precision=HIGHEST)


def meet(rows):
    return lax.all_gather(rows, GROUP, axis=0, tiled=True)


def part(rows):
    return lax.psum_scatter(rows, GROUP, scatter_dimension=0, tiled=True)


def mm(form, first, second):
    return jnp.einsum(form, first, second, preferred_element_type=F32)


def head_blocks(matrix):
    span = HEADS // OUTER * HD
    return jnp.stack([matrix[:, k * span : (k + 1) * span] for k in range(OUTER)])


def join_blocks(blocks):
    return jnp.concatenate([blocks[k] for k in range(OUTER)], axis=1)


def exchange(blocks):
    return lax.all_to_all(blocks, "o", split_axis=0, concat_axis=0, tiled=True)


def gather_heads(places, query_weight, kv_weight, beside):
    whole = HEADS * HD
    rows = query_weight.shape[0]
    here = exchange(
        jnp.concatenate(
            [
                head_blocks(query_weight),
                head_blocks(kv_weight[:, :whole]),
                head_blocks(kv_weight[:, whole:]),
            ],
            axis=1,
        )
    )
    here = after(here, *beside)
    span = here.shape[2]
    kv = ring_gather(here[:, rows:].reshape(OUTER, 2, -1, span), "i")
    query = ring_gather(after(here[:, :rows], kv[-1]), "i")
    kv = ring_gather(jnp.stack(kv), "y")
    kv = after(kv, query)
    query = in_order(query, "i", 1).reshape(-1, span)
    seen = kv[-1][0, 0, 0, 0]
    kv = jnp.stack(ring_gather(jnp.stack(kv), "c"))
    return query, arrange(places, kv), seen


def scatter_query(grad, *others):
    inner = lax.axis_size("i")
    blocks = grad.reshape(OUTER, inner, -1, grad.shape[1])
    blocks = from_order([blocks[:, k] for k in range(inner)], "i")
    mine = ring_scatter(blocks[:1] + list(after(blocks[1:], *others)), "i").astype(BF16)
    return exchange(mine)


def scatter_kv(kept, sent):
    mine = lax.ppermute(sent, "c", [(0, 1), (1, 0)]).astype(F32) + kept
    high, inner = lax.axis_size("y"), lax.axis_size("i")
    wide = kept.shape[-1]
    mine = mine.reshape(high, OUTER, inner, -1, wide)
    blocks = from_order([mine[k] for k in range(high)], "y")
    sent = blocks[1].astype(BF16)
    own, arrived = ring_open([blocks[0], sent] + blocks[2:], "y")
    mine = arrived.astype(F32) + own
    mine = ring_scatter(from_order([mine[:, k] for k in range(inner)], "i"), "i").astype(BF16)
    here = exchange(mine)
    half = wide // 2
    whole = jnp.concatenate(
        [join_blocks(here[:, :, :half]), join_blocks(here[:, :, half:])], axis=1
    )
    return whole.astype(F32), sent, arrived, mine


def own_places():
    return jnp.stack([lax.axis_index(axis) for axis in ALL]).astype(jnp.int32)


def add_low(first, second):
    return (first.astype(F32) + second.astype(F32)).astype(BF16)


def ring_low(blocks, axis):
    travelling = blocks[1]
    for j in range(2, lax.axis_size(axis)):
        travelling = add_low(shift(travelling, axis), blocks[j])
    return add_low(shift(travelling, axis), blocks[0])


def part_low(rows):
    return ring_low([rows[k] for k in range(rows.shape[0])], "c")


def part_first(rows):
    half = rows.shape[2] // 2
    first, second = rows[:, :, :half], rows[:, :, half:]
    first = ring_low([first[k] for k in range(first.shape[0])], "y")
    second = ring_low([second[:, k] for k in range(second.shape[1])], "o")
    return first, second


def part_second(first, second):
    first = ring_low([first[k] for k in range(first.shape[0])], "o")
    second = ring_low([second[k] for k in range(second.shape[0])], "y")
    return jnp.concatenate([first, second])


VMEM = 56 * 1024 * 1024
ROW_STEP = 256


def nn(first, second):
    return jnp.dot(first, second, preferred_element_type=F32)


def nt(first, second):
    return lax.dot_general(first, second, (((1,), (1,)), ((), ())), preferred_element_type=F32)


def tn(first, second):
    return lax.dot_general(first, second, (((0,), (0,)), ((), ())), preferred_element_type=F32)


def as_column(row, rows):
    return jnp.broadcast_to(row, (rows, rows)).T[:, :1]


def turn(head, cosine, sine):
    return head * cosine + pltpu.roll(head, HD // 2, 1) * sine


def turn_back(head, cosine, sine):
    return head * cosine - pltpu.roll(head, HD // 2, 1) * sine


def allowed_keys(segment, length):
    keys = jnp.broadcast_to(segment, (length, length))
    row = lax.broadcasted_iota(jnp.int32, (length, length), 0)
    column = lax.broadcasted_iota(jnp.int32, (length, length), 1)
    return (keys == keys.T) & (column <= row)


def heads_nt(first, second):
    return lax.dot_general(first, second, (((2,), (2,)), ((0,), (0,))), preferred_element_type=F32)


def heads_nn(first, second):
    return lax.dot_general(first, second, (((2,), (1,)), ((0,), (0,))), preferred_element_type=F32)


def heads_tn(first, second):
    return lax.dot_general(first, second, (((1,), (1,)), ((0,), (0,))), preferred_element_type=F32)


def softmax_rows(queries, keys, allowed):
    scores = jnp.where(allowed[None], heads_nt(queries, keys) * (1.0 / math.sqrt(HD)), MASKED)
    exponent = jnp.exp(scores - jnp.max(scores, axis=-1, keepdims=True))
    return exponent / jnp.sum(exponent, axis=-1, keepdims=True)


def place_rows(places_ref, part_ref, value, length):
    count = part_ref.shape[2]
    for seq in range(count):
        slot = lax.rem(seq - places_ref[2] + count, count)
        part_ref[0, 0, slot] = value[seq * length : (seq + 1) * length]


def arrange_kernel(places_ref, in_ref, out_ref):
    del places_ref
    half = in_ref.shape[-1]
    for outer in range(OUTER):
        out_ref[0, 0, outer, 0, :, :half] = in_ref[0, 0, 0, outer, 0]
        out_ref[0, 0, outer, 0, :, half:] = in_ref[0, 0, 0, outer, 1]


def attend_kernel(
    places_ref,
    x_ref,
    info_ref,
    cos_ref,
    sin_ref,
    query_ref,
    kv_ref,
    qkv_ref,
    gated_ref,
):
    del places_ref
    length = cos_ref.shape[0]
    span = query_ref.shape[1]
    raw_query = nn(x_ref[...], query_ref[...])
    raw = nn(x_ref[...], kv_ref[...])
    cosine, sine = cos_ref[...], sin_ref[...]
    starts = range(0, span, HD)
    for seq in range(info_ref.shape[0]):
        rows = slice(seq * length, (seq + 1) * length)
        gate = as_column(info_ref[seq, 0:1, :], length)
        allowed = allowed_keys(info_ref[seq, 1:2, :], length)
        queries, keys, values = [], [], []
        for at in starts:
            head = raw_query[rows, at : at + HD].astype(BF16).astype(F32)
            queries.append(turn(head, cosine, sine).astype(BF16))
            keys.append(turn(raw[rows, at : at + HD], cosine, sine).astype(BF16))
            values.append(raw[rows, span + at : span + at + HD].astype(BF16))
            qkv_ref[rows, at : at + HD] = queries[-1]
            qkv_ref[rows, span + at : span + at + HD] = keys[-1]
            qkv_ref[rows, 2 * span + at : 2 * span + at + HD] = values[-1]
        probs = softmax_rows(jnp.stack(queries), jnp.stack(keys), allowed)
        gated = (heads_nn(probs.astype(BF16), jnp.stack(values)) * gate[None]).astype(BF16)
        for number, at in enumerate(starts):
            gated_ref[rows, at : at + HD] = gated[number]


def attend_back_kernel(
    places_ref,
    mid_ref,
    info_ref,
    cos_ref,
    sin_ref,
    qkv_ref,
    x_ref,
    query_ref,
    kv_ref,
    out_ref,
    d_query_ref,
    d_kv_ref,
    part_ref,
    d_gate_ref,
    d_gain_ref,
):
    del places_ref
    length = cos_ref.shape[0]
    span = out_ref.shape[0]
    scale = 1.0 / math.sqrt(HD)
    d_rows = nt(mid_ref[...], out_ref[...])
    cosine, sine = cos_ref[...], sin_ref[...]
    starts = range(0, span, HD)
    for seq in range(info_ref.shape[0]):
        rows = slice(seq * length, (seq + 1) * length)
        gate = as_column(info_ref[seq, 0:1, :], length)[None]
        allowed = allowed_keys(info_ref[seq, 1:2, :], length)
        queries = jnp.stack([qkv_ref[rows, at : at + HD] for at in starts])
        keys = jnp.stack([qkv_ref[rows, span + at : span + at + HD] for at in starts])
        values = jnp.stack([qkv_ref[rows, 2 * span + at : 2 * span + at + HD] for at in starts])
        d_heads = jnp.stack([d_rows[rows, at : at + HD] for at in starts])
        probs = softmax_rows(queries, keys, allowed)
        weighted = probs * heads_nt(d_heads.astype(BF16), values)
        sums = jnp.sum(weighted, axis=-1, keepdims=True)
        d_scores = ((weighted - probs * sums) * gate).astype(BF16)
        d_queries = heads_nn(d_scores, keys) * scale
        d_keys = heads_tn(d_scores, queries) * scale
        d_values = heads_tn(probs.astype(BF16), (d_heads * gate).astype(BF16))
        for number, at in enumerate(starts):
            cols = slice(at, at + HD)
            d_query_ref[rows, cols] = turn_back(d_queries[number], cosine, sine).astype(BF16)
            d_kv_ref[rows, cols] = turn_back(d_keys[number], cosine, sine).astype(BF16)
            d_kv_ref[rows, span + at : span + at + HD] = d_values[number].astype(BF16)
        total = jnp.broadcast_to(jnp.sum(sums, axis=0), (length, length))
        d_gate_ref[seq] = total.T[:1]
    d_input = nt(d_query_ref[...], query_ref[...]) + nt(d_kv_ref[...], kv_ref[...])

    @pl.when(pl.program_id(0) == 0)
    def _():
        d_gain_ref[...] = jnp.zeros_like(d_gain_ref)

    d_gain_ref[...] += jnp.sum(d_input * x_ref[...].astype(F32), axis=0, keepdims=True)
    part_ref[...] = d_input.astype(BF16)


def rows_kernel(parts, places_ref, *refs):
    gated_refs, down_refs, part_ref = refs[:parts], refs[parts : 2 * parts], refs[2 * parts]
    length = part_ref.shape[3]
    value = nn(gated_refs[0][...], down_refs[0][...])
    for part in range(1, parts):
        value = value + nn(gated_refs[part][...], down_refs[part][...])
    place_rows(places_ref, part_ref, value.astype(BF16), length)


def fixed(shape):
    return pl.BlockSpec(shape, lambda step, places: (0,) * len(shape))


def rows_spec(rows, columns):
    return pl.BlockSpec((rows, columns), lambda step, places: (step, 0))


def info_spec(seqs, kinds, length):
    return pl.BlockSpec((seqs, kinds, length), lambda step, places: (step, 0, 0))


def place_spec(high, length, width):
    def index(step, places):
        low = lax.rem(lax.rem(step, 2) - places[1] + 2, 2)
        return (low, lax.rem(lax.div(step, 2) - places[0] + high, high), 0, 0, 0)

    return pl.BlockSpec((1, 1, OUTER, length, width), index)


def shape(dims, dtype=BF16):
    return jax.ShapeDtypeStruct(dims, dtype)


def call(kernel, name, steps, in_specs, out_specs, out_shape, flops, moved, operands):
    return pl.pallas_call(
        kernel,
        grid_spec=pltpu.PrefetchScalarGridSpec(
            num_scalar_prefetch=1, grid=(steps,), in_specs=in_specs, out_specs=out_specs
        ),
        out_shape=out_shape,
        compiler_params=pltpu.CompilerParams(vmem_limit_bytes=VMEM),
        cost_estimate=pl.CostEstimate(flops=flops, bytes_accessed=moved, transcendentals=0),
        name=name,
    )(*operands)


def arrange(places, value):
    low, high, inner, outer, kinds, rows, span = value.shape

    def index(step, places):
        y = lax.div(step, 2 * inner)
        c = lax.rem(lax.div(step, inner), 2)
        i = lax.rem(step, inner)
        return (
            lax.rem(c - places[1] + 2, 2),
            lax.rem(y - places[0] + high, high),
            lax.rem(i - places[3] + inner, inner),
            0,
            0,
            0,
            0,
        )

    def out_index(step, places):
        return (
            lax.div(step, 2 * inner),
            lax.rem(lax.div(step, inner), 2),
            0,
            lax.rem(step, inner),
            0,
            0,
        )

    dims = (high, low, outer, inner, rows, kinds * span)
    found = call(
        arrange_kernel,
        "arrange",
        high * low * inner,
        [pl.BlockSpec((1, 1, 1, outer, kinds, rows, span), index)],
        pl.BlockSpec((1, 1, outer, 1, rows, kinds * span), out_index),
        shape(dims),
        0,
        4 * value.size,
        (places, value),
    )
    return found.reshape(-1, kinds * span)


def attend(places, rows, info, cosine, sine, query_mat, kv_mat):
    count, width = rows.shape
    span = query_mat.shape[1]
    length = cosine.shape[0]
    step = OUTER * length
    return call(
        attend_kernel,
        "attend",
        count // step,
        [
            rows_spec(step, width),
            info_spec(OUTER, 2, length),
            fixed(cosine.shape),
            fixed(sine.shape),
            fixed(query_mat.shape),
            fixed(kv_mat.shape),
        ],
        [rows_spec(step, 3 * span), rows_spec(step, span)],
        [shape((count, 3 * span)), shape((count, span))],
        2 * count * width * 3 * span + 4 * count * length * span,
        4 * count * (width + 2 * span),
        (places, rows, info, cosine, sine, query_mat, kv_mat),
    )


def attend_back(places, d_middle, info, cosine, sine, qkv, rows, query_mat, kv_mat, out_mat):
    count, width = d_middle.shape
    length = cosine.shape[0]
    step = OUTER * length
    span = out_mat.shape[0]
    return call(
        attend_back_kernel,
        "attend_back",
        count // step,
        [
            rows_spec(step, width),
            info_spec(OUTER, 2, length),
            fixed(cosine.shape),
            fixed(sine.shape),
            rows_spec(step, 3 * span),
            rows_spec(step, width),
            fixed(query_mat.shape),
            fixed(kv_mat.shape),
            fixed(out_mat.shape),
        ],
        [
            rows_spec(step, span),
            rows_spec(step, 2 * span),
            rows_spec(step, width),
            info_spec(OUTER, 1, length),
            fixed((1, width)),
        ],
        [
            shape((count, span)),
            shape((count, 2 * span)),
            shape((count, width)),
            shape((count // length, 1, length), F32),
            shape((1, width), F32),
        ],
        2 * count * width * 4 * span + 10 * count * length * span,
        4 * count * (2 * width + 3 * span),
        (places, d_middle, info, cosine, sine, qkv, rows, query_mat, kv_mat, out_mat),
    )


def ring_rows(places, gated_units, down_parts, length):
    count, units = gated_units[0].shape
    width = down_parts[0].shape[1]
    parts = len(down_parts)
    step = OUTER * length
    high = count // (2 * step)
    return call(
        functools.partial(rows_kernel, parts),
        "rows",
        count // step,
        [rows_spec(step, units)] * parts + [fixed(down.shape) for down in down_parts],
        place_spec(high, length, width),
        shape((2, high, OUTER, length, width)),
        2 * count * width * units * parts,
        4 * count * (width + units * parts),
        (places, *gated_units, *down_parts),
    )


def units_kernel(places_ref, x_ref, info_ref, d_units_ref, first_ref, second_ref, *refs):
    del places_ref
    sums_refs, (d_both_ref, gated_ref, back_ref, d_gate_ref) = refs[:-4], refs[-4:]
    length = info_ref.shape[2]
    seqs = info_ref.shape[0]
    units = first_ref.shape[0]
    rows = x_ref[...]
    gate = jnp.concatenate([as_column(info_ref[seq], length) for seq in range(seqs)], axis=0)
    gate_in = nt(rows, first_ref[...])
    up_in = nt(rows, second_ref[...])
    sigma = jax.nn.sigmoid(gate_in)
    active = gate_in * sigma
    hidden_units = active * up_in
    d_units = d_units_ref[...].astype(F32)
    d_gate = jnp.sum(hidden_units * d_units, axis=-1, keepdims=True)
    gated_ref[...] = (hidden_units * gate).astype(BF16)
    d_units = d_units * gate
    d_first = (d_units * up_in * (sigma + active * (1.0 - sigma))).astype(BF16)
    d_second = (d_units * active).astype(BF16)
    d_both_ref[:, :units] = d_first
    d_both_ref[:, units:] = d_second
    back = nn(d_first, first_ref[...]) + nn(d_second, second_ref[...])
    if sums_refs:
        back = back + sums_refs[0][...]
    back_ref[...] = back.astype(back_ref.dtype)
    for seq in range(seqs):
        column = jnp.broadcast_to(d_gate[seq * length : (seq + 1) * length], (length, length))
        d_gate_ref[seq] = column.T[:1]


def run_units(places, rows, info, d_units, first, second, sums, last):
    count, width = rows.shape
    length = info.shape[2]
    units = d_units.shape[1]
    seqs = ROW_STEP // length

    def weight_spec(block):
        return pl.BlockSpec((units, width), lambda step, places: (block, 0))

    extra = [] if sums is None else [sums]
    return call(
        units_kernel,
        "units",
        count // ROW_STEP,
        [rows_spec(ROW_STEP, width), info_spec(seqs, 1, length), rows_spec(ROW_STEP, units)]
        + [weight_spec(first[1]), weight_spec(second[1])]
        + [rows_spec(ROW_STEP, width) for _ in extra],
        [
            rows_spec(ROW_STEP, 2 * units),
            rows_spec(ROW_STEP, units),
            rows_spec(ROW_STEP, width),
            info_spec(seqs, 1, length),
        ],
        [
            shape((count, 2 * units)),
            shape((count, units)),
            shape((count, width), BF16 if last else F32),
            shape((count // length, 1, length), F32),
        ],
        0,
        0,
        (places, rows, info, d_units, first[0], second[0], *extra),
    )


def shards(
    hidden_in,
    segment_ids,
    att_route,
    mlp_route,
    norm_gain1,
    norm_gain2,
    att_router,
    mlp_router,
    kv_weight,
    query_weight,
    out_weight,
    att_bias,
    up_weight,
    down_weight,
    mlp_bias,
    cotangent,
):
    experts = lax.axis_size(EXPERT)
    inner = lax.axis_size("i")
    tokens, width = hidden_in.shape
    span = HEADS // OUTER * HD
    cosine, sine_table = rope_tables(tokens)

    places = own_places()

    down_parts = ring_gather(down_weight[0], "i")
    query_mat, kv_mat, seen = gather_heads(
        places, query_weight[0], kv_weight, down_parts[1:]
    )
    out_parts = ring_gather(after(out_weight[0], seen), "i")
    own_up = up_weight[0].reshape(-1, width)

    residual = hidden_in.astype(F32)
    normed_one, inverse_one = norm_rows(residual, norm_gain1)
    attn_input = normed_one.astype(BF16)
    att_gate, att_onehot = pair_gates(attn_input, att_router, att_route, experts)
    info = to_experts(att_gate, att_onehot, segment_ids[0].astype(F32))
    all_attn = meet(attn_input)
    all_cot = meet(after(cotangent.astype(BF16), seen))
    qkv, gated = attend(places, all_attn, info, cosine, sine_table, query_mat, kv_mat)
    out_parts = out_parts[:1] + list(after(out_parts[1:], gated))
    out_mat = in_order(out_parts, "i").reshape(span, width)
    branch = part_low(ring_rows(places, [gated], [out_mat], tokens))
    branch = part_second(*part_first(branch))

    d_units = [mm("td,fd->tf", all_cot, down).astype(BF16) for down in down_parts]
    branch = after(branch, d_units)
    middle = residual + branch.astype(F32) + att_bias
    normed_two, inverse_two = norm_rows(middle, norm_gain2)
    mlp_input = normed_two.astype(BF16)
    mlp_gate, mlp_onehot = pair_gates(mlp_input, mlp_router, mlp_route, experts)
    up_parts = ring_gather(after(own_up, gated), "i")
    all_mlp = meet(mlp_input)
    gate_m = to_experts(mlp_gate, mlp_onehot, None)
    d_both, gated_units, rows_back, d_gate_m = [], [], None, None
    for number, up in enumerate(up_parts):
        source = own_up if number == 0 else up
        found = run_units(
            places,
            all_mlp,
            gate_m,
            d_units[number],
            (source, 0),
            (source, 1),
            rows_back,
            number == inner - 1,
        )
        d_both.append(found[0])
        gated_units.append(found[1])
        rows_back = found[2]
        d_gate_m = found[3] if d_gate_m is None else d_gate_m + found[3]
    d_mlp_input = part(rows_back)
    d_mlp_gate = from_experts(d_gate_m[:, 0], mlp_onehot, experts)
    grad_up = [mm("tf,td->fd", d_here, all_mlp) for d_here in d_both]
    grad_down = [mm("tf,td->fd", here, all_cot) for here in gated_units]
    low_up = [one.astype(BF16) for one in grad_up[1:]]
    low_down = [one.astype(BF16) for one in grad_down[1:]]
    rows_out = part_low(ring_rows(places, gated_units, down_parts, tokens))
    half = tokens // 2
    rows_first, rows_second = rows_out[:, :, :half], rows_out[:, :, half:]
    lower_own, lower_last = ring_open(grad_down[:1] + low_down, "i")
    upper_own, upper_last = ring_open(grad_up[:1] + low_up, "i")
    d_mlp_input = after(d_mlp_input, rows_out, low_up, lower_last)
    d_mlp_router, d_mlp_from_router = gates_back(
        mlp_gate, mlp_onehot, d_mlp_gate, mlp_input, mlp_router
    )
    d_norm_two, d_gain_two = norm_back(
        middle, inverse_two, norm_gain2, d_mlp_input.astype(F32) + d_mlp_from_router
    )
    d_middle = cotangent + d_norm_two
    sums = jnp.concatenate(
        [
            jnp.stack([d_gain_two, jnp.sum(d_middle, axis=0), jnp.sum(cotangent, axis=0)]),
            d_mlp_router,
        ]
    )

    all_mid = meet(d_middle.astype(BF16))
    rows_second = ring_low([rows_second[:, k] for k in range(OUTER)], "o")
    all_mid = after(all_mid, rows_second)
    d_heads, d_kv, rows_one, d_gate_a, d_gain_a = attend_back(
        places, all_mid, info, cosine, sine_table, qkv, all_attn, query_mat, kv_mat, out_mat
    )
    rows_first = after(rows_first, all_mid)
    rows_first = [rows_first[k] for k in range(rows_first.shape[0])]
    rows_first = ring_low(rows_first, "y")
    d_attn_input = part(rows_one)
    d_att_gate = from_experts(d_gate_a[:, 0], att_onehot, experts)
    d_kv_mat = mm("td,tf->df", all_attn, d_kv).reshape(experts // 2, 2, -1, 2 * span)
    d_kv_mat = from_order([d_kv_mat[:, 0], d_kv_mat[:, 1]], "c")
    d_kv_sent = d_kv_mat[1].astype(BF16)
    d_kv_weight, kv_sent, kv_arrived, kv_last = scatter_kv(d_kv_mat[0], d_kv_sent)
    d_heads, all_mid = after((d_heads, all_mid), kv_sent)
    d_att_router, d_att_from_router = gates_back(
        att_gate, att_onehot, d_att_gate, attn_input, att_router
    )
    d_gain_one = d_gain_a / norm_gain1 + jnp.sum(
        d_att_from_router * residual * inverse_one, axis=0, keepdims=True
    )
    summed = sum_over(jnp.concatenate([d_gain_one, sums, d_att_router]), ("i",))
    d_query = scatter_query(mm("td,tf->df", all_attn, d_heads), summed)
    d_out = mm("tf,td->fd", gated, all_mid).reshape(inner, -1, width)
    d_out = from_order([d_out[k] for k in range(inner)], "i")
    d_out = d_out[:1] + list(after(d_out[1:], kv_arrived))
    d_output = ring_scatter(d_out, "i", d_query)[None]
    d_query = join_blocks(d_query).astype(F32)[None]
    rows_out = part_second(*after((rows_first, rows_second), kv_arrived))
    layer_out = middle + rows_out.astype(F32) + mlp_bias
    d_upper = (after(upper_last, kv_sent).astype(F32) + upper_own).reshape(up_weight.shape)
    d_lower = (lower_last.astype(F32) + lower_own)[None]
    summed = sum_over(after(summed, kv_last), ("c", "o", "y"))
    d_attn_input = after(d_attn_input, summed)
    d_norm_one, _ = norm_back(
        residual, inverse_one, norm_gain1, d_attn_input.astype(F32) + d_att_from_router
    )
    d_input = d_middle + d_norm_one
    return (
        layer_out,
        d_input,
        summed[0],
        summed[1],
        summed[4 + experts :].T,
        summed[4 : 4 + experts].T,
        d_kv_weight,
        d_query,
        d_output,
        summed[2],
        d_upper,
        d_lower,
        summed[3],
    )


def solution(mesh):
    experts, fsdp = mesh.shape["expert"], mesh.shape["fsdp"]
    fine = Mesh(mesh.devices.reshape(experts // 2, 2, OUTER, fsdp // OUTER), ALL)
    shard = ("o", "i")
    rows = P(ALL, None)
    placed = (
        rows,
        rows,
        rows,
        rows,
        P(),
        P(),
        P(),
        P(),
        rows,
        P(EXPERT, shard, None),
        P(EXPERT, shard, None),
        P(),
        P(EXPERT, None, shard, None),
        P(EXPERT, shard, None),
        P(),
        rows,
    )
    return jax.shard_map(
        shards,
        mesh=fine,
        in_specs=placed,
        out_specs=(
            rows,
            rows,
            P(),
            P(),
            P(),
            P(),
            rows,
            P(EXPERT, shard, None),
            P(EXPERT, shard, None),
            P(),
            P(EXPERT, None, shard, None),
            P(EXPERT, shard, None),
            P(),
        ),
        check_vma=False,
    )
```

```python
import functools
import math

import jax
import jax.numpy as jnp
from jax import lax
from jax.experimental import pallas as pl
from jax.experimental.pallas import tpu as pltpu
from jax.sharding import Mesh, PartitionSpec as P

HEADS = 16
HD = 128
TOP = 2


EPSILON = 1e-06
HIGHEST = lax.Precision.HIGHEST
MASKED = -1e30

GROUP = ("y", "c", "o")
EXPERT = ("y", "c")
ALL = ("y", "c", "o", "i")
OUTER = 4
F32 = jnp.float32
BF16 = jnp.bfloat16


def rope_tables(length):
    half_dim = HD // 2
    frequency = jnp.exp(jnp.arange(half_dim, dtype=F32) * (-2.0 * math.log(10000.0) / HD))
    angles = jnp.arange(length, dtype=F32)[:, None] * frequency[None, :]
    cosine, sine = jnp.cos(angles), jnp.sin(angles)
    return (
        jnp.concatenate([cosine, cosine], axis=1),
        jnp.concatenate([-sine, sine], axis=1),
    )


def norm_rows(stream, gain):
    inverse = lax.rsqrt(jnp.mean(stream * stream, axis=-1, keepdims=True) + EPSILON)
    return (stream * inverse * gain, inverse)


def norm_back(stream, inverse, gain, upstream):
    scaled = upstream * gain
    d_stream = inverse * scaled - stream * inverse**3 * jnp.mean(
        scaled * stream, axis=-1, keepdims=True
    )
    d_gain = jnp.sum(upstream * stream * inverse, axis=0)
    return (d_stream, d_gain)


def shift(value, axis):
    size = lax.axis_size(axis)
    return lax.ppermute(value, axis, [((k + 1) % size, k) for k in range(size)])


def after(value, *others):
    token, _ = lax.optimization_barrier((lax.create_token(), others))
    return lax.optimization_barrier((token, value))[1]


def ring_gather(value, axis):
    parts = [value]
    for _ in range(lax.axis_size(axis) - 1):
        parts.append(shift(parts[-1], axis))
    return parts


def ring_open(blocks, axis):
    size = lax.axis_size(axis)
    travelling = blocks[1].astype(BF16)
    for j in range(2, size):
        travelling = (shift(travelling, axis).astype(F32) + blocks[j].astype(F32)).astype(BF16)
    return blocks[0], shift(travelling, axis)


def ring_scatter(blocks, axis, *others):
    own, arrived = ring_open(blocks, axis)
    if others:
        arrived = after(arrived, *others)
    return arrived.astype(F32) + own


def in_order(parts, axis, place=0):
    if len(parts) == 2:
        first = lax.axis_index(axis) == 0
        return jnp.stack([jnp.where(first, *parts), jnp.where(first, *parts[::-1])], axis=place)
    return jnp.roll(jnp.stack(parts, axis=place), lax.axis_index(axis), axis=place)


def from_order(parts, axis):
    if len(parts) == 2:
        first = lax.axis_index(axis) == 0
        return [jnp.where(first, *parts), jnp.where(first, *parts[::-1])]
    return list(jnp.roll(jnp.stack(parts), -lax.axis_index(axis), axis=0))


def sum_over(value, axes):
    for axis in axes:
        size = lax.axis_size(axis)
        step = 1
        while step < size:
            value = value + lax.ppermute(value, axis, [(k, k ^ step) for k in range(size)])
            step *= 2
    return value


def pair_gates(normed, router, route, experts):
    logits = jnp.dot(normed.astype(F32), router, precision=HIGHEST)
    onehot = (route[:, :, None] == jnp.arange(experts, dtype=jnp.int32)[None, None, :]).astype(F32)
    picked = jnp.sum(logits[:, None, :] * onehot, axis=-1)
    return (jax.nn.softmax(picked, axis=-1), onehot)


def gates_back(gates, onehot, d_gates, normed, router):
    d_picked = gates * (d_gates - jnp.sum(gates * d_gates, axis=-1, keepdims=True))
    d_logits = jnp.sum(d_picked[:, :, None] * onehot, axis=1)
    d_router = jnp.dot(d_logits.T, normed.astype(F32), precision=HIGHEST)
    d_normed = jnp.dot(d_logits, router.T, precision=HIGHEST)
    return (d_router, d_normed)


def to_experts(gates, onehot, extra):
    by_expert = jnp.sum(gates[:, :, None] * onehot, axis=1).T
    rows = jnp.repeat(by_expert, OUTER, axis=0)[:, None, :]
    if extra is not None:
        rows = jnp.concatenate(
            [rows, jnp.broadcast_to(extra[None, None, :], rows.shape)], axis=1
        )
    return lax.all_to_all(rows, GROUP, split_axis=0, concat_axis=0, tiled=True)


def from_experts(d_gates, onehot, experts):
    rows = lax.all_to_all(d_gates, GROUP, split_axis=0, concat_axis=0, tiled=True)
    by_expert = jnp.sum(rows.reshape(experts, OUTER, -1), axis=1)
    return jnp.einsum("tce,et->tc", onehot, by_expert, precision=HIGHEST)


def meet(rows):
    return lax.all_gather(rows, GROUP, axis=0, tiled=True)


def part(rows):
    return lax.psum_scatter(rows, GROUP, scatter_dimension=0, tiled=True)


def mm(form, first, second):
    return jnp.einsum(form, first, second, preferred_element_type=F32)


def head_blocks(matrix):
    span = HEADS // OUTER * HD
    return jnp.stack([matrix[:, k * span : (k + 1) * span] for k in range(OUTER)])


def join_blocks(blocks):
    return jnp.concatenate([blocks[k] for k in range(OUTER)], axis=1)


def exchange(blocks):
    return lax.all_to_all(blocks, "o", split_axis=0, concat_axis=0, tiled=True)


def gather_heads(query_weight, kv_weight, beside):
    whole = HEADS * HD
    rows = query_weight.shape[0]
    here = exchange(
        jnp.concatenate(
            [
                head_blocks(query_weight),
                head_blocks(kv_weight[:, :whole]),
                head_blocks(kv_weight[:, whole:]),
            ],
            axis=1,
        )
    )
    here = after(here, *beside)
    span = here.shape[2]
    kv = ring_gather(here[:, rows:].reshape(OUTER, 2, -1, span), "i")
    query = ring_gather(after(here[:, :rows], kv[-1]), "i")
    kv = ring_gather(jnp.stack(kv), "y")
    kv = after(kv, query)
    query = in_order(query, "i", 1).reshape(-1, span)
    seen = kv[-1][0, 0, 0, 0]
    return query, ring_gather(jnp.stack(kv), "c"), seen


def scatter_query(grad, *others):
    inner = lax.axis_size("i")
    blocks = grad.reshape(OUTER, inner, -1, grad.shape[1])
    blocks = from_order([blocks[:, k] for k in range(inner)], "i")
    return ring_scatter(blocks[:1] + list(after(blocks[1:], *others)), "i").astype(BF16)


def scatter_kv(kept, sent):
    mine = lax.ppermute(sent, "c", [(0, 1), (1, 0)]).astype(F32) + kept
    high, inner = lax.axis_size("y"), lax.axis_size("i")
    mine = mine.reshape(high, OUTER, inner, -1, kept.shape[-1])
    blocks = from_order([mine[k] for k in range(high)], "y")
    sent = blocks[1].astype(BF16)
    own, arrived = ring_open([blocks[0], sent] + blocks[2:], "y")
    mine = arrived.astype(F32) + own
    mine = ring_scatter(from_order([mine[:, k] for k in range(inner)], "i"), "i").astype(BF16)
    return mine, sent, arrived


def scatter_heads(query, kv, *others):
    half = kv.shape[2] // 2
    rows, kv_rows = query.shape[1], kv.shape[1]
    sent = jnp.concatenate([query, kv[:, :, :half], kv[:, :, half:]], axis=1)
    here = exchange(after(sent, *others)).astype(F32)
    whole = [
        join_blocks(here[:, rows + k * kv_rows : rows + (k + 1) * kv_rows]) for k in range(2)
    ]
    return join_blocks(here[:, :rows]), jnp.concatenate(whole, axis=1)


def own_places():
    return jnp.stack([lax.axis_index(axis) for axis in ALL]).astype(jnp.int32)


def add_low(first, second):
    return (first.astype(F32) + second.astype(F32)).astype(BF16)


def ring_low(blocks, axis):
    travelling = blocks[1]
    for j in range(2, lax.axis_size(axis)):
        travelling = add_low(shift(travelling, axis), blocks[j])
    return add_low(shift(travelling, axis), blocks[0])


def part_low(own, other):
    return ring_low([own, other], "c")


def part_first(rows):
    half = rows.shape[2] // 2
    first, second = rows[:, :, :half], rows[:, :, half:]
    first = ring_low([first[k] for k in range(first.shape[0])], "y")
    second = ring_low([second[:, k] for k in range(second.shape[1])], "o")
    return first, second


def part_second(first, second):
    first = ring_low([first[k] for k in range(first.shape[0])], "o")
    second = ring_low([second[k] for k in range(second.shape[0])], "y")
    return jnp.concatenate([first, second])


VMEM = 56 * 1024 * 1024
ROW_STEP = 256


def nn(first, second):
    return jnp.dot(first, second, preferred_element_type=F32)


def nt(first, second):
    return lax.dot_general(first, second, (((1,), (1,)), ((), ())), preferred_element_type=F32)


def tn(first, second):
    return lax.dot_general(first, second, (((0,), (0,)), ((), ())), preferred_element_type=F32)


def as_column(row, rows):
    return jnp.broadcast_to(row, (rows, rows)).T[:, :1]


def turn(head, cosine, sine):
    return head * cosine + pltpu.roll(head, HD // 2, 1) * sine


def turn_back(head, cosine, sine):
    return head * cosine - pltpu.roll(head, HD // 2, 1) * sine


def allowed_keys(segment, length):
    keys = jnp.broadcast_to(segment, (length, length))
    row = lax.broadcasted_iota(jnp.int32, (length, length), 0)
    column = lax.broadcasted_iota(jnp.int32, (length, length), 1)
    return (keys == keys.T) & (column <= row)


def heads_nt(first, second):
    return lax.dot_general(first, second, (((2,), (2,)), ((0,), (0,))), preferred_element_type=F32)


def heads_nn(first, second):
    return lax.dot_general(first, second, (((2,), (1,)), ((0,), (0,))), preferred_element_type=F32)


def heads_tn(first, second):
    return lax.dot_general(first, second, (((1,), (1,)), ((0,), (0,))), preferred_element_type=F32)


def softmax_rows(queries, keys, allowed):
    scores = jnp.where(allowed[None], heads_nt(queries, keys) * (1.0 / math.sqrt(HD)), MASKED)
    exponent = jnp.exp(scores - jnp.max(scores, axis=-1, keepdims=True))
    return exponent / jnp.sum(exponent, axis=-1, keepdims=True)


def place_rows(places_ref, part_ref, value, length):
    count = part_ref.shape[1]
    for seq in range(count):
        slot = lax.rem(seq - places_ref[2] + count, count)
        part_ref[0, slot] = value[seq * length : (seq + 1) * length]


def arrange(places_ref, part_refs, out_ref):
    high, inner, outer, kinds, rows, span = part_refs[0].shape
    for low, part_ref in enumerate(part_refs):
        c = lax.rem(low + places_ref[1], 2)
        for first in range(high):
            y = lax.rem(first + places_ref[0], high)
            for second in range(inner):
                i = lax.rem(second + places_ref[3], inner)
                for o in range(outer):
                    start = (((y * 2 + c) * outer + o) * inner + i) * rows
                    for kind in range(kinds):
                        out_ref[
                            pl.ds(pl.multiple_of(start, 16), rows), kind * span : (kind + 1) * span
                        ] = part_ref[first, second, o, kind]


def attend_kernel(
    places_ref,
    x_ref,
    info_ref,
    cos_ref,
    sin_ref,
    query_ref,
    own_ref,
    other_ref,
    qkv_ref,
    gated_ref,
    kv_ref,
):
    @pl.when(pl.program_id(0) == 0)
    def _():
        arrange(places_ref, (own_ref, other_ref), kv_ref)

    length = cos_ref.shape[0]
    span = query_ref.shape[1]
    raw_query = nn(x_ref[...], query_ref[...])
    raw = nn(x_ref[...], kv_ref[...])
    cosine, sine = cos_ref[...], sin_ref[...]
    starts = range(0, span, HD)
    for seq in range(info_ref.shape[0]):
        rows = slice(seq * length, (seq + 1) * length)
        gate = as_column(info_ref[seq, 0:1, :], length)
        allowed = allowed_keys(info_ref[seq, 1:2, :], length)
        queries, keys, values = [], [], []
        for at in starts:
            head = raw_query[rows, at : at + HD].astype(BF16).astype(F32)
            queries.append(turn(head, cosine, sine).astype(BF16))
            keys.append(turn(raw[rows, at : at + HD], cosine, sine).astype(BF16))
            values.append(raw[rows, span + at : span + at + HD].astype(BF16))
            qkv_ref[rows, at : at + HD] = queries[-1]
            qkv_ref[rows, span + at : span + at + HD] = keys[-1]
            qkv_ref[rows, 2 * span + at : 2 * span + at + HD] = values[-1]
        probs = softmax_rows(jnp.stack(queries), jnp.stack(keys), allowed)
        gated = (heads_nn(probs.astype(BF16), jnp.stack(values)) * gate[None]).astype(BF16)
        for number, at in enumerate(starts):
            gated_ref[rows, at : at + HD] = gated[number]


def attend_back_kernel(
    places_ref,
    mid_ref,
    info_ref,
    cos_ref,
    sin_ref,
    qkv_ref,
    x_ref,
    query_ref,
    kv_ref,
    out_ref,
    d_query_ref,
    d_kv_ref,
    part_ref,
    d_gate_ref,
    d_gain_ref,
):
    del places_ref
    length = cos_ref.shape[0]
    span = out_ref.shape[0]
    scale = 1.0 / math.sqrt(HD)
    d_rows = nt(mid_ref[...], out_ref[...])
    cosine, sine = cos_ref[...], sin_ref[...]
    starts = range(0, span, HD)
    for seq in range(info_ref.shape[0]):
        rows = slice(seq * length, (seq + 1) * length)
        gate = as_column(info_ref[seq, 0:1, :], length)[None]
        allowed = allowed_keys(info_ref[seq, 1:2, :], length)
        queries = jnp.stack([qkv_ref[rows, at : at + HD] for at in starts])
        keys = jnp.stack([qkv_ref[rows, span + at : span + at + HD] for at in starts])
        values = jnp.stack([qkv_ref[rows, 2 * span + at : 2 * span + at + HD] for at in starts])
        d_heads = jnp.stack([d_rows[rows, at : at + HD] for at in starts])
        probs = softmax_rows(queries, keys, allowed)
        weighted = probs * heads_nt(d_heads.astype(BF16), values)
        sums = jnp.sum(weighted, axis=-1, keepdims=True)
        d_scores = ((weighted - probs * sums) * gate).astype(BF16)
        d_queries = heads_nn(d_scores, keys) * scale
        d_keys = heads_tn(d_scores, queries) * scale
        d_values = heads_tn(probs.astype(BF16), (d_heads * gate).astype(BF16))
        for number, at in enumerate(starts):
            cols = slice(at, at + HD)
            d_query_ref[rows, cols] = turn_back(d_queries[number], cosine, sine).astype(BF16)
            d_kv_ref[rows, cols] = turn_back(d_keys[number], cosine, sine).astype(BF16)
            d_kv_ref[rows, span + at : span + at + HD] = d_values[number].astype(BF16)
        total = jnp.broadcast_to(jnp.sum(sums, axis=0), (length, length))
        d_gate_ref[seq] = total.T[:1]
    d_input = nt(d_query_ref[...], query_ref[...]) + nt(d_kv_ref[...], kv_ref[...])

    @pl.when(pl.program_id(0) == 0)
    def _():
        d_gain_ref[...] = jnp.zeros_like(d_gain_ref)

    d_gain_ref[...] += jnp.sum(d_input * x_ref[...].astype(F32), axis=0, keepdims=True)
    part_ref[...] = d_input.astype(BF16)


def rows_kernel(parts, places_ref, *refs):
    gated_refs, down_refs, (own_ref, other_ref) = refs[:parts], refs[parts : 2 * parts], refs[2 * parts :]
    length = own_ref.shape[2]
    value = nn(gated_refs[0][...], down_refs[0][...])
    for part in range(1, parts):
        value = value + nn(gated_refs[part][...], down_refs[part][...])
    value = value.astype(BF16)
    other_first = pl.num_programs(0) // 2

    @pl.when(pl.program_id(0) < other_first)
    def _():
        place_rows(places_ref, other_ref, value, length)

    @pl.when(pl.program_id(0) >= other_first)
    def _():
        place_rows(places_ref, own_ref, value, length)


def fixed(shape):
    return pl.BlockSpec(shape, lambda step, places: (0,) * len(shape))


def rows_spec(rows, columns):
    return pl.BlockSpec((rows, columns), lambda step, places: (step, 0))


def info_spec(seqs, kinds, length):
    return pl.BlockSpec((seqs, kinds, length), lambda step, places: (step, 0, 0))


def shape(dims, dtype=BF16):
    return jax.ShapeDtypeStruct(dims, dtype)


def call(kernel, name, steps, in_specs, out_specs, out_shape, flops, moved, operands):
    return pl.pallas_call(
        kernel,
        grid_spec=pltpu.PrefetchScalarGridSpec(
            num_scalar_prefetch=1, grid=(steps,), in_specs=in_specs, out_specs=out_specs
        ),
        out_shape=out_shape,
        compiler_params=pltpu.CompilerParams(vmem_limit_bytes=VMEM),
        cost_estimate=pl.CostEstimate(flops=flops, bytes_accessed=moved, transcendentals=0),
        name=name,
    )(*operands)


def attend(places, rows, info, cosine, sine, query_mat, kv_parts):
    count, width = rows.shape
    span = query_mat.shape[1]
    length = cosine.shape[0]
    step = OUTER * length
    return call(
        attend_kernel,
        "attend",
        count // step,
        [
            rows_spec(step, width),
            info_spec(OUTER, 2, length),
            fixed(cosine.shape),
            fixed(sine.shape),
            fixed(query_mat.shape),
            *[fixed(one.shape) for one in kv_parts],
        ],
        [rows_spec(step, 3 * span), rows_spec(step, span), fixed((width, 2 * span))],
        [shape((count, 3 * span)), shape((count, span)), shape((width, 2 * span))],
        2 * count * width * 3 * span + 4 * count * length * span,
        4 * count * (width + 2 * span),
        (places, rows, info, cosine, sine, query_mat, *kv_parts),
    )


def attend_back(places, d_middle, info, cosine, sine, qkv, rows, query_mat, kv_mat, out_mat):
    count, width = d_middle.shape
    length = cosine.shape[0]
    step = OUTER * length
    span = out_mat.shape[0]
    return call(
        attend_back_kernel,
        "attend_back",
        count // step,
        [
            rows_spec(step, width),
            info_spec(OUTER, 2, length),
            fixed(cosine.shape),
            fixed(sine.shape),
            rows_spec(step, 3 * span),
            rows_spec(step, width),
            fixed(query_mat.shape),
            fixed(kv_mat.shape),
            fixed(out_mat.shape),
        ],
        [
            rows_spec(step, span),
            rows_spec(step, 2 * span),
            rows_spec(step, width),
            info_spec(OUTER, 1, length),
            fixed((1, width)),
        ],
        [
            shape((count, span)),
            shape((count, 2 * span)),
            shape((count, width)),
            shape((count // length, 1, length), F32),
            shape((1, width), F32),
        ],
        2 * count * width * 4 * span + 10 * count * length * span,
        4 * count * (2 * width + 3 * span),
        (places, d_middle, info, cosine, sine, qkv, rows, query_mat, kv_mat, out_mat),
    )


def ring_rows(places, gated, mats, length):
    count, units = gated[0].shape
    width = mats[0].shape[1]
    parts = len(mats)
    step = OUTER * length
    high = count // (2 * step)

    def pair(number, places):
        c = lax.rem(lax.div(number, high) + 1 + places[1], 2)
        return (lax.rem(lax.rem(number, high) + places[0], high) * 2 + c, 0)

    block = (1, OUTER, length, width)
    return call(
        functools.partial(rows_kernel, parts),
        "rows",
        count // step,
        [pl.BlockSpec((step, units), pair)] * parts + [fixed(one.shape) for one in mats],
        [
            pl.BlockSpec(block, lambda number, places: (lax.max(number - high, 0), 0, 0, 0)),
            pl.BlockSpec(block, lambda number, places: (lax.min(number, high - 1), 0, 0, 0)),
        ],
        [shape((high, OUTER, length, width))] * 2,
        2 * count * width * units * parts,
        4 * count * (width + units * parts),
        (places, *gated, *mats),
    )


def units_kernel(places_ref, x_ref, info_ref, d_units_ref, first_ref, second_ref, *refs):
    del places_ref
    sums_refs, (d_both_ref, gated_ref, back_ref, d_gate_ref) = refs[:-4], refs[-4:]
    length = info_ref.shape[2]
    seqs = info_ref.shape[0]
    units = first_ref.shape[0]
    rows = x_ref[...]
    gate = jnp.concatenate([as_column(info_ref[seq], length) for seq in range(seqs)], axis=0)
    gate_in = nt(rows, first_ref[...])
    up_in = nt(rows, second_ref[...])
    sigma = jax.nn.sigmoid(gate_in)
    active = gate_in * sigma
    hidden_units = active * up_in
    d_units = d_units_ref[...].astype(F32)
    d_gate = jnp.sum(hidden_units * d_units, axis=-1, keepdims=True)
    gated_ref[...] = (hidden_units * gate).astype(BF16)
    d_units = d_units * gate
    d_first = (d_units * up_in * (sigma + active * (1.0 - sigma))).astype(BF16)
    d_second = (d_units * active).astype(BF16)
    d_both_ref[:, :units] = d_first
    d_both_ref[:, units:] = d_second
    back = nn(d_first, first_ref[...]) + nn(d_second, second_ref[...])
    if sums_refs:
        back = back + sums_refs[0][...]
    back_ref[...] = back.astype(back_ref.dtype)
    for seq in range(seqs):
        column = jnp.broadcast_to(d_gate[seq * length : (seq + 1) * length], (length, length))
        d_gate_ref[seq] = column.T[:1]


def run_units(places, rows, info, d_units, first, second, sums, last):
    count, width = rows.shape
    length = info.shape[2]
    units = d_units.shape[1]
    seqs = ROW_STEP // length

    def weight_spec(block):
        return pl.BlockSpec((units, width), lambda step, places: (block, 0))

    extra = [] if sums is None else [sums]
    return call(
        units_kernel,
        "units",
        count // ROW_STEP,
        [rows_spec(ROW_STEP, width), info_spec(seqs, 1, length), rows_spec(ROW_STEP, units)]
        + [weight_spec(first[1]), weight_spec(second[1])]
        + [rows_spec(ROW_STEP, width) for _ in extra],
        [
            rows_spec(ROW_STEP, 2 * units),
            rows_spec(ROW_STEP, units),
            rows_spec(ROW_STEP, width),
            info_spec(seqs, 1, length),
        ],
        [
            shape((count, 2 * units)),
            shape((count, units)),
            shape((count, width), BF16 if last else F32),
            shape((count // length, 1, length), F32),
        ],
        0,
        0,
        (places, rows, info, d_units, first[0], second[0], *extra),
    )


def shards(
    hidden_in,
    segment_ids,
    att_route,
    mlp_route,
    norm_gain1,
    norm_gain2,
    att_router,
    mlp_router,
    kv_weight,
    query_weight,
    out_weight,
    att_bias,
    up_weight,
    down_weight,
    mlp_bias,
    cotangent,
):
    experts = lax.axis_size(EXPERT)
    inner = lax.axis_size("i")
    tokens, width = hidden_in.shape
    span = HEADS // OUTER * HD
    cosine, sine_table = rope_tables(tokens)

    places = own_places()

    down_parts = ring_gather(down_weight[0], "i")
    query_mat, kv_parts, seen = gather_heads(query_weight[0], kv_weight, down_parts[1:])
    out_parts = ring_gather(after(out_weight[0], seen), "i")
    own_up = up_weight[0].reshape(-1, width)

    residual = hidden_in.astype(F32)
    normed_one, inverse_one = norm_rows(residual, norm_gain1)
    attn_input = normed_one.astype(BF16)
    att_gate, att_onehot = pair_gates(attn_input, att_router, att_route, experts)
    info = to_experts(att_gate, att_onehot, segment_ids[0].astype(F32))
    all_attn = meet(attn_input)
    all_cot = meet(after(cotangent.astype(BF16), seen))
    qkv, gated, kv_mat = attend(
        places, all_attn, info, cosine, sine_table, query_mat, kv_parts
    )
    out_parts = out_parts[:1] + list(after(out_parts[1:], gated))
    out_mat = in_order(out_parts, "i").reshape(span, width)
    branch = part_low(*ring_rows(places, [gated], [out_mat], tokens))
    branch = part_second(*part_first(branch))

    d_units = [mm("td,fd->tf", all_cot, down).astype(BF16) for down in down_parts]
    branch = after(branch, d_units)
    middle = residual + branch.astype(F32) + att_bias
    normed_two, inverse_two = norm_rows(middle, norm_gain2)
    mlp_input = normed_two.astype(BF16)
    mlp_gate, mlp_onehot = pair_gates(mlp_input, mlp_router, mlp_route, experts)
    up_parts = ring_gather(after(own_up, gated), "i")
    all_mlp = meet(mlp_input)
    gate_m = to_experts(mlp_gate, mlp_onehot, None)
    d_both, gated_units, rows_back, d_gate_m = [], [], None, None
    for number, up in enumerate(up_parts):
        source = own_up if number == 0 else up
        found = run_units(
            places,
            all_mlp,
            gate_m,
            d_units[number],
            (source, 0),
            (source, 1),
            rows_back,
            number == inner - 1,
        )
        d_both.append(found[0])
        gated_units.append(found[1])
        rows_back = found[2]
        d_gate_m = found[3] if d_gate_m is None else d_gate_m + found[3]
    d_mlp_input = part(rows_back)
    d_mlp_gate = from_experts(d_gate_m[:, 0], mlp_onehot, experts)
    grad_up = [mm("tf,td->fd", d_here, all_mlp) for d_here in d_both]
    grad_down = [mm("tf,td->fd", here, all_cot) for here in gated_units]
    low_up = [one.astype(BF16) for one in grad_up[1:]]
    low_down = [one.astype(BF16) for one in grad_down[1:]]
    rows_out = part_low(*ring_rows(places, gated_units, down_parts, tokens))
    half = tokens // 2
    rows_first, rows_second = rows_out[:, :, :half], rows_out[:, :, half:]
    lower_own, lower_last = ring_open(grad_down[:1] + low_down, "i")
    upper_own, upper_last = ring_open(grad_up[:1] + low_up, "i")
    d_mlp_input = after(d_mlp_input, rows_out, low_up, lower_last)
    d_mlp_router, d_mlp_from_router = gates_back(
        mlp_gate, mlp_onehot, d_mlp_gate, mlp_input, mlp_router
    )
    d_norm_two, d_gain_two = norm_back(
        middle, inverse_two, norm_gain2, d_mlp_input.astype(F32) + d_mlp_from_router
    )
    d_middle = cotangent + d_norm_two
    sums = jnp.concatenate(
        [
            jnp.stack([d_gain_two, jnp.sum(d_middle, axis=0), jnp.sum(cotangent, axis=0)]),
            d_mlp_router,
        ]
    )

    all_mid = meet(d_middle.astype(BF16))
    rows_second = ring_low([rows_second[:, k] for k in range(OUTER)], "o")
    all_mid = after(all_mid, rows_second)
    d_heads, d_kv, rows_one, d_gate_a, d_gain_a = attend_back(
        places, all_mid, info, cosine, sine_table, qkv, all_attn, query_mat, kv_mat, out_mat
    )
    rows_first = after(rows_first, all_mid)
    rows_first = [rows_first[k] for k in range(rows_first.shape[0])]
    rows_first = ring_low(rows_first, "y")
    d_attn_input = part(rows_one)
    d_att_gate = from_experts(d_gate_a[:, 0], att_onehot, experts)
    d_kv_mat = mm("td,tf->df", all_attn, d_kv).reshape(experts // 2, 2, -1, 2 * span)
    d_kv_mat = from_order([d_kv_mat[:, 0], d_kv_mat[:, 1]], "c")
    d_kv_sent = d_kv_mat[1].astype(BF16)
    d_kv_last, kv_sent, kv_arrived = scatter_kv(d_kv_mat[0], d_kv_sent)
    d_heads, all_mid = after((d_heads, all_mid), kv_sent)
    d_att_router, d_att_from_router = gates_back(
        att_gate, att_onehot, d_att_gate, attn_input, att_router
    )
    d_gain_one = d_gain_a / norm_gain1 + jnp.sum(
        d_att_from_router * residual * inverse_one, axis=0, keepdims=True
    )
    summed = sum_over(jnp.concatenate([d_gain_one, sums, d_att_router]), ("i",))
    d_query_last = scatter_query(mm("td,tf->df", all_attn, d_heads), summed)
    d_query, d_kv_weight = scatter_heads(d_query_last, d_kv_last, d_attn_input)
    d_query = d_query[None]
    d_out = mm("tf,td->fd", gated, all_mid).reshape(inner, -1, width)
    d_out = from_order([d_out[k] for k in range(inner)], "i")
    d_out = d_out[:1] + list(after(d_out[1:], kv_arrived))
    d_output = ring_scatter(d_out, "i", d_query)[None]
    rows_out = part_second(*after((rows_first, rows_second), kv_arrived))
    layer_out = middle + rows_out.astype(F32) + mlp_bias
    d_upper = (after(upper_last, kv_sent).astype(F32) + upper_own).reshape(up_weight.shape)
    d_lower = (lower_last.astype(F32) + lower_own)[None]
    summed = sum_over(after(summed, d_kv_last), ("c", "o", "y"))
    d_attn_input = after(d_attn_input, summed)
    d_norm_one, _ = norm_back(
        residual, inverse_one, norm_gain1, d_attn_input.astype(F32) + d_att_from_router
    )
    d_input = d_middle + d_norm_one
    return (
        layer_out,
        d_input,
        summed[0],
        summed[1],
        summed[4 + experts :].T,
        summed[4 : 4 + experts].T,
        d_kv_weight,
        d_query,
        d_output,
        summed[2],
        d_upper,
        d_lower,
        summed[3],
    )


def solution(mesh):
    experts, fsdp = mesh.shape["expert"], mesh.shape["fsdp"]
    fine = Mesh(mesh.devices.reshape(experts // 2, 2, OUTER, fsdp // OUTER), ALL)
    shard = ("o", "i")
    rows = P(ALL, None)
    placed = (
        rows,
        rows,
        rows,
        rows,
        P(),
        P(),
        P(),
        P(),
        rows,
        P(EXPERT, shard, None),
        P(EXPERT, shard, None),
        P(),
        P(EXPERT, None, shard, None),
        P(EXPERT, shard, None),
        P(),
        rows,
    )
    return jax.shard_map(
        shards,
        mesh=fine,
        in_specs=placed,
        out_specs=(
            rows,
            rows,
            P(),
            P(),
            P(),
            P(),
            rows,
            P(EXPERT, shard, None),
            P(EXPERT, shard, None),
            P(),
            P(EXPERT, None, shard, None),
            P(EXPERT, shard, None),
            P(),
        ),
        check_vma=False,
    )
```

```python
import functools
import math

import jax
import jax.numpy as jnp
from jax import lax
from jax.experimental import pallas as pl
from jax.experimental.pallas import tpu as pltpu
from jax.sharding import Mesh, PartitionSpec as P

HEADS = 16
HD = 128
TOP = 2


EPSILON = 1e-06
HIGHEST = lax.Precision.HIGHEST
MASKED = -1e30

GROUP = ("y", "c", "o")
EXPERT = ("y", "c")
ALL = ("y", "c", "o", "i")
OUTER = 4
F32 = jnp.float32
BF16 = jnp.bfloat16


def rope_tables(length):
    half_dim = HD // 2
    frequency = jnp.exp(jnp.arange(half_dim, dtype=F32) * (-2.0 * math.log(10000.0) / HD))
    angles = jnp.arange(length, dtype=F32)[:, None] * frequency[None, :]
    cosine, sine = jnp.cos(angles), jnp.sin(angles)
    return (
        jnp.concatenate([cosine, cosine], axis=1),
        jnp.concatenate([-sine, sine], axis=1),
    )


def norm_rows(stream, gain):
    inverse = lax.rsqrt(jnp.mean(stream * stream, axis=-1, keepdims=True) + EPSILON)
    return (stream * inverse * gain, inverse)


def norm_back(stream, inverse, gain, upstream):
    scaled = upstream * gain
    d_stream = inverse * scaled - stream * inverse**3 * jnp.mean(
        scaled * stream, axis=-1, keepdims=True
    )
    d_gain = jnp.sum(upstream * stream * inverse, axis=0)
    return (d_stream, d_gain)


def shift(value, axis):
    size = lax.axis_size(axis)
    return lax.ppermute(value, axis, [((k + 1) % size, k) for k in range(size)])


def after(value, *others):
    token, _ = lax.optimization_barrier((lax.create_token(), others))
    return lax.optimization_barrier((token, value))[1]


def ring_gather(value, axis):
    parts = [value]
    for _ in range(lax.axis_size(axis) - 1):
        parts.append(shift(parts[-1], axis))
    return parts


def ring_open(blocks, axis):
    size = lax.axis_size(axis)
    travelling = blocks[1].astype(BF16)
    for j in range(2, size):
        travelling = (shift(travelling, axis).astype(F32) + blocks[j].astype(F32)).astype(BF16)
    return blocks[0], shift(travelling, axis)


def ring_scatter(blocks, axis, *others):
    own, arrived = ring_open(blocks, axis)
    if others:
        arrived = after(arrived, *others)
    return arrived.astype(F32) + own


def in_order(parts, axis, place=0):
    if len(parts) == 2:
        first = lax.axis_index(axis) == 0
        return jnp.stack([jnp.where(first, *parts), jnp.where(first, *parts[::-1])], axis=place)
    return jnp.roll(jnp.stack(parts, axis=place), lax.axis_index(axis), axis=place)


def from_order(parts, axis):
    if len(parts) == 2:
        first = lax.axis_index(axis) == 0
        return [jnp.where(first, *parts), jnp.where(first, *parts[::-1])]
    return list(jnp.roll(jnp.stack(parts), -lax.axis_index(axis), axis=0))


def sum_over(value, axes):
    for axis in axes:
        size = lax.axis_size(axis)
        step = 1
        while step < size:
            value = value + lax.ppermute(value, axis, [(k, k ^ step) for k in range(size)])
            step *= 2
    return value


def pair_gates(normed, router, route, experts):
    logits = jnp.dot(normed.astype(F32), router, precision=HIGHEST)
    onehot = (route[:, :, None] == jnp.arange(experts, dtype=jnp.int32)[None, None, :]).astype(F32)
    picked = jnp.sum(logits[:, None, :] * onehot, axis=-1)
    return (jax.nn.softmax(picked, axis=-1), onehot)


def gates_back(gates, onehot, d_gates, normed, router):
    d_picked = gates * (d_gates - jnp.sum(gates * d_gates, axis=-1, keepdims=True))
    d_logits = jnp.sum(d_picked[:, :, None] * onehot, axis=1)
    d_router = jnp.dot(d_logits.T, normed.astype(F32), precision=HIGHEST)
    d_normed = jnp.dot(d_logits, router.T, precision=HIGHEST)
    return (d_router, d_normed)


def to_experts(gates, onehot, extra):
    by_expert = jnp.sum(gates[:, :, None] * onehot, axis=1).T
    rows = jnp.repeat(by_expert, OUTER, axis=0)[:, None, :]
    if extra is not None:
        rows = jnp.concatenate(
            [rows, jnp.broadcast_to(extra[None, None, :], rows.shape)], axis=1
        )
    return lax.all_to_all(rows, GROUP, split_axis=0, concat_axis=0, tiled=True)


def from_experts(d_gates, onehot, experts):
    rows = lax.all_to_all(d_gates, GROUP, split_axis=0, concat_axis=0, tiled=True)
    by_expert = jnp.sum(rows.reshape(experts, OUTER, -1), axis=1)
    return jnp.einsum("tce,et->tc", onehot, by_expert, precision=HIGHEST)


def meet(rows):
    return lax.all_gather(rows, GROUP, axis=0, tiled=True)


def part(rows):
    return lax.psum_scatter(rows, GROUP, scatter_dimension=0, tiled=True)


def mm(form, first, second):
    return jnp.einsum(form, first, second, preferred_element_type=F32)


def head_blocks(matrix):
    span = HEADS // OUTER * HD
    return jnp.stack([matrix[:, k * span : (k + 1) * span] for k in range(OUTER)])


def join_blocks(blocks):
    return jnp.concatenate([blocks[k] for k in range(OUTER)], axis=1)


def exchange(blocks):
    return lax.all_to_all(blocks, "o", split_axis=0, concat_axis=0, tiled=True)


def gather_heads(query_weight, kv_weight, beside):
    whole = HEADS * HD
    rows = query_weight.shape[0]
    here = exchange(
        jnp.concatenate(
            [
                head_blocks(query_weight),
                head_blocks(kv_weight[:, :whole]),
                head_blocks(kv_weight[:, whole:]),
            ],
            axis=1,
        )
    )
    here = after(here, *beside)
    span = here.shape[2]
    kv = ring_gather(here[:, rows:].reshape(OUTER, 2, -1, span), "i")
    query = ring_gather(after(here[:, :rows], kv[-1]), "i")
    kv = ring_gather(jnp.stack(kv), "y")
    kv = after(kv, query)
    query = in_order(query, "i", 1).reshape(-1, span)
    seen = kv[-1][0, 0, 0, 0]
    return query, ring_gather(jnp.stack(kv), "c"), seen


def scatter_query(grad, *others):
    inner = lax.axis_size("i")
    blocks = grad.reshape(OUTER, inner, -1, grad.shape[1])
    blocks = from_order([blocks[:, k] for k in range(inner)], "i")
    return ring_scatter(blocks[:1] + list(after(blocks[1:], *others)), "i").astype(BF16)


def scatter_kv(kept, sent):
    mine = lax.ppermute(sent, "c", [(0, 1), (1, 0)]).astype(F32) + kept
    high, inner = lax.axis_size("y"), lax.axis_size("i")
    mine = mine.reshape(high, OUTER, inner, -1, kept.shape[-1])
    blocks = from_order([mine[k] for k in range(high)], "y")
    sent = blocks[1].astype(BF16)
    own, arrived = ring_open([blocks[0], sent] + blocks[2:], "y")
    mine = arrived.astype(F32) + own
    mine = ring_scatter(from_order([mine[:, k] for k in range(inner)], "i"), "i").astype(BF16)
    return mine, sent, arrived


def scatter_heads(query, kv, *others):
    half = kv.shape[2] // 2
    rows, kv_rows = query.shape[1], kv.shape[1]
    sent = jnp.concatenate([query, kv[:, :, :half], kv[:, :, half:]], axis=1)
    sent = after(sent, *others)
    here = exchange(sent).astype(F32)
    whole = [
        join_blocks(here[:, rows + k * kv_rows : rows + (k + 1) * kv_rows]) for k in range(2)
    ]
    return join_blocks(here[:, :rows]), jnp.concatenate(whole, axis=1), sent


def own_places():
    return jnp.stack([lax.axis_index(axis) for axis in ALL]).astype(jnp.int32)


def add_low(first, second):
    return (first.astype(F32) + second.astype(F32)).astype(BF16)


def ring_low(blocks, axis):
    travelling = blocks[1]
    for j in range(2, lax.axis_size(axis)):
        travelling = add_low(shift(travelling, axis), blocks[j])
    return add_low(shift(travelling, axis), blocks[0])


def part_low(own, other):
    return ring_low([own, other], "c")


def part_first(rows):
    half = rows.shape[2] // 2
    first, second = rows[:, :, :half], rows[:, :, half:]
    first = ring_low([first[k] for k in range(first.shape[0])], "y")
    second = ring_low([second[:, k] for k in range(second.shape[1])], "o")
    return first, second


def part_second(first, second):
    first = ring_low([first[k] for k in range(first.shape[0])], "o")
    second = ring_low([second[k] for k in range(second.shape[0])], "y")
    return jnp.concatenate([first, second])


VMEM = 56 * 1024 * 1024
ROW_STEP = 256


def nn(first, second):
    return jnp.dot(first, second, preferred_element_type=F32)


def nt(first, second):
    return lax.dot_general(first, second, (((1,), (1,)), ((), ())), preferred_element_type=F32)


def tn(first, second):
    return lax.dot_general(first, second, (((0,), (0,)), ((), ())), preferred_element_type=F32)


def as_column(row, rows):
    return jnp.broadcast_to(row, (rows, rows)).T[:, :1]


def turn(head, cosine, sine):
    return head * cosine + pltpu.roll(head, HD // 2, 1) * sine


def turn_back(head, cosine, sine):
    return head * cosine - pltpu.roll(head, HD // 2, 1) * sine


def allowed_keys(segment, length):
    keys = jnp.broadcast_to(segment, (length, length))
    row = lax.broadcasted_iota(jnp.int32, (length, length), 0)
    column = lax.broadcasted_iota(jnp.int32, (length, length), 1)
    return (keys == keys.T) & (column <= row)


def heads_nt(first, second):
    return lax.dot_general(first, second, (((2,), (2,)), ((0,), (0,))), preferred_element_type=F32)


def heads_nn(first, second):
    return lax.dot_general(first, second, (((2,), (1,)), ((0,), (0,))), preferred_element_type=F32)


def heads_tn(first, second):
    return lax.dot_general(first, second, (((1,), (1,)), ((0,), (0,))), preferred_element_type=F32)


def softmax_rows(queries, keys, allowed):
    scores = jnp.where(allowed[None], heads_nt(queries, keys) * (1.0 / math.sqrt(HD)), MASKED)
    exponent = jnp.exp(scores - jnp.max(scores, axis=-1, keepdims=True))
    return exponent / jnp.sum(exponent, axis=-1, keepdims=True)


def place_rows(places_ref, part_ref, value, length):
    count = part_ref.shape[1]
    for seq in range(count):
        slot = lax.rem(seq - places_ref[2] + count, count)
        part_ref[0, slot] = value[seq * length : (seq + 1) * length]


def arrange(places_ref, part_refs, out_ref):
    high, inner, outer, kinds, rows, span = part_refs[0].shape
    for low, part_ref in enumerate(part_refs):
        c = lax.rem(low + places_ref[1], 2)
        for first in range(high):
            y = lax.rem(first + places_ref[0], high)
            for second in range(inner):
                i = lax.rem(second + places_ref[3], inner)
                for o in range(outer):
                    start = (((y * 2 + c) * outer + o) * inner + i) * rows
                    for kind in range(kinds):
                        out_ref[
                            pl.ds(pl.multiple_of(start, 16), rows), kind * span : (kind + 1) * span
                        ] = part_ref[first, second, o, kind]


def attend_kernel(
    places_ref,
    x_ref,
    info_ref,
    cos_ref,
    sin_ref,
    query_ref,
    own_ref,
    other_ref,
    qkv_ref,
    gated_ref,
    kv_ref,
):
    @pl.when(pl.program_id(0) == 0)
    def _():
        arrange(places_ref, (own_ref, other_ref), kv_ref)

    length = cos_ref.shape[0]
    span = query_ref.shape[1]
    raw_query = nn(x_ref[...], query_ref[...])
    raw = nn(x_ref[...], kv_ref[...])
    cosine, sine = cos_ref[...], sin_ref[...]
    starts = range(0, span, HD)
    for seq in range(info_ref.shape[0]):
        rows = slice(seq * length, (seq + 1) * length)
        gate = as_column(info_ref[seq, 0:1, :], length)
        allowed = allowed_keys(info_ref[seq, 1:2, :], length)
        queries, keys, values = [], [], []
        for at in starts:
            head = raw_query[rows, at : at + HD].astype(BF16).astype(F32)
            queries.append(turn(head, cosine, sine).astype(BF16))
            keys.append(turn(raw[rows, at : at + HD], cosine, sine).astype(BF16))
            values.append(raw[rows, span + at : span + at + HD].astype(BF16))
            qkv_ref[rows, at : at + HD] = queries[-1]
            qkv_ref[rows, span + at : span + at + HD] = keys[-1]
            qkv_ref[rows, 2 * span + at : 2 * span + at + HD] = values[-1]
        probs = softmax_rows(jnp.stack(queries), jnp.stack(keys), allowed)
        gated = (heads_nn(probs.astype(BF16), jnp.stack(values)) * gate[None]).astype(BF16)
        for number, at in enumerate(starts):
            gated_ref[rows, at : at + HD] = gated[number]


def attend_back_kernel(
    places_ref,
    mid_ref,
    info_ref,
    cos_ref,
    sin_ref,
    qkv_ref,
    x_ref,
    query_ref,
    kv_ref,
    out_ref,
    d_query_ref,
    d_kv_ref,
    part_ref,
    d_gate_ref,
    d_gain_ref,
):
    del places_ref
    length = cos_ref.shape[0]
    span = out_ref.shape[0]
    scale = 1.0 / math.sqrt(HD)
    d_rows = nt(mid_ref[...], out_ref[...])
    cosine, sine = cos_ref[...], sin_ref[...]
    starts = range(0, span, HD)
    for seq in range(info_ref.shape[0]):
        rows = slice(seq * length, (seq + 1) * length)
        gate = as_column(info_ref[seq, 0:1, :], length)[None]
        allowed = allowed_keys(info_ref[seq, 1:2, :], length)
        queries = jnp.stack([qkv_ref[rows, at : at + HD] for at in starts])
        keys = jnp.stack([qkv_ref[rows, span + at : span + at + HD] for at in starts])
        values = jnp.stack([qkv_ref[rows, 2 * span + at : 2 * span + at + HD] for at in starts])
        d_heads = jnp.stack([d_rows[rows, at : at + HD] for at in starts])
        probs = softmax_rows(queries, keys, allowed)
        weighted = probs * heads_nt(d_heads.astype(BF16), values)
        sums = jnp.sum(weighted, axis=-1, keepdims=True)
        d_scores = ((weighted - probs * sums) * gate).astype(BF16)
        d_queries = heads_nn(d_scores, keys) * scale
        d_keys = heads_tn(d_scores, queries) * scale
        d_values = heads_tn(probs.astype(BF16), (d_heads * gate).astype(BF16))
        for number, at in enumerate(starts):
            cols = slice(at, at + HD)
            d_query_ref[rows, cols] = turn_back(d_queries[number], cosine, sine).astype(BF16)
            d_kv_ref[rows, cols] = turn_back(d_keys[number], cosine, sine).astype(BF16)
            d_kv_ref[rows, span + at : span + at + HD] = d_values[number].astype(BF16)
        total = jnp.broadcast_to(jnp.sum(sums, axis=0), (length, length))
        d_gate_ref[seq] = total.T[:1]
    d_input = nt(d_query_ref[...], query_ref[...]) + nt(d_kv_ref[...], kv_ref[...])

    @pl.when(pl.program_id(0) == 0)
    def _():
        d_gain_ref[...] = jnp.zeros_like(d_gain_ref)

    d_gain_ref[...] += jnp.sum(d_input * x_ref[...].astype(F32), axis=0, keepdims=True)
    part_ref[...] = d_input.astype(BF16)


def rows_kernel(parts, places_ref, *refs):
    gated_refs, down_refs, (own_ref, other_ref) = refs[:parts], refs[parts : 2 * parts], refs[2 * parts :]
    length = own_ref.shape[2]
    value = nn(gated_refs[0][...], down_refs[0][...])
    for part in range(1, parts):
        value = value + nn(gated_refs[part][...], down_refs[part][...])
    value = value.astype(BF16)
    other_first = pl.num_programs(0) // 2

    @pl.when(pl.program_id(0) < other_first)
    def _():
        place_rows(places_ref, other_ref, value, length)

    @pl.when(pl.program_id(0) >= other_first)
    def _():
        place_rows(places_ref, own_ref, value, length)


def fixed(shape):
    return pl.BlockSpec(shape, lambda step, places: (0,) * len(shape))


def rows_spec(rows, columns):
    return pl.BlockSpec((rows, columns), lambda step, places: (step, 0))


def info_spec(seqs, kinds, length):
    return pl.BlockSpec((seqs, kinds, length), lambda step, places: (step, 0, 0))


def shape(dims, dtype=BF16):
    return jax.ShapeDtypeStruct(dims, dtype)


def call(kernel, name, steps, in_specs, out_specs, out_shape, flops, moved, operands):
    return pl.pallas_call(
        kernel,
        grid_spec=pltpu.PrefetchScalarGridSpec(
            num_scalar_prefetch=1, grid=(steps,), in_specs=in_specs, out_specs=out_specs
        ),
        out_shape=out_shape,
        compiler_params=pltpu.CompilerParams(vmem_limit_bytes=VMEM),
        cost_estimate=pl.CostEstimate(flops=flops, bytes_accessed=moved, transcendentals=0),
        name=name,
    )(*operands)


def attend(places, rows, info, cosine, sine, query_mat, kv_parts):
    count, width = rows.shape
    span = query_mat.shape[1]
    length = cosine.shape[0]
    step = OUTER * length
    return call(
        attend_kernel,
        "attend",
        count // step,
        [
            rows_spec(step, width),
            info_spec(OUTER, 2, length),
            fixed(cosine.shape),
            fixed(sine.shape),
            fixed(query_mat.shape),
            *[fixed(one.shape) for one in kv_parts],
        ],
        [rows_spec(step, 3 * span), rows_spec(step, span), fixed((width, 2 * span))],
        [shape((count, 3 * span)), shape((count, span)), shape((width, 2 * span))],
        2 * count * width * 3 * span + 4 * count * length * span,
        4 * count * (width + 2 * span),
        (places, rows, info, cosine, sine, query_mat, *kv_parts),
    )


def attend_back(places, d_middle, info, cosine, sine, qkv, rows, query_mat, kv_mat, out_mat):
    count, width = d_middle.shape
    length = cosine.shape[0]
    step = OUTER * length
    span = out_mat.shape[0]
    return call(
        attend_back_kernel,
        "attend_back",
        count // step,
        [
            rows_spec(step, width),
            info_spec(OUTER, 2, length),
            fixed(cosine.shape),
            fixed(sine.shape),
            rows_spec(step, 3 * span),
            rows_spec(step, width),
            fixed(query_mat.shape),
            fixed(kv_mat.shape),
            fixed(out_mat.shape),
        ],
        [
            rows_spec(step, span),
            rows_spec(step, 2 * span),
            rows_spec(step, width),
            info_spec(OUTER, 1, length),
            fixed((1, width)),
        ],
        [
            shape((count, span)),
            shape((count, 2 * span)),
            shape((count, width)),
            shape((count // length, 1, length), F32),
            shape((1, width), F32),
        ],
        2 * count * width * 4 * span + 10 * count * length * span,
        4 * count * (2 * width + 3 * span),
        (places, d_middle, info, cosine, sine, qkv, rows, query_mat, kv_mat, out_mat),
    )


def ring_rows(places, gated, mats, length):
    count, units = gated[0].shape
    width = mats[0].shape[1]
    parts = len(mats)
    step = OUTER * length
    high = count // (2 * step)

    def pair(number, places):
        c = lax.rem(lax.div(number, high) + 1 + places[1], 2)
        return (lax.rem(lax.rem(number, high) + places[0], high) * 2 + c, 0)

    block = (1, OUTER, length, width)
    return call(
        functools.partial(rows_kernel, parts),
        "rows",
        count // step,
        [pl.BlockSpec((step, units), pair)] * parts + [fixed(one.shape) for one in mats],
        [
            pl.BlockSpec(block, lambda number, places: (lax.max(number - high, 0), 0, 0, 0)),
            pl.BlockSpec(block, lambda number, places: (lax.min(number, high - 1), 0, 0, 0)),
        ],
        [shape((high, OUTER, length, width))] * 2,
        2 * count * width * units * parts,
        4 * count * (width + units * parts),
        (places, *gated, *mats),
    )


def units_kernel(places_ref, x_ref, info_ref, d_units_ref, first_ref, second_ref, *refs):
    del places_ref
    sums_refs, (d_both_ref, gated_ref, back_ref, d_gate_ref) = refs[:-4], refs[-4:]
    length = info_ref.shape[2]
    seqs = info_ref.shape[0]
    units = first_ref.shape[0]
    rows = x_ref[...]
    gate = jnp.concatenate([as_column(info_ref[seq], length) for seq in range(seqs)], axis=0)
    gate_in = nt(rows, first_ref[...])
    up_in = nt(rows, second_ref[...])
    sigma = jax.nn.sigmoid(gate_in)
    active = gate_in * sigma
    hidden_units = active * up_in
    d_units = d_units_ref[...].astype(F32)
    d_gate = jnp.sum(hidden_units * d_units, axis=-1, keepdims=True)
    gated_ref[...] = (hidden_units * gate).astype(BF16)
    d_units = d_units * gate
    d_first = (d_units * up_in * (sigma + active * (1.0 - sigma))).astype(BF16)
    d_second = (d_units * active).astype(BF16)
    d_both_ref[:, :units] = d_first
    d_both_ref[:, units:] = d_second
    back = nn(d_first, first_ref[...]) + nn(d_second, second_ref[...])
    if sums_refs:
        back = back + sums_refs[0][...]
    back_ref[...] = back.astype(back_ref.dtype)
    for seq in range(seqs):
        column = jnp.broadcast_to(d_gate[seq * length : (seq + 1) * length], (length, length))
        d_gate_ref[seq] = column.T[:1]


def run_units(places, rows, info, d_units, first, second, sums, last):
    count, width = rows.shape
    length = info.shape[2]
    units = d_units.shape[1]
    seqs = ROW_STEP // length

    def weight_spec(block):
        return pl.BlockSpec((units, width), lambda step, places: (block, 0))

    extra = [] if sums is None else [sums]
    return call(
        units_kernel,
        "units",
        count // ROW_STEP,
        [rows_spec(ROW_STEP, width), info_spec(seqs, 1, length), rows_spec(ROW_STEP, units)]
        + [weight_spec(first[1]), weight_spec(second[1])]
        + [rows_spec(ROW_STEP, width) for _ in extra],
        [
            rows_spec(ROW_STEP, 2 * units),
            rows_spec(ROW_STEP, units),
            rows_spec(ROW_STEP, width),
            info_spec(seqs, 1, length),
        ],
        [
            shape((count, 2 * units)),
            shape((count, units)),
            shape((count, width), BF16 if last else F32),
            shape((count // length, 1, length), F32),
        ],
        0,
        0,
        (places, rows, info, d_units, first[0], second[0], *extra),
    )


def shards(
    hidden_in,
    segment_ids,
    att_route,
    mlp_route,
    norm_gain1,
    norm_gain2,
    att_router,
    mlp_router,
    kv_weight,
    query_weight,
    out_weight,
    att_bias,
    up_weight,
    down_weight,
    mlp_bias,
    cotangent,
):
    experts = lax.axis_size(EXPERT)
    inner = lax.axis_size("i")
    tokens, width = hidden_in.shape
    span = HEADS // OUTER * HD
    cosine, sine_table = rope_tables(tokens)

    places = own_places()

    down_parts = ring_gather(down_weight[0], "i")
    query_mat, kv_parts, seen = gather_heads(query_weight[0], kv_weight, down_parts[1:])
    out_parts = ring_gather(after(out_weight[0], seen), "i")
    own_up = up_weight[0].reshape(-1, width)

    residual = hidden_in.astype(F32)
    normed_one, inverse_one = norm_rows(residual, norm_gain1)
    attn_input = normed_one.astype(BF16)
    att_gate, att_onehot = pair_gates(attn_input, att_router, att_route, experts)
    info = to_experts(att_gate, att_onehot, segment_ids[0].astype(F32))
    all_attn = meet(attn_input)
    all_cot = meet(after(cotangent.astype(BF16), seen))
    qkv, gated, kv_mat = attend(
        places, all_attn, info, cosine, sine_table, query_mat, kv_parts
    )
    out_parts = out_parts[:1] + list(after(out_parts[1:], gated))
    out_mat = in_order(out_parts, "i").reshape(span, width)
    branch = part_low(*ring_rows(places, [gated], [out_mat], tokens))
    branch = part_second(*part_first(branch))

    d_units = [mm("td,fd->tf", all_cot, down).astype(BF16) for down in down_parts]
    branch = after(branch, d_units)
    middle = residual + branch.astype(F32) + att_bias
    normed_two, inverse_two = norm_rows(middle, norm_gain2)
    mlp_input = normed_two.astype(BF16)
    mlp_gate, mlp_onehot = pair_gates(mlp_input, mlp_router, mlp_route, experts)
    up_parts = ring_gather(after(own_up, gated), "i")
    all_mlp = meet(mlp_input)
    gate_m = to_experts(mlp_gate, mlp_onehot, None)
    d_both, gated_units, rows_back, d_gate_m = [], [], None, None
    for number, up in enumerate(up_parts):
        source = own_up if number == 0 else up
        found = run_units(
            places,
            all_mlp,
            gate_m,
            d_units[number],
            (source, 0),
            (source, 1),
            rows_back,
            number == inner - 1,
        )
        d_both.append(found[0])
        gated_units.append(found[1])
        rows_back = found[2]
        d_gate_m = found[3] if d_gate_m is None else d_gate_m + found[3]
    d_mlp_input = part(rows_back)
    d_mlp_gate = from_experts(d_gate_m[:, 0], mlp_onehot, experts)
    grad_up = [mm("tf,td->fd", d_here, all_mlp) for d_here in d_both]
    grad_down = [mm("tf,td->fd", here, all_cot) for here in gated_units]
    low_up = [one.astype(BF16) for one in grad_up[1:]]
    low_down = [one.astype(BF16) for one in grad_down[1:]]
    rows_out = part_low(*ring_rows(places, after(gated_units, low_down), down_parts, tokens))
    half = tokens // 2
    rows_first, rows_second = rows_out[:, :, :half], rows_out[:, :, half:]
    lower_own, lower_last = ring_open(grad_down[:1] + low_down, "i")
    upper_own, upper_last = ring_open(grad_up[:1] + low_up, "i")
    d_mlp_input = after(d_mlp_input, rows_out, low_up, lower_last)
    d_mlp_router, d_mlp_from_router = gates_back(
        mlp_gate, mlp_onehot, d_mlp_gate, mlp_input, mlp_router
    )
    d_norm_two, d_gain_two = norm_back(
        middle, inverse_two, norm_gain2, d_mlp_input.astype(F32) + d_mlp_from_router
    )
    d_middle = cotangent + d_norm_two
    sums = jnp.concatenate(
        [
            jnp.stack([d_gain_two, jnp.sum(d_middle, axis=0), jnp.sum(cotangent, axis=0)]),
            d_mlp_router,
        ]
    )

    all_mid = meet(d_middle.astype(BF16))
    rows_second = ring_low([rows_second[:, k] for k in range(OUTER)], "o")
    all_mid = after(all_mid, rows_second)
    d_heads, d_kv, rows_one, d_gate_a, d_gain_a = attend_back(
        places, all_mid, info, cosine, sine_table, qkv, all_attn, query_mat, kv_mat, out_mat
    )
    rows_first = after(rows_first, all_mid)
    rows_first = [rows_first[k] for k in range(rows_first.shape[0])]
    rows_first = ring_low(rows_first, "y")
    d_attn_input = part(rows_one)
    d_att_gate = from_experts(d_gate_a[:, 0], att_onehot, experts)
    d_kv_mat = mm("td,tf->df", all_attn, d_kv).reshape(experts // 2, 2, -1, 2 * span)
    d_kv_mat = from_order([d_kv_mat[:, 0], d_kv_mat[:, 1]], "c")
    d_kv_sent = d_kv_mat[1].astype(BF16)
    d_kv_last, kv_sent, kv_arrived = scatter_kv(d_kv_mat[0], d_kv_sent)
    d_heads, all_mid = after((d_heads, all_mid), kv_sent)
    d_att_router, d_att_from_router = gates_back(
        att_gate, att_onehot, d_att_gate, attn_input, att_router
    )
    d_gain_one = d_gain_a / norm_gain1 + jnp.sum(
        d_att_from_router * residual * inverse_one, axis=0, keepdims=True
    )
    summed = sum_over(jnp.concatenate([d_gain_one, sums, d_att_router]), ("i",))
    d_query_last = scatter_query(mm("td,tf->df", all_attn, d_heads), summed)
    d_query, d_kv_weight, heads_sent = scatter_heads(d_query_last, d_kv_last, d_attn_input)
    d_query = d_query[None]
    d_out = mm("tf,td->fd", gated, all_mid).reshape(inner, -1, width)
    d_out = from_order([d_out[k] for k in range(inner)], "i")
    d_out = d_out[:1] + list(after(d_out[1:], kv_arrived))
    d_output = ring_scatter(d_out, "i", d_query)[None]
    rows_out = part_second(*after((rows_first, rows_second), kv_arrived))
    layer_out = middle + rows_out.astype(F32) + mlp_bias
    d_upper = (after(upper_last, kv_sent).astype(F32) + upper_own).reshape(up_weight.shape)
    d_lower = (lower_last.astype(F32) + lower_own)[None]
    d_attn_input = after(d_attn_input, summed)
    summed = sum_over(after(summed, heads_sent), ("c", "o", "y"))
    d_norm_one, _ = norm_back(
        residual, inverse_one, norm_gain1, d_attn_input.astype(F32) + d_att_from_router
    )
    d_input = d_middle + d_norm_one
    return (
        layer_out,
        d_input,
        summed[0],
        summed[1],
        summed[4 + experts :].T,
        summed[4 : 4 + experts].T,
        d_kv_weight,
        d_query,
        d_output,
        summed[2],
        d_upper,
        d_lower,
        summed[3],
    )


def solution(mesh):
    experts, fsdp = mesh.shape["expert"], mesh.shape["fsdp"]
    fine = Mesh(mesh.devices.reshape(experts // 2, 2, OUTER, fsdp // OUTER), ALL)
    shard = ("o", "i")
    rows = P(ALL, None)
    placed = (
        rows,
        rows,
        rows,
        rows,
        P(),
        P(),
        P(),
        P(),
        rows,
        P(EXPERT, shard, None),
        P(EXPERT, shard, None),
        P(),
        P(EXPERT, None, shard, None),
        P(EXPERT, shard, None),
        P(),
        rows,
    )
    return jax.shard_map(
        shards,
        mesh=fine,
        in_specs=placed,
        out_specs=(
            rows,
            rows,
            P(),
            P(),
            P(),
            P(),
            rows,
            P(EXPERT, shard, None),
            P(EXPERT, shard, None),
            P(),
            P(EXPERT, None, shard, None),
            P(EXPERT, shard, None),
            P(),
        ),
        check_vma=False,
    )
```

```python
import functools
import math

import jax
import jax.numpy as jnp
from jax import lax
from jax.experimental import pallas as pl
from jax.experimental.pallas import tpu as pltpu
from jax.sharding import Mesh, PartitionSpec as P

HEADS = 16
HD = 128
TOP = 2


EPSILON = 1e-06
HIGHEST = lax.Precision.HIGHEST
MASKED = -1e30

GROUP = ("y", "c", "o")
EXPERT = ("y", "c")
ALL = ("y", "c", "o", "i")
OUTER = 4
F32 = jnp.float32
BF16 = jnp.bfloat16


def rope_tables(length):
    half_dim = HD // 2
    frequency = jnp.exp(jnp.arange(half_dim, dtype=F32) * (-2.0 * math.log(10000.0) / HD))
    angles = jnp.arange(length, dtype=F32)[:, None] * frequency[None, :]
    cosine, sine = jnp.cos(angles), jnp.sin(angles)
    return (
        jnp.concatenate([cosine, cosine], axis=1),
        jnp.concatenate([-sine, sine], axis=1),
    )


def norm_rows(stream, gain):
    inverse = lax.rsqrt(jnp.mean(stream * stream, axis=-1, keepdims=True) + EPSILON)
    return (stream * inverse * gain, inverse)


def norm_back(stream, inverse, gain, upstream):
    scaled = upstream * gain
    d_stream = inverse * scaled - stream * inverse**3 * jnp.mean(
        scaled * stream, axis=-1, keepdims=True
    )
    d_gain = jnp.sum(upstream * stream * inverse, axis=0)
    return (d_stream, d_gain)


def shift(value, axis):
    size = lax.axis_size(axis)
    return lax.ppermute(value, axis, [((k + 1) % size, k) for k in range(size)])


def after(value, *others):
    token, _ = lax.optimization_barrier((lax.create_token(), others))
    return lax.optimization_barrier((token, value))[1]


def ring_gather(value, axis):
    parts = [value]
    for _ in range(lax.axis_size(axis) - 1):
        parts.append(shift(parts[-1], axis))
    return parts


def ring_open(blocks, axis):
    size = lax.axis_size(axis)
    travelling = blocks[1].astype(BF16)
    for j in range(2, size):
        travelling = (shift(travelling, axis).astype(F32) + blocks[j].astype(F32)).astype(BF16)
    return blocks[0], shift(travelling, axis)


def ring_scatter(blocks, axis, *others):
    own, arrived = ring_open(blocks, axis)
    if others:
        arrived = after(arrived, *others)
    return arrived.astype(F32) + own


def in_order(parts, axis, place=0):
    if len(parts) == 2:
        first = lax.axis_index(axis) == 0
        return jnp.stack([jnp.where(first, *parts), jnp.where(first, *parts[::-1])], axis=place)
    return jnp.roll(jnp.stack(parts, axis=place), lax.axis_index(axis), axis=place)


def from_order(parts, axis):
    if len(parts) == 2:
        first = lax.axis_index(axis) == 0
        return [jnp.where(first, *parts), jnp.where(first, *parts[::-1])]
    return list(jnp.roll(jnp.stack(parts), -lax.axis_index(axis), axis=0))


def sum_over(value, axes):
    for axis in axes:
        size = lax.axis_size(axis)
        step = 1
        while step < size:
            value = value + lax.ppermute(value, axis, [(k, k ^ step) for k in range(size)])
            step *= 2
    return value


def pair_gates(normed, router, route, experts):
    logits = jnp.dot(normed.astype(F32), router, precision=HIGHEST)
    onehot = (route[:, :, None] == jnp.arange(experts, dtype=jnp.int32)[None, None, :]).astype(F32)
    picked = jnp.sum(logits[:, None, :] * onehot, axis=-1)
    return (jax.nn.softmax(picked, axis=-1), onehot)


def gates_back(gates, onehot, d_gates, normed, router):
    d_picked = gates * (d_gates - jnp.sum(gates * d_gates, axis=-1, keepdims=True))
    d_logits = jnp.sum(d_picked[:, :, None] * onehot, axis=1)
    d_router = jnp.dot(d_logits.T, normed.astype(F32), precision=HIGHEST)
    d_normed = jnp.dot(d_logits, router.T, precision=HIGHEST)
    return (d_router, d_normed)


def to_experts(gates, onehot, extra):
    by_expert = jnp.sum(gates[:, :, None] * onehot, axis=1).T
    rows = jnp.repeat(by_expert, OUTER, axis=0)[:, None, :]
    if extra is not None:
        rows = jnp.concatenate(
            [rows, jnp.broadcast_to(extra[None, None, :], rows.shape)], axis=1
        )
    return lax.all_to_all(rows, GROUP, split_axis=0, concat_axis=0, tiled=True)


def from_experts(d_gates, onehot, experts):
    rows = lax.all_to_all(d_gates, GROUP, split_axis=0, concat_axis=0, tiled=True)
    by_expert = jnp.sum(rows.reshape(experts, OUTER, -1), axis=1)
    return jnp.einsum("tce,et->tc", onehot, by_expert, precision=HIGHEST)


def meet(rows):
    return lax.all_gather(rows, GROUP, axis=0, tiled=True)


def part(rows):
    return lax.psum_scatter(rows, GROUP, scatter_dimension=0, tiled=True)


def mm(form, first, second):
    return jnp.einsum(form, first, second, preferred_element_type=F32)


def head_blocks(matrix):
    span = HEADS // OUTER * HD
    return jnp.stack([matrix[:, k * span : (k + 1) * span] for k in range(OUTER)])


def join_blocks(blocks):
    return jnp.concatenate([blocks[k] for k in range(OUTER)], axis=1)


def exchange(blocks):
    return lax.all_to_all(blocks, "o", split_axis=0, concat_axis=0, tiled=True)


def gather_heads(query_weight, kv_weight, beside):
    whole = HEADS * HD
    kv = exchange(
        jnp.concatenate(
            [head_blocks(kv_weight[:, :whole]), head_blocks(kv_weight[:, whole:])], axis=1
        )
    )
    span = kv.shape[2]
    query = exchange(after(head_blocks(query_weight), kv))
    kv = ring_gather(kv.reshape(OUTER, 2, -1, span), "i")
    query = ring_gather(after(query, kv[-1]), "i")
    query = in_order(query, "i", 1).reshape(-1, span)
    kv = ring_gather(jnp.stack(kv), "y")
    kv = after(kv, *beside)
    seen = kv[-1][0, 0, 0, 0]
    return query, ring_gather(jnp.stack(kv), "c"), seen


def scatter_query(grad, *others):
    inner = lax.axis_size("i")
    blocks = grad.reshape(OUTER, inner, -1, grad.shape[1])
    blocks = from_order([blocks[:, k] for k in range(inner)], "i")
    return ring_scatter(blocks[:1] + list(after(blocks[1:], *others)), "i").astype(BF16)


def scatter_kv(kept, sent):
    mine = lax.ppermute(sent, "c", [(0, 1), (1, 0)]).astype(F32) + kept
    high, inner = lax.axis_size("y"), lax.axis_size("i")
    mine = mine.reshape(high, OUTER, inner, -1, kept.shape[-1])
    blocks = from_order([mine[k] for k in range(high)], "y")
    sent = blocks[1].astype(BF16)
    own, arrived = ring_open([blocks[0], sent] + blocks[2:], "y")
    mine = arrived.astype(F32) + own
    mine = ring_scatter(from_order([mine[:, k] for k in range(inner)], "i"), "i").astype(BF16)
    return mine, sent, arrived


def scatter_heads(query, kv, *others):
    half = kv.shape[2] // 2
    rows, kv_rows = query.shape[1], kv.shape[1]
    sent = jnp.concatenate([query, kv[:, :, :half], kv[:, :, half:]], axis=1)
    sent = after(sent, *others)
    here = exchange(sent)
    whole = [
        join_blocks(here[:, rows + k * kv_rows : rows + (k + 1) * kv_rows]) for k in range(2)
    ]
    return join_blocks(here[:, :rows]).astype(F32), jnp.concatenate(whole, axis=1).astype(F32), sent


def own_places():
    return jnp.stack([lax.axis_index(axis) for axis in ALL]).astype(jnp.int32)


def add_low(first, second):
    return (first.astype(F32) + second.astype(F32)).astype(BF16)


def ring_low(blocks, axis):
    travelling = blocks[1]
    for j in range(2, lax.axis_size(axis)):
        travelling = add_low(shift(travelling, axis), blocks[j])
    return add_low(shift(travelling, axis), blocks[0])


def part_low(own, other):
    return ring_low([own, other], "c")


def part_first(rows):
    half = rows.shape[2] // 2
    first, second = rows[:, :, :half], rows[:, :, half:]
    first = ring_low([first[k] for k in range(first.shape[0])], "y")
    second = ring_low([second[:, k] for k in range(second.shape[1])], "o")
    return first, second


def part_second(first, second):
    first = ring_low([first[k] for k in range(first.shape[0])], "o")
    second = ring_low([second[k] for k in range(second.shape[0])], "y")
    return jnp.concatenate([first, second])


VMEM = 56 * 1024 * 1024
ROW_STEP = 256


def nn(first, second):
    return jnp.dot(first, second, preferred_element_type=F32)


def nt(first, second):
    return lax.dot_general(first, second, (((1,), (1,)), ((), ())), preferred_element_type=F32)


def tn(first, second):
    return lax.dot_general(first, second, (((0,), (0,)), ((), ())), preferred_element_type=F32)


def as_column(row, rows):
    return jnp.broadcast_to(row, (rows, rows)).T[:, :1]


def turn(head, cosine, sine):
    return head * cosine + pltpu.roll(head, HD // 2, 1) * sine


def turn_back(head, cosine, sine):
    return head * cosine - pltpu.roll(head, HD // 2, 1) * sine


def allowed_keys(segment, length):
    keys = jnp.broadcast_to(segment, (length, length))
    row = lax.broadcasted_iota(jnp.int32, (length, length), 0)
    column = lax.broadcasted_iota(jnp.int32, (length, length), 1)
    return (keys == keys.T) & (column <= row)


def heads_nt(first, second):
    return lax.dot_general(first, second, (((2,), (2,)), ((0,), (0,))), preferred_element_type=F32)


def heads_nn(first, second):
    return lax.dot_general(first, second, (((2,), (1,)), ((0,), (0,))), preferred_element_type=F32)


def heads_tn(first, second):
    return lax.dot_general(first, second, (((1,), (1,)), ((0,), (0,))), preferred_element_type=F32)


def softmax_rows(queries, keys, allowed):
    scores = jnp.where(allowed[None], heads_nt(queries, keys) * (1.0 / math.sqrt(HD)), MASKED)
    exponent = jnp.exp(scores - jnp.max(scores, axis=-1, keepdims=True))
    return exponent / jnp.sum(exponent, axis=-1, keepdims=True)


def place_rows(places_ref, part_ref, value, length):
    count = part_ref.shape[1]
    for seq in range(count):
        slot = lax.rem(seq - places_ref[2] + count, count)
        part_ref[0, slot] = value[seq * length : (seq + 1) * length]


def arrange(places_ref, part_refs, out_ref):
    high, inner, outer, kinds, rows, span = part_refs[0].shape
    for low, part_ref in enumerate(part_refs):
        c = lax.rem(low + places_ref[1], 2)
        for first in range(high):
            y = lax.rem(first + places_ref[0], high)
            for second in range(inner):
                i = lax.rem(second + places_ref[3], inner)
                for o in range(outer):
                    start = (((y * 2 + c) * outer + o) * inner + i) * rows
                    for kind in range(kinds):
                        out_ref[
                            pl.ds(pl.multiple_of(start, 16), rows), kind * span : (kind + 1) * span
                        ] = part_ref[first, second, o, kind]


def attend_kernel(
    places_ref,
    x_ref,
    info_ref,
    cos_ref,
    sin_ref,
    query_ref,
    own_ref,
    other_ref,
    qkv_ref,
    gated_ref,
    kv_ref,
):
    @pl.when(pl.program_id(0) == 0)
    def _():
        arrange(places_ref, (own_ref, other_ref), kv_ref)

    length = cos_ref.shape[0]
    span = query_ref.shape[1]
    raw_query = nn(x_ref[...], query_ref[...])
    raw = nn(x_ref[...], kv_ref[...])
    cosine, sine = cos_ref[...], sin_ref[...]
    starts = range(0, span, HD)
    for seq in range(info_ref.shape[0]):
        rows = slice(seq * length, (seq + 1) * length)
        gate = as_column(info_ref[seq, 0:1, :], length)
        allowed = allowed_keys(info_ref[seq, 1:2, :], length)
        queries, keys, values = [], [], []
        for at in starts:
            head = raw_query[rows, at : at + HD].astype(BF16).astype(F32)
            queries.append(turn(head, cosine, sine).astype(BF16))
            keys.append(turn(raw[rows, at : at + HD], cosine, sine).astype(BF16))
            values.append(raw[rows, span + at : span + at + HD].astype(BF16))
            qkv_ref[rows, at : at + HD] = queries[-1]
            qkv_ref[rows, span + at : span + at + HD] = keys[-1]
            qkv_ref[rows, 2 * span + at : 2 * span + at + HD] = values[-1]
        probs = softmax_rows(jnp.stack(queries), jnp.stack(keys), allowed)
        gated = (heads_nn(probs.astype(BF16), jnp.stack(values)) * gate[None]).astype(BF16)
        for number, at in enumerate(starts):
            gated_ref[rows, at : at + HD] = gated[number]


def attend_back_kernel(
    places_ref,
    mid_ref,
    info_ref,
    cos_ref,
    sin_ref,
    qkv_ref,
    x_ref,
    query_ref,
    kv_ref,
    out_ref,
    d_query_ref,
    d_kv_ref,
    part_ref,
    d_gate_ref,
    d_gain_ref,
):
    del places_ref
    length = cos_ref.shape[0]
    span = out_ref.shape[0]
    scale = 1.0 / math.sqrt(HD)
    d_rows = nt(mid_ref[...], out_ref[...])
    cosine, sine = cos_ref[...], sin_ref[...]
    starts = range(0, span, HD)
    for seq in range(info_ref.shape[0]):
        rows = slice(seq * length, (seq + 1) * length)
        gate = as_column(info_ref[seq, 0:1, :], length)[None]
        allowed = allowed_keys(info_ref[seq, 1:2, :], length)
        queries = jnp.stack([qkv_ref[rows, at : at + HD] for at in starts])
        keys = jnp.stack([qkv_ref[rows, span + at : span + at + HD] for at in starts])
        values = jnp.stack([qkv_ref[rows, 2 * span + at : 2 * span + at + HD] for at in starts])
        d_heads = jnp.stack([d_rows[rows, at : at + HD] for at in starts])
        probs = softmax_rows(queries, keys, allowed)
        weighted = probs * heads_nt(d_heads.astype(BF16), values)
        sums = jnp.sum(weighted, axis=-1, keepdims=True)
        d_scores = ((weighted - probs * sums) * gate).astype(BF16)
        d_queries = heads_nn(d_scores, keys) * scale
        d_keys = heads_tn(d_scores, queries) * scale
        d_values = heads_tn(probs.astype(BF16), (d_heads * gate).astype(BF16))
        for number, at in enumerate(starts):
            cols = slice(at, at + HD)
            d_query_ref[rows, cols] = turn_back(d_queries[number], cosine, sine).astype(BF16)
            d_kv_ref[rows, cols] = turn_back(d_keys[number], cosine, sine).astype(BF16)
            d_kv_ref[rows, span + at : span + at + HD] = d_values[number].astype(BF16)
        total = jnp.broadcast_to(jnp.sum(sums, axis=0), (length, length))
        d_gate_ref[seq] = total.T[:1]
    d_input = nt(d_query_ref[...], query_ref[...]) + nt(d_kv_ref[...], kv_ref[...])

    @pl.when(pl.program_id(0) == 0)
    def _():
        d_gain_ref[...] = jnp.zeros_like(d_gain_ref)

    d_gain_ref[...] += jnp.sum(d_input * x_ref[...].astype(F32), axis=0, keepdims=True)
    part_ref[...] = d_input.astype(BF16)


def rows_kernel(parts, places_ref, *refs):
    gated_refs, down_refs, (own_ref, other_ref) = refs[:parts], refs[parts : 2 * parts], refs[2 * parts :]
    length = own_ref.shape[2]
    value = nn(gated_refs[0][...], down_refs[0][...])
    for part in range(1, parts):
        value = value + nn(gated_refs[part][...], down_refs[part][...])
    value = value.astype(BF16)
    other_first = pl.num_programs(0) // 2

    @pl.when(pl.program_id(0) < other_first)
    def _():
        place_rows(places_ref, other_ref, value, length)

    @pl.when(pl.program_id(0) >= other_first)
    def _():
        place_rows(places_ref, own_ref, value, length)


def fixed(shape):
    return pl.BlockSpec(shape, lambda step, places: (0,) * len(shape))


def rows_spec(rows, columns):
    return pl.BlockSpec((rows, columns), lambda step, places: (step, 0))


def info_spec(seqs, kinds, length):
    return pl.BlockSpec((seqs, kinds, length), lambda step, places: (step, 0, 0))


def shape(dims, dtype=BF16):
    return jax.ShapeDtypeStruct(dims, dtype)


def call(kernel, name, steps, in_specs, out_specs, out_shape, flops, moved, operands):
    return pl.pallas_call(
        kernel,
        grid_spec=pltpu.PrefetchScalarGridSpec(
            num_scalar_prefetch=1, grid=(steps,), in_specs=in_specs, out_specs=out_specs
        ),
        out_shape=out_shape,
        compiler_params=pltpu.CompilerParams(vmem_limit_bytes=VMEM),
        cost_estimate=pl.CostEstimate(flops=flops, bytes_accessed=moved, transcendentals=0),
        name=name,
    )(*operands)


def attend(places, rows, info, cosine, sine, query_mat, kv_parts):
    count, width = rows.shape
    span = query_mat.shape[1]
    length = cosine.shape[0]
    step = OUTER * length
    return call(
        attend_kernel,
        "attend",
        count // step,
        [
            rows_spec(step, width),
            info_spec(OUTER, 2, length),
            fixed(cosine.shape),
            fixed(sine.shape),
            fixed(query_mat.shape),
            *[fixed(one.shape) for one in kv_parts],
        ],
        [rows_spec(step, 3 * span), rows_spec(step, span), fixed((width, 2 * span))],
        [shape((count, 3 * span)), shape((count, span)), shape((width, 2 * span))],
        2 * count * width * 3 * span + 4 * count * length * span,
        4 * count * (width + 2 * span),
        (places, rows, info, cosine, sine, query_mat, *kv_parts),
    )


def attend_back(places, d_middle, info, cosine, sine, qkv, rows, query_mat, kv_mat, out_mat):
    count, width = d_middle.shape
    length = cosine.shape[0]
    step = OUTER * length
    span = out_mat.shape[0]
    return call(
        attend_back_kernel,
        "attend_back",
        count // step,
        [
            rows_spec(step, width),
            info_spec(OUTER, 2, length),
            fixed(cosine.shape),
            fixed(sine.shape),
            rows_spec(step, 3 * span),
            rows_spec(step, width),
            fixed(query_mat.shape),
            fixed(kv_mat.shape),
            fixed(out_mat.shape),
        ],
        [
            rows_spec(step, span),
            rows_spec(step, 2 * span),
            rows_spec(step, width),
            info_spec(OUTER, 1, length),
            fixed((1, width)),
        ],
        [
            shape((count, span)),
            shape((count, 2 * span)),
            shape((count, width)),
            shape((count // length, 1, length), F32),
            shape((1, width), F32),
        ],
        2 * count * width * 4 * span + 10 * count * length * span,
        4 * count * (2 * width + 3 * span),
        (places, d_middle, info, cosine, sine, qkv, rows, query_mat, kv_mat, out_mat),
    )


def ring_rows(places, gated, mats, length):
    count, units = gated[0].shape
    width = mats[0].shape[1]
    parts = len(mats)
    step = OUTER * length
    high = count // (2 * step)

    def pair(number, places):
        c = lax.rem(lax.div(number, high) + 1 + places[1], 2)
        return (lax.rem(lax.rem(number, high) + places[0], high) * 2 + c, 0)

    block = (1, OUTER, length, width)
    return call(
        functools.partial(rows_kernel, parts),
        "rows",
        count // step,
        [pl.BlockSpec((step, units), pair)] * parts + [fixed(one.shape) for one in mats],
        [
            pl.BlockSpec(block, lambda number, places: (lax.max(number - high, 0), 0, 0, 0)),
            pl.BlockSpec(block, lambda number, places: (lax.min(number, high - 1), 0, 0, 0)),
        ],
        [shape((high, OUTER, length, width))] * 2,
        2 * count * width * units * parts,
        4 * count * (width + units * parts),
        (places, *gated, *mats),
    )


def units_kernel(places_ref, x_ref, info_ref, d_units_ref, first_ref, second_ref, *refs):
    del places_ref
    sums_refs, (d_both_ref, gated_ref, back_ref, d_gate_ref) = refs[:-4], refs[-4:]
    length = info_ref.shape[2]
    seqs = info_ref.shape[0]
    units = first_ref.shape[0]
    rows = x_ref[...]
    gate = jnp.concatenate([as_column(info_ref[seq], length) for seq in range(seqs)], axis=0)
    gate_in = nt(rows, first_ref[...])
    up_in = nt(rows, second_ref[...])
    sigma = jax.nn.sigmoid(gate_in)
    active = gate_in * sigma
    hidden_units = active * up_in
    d_units = d_units_ref[...].astype(F32)
    d_gate = jnp.sum(hidden_units * d_units, axis=-1, keepdims=True)
    gated_ref[...] = (hidden_units * gate).astype(BF16)
    d_units = d_units * gate
    d_first = (d_units * up_in * (sigma + active * (1.0 - sigma))).astype(BF16)
    d_second = (d_units * active).astype(BF16)
    d_both_ref[:, :units] = d_first
    d_both_ref[:, units:] = d_second
    back = nn(d_first, first_ref[...]) + nn(d_second, second_ref[...])
    if sums_refs:
        back = back + sums_refs[0][...]
    back_ref[...] = back.astype(back_ref.dtype)
    for seq in range(seqs):
        column = jnp.broadcast_to(d_gate[seq * length : (seq + 1) * length], (length, length))
        d_gate_ref[seq] = column.T[:1]


def run_units(places, rows, info, d_units, first, second, sums, last):
    count, width = rows.shape
    length = info.shape[2]
    units = d_units.shape[1]
    seqs = ROW_STEP // length

    def weight_spec(block):
        return pl.BlockSpec((units, width), lambda step, places: (block, 0))

    extra = [] if sums is None else [sums]
    return call(
        units_kernel,
        "units",
        count // ROW_STEP,
        [rows_spec(ROW_STEP, width), info_spec(seqs, 1, length), rows_spec(ROW_STEP, units)]
        + [weight_spec(first[1]), weight_spec(second[1])]
        + [rows_spec(ROW_STEP, width) for _ in extra],
        [
            rows_spec(ROW_STEP, 2 * units),
            rows_spec(ROW_STEP, units),
            rows_spec(ROW_STEP, width),
            info_spec(seqs, 1, length),
        ],
        [
            shape((count, 2 * units)),
            shape((count, units)),
            shape((count, width), BF16 if last else F32),
            shape((count // length, 1, length), F32),
        ],
        0,
        0,
        (places, rows, info, d_units, first[0], second[0], *extra),
    )


def shards(
    hidden_in,
    segment_ids,
    att_route,
    mlp_route,
    norm_gain1,
    norm_gain2,
    att_router,
    mlp_router,
    kv_weight,
    query_weight,
    out_weight,
    att_bias,
    up_weight,
    down_weight,
    mlp_bias,
    cotangent,
):
    experts = lax.axis_size(EXPERT)
    inner = lax.axis_size("i")
    tokens, width = hidden_in.shape
    span = HEADS // OUTER * HD
    cosine, sine_table = rope_tables(tokens)

    places = own_places()

    down_parts = ring_gather(down_weight[0], "i")
    query_mat, kv_parts, seen = gather_heads(query_weight[0], kv_weight, down_parts[1:])
    out_parts = ring_gather(after(out_weight[0], seen), "i")
    own_up = up_weight[0].reshape(-1, width)

    residual = hidden_in.astype(F32)
    normed_one, inverse_one = norm_rows(residual, norm_gain1)
    attn_input = normed_one.astype(BF16)
    att_gate, att_onehot = pair_gates(attn_input, att_router, att_route, experts)
    info = to_experts(att_gate, att_onehot, segment_ids[0].astype(F32))
    all_attn = meet(attn_input)
    all_cot = meet(after(cotangent.astype(BF16), seen))
    qkv, gated, kv_mat = attend(
        places, all_attn, info, cosine, sine_table, query_mat, kv_parts
    )
    out_parts = out_parts[:1] + list(after(out_parts[1:], gated))
    out_mat = in_order(out_parts, "i").reshape(span, width)
    branch = part_low(*ring_rows(places, [gated], [out_mat], tokens))
    branch = part_second(*part_first(branch))

    d_units = [mm("td,fd->tf", all_cot, down).astype(BF16) for down in down_parts]
    branch = after(branch, d_units)
    middle = residual + branch.astype(F32) + att_bias
    normed_two, inverse_two = norm_rows(middle, norm_gain2)
    mlp_input = normed_two.astype(BF16)
    mlp_gate, mlp_onehot = pair_gates(mlp_input, mlp_router, mlp_route, experts)
    up_parts = ring_gather(after(own_up, gated), "i")
    all_mlp = meet(mlp_input)
    gate_m = to_experts(mlp_gate, mlp_onehot, None)
    d_both, gated_units, rows_back, d_gate_m = [], [], None, None
    for number, up in enumerate(up_parts):
        source = own_up if number == 0 else up
        found = run_units(
            places,
            all_mlp,
            gate_m,
            d_units[number],
            (source, 0),
            (source, 1),
            rows_back,
            number == inner - 1,
        )
        d_both.append(found[0])
        gated_units.append(found[1])
        rows_back = found[2]
        d_gate_m = found[3] if d_gate_m is None else d_gate_m + found[3]
    d_mlp_input = part(rows_back)
    d_mlp_gate = from_experts(d_gate_m[:, 0], mlp_onehot, experts)
    grad_up = [mm("tf,td->fd", d_here, all_mlp) for d_here in d_both]
    grad_down = [mm("tf,td->fd", here, all_cot) for here in gated_units]
    low_up = [one.astype(BF16) for one in grad_up[1:]]
    low_down = [one.astype(BF16) for one in grad_down[1:]]
    rows_out = part_low(*ring_rows(places, after(gated_units, low_down), down_parts, tokens))
    half = tokens // 2
    rows_first, rows_second = rows_out[:, :, :half], rows_out[:, :, half:]
    lower_own, lower_last = ring_open(grad_down[:1] + low_down, "i")
    upper_own, upper_last = ring_open(grad_up[:1] + low_up, "i")
    d_mlp_input = after(d_mlp_input, rows_out, low_up, lower_last)
    d_mlp_router, d_mlp_from_router = gates_back(
        mlp_gate, mlp_onehot, d_mlp_gate, mlp_input, mlp_router
    )
    d_norm_two, d_gain_two = norm_back(
        middle, inverse_two, norm_gain2, d_mlp_input.astype(F32) + d_mlp_from_router
    )
    d_middle = cotangent + d_norm_two
    sums = jnp.concatenate(
        [
            jnp.stack([d_gain_two, jnp.sum(d_middle, axis=0), jnp.sum(cotangent, axis=0)]),
            d_mlp_router,
        ]
    )

    all_mid = meet(d_middle.astype(BF16))
    rows_second = ring_low([rows_second[:, k] for k in range(OUTER)], "o")
    all_mid = after(all_mid, rows_second)
    d_heads, d_kv, rows_one, d_gate_a, d_gain_a = attend_back(
        places, all_mid, info, cosine, sine_table, qkv, all_attn, query_mat, kv_mat, out_mat
    )
    rows_first = after(rows_first, all_mid)
    rows_first = [rows_first[k] for k in range(rows_first.shape[0])]
    rows_first = ring_low(rows_first, "y")
    d_attn_input = part(rows_one)
    d_att_gate = from_experts(d_gate_a[:, 0], att_onehot, experts)
    d_kv_mat = mm("td,tf->df", all_attn, d_kv).reshape(experts // 2, 2, -1, 2 * span)
    d_kv_mat = from_order([d_kv_mat[:, 0], d_kv_mat[:, 1]], "c")
    d_kv_sent = d_kv_mat[1].astype(BF16)
    d_kv_last, kv_sent, kv_arrived = scatter_kv(d_kv_mat[0], d_kv_sent)
    d_heads, all_mid = after((d_heads, all_mid), kv_sent)
    d_att_router, d_att_from_router = gates_back(
        att_gate, att_onehot, d_att_gate, attn_input, att_router
    )
    d_gain_one = d_gain_a / norm_gain1 + jnp.sum(
        d_att_from_router * residual * inverse_one, axis=0, keepdims=True
    )
    summed = sum_over(jnp.concatenate([d_gain_one, sums, d_att_router]), ("i",))
    d_query_last = scatter_query(mm("td,tf->df", all_attn, d_heads), summed)
    d_query, d_kv_weight, heads_sent = scatter_heads(d_query_last, d_kv_last, d_attn_input)
    d_query = d_query[None]
    d_out = mm("tf,td->fd", gated, all_mid).reshape(inner, -1, width)
    d_out = from_order([d_out[k] for k in range(inner)], "i")
    d_out = d_out[:1] + list(after(d_out[1:], d_kv_last))
    d_output = ring_scatter(d_out, "i", heads_sent)[None]
    rows_out = part_second(*after((rows_first, rows_second), kv_arrived))
    layer_out = middle + rows_out.astype(F32) + mlp_bias
    d_upper = (after(upper_last, kv_sent).astype(F32) + upper_own).reshape(up_weight.shape)
    d_lower = (lower_last.astype(F32) + lower_own)[None]
    d_attn_input = after(d_attn_input, summed)
    summed = sum_over(after(summed, heads_sent), ("c", "y", "o"))
    d_norm_one, _ = norm_back(
        residual, inverse_one, norm_gain1, d_attn_input.astype(F32) + d_att_from_router
    )
    d_input = d_middle + d_norm_one
    return (
        layer_out,
        d_input,
        summed[0],
        summed[1],
        summed[4 + experts :].T,
        summed[4 : 4 + experts].T,
        d_kv_weight,
        d_query,
        d_output,
        summed[2],
        d_upper,
        d_lower,
        summed[3],
    )


def solution(mesh):
    experts, fsdp = mesh.shape["expert"], mesh.shape["fsdp"]
    fine = Mesh(mesh.devices.reshape(experts // 2, 2, OUTER, fsdp // OUTER), ALL)
    shard = ("o", "i")
    rows = P(ALL, None)
    placed = (
        rows,
        rows,
        rows,
        rows,
        P(),
        P(),
        P(),
        P(),
        rows,
        P(EXPERT, shard, None),
        P(EXPERT, shard, None),
        P(),
        P(EXPERT, None, shard, None),
        P(EXPERT, shard, None),
        P(),
        rows,
    )
    return jax.shard_map(
        shards,
        mesh=fine,
        in_specs=placed,
        out_specs=(
            rows,
            rows,
            P(),
            P(),
            P(),
            P(),
            rows,
            P(EXPERT, shard, None),
            P(EXPERT, shard, None),
            P(),
            P(EXPERT, None, shard, None),
            P(EXPERT, shard, None),
            P(),
        ),
        check_vma=False,
    )
```

```python
import functools
import math

import jax
import jax.numpy as jnp
from jax import lax
from jax.experimental import pallas as pl
from jax.experimental.pallas import tpu as pltpu
from jax.sharding import Mesh, PartitionSpec as P

HEADS = 16
HD = 128
TOP = 2


EPSILON = 1e-06
HIGHEST = lax.Precision.HIGHEST
MASKED = -1e30

GROUP = ("y", "c", "o")
EXPERT = ("y", "c")
ALL = ("y", "c", "o", "i")
OUTER = 4
F32 = jnp.float32
BF16 = jnp.bfloat16


def rope_tables(length):
    half_dim = HD // 2
    frequency = jnp.exp(jnp.arange(half_dim, dtype=F32) * (-2.0 * math.log(10000.0) / HD))
    angles = jnp.arange(length, dtype=F32)[:, None] * frequency[None, :]
    cosine, sine = jnp.cos(angles), jnp.sin(angles)
    return (
        jnp.concatenate([cosine, cosine], axis=1),
        jnp.concatenate([-sine, sine], axis=1),
    )


def norm_rows(stream, gain):
    inverse = lax.rsqrt(jnp.mean(stream * stream, axis=-1, keepdims=True) + EPSILON)
    return (stream * inverse * gain, inverse)


def norm_back(stream, inverse, gain, upstream):
    scaled = upstream * gain
    d_stream = inverse * scaled - stream * inverse**3 * jnp.mean(
        scaled * stream, axis=-1, keepdims=True
    )
    d_gain = jnp.sum(upstream * stream * inverse, axis=0)
    return (d_stream, d_gain)


def shift(value, axis):
    size = lax.axis_size(axis)
    return lax.ppermute(value, axis, [((k + 1) % size, k) for k in range(size)])


def after(value, *others):
    token, _ = lax.optimization_barrier((lax.create_token(), others))
    return lax.optimization_barrier((token, value))[1]


def ring_gather(value, axis):
    parts = [value]
    for _ in range(lax.axis_size(axis) - 1):
        parts.append(shift(parts[-1], axis))
    return parts


def ring_open(blocks, axis):
    size = lax.axis_size(axis)
    travelling = blocks[1].astype(BF16)
    for j in range(2, size):
        travelling = (shift(travelling, axis).astype(F32) + blocks[j].astype(F32)).astype(BF16)
    return blocks[0], shift(travelling, axis)


def ring_scatter(blocks, axis, *others):
    own, arrived = ring_open(blocks, axis)
    if others:
        arrived = after(arrived, *others)
    return arrived.astype(F32) + own


def in_order(parts, axis, place=0):
    if len(parts) == 2:
        first = lax.axis_index(axis) == 0
        return jnp.stack([jnp.where(first, *parts), jnp.where(first, *parts[::-1])], axis=place)
    return jnp.roll(jnp.stack(parts, axis=place), lax.axis_index(axis), axis=place)


def from_order(parts, axis):
    if len(parts) == 2:
        first = lax.axis_index(axis) == 0
        return [jnp.where(first, *parts), jnp.where(first, *parts[::-1])]
    return list(jnp.roll(jnp.stack(parts), -lax.axis_index(axis), axis=0))


def sum_over(value, axes):
    for axis in axes:
        size = lax.axis_size(axis)
        step = 1
        while step < size:
            value = value + lax.ppermute(value, axis, [(k, k ^ step) for k in range(size)])
            step *= 2
    return value


def pair_gates(normed, router, route, experts):
    logits = jnp.dot(normed.astype(F32), router, precision=HIGHEST)
    onehot = (route[:, :, None] == jnp.arange(experts, dtype=jnp.int32)[None, None, :]).astype(F32)
    picked = jnp.sum(logits[:, None, :] * onehot, axis=-1)
    return (jax.nn.softmax(picked, axis=-1), onehot)


def gates_back(gates, onehot, d_gates, normed, router):
    d_picked = gates * (d_gates - jnp.sum(gates * d_gates, axis=-1, keepdims=True))
    d_logits = jnp.sum(d_picked[:, :, None] * onehot, axis=1)
    d_router = jnp.dot(d_logits.T, normed.astype(F32), precision=HIGHEST)
    d_normed = jnp.dot(d_logits, router.T, precision=HIGHEST)
    return (d_router, d_normed)


def to_experts(gates, onehot, extra):
    by_expert = jnp.sum(gates[:, :, None] * onehot, axis=1).T
    rows = jnp.repeat(by_expert, OUTER, axis=0)[:, None, :]
    if extra is not None:
        rows = jnp.concatenate(
            [rows, jnp.broadcast_to(extra[None, None, :], rows.shape)], axis=1
        )
    return lax.all_to_all(rows, GROUP, split_axis=0, concat_axis=0, tiled=True)


def from_experts(d_gates, onehot, experts):
    rows = lax.all_to_all(d_gates, GROUP, split_axis=0, concat_axis=0, tiled=True)
    by_expert = jnp.sum(rows.reshape(experts, OUTER, -1), axis=1)
    return jnp.einsum("tce,et->tc", onehot, by_expert, precision=HIGHEST)


def meet(rows):
    return lax.all_gather(rows, GROUP, axis=0, tiled=True)


def part(rows):
    return lax.psum_scatter(rows, GROUP, scatter_dimension=0, tiled=True)


def mm(form, first, second):
    return jnp.einsum(form, first, second, preferred_element_type=F32)


def head_blocks(matrix):
    span = HEADS // OUTER * HD
    return jnp.stack([matrix[:, k * span : (k + 1) * span] for k in range(OUTER)])


def join_blocks(blocks):
    return jnp.concatenate([blocks[k] for k in range(OUTER)], axis=1)


def exchange(blocks):
    return lax.all_to_all(blocks, "o", split_axis=0, concat_axis=0, tiled=True)


def gather_heads(query_weight, kv_weight, beside):
    whole = HEADS * HD
    rows = query_weight.shape[0]
    here = exchange(
        jnp.concatenate(
            [
                head_blocks(query_weight),
                head_blocks(kv_weight[:, :whole]),
                head_blocks(kv_weight[:, whole:]),
            ],
            axis=1,
        )
    )
    here = after(here, *beside)
    span = here.shape[2]
    kv = ring_gather(here[:, rows:].reshape(OUTER, 2, -1, span), "i")
    query = ring_gather(after(here[:, :rows], kv[-1]), "i")
    kv = ring_gather(jnp.stack(kv), "y")
    kv = after(kv, query)
    query = in_order(query, "i", 1).reshape(-1, span)
    seen = kv[-1][0, 0, 0, 0]
    return query, ring_gather(jnp.stack(kv), "c"), seen


def scatter_query(grad, *others):
    inner = lax.axis_size("i")
    blocks = grad.reshape(OUTER, inner, -1, grad.shape[1])
    blocks = from_order([blocks[:, k] for k in range(inner)], "i")
    return ring_scatter(blocks[:1] + list(after(blocks[1:], *others)), "i").astype(BF16)


def scatter_kv(kept, sent):
    mine = lax.ppermute(sent, "c", [(0, 1), (1, 0)]).astype(F32) + kept
    high, inner = lax.axis_size("y"), lax.axis_size("i")
    mine = mine.reshape(high, OUTER, inner, -1, kept.shape[-1])
    blocks = from_order([mine[k] for k in range(high)], "y")
    sent = blocks[1].astype(BF16)
    own, arrived = ring_open([blocks[0], sent] + blocks[2:], "y")
    mine = arrived.astype(F32) + own
    mine = ring_scatter(from_order([mine[:, k] for k in range(inner)], "i"), "i").astype(BF16)
    return mine, sent, arrived


def scatter_heads(query, kv, *others):
    half = kv.shape[2] // 2
    rows, kv_rows = query.shape[1], kv.shape[1]
    sent = jnp.concatenate([query, kv[:, :, :half], kv[:, :, half:]], axis=1)
    sent = after(sent, *others)
    here = exchange(sent)
    whole = [
        join_blocks(here[:, rows + k * kv_rows : rows + (k + 1) * kv_rows]) for k in range(2)
    ]
    return join_blocks(here[:, :rows]).astype(F32), jnp.concatenate(whole, axis=1).astype(F32), sent


def own_places():
    return jnp.stack([lax.axis_index(axis) for axis in ALL]).astype(jnp.int32)


def add_low(first, second):
    return (first.astype(F32) + second.astype(F32)).astype(BF16)


def ring_low(blocks, axis):
    travelling = blocks[1]
    for j in range(2, lax.axis_size(axis)):
        travelling = add_low(shift(travelling, axis), blocks[j])
    return add_low(shift(travelling, axis), blocks[0])


def part_low(own, other):
    return ring_low([own, other], "c")


def part_first(rows):
    half = rows.shape[2] // 2
    first, second = rows[:, :, :half], rows[:, :, half:]
    first = ring_low([first[k] for k in range(first.shape[0])], "y")
    second = ring_low([second[:, k] for k in range(second.shape[1])], "o")
    return first, second


def part_second(first, second):
    first = ring_low([first[k] for k in range(first.shape[0])], "o")
    second = ring_low([second[k] for k in range(second.shape[0])], "y")
    return jnp.concatenate([first, second])


VMEM = 56 * 1024 * 1024
ROW_STEP = 256


def nn(first, second):
    return jnp.dot(first, second, preferred_element_type=F32)


def nt(first, second):
    return lax.dot_general(first, second, (((1,), (1,)), ((), ())), preferred_element_type=F32)


def tn(first, second):
    return lax.dot_general(first, second, (((0,), (0,)), ((), ())), preferred_element_type=F32)


def as_column(row, rows):
    return jnp.broadcast_to(row, (rows, rows)).T[:, :1]


def turn(head, cosine, sine):
    return head * cosine + pltpu.roll(head, HD // 2, 1) * sine


def turn_back(head, cosine, sine):
    return head * cosine - pltpu.roll(head, HD // 2, 1) * sine


def allowed_keys(segment, length):
    keys = jnp.broadcast_to(segment, (length, length))
    row = lax.broadcasted_iota(jnp.int32, (length, length), 0)
    column = lax.broadcasted_iota(jnp.int32, (length, length), 1)
    return (keys == keys.T) & (column <= row)


def heads_nt(first, second):
    return lax.dot_general(first, second, (((2,), (2,)), ((0,), (0,))), preferred_element_type=F32)


def heads_nn(first, second):
    return lax.dot_general(first, second, (((2,), (1,)), ((0,), (0,))), preferred_element_type=F32)


def heads_tn(first, second):
    return lax.dot_general(first, second, (((1,), (1,)), ((0,), (0,))), preferred_element_type=F32)


def softmax_rows(queries, keys, allowed):
    scores = jnp.where(allowed[None], heads_nt(queries, keys) * (1.0 / math.sqrt(HD)), MASKED)
    exponent = jnp.exp(scores - jnp.max(scores, axis=-1, keepdims=True))
    return exponent / jnp.sum(exponent, axis=-1, keepdims=True)


def place_rows(places_ref, part_ref, value, length):
    count = part_ref.shape[1]
    for seq in range(count):
        slot = lax.rem(seq - places_ref[2] + count, count)
        part_ref[0, slot] = value[seq * length : (seq + 1) * length]


def arrange(places_ref, part_refs, out_ref):
    high, inner, outer, kinds, rows, span = part_refs[0].shape
    for low, part_ref in enumerate(part_refs):
        c = lax.rem(low + places_ref[1], 2)
        for first in range(high):
            y = lax.rem(first + places_ref[0], high)
            for second in range(inner):
                i = lax.rem(second + places_ref[3], inner)
                for o in range(outer):
                    start = (((y * 2 + c) * outer + o) * inner + i) * rows
                    for kind in range(kinds):
                        out_ref[
                            pl.ds(pl.multiple_of(start, 16), rows), kind * span : (kind + 1) * span
                        ] = part_ref[first, second, o, kind]


def attend_kernel(
    places_ref,
    x_ref,
    info_ref,
    cos_ref,
    sin_ref,
    query_ref,
    own_ref,
    other_ref,
    qkv_ref,
    gated_ref,
    kv_ref,
):
    @pl.when(pl.program_id(0) == 0)
    def _():
        arrange(places_ref, (own_ref, other_ref), kv_ref)

    length = cos_ref.shape[0]
    span = query_ref.shape[1]
    raw_query = nn(x_ref[...], query_ref[...])
    raw = nn(x_ref[...], kv_ref[...])
    cosine, sine = cos_ref[...], sin_ref[...]
    starts = range(0, span, HD)
    for seq in range(info_ref.shape[0]):
        rows = slice(seq * length, (seq + 1) * length)
        gate = as_column(info_ref[seq, 0:1, :], length)
        allowed = allowed_keys(info_ref[seq, 1:2, :], length)
        queries, keys, values = [], [], []
        for at in starts:
            head = raw_query[rows, at : at + HD].astype(BF16).astype(F32)
            queries.append(turn(head, cosine, sine).astype(BF16))
            keys.append(turn(raw[rows, at : at + HD], cosine, sine).astype(BF16))
            values.append(raw[rows, span + at : span + at + HD].astype(BF16))
            qkv_ref[rows, at : at + HD] = queries[-1]
            qkv_ref[rows, span + at : span + at + HD] = keys[-1]
            qkv_ref[rows, 2 * span + at : 2 * span + at + HD] = values[-1]
        probs = softmax_rows(jnp.stack(queries), jnp.stack(keys), allowed)
        gated = (heads_nn(probs.astype(BF16), jnp.stack(values)) * gate[None]).astype(BF16)
        for number, at in enumerate(starts):
            gated_ref[rows, at : at + HD] = gated[number]


def attend_back_kernel(
    places_ref,
    mid_ref,
    info_ref,
    cos_ref,
    sin_ref,
    qkv_ref,
    x_ref,
    query_ref,
    kv_ref,
    out_ref,
    d_query_ref,
    d_kv_ref,
    part_ref,
    d_gate_ref,
    d_gain_ref,
):
    del places_ref
    length = cos_ref.shape[0]
    span = out_ref.shape[0]
    scale = 1.0 / math.sqrt(HD)
    d_rows = nt(mid_ref[...], out_ref[...])
    cosine, sine = cos_ref[...], sin_ref[...]
    starts = range(0, span, HD)
    for seq in range(info_ref.shape[0]):
        rows = slice(seq * length, (seq + 1) * length)
        gate = as_column(info_ref[seq, 0:1, :], length)[None]
        allowed = allowed_keys(info_ref[seq, 1:2, :], length)
        queries = jnp.stack([qkv_ref[rows, at : at + HD] for at in starts])
        keys = jnp.stack([qkv_ref[rows, span + at : span + at + HD] for at in starts])
        values = jnp.stack([qkv_ref[rows, 2 * span + at : 2 * span + at + HD] for at in starts])
        d_heads = jnp.stack([d_rows[rows, at : at + HD] for at in starts])
        probs = softmax_rows(queries, keys, allowed)
        weighted = probs * heads_nt(d_heads.astype(BF16), values)
        sums = jnp.sum(weighted, axis=-1, keepdims=True)
        d_scores = ((weighted - probs * sums) * gate).astype(BF16)
        d_queries = heads_nn(d_scores, keys) * scale
        d_keys = heads_tn(d_scores, queries) * scale
        d_values = heads_tn(probs.astype(BF16), (d_heads * gate).astype(BF16))
        for number, at in enumerate(starts):
            cols = slice(at, at + HD)
            d_query_ref[rows, cols] = turn_back(d_queries[number], cosine, sine).astype(BF16)
            d_kv_ref[rows, cols] = turn_back(d_keys[number], cosine, sine).astype(BF16)
            d_kv_ref[rows, span + at : span + at + HD] = d_values[number].astype(BF16)
        total = jnp.broadcast_to(jnp.sum(sums, axis=0), (length, length))
        d_gate_ref[seq] = total.T[:1]
    d_input = nt(d_query_ref[...], query_ref[...]) + nt(d_kv_ref[...], kv_ref[...])

    @pl.when(pl.program_id(0) == 0)
    def _():
        d_gain_ref[...] = jnp.zeros_like(d_gain_ref)

    d_gain_ref[...] += jnp.sum(d_input * x_ref[...].astype(F32), axis=0, keepdims=True)
    part_ref[...] = d_input.astype(BF16)


def rows_kernel(parts, places_ref, *refs):
    gated_refs, down_refs, (own_ref, other_ref) = refs[:parts], refs[parts : 2 * parts], refs[2 * parts :]
    length = own_ref.shape[2]
    value = nn(gated_refs[0][...], down_refs[0][...])
    for part in range(1, parts):
        value = value + nn(gated_refs[part][...], down_refs[part][...])
    value = value.astype(BF16)
    other_first = pl.num_programs(0) // 2

    @pl.when(pl.program_id(0) < other_first)
    def _():
        place_rows(places_ref, other_ref, value, length)

    @pl.when(pl.program_id(0) >= other_first)
    def _():
        place_rows(places_ref, own_ref, value, length)


def fixed(shape):
    return pl.BlockSpec(shape, lambda step, places: (0,) * len(shape))


def rows_spec(rows, columns):
    return pl.BlockSpec((rows, columns), lambda step, places: (step, 0))


def info_spec(seqs, kinds, length):
    return pl.BlockSpec((seqs, kinds, length), lambda step, places: (step, 0, 0))


def shape(dims, dtype=BF16):
    return jax.ShapeDtypeStruct(dims, dtype)


def call(kernel, name, steps, in_specs, out_specs, out_shape, flops, moved, operands):
    return pl.pallas_call(
        kernel,
        grid_spec=pltpu.PrefetchScalarGridSpec(
            num_scalar_prefetch=1, grid=(steps,), in_specs=in_specs, out_specs=out_specs
        ),
        out_shape=out_shape,
        compiler_params=pltpu.CompilerParams(vmem_limit_bytes=VMEM),
        cost_estimate=pl.CostEstimate(flops=flops, bytes_accessed=moved, transcendentals=0),
        name=name,
    )(*operands)


def attend(places, rows, info, cosine, sine, query_mat, kv_parts):
    count, width = rows.shape
    span = query_mat.shape[1]
    length = cosine.shape[0]
    step = OUTER * length
    return call(
        attend_kernel,
        "attend",
        count // step,
        [
            rows_spec(step, width),
            info_spec(OUTER, 2, length),
            fixed(cosine.shape),
            fixed(sine.shape),
            fixed(query_mat.shape),
            *[fixed(one.shape) for one in kv_parts],
        ],
        [rows_spec(step, 3 * span), rows_spec(step, span), fixed((width, 2 * span))],
        [shape((count, 3 * span)), shape((count, span)), shape((width, 2 * span))],
        2 * count * width * 3 * span + 4 * count * length * span,
        4 * count * (width + 2 * span),
        (places, rows, info, cosine, sine, query_mat, *kv_parts),
    )


def attend_back(places, d_middle, info, cosine, sine, qkv, rows, query_mat, kv_mat, out_mat):
    count, width = d_middle.shape
    length = cosine.shape[0]
    step = OUTER * length
    span = out_mat.shape[0]
    return call(
        attend_back_kernel,
        "attend_back",
        count // step,
        [
            rows_spec(step, width),
            info_spec(OUTER, 2, length),
            fixed(cosine.shape),
            fixed(sine.shape),
            rows_spec(step, 3 * span),
            rows_spec(step, width),
            fixed(query_mat.shape),
            fixed(kv_mat.shape),
            fixed(out_mat.shape),
        ],
        [
            rows_spec(step, span),
            rows_spec(step, 2 * span),
            rows_spec(step, width),
            info_spec(OUTER, 1, length),
            fixed((1, width)),
        ],
        [
            shape((count, span)),
            shape((count, 2 * span)),
            shape((count, width)),
            shape((count // length, 1, length), F32),
            shape((1, width), F32),
        ],
        2 * count * width * 4 * span + 10 * count * length * span,
        4 * count * (2 * width + 3 * span),
        (places, d_middle, info, cosine, sine, qkv, rows, query_mat, kv_mat, out_mat),
    )


def ring_rows(places, gated, mats, length):
    count, units = gated[0].shape
    width = mats[0].shape[1]
    parts = len(mats)
    step = OUTER * length
    high = count // (2 * step)

    def pair(number, places):
        c = lax.rem(lax.div(number, high) + 1 + places[1], 2)
        return (lax.rem(lax.rem(number, high) + places[0], high) * 2 + c, 0)

    block = (1, OUTER, length, width)
    return call(
        functools.partial(rows_kernel, parts),
        "rows",
        count // step,
        [pl.BlockSpec((step, units), pair)] * parts + [fixed(one.shape) for one in mats],
        [
            pl.BlockSpec(block, lambda number, places: (lax.max(number - high, 0), 0, 0, 0)),
            pl.BlockSpec(block, lambda number, places: (lax.min(number, high - 1), 0, 0, 0)),
        ],
        [shape((high, OUTER, length, width))] * 2,
        2 * count * width * units * parts,
        4 * count * (width + units * parts),
        (places, *gated, *mats),
    )


def units_kernel(places_ref, x_ref, info_ref, d_units_ref, first_ref, second_ref, *refs):
    del places_ref
    sums_refs, (d_both_ref, gated_ref, back_ref, d_gate_ref) = refs[:-4], refs[-4:]
    length = info_ref.shape[2]
    seqs = info_ref.shape[0]
    units = first_ref.shape[0]
    rows = x_ref[...]
    gate = jnp.concatenate([as_column(info_ref[seq], length) for seq in range(seqs)], axis=0)
    gate_in = nt(rows, first_ref[...])
    up_in = nt(rows, second_ref[...])
    sigma = jax.nn.sigmoid(gate_in)
    active = gate_in * sigma
    hidden_units = active * up_in
    d_units = d_units_ref[...].astype(F32)
    d_gate = jnp.sum(hidden_units * d_units, axis=-1, keepdims=True)
    gated_ref[...] = (hidden_units * gate).astype(BF16)
    d_units = d_units * gate
    d_first = (d_units * up_in * (sigma + active * (1.0 - sigma))).astype(BF16)
    d_second = (d_units * active).astype(BF16)
    d_both_ref[:, :units] = d_first
    d_both_ref[:, units:] = d_second
    back = nn(d_first, first_ref[...]) + nn(d_second, second_ref[...])
    if sums_refs:
        back = back + sums_refs[0][...]
    back_ref[...] = back.astype(back_ref.dtype)
    for seq in range(seqs):
        column = jnp.broadcast_to(d_gate[seq * length : (seq + 1) * length], (length, length))
        d_gate_ref[seq] = column.T[:1]


def run_units(places, rows, info, d_units, first, second, sums, last):
    count, width = rows.shape
    length = info.shape[2]
    units = d_units.shape[1]
    seqs = ROW_STEP // length

    def weight_spec(block):
        return pl.BlockSpec((units, width), lambda step, places: (block, 0))

    extra = [] if sums is None else [sums]
    return call(
        units_kernel,
        "units",
        count // ROW_STEP,
        [rows_spec(ROW_STEP, width), info_spec(seqs, 1, length), rows_spec(ROW_STEP, units)]
        + [weight_spec(first[1]), weight_spec(second[1])]
        + [rows_spec(ROW_STEP, width) for _ in extra],
        [
            rows_spec(ROW_STEP, 2 * units),
            rows_spec(ROW_STEP, units),
            rows_spec(ROW_STEP, width),
            info_spec(seqs, 1, length),
        ],
        [
            shape((count, 2 * units)),
            shape((count, units)),
            shape((count, width), BF16 if last else F32),
            shape((count // length, 1, length), F32),
        ],
        0,
        0,
        (places, rows, info, d_units, first[0], second[0], *extra),
    )


def shards(
    hidden_in,
    segment_ids,
    att_route,
    mlp_route,
    norm_gain1,
    norm_gain2,
    att_router,
    mlp_router,
    kv_weight,
    query_weight,
    out_weight,
    att_bias,
    up_weight,
    down_weight,
    mlp_bias,
    cotangent,
):
    experts = lax.axis_size(EXPERT)
    inner = lax.axis_size("i")
    tokens, width = hidden_in.shape
    span = HEADS // OUTER * HD
    cosine, sine_table = rope_tables(tokens)

    places = own_places()

    down_parts = ring_gather(down_weight[0], "i")
    query_mat, kv_parts, seen = gather_heads(query_weight[0], kv_weight, down_parts[1:])
    out_parts = ring_gather(after(out_weight[0], seen), "i")
    own_up = up_weight[0].reshape(-1, width)

    residual = hidden_in.astype(F32)
    normed_one, inverse_one = norm_rows(residual, norm_gain1)
    attn_input = normed_one.astype(BF16)
    att_gate, att_onehot = pair_gates(attn_input, att_router, att_route, experts)
    info = to_experts(att_gate, att_onehot, segment_ids[0].astype(F32))
    all_attn = meet(attn_input)
    all_cot = meet(after(cotangent.astype(BF16), seen))
    qkv, gated, kv_mat = attend(
        places, all_attn, info, cosine, sine_table, query_mat, kv_parts
    )
    out_parts = out_parts[:1] + list(after(out_parts[1:], gated))
    out_mat = in_order(out_parts, "i").reshape(span, width)
    branch = part_low(*ring_rows(places, [gated], [out_mat], tokens))
    branch = part_second(*part_first(branch))

    d_units = [mm("td,fd->tf", all_cot, down).astype(BF16) for down in down_parts]
    branch = after(branch, d_units)
    middle = residual + branch.astype(F32) + att_bias
    normed_two, inverse_two = norm_rows(middle, norm_gain2)
    mlp_input = normed_two.astype(BF16)
    mlp_gate, mlp_onehot = pair_gates(mlp_input, mlp_router, mlp_route, experts)
    up_parts = ring_gather(after(own_up, gated), "i")
    all_mlp = meet(mlp_input)
    gate_m = to_experts(mlp_gate, mlp_onehot, None)
    d_both, gated_units, rows_back, d_gate_m = [], [], None, None
    for number, up in enumerate(up_parts):
        source = own_up if number == 0 else up
        found = run_units(
            places,
            all_mlp,
            gate_m,
            d_units[number],
            (source, 0),
            (source, 1),
            rows_back,
            number == inner - 1,
        )
        d_both.append(found[0])
        gated_units.append(found[1])
        rows_back = found[2]
        d_gate_m = found[3] if d_gate_m is None else d_gate_m + found[3]
    d_mlp_input = part(rows_back)
    d_mlp_gate = from_experts(d_gate_m[:, 0], mlp_onehot, experts)
    grad_up = [mm("tf,td->fd", d_here, all_mlp) for d_here in d_both]
    grad_down = [mm("tf,td->fd", here, all_cot) for here in gated_units]
    low_up = [one.astype(BF16) for one in grad_up[1:]]
    low_down = [one.astype(BF16) for one in grad_down[1:]]
    rows_out = part_low(*ring_rows(places, after(gated_units, low_down), down_parts, tokens))
    half = tokens // 2
    rows_first, rows_second = rows_out[:, :, :half], rows_out[:, :, half:]
    lower_own, lower_last = ring_open(grad_down[:1] + low_down, "i")
    upper_own, upper_last = ring_open(grad_up[:1] + low_up, "i")
    d_mlp_input = after(d_mlp_input, rows_out, low_up, lower_last)
    d_mlp_router, d_mlp_from_router = gates_back(
        mlp_gate, mlp_onehot, d_mlp_gate, mlp_input, mlp_router
    )
    d_norm_two, d_gain_two = norm_back(
        middle, inverse_two, norm_gain2, d_mlp_input.astype(F32) + d_mlp_from_router
    )
    d_middle = cotangent + d_norm_two
    sums = jnp.concatenate(
        [
            jnp.stack([d_gain_two, jnp.sum(d_middle, axis=0), jnp.sum(cotangent, axis=0)]),
            d_mlp_router,
        ]
    )

    all_mid = meet(d_middle.astype(BF16))
    rows_second = ring_low([rows_second[:, k] for k in range(OUTER)], "o")
    all_mid = after(all_mid, rows_second)
    d_heads, d_kv, rows_one, d_gate_a, d_gain_a = attend_back(
        places, all_mid, info, cosine, sine_table, qkv, all_attn, query_mat, kv_mat, out_mat
    )
    rows_first = after(rows_first, all_mid)
    rows_first = [rows_first[k] for k in range(rows_first.shape[0])]
    rows_first = ring_low(rows_first, "y")
    d_attn_input = part(rows_one)
    d_att_gate = from_experts(d_gate_a[:, 0], att_onehot, experts)
    d_kv_mat = mm("td,tf->df", all_attn, d_kv).reshape(experts // 2, 2, -1, 2 * span)
    d_kv_mat = from_order([d_kv_mat[:, 0], d_kv_mat[:, 1]], "c")
    d_kv_sent = d_kv_mat[1].astype(BF16)
    d_kv_last, kv_sent, kv_arrived = scatter_kv(d_kv_mat[0], d_kv_sent)
    d_heads, all_mid = after((d_heads, all_mid), kv_sent)
    d_att_router, d_att_from_router = gates_back(
        att_gate, att_onehot, d_att_gate, attn_input, att_router
    )
    d_gain_one = d_gain_a / norm_gain1 + jnp.sum(
        d_att_from_router * residual * inverse_one, axis=0, keepdims=True
    )
    summed = sum_over(jnp.concatenate([d_gain_one, sums, d_att_router]), ("i",))
    d_query_last = scatter_query(mm("td,tf->df", all_attn, d_heads), summed)
    d_query, d_kv_weight, heads_sent = scatter_heads(d_query_last, d_kv_last, d_attn_input)
    d_query = d_query[None]
    d_out = mm("tf,td->fd", gated, all_mid).reshape(inner, -1, width)
    d_out = from_order([d_out[k] for k in range(inner)], "i")
    d_out = d_out[:1] + list(after(d_out[1:], d_kv_last))
    d_output = ring_scatter(d_out, "i", heads_sent)[None]
    rows_out = part_second(*after((rows_first, rows_second), kv_arrived))
    layer_out = middle + rows_out.astype(F32) + mlp_bias
    d_upper = (after(upper_last, kv_sent).astype(F32) + upper_own).reshape(up_weight.shape)
    d_lower = (lower_last.astype(F32) + lower_own)[None]
    d_attn_input = after(d_attn_input, summed)
    summed = sum_over(after(summed, heads_sent), ("c", "y", "o"))
    d_norm_one, _ = norm_back(
        residual, inverse_one, norm_gain1, d_attn_input.astype(F32) + d_att_from_router
    )
    d_input = d_middle + d_norm_one
    return (
        layer_out,
        d_input,
        summed[0],
        summed[1],
        summed[4 + experts :].T,
        summed[4 : 4 + experts].T,
        d_kv_weight,
        d_query,
        d_output,
        summed[2],
        d_upper,
        d_lower,
        summed[3],
    )


def solution(mesh):
    experts, fsdp = mesh.shape["expert"], mesh.shape["fsdp"]
    fine = Mesh(mesh.devices.reshape(experts // 2, 2, OUTER, fsdp // OUTER), ALL)
    shard = ("o", "i")
    rows = P(ALL, None)
    placed = (
        rows,
        rows,
        rows,
        rows,
        P(),
        P(),
        P(),
        P(),
        rows,
        P(EXPERT, shard, None),
        P(EXPERT, shard, None),
        P(),
        P(EXPERT, None, shard, None),
        P(EXPERT, shard, None),
        P(),
        rows,
    )
    return jax.shard_map(
        shards,
        mesh=fine,
        in_specs=placed,
        out_specs=(
            rows,
            rows,
            P(),
            P(),
            P(),
            P(),
            rows,
            P(EXPERT, shard, None),
            P(EXPERT, shard, None),
            P(),
            P(EXPERT, None, shard, None),
            P(EXPERT, shard, None),
            P(),
        ),
        check_vma=False,
    )
```

```python
import functools
import math

import jax
import jax.numpy as jnp
from jax import lax
from jax.experimental import pallas as pl
from jax.experimental.pallas import tpu as pltpu
from jax.sharding import Mesh, PartitionSpec as P

HEADS = 16
HD = 128
TOP = 2


EPSILON = 1e-06
HIGHEST = lax.Precision.HIGHEST
MASKED = -1e30

GROUP = ("y", "c", "o")
EXPERT = ("y", "c")
ALL = ("y", "c", "o", "i")
OUTER = 4
F32 = jnp.float32
BF16 = jnp.bfloat16


def rope_tables(length):
    half_dim = HD // 2
    frequency = jnp.exp(jnp.arange(half_dim, dtype=F32) * (-2.0 * math.log(10000.0) / HD))
    angles = jnp.arange(length, dtype=F32)[:, None] * frequency[None, :]
    cosine, sine = jnp.cos(angles), jnp.sin(angles)
    return (
        jnp.concatenate([cosine, cosine], axis=1),
        jnp.concatenate([-sine, sine], axis=1),
    )


def norm_rows(stream, gain):
    inverse = lax.rsqrt(jnp.mean(stream * stream, axis=-1, keepdims=True) + EPSILON)
    return (stream * inverse * gain, inverse)


def norm_back(stream, inverse, gain, upstream):
    scaled = upstream * gain
    d_stream = inverse * scaled - stream * inverse**3 * jnp.mean(
        scaled * stream, axis=-1, keepdims=True
    )
    d_gain = jnp.sum(upstream * stream * inverse, axis=0)
    return (d_stream, d_gain)


def shift(value, axis):
    size = lax.axis_size(axis)
    return lax.ppermute(value, axis, [((k + 1) % size, k) for k in range(size)])


def after(value, *others):
    token, _ = lax.optimization_barrier((lax.create_token(), others))
    return lax.optimization_barrier((token, value))[1]


def ring_gather(value, axis):
    parts = [value]
    for _ in range(lax.axis_size(axis) - 1):
        parts.append(shift(parts[-1], axis))
    return parts


def ring_open(blocks, axis):
    size = lax.axis_size(axis)
    travelling = blocks[1].astype(BF16)
    for j in range(2, size):
        travelling = (shift(travelling, axis).astype(F32) + blocks[j].astype(F32)).astype(BF16)
    return blocks[0], shift(travelling, axis)


def ring_scatter(blocks, axis, *others):
    own, arrived = ring_open(blocks, axis)
    if others:
        arrived = after(arrived, *others)
    return arrived.astype(F32) + own


def in_order(parts, axis, place=0):
    if len(parts) == 2:
        first = lax.axis_index(axis) == 0
        return jnp.stack([jnp.where(first, *parts), jnp.where(first, *parts[::-1])], axis=place)
    return jnp.roll(jnp.stack(parts, axis=place), lax.axis_index(axis), axis=place)


def from_order(parts, axis):
    if len(parts) == 2:
        first = lax.axis_index(axis) == 0
        return [jnp.where(first, *parts), jnp.where(first, *parts[::-1])]
    return list(jnp.roll(jnp.stack(parts), -lax.axis_index(axis), axis=0))


def sum_over(value, axes):
    for axis in axes:
        size = lax.axis_size(axis)
        step = 1
        while step < size:
            value = value + lax.ppermute(value, axis, [(k, k ^ step) for k in range(size)])
            step *= 2
    return value


def pair_gates(normed, router, route, experts):
    logits = jnp.dot(normed.astype(F32), router, precision=HIGHEST)
    onehot = (route[:, :, None] == jnp.arange(experts, dtype=jnp.int32)[None, None, :]).astype(F32)
    picked = jnp.sum(logits[:, None, :] * onehot, axis=-1)
    return (jax.nn.softmax(picked, axis=-1), onehot)


def gates_back(gates, onehot, d_gates, normed, router):
    d_picked = gates * (d_gates - jnp.sum(gates * d_gates, axis=-1, keepdims=True))
    d_logits = jnp.sum(d_picked[:, :, None] * onehot, axis=1)
    d_router = jnp.dot(d_logits.T, normed.astype(F32), precision=HIGHEST)
    d_normed = jnp.dot(d_logits, router.T, precision=HIGHEST)
    return (d_router, d_normed)


def to_experts(gates, onehot, extra):
    by_expert = jnp.sum(gates[:, :, None] * onehot, axis=1).T
    rows = jnp.repeat(by_expert, OUTER, axis=0)[:, None, :]
    if extra is not None:
        rows = jnp.concatenate(
            [rows, jnp.broadcast_to(extra[None, None, :], rows.shape)], axis=1
        )
    return lax.all_to_all(rows, GROUP, split_axis=0, concat_axis=0, tiled=True)


def from_experts(d_gates, onehot, experts):
    rows = lax.all_to_all(d_gates, GROUP, split_axis=0, concat_axis=0, tiled=True)
    by_expert = jnp.sum(rows.reshape(experts, OUTER, -1), axis=1)
    return jnp.einsum("tce,et->tc", onehot, by_expert, precision=HIGHEST)


def meet(rows):
    return lax.all_gather(rows, GROUP, axis=0, tiled=True)


def part(rows):
    return lax.psum_scatter(rows, GROUP, scatter_dimension=0, tiled=True)


def mm(form, first, second):
    return jnp.einsum(form, first, second, preferred_element_type=F32)


def head_blocks(matrix):
    span = HEADS // OUTER * HD
    return jnp.stack([matrix[:, k * span : (k + 1) * span] for k in range(OUTER)])


def join_blocks(blocks):
    return jnp.concatenate([blocks[k] for k in range(OUTER)], axis=1)


def exchange(blocks):
    return lax.all_to_all(blocks, "o", split_axis=0, concat_axis=0, tiled=True)


def gather_heads(query_weight, kv_weight, beside):
    whole = HEADS * HD
    rows = query_weight.shape[0]
    here = exchange(
        jnp.concatenate(
            [
                head_blocks(query_weight),
                head_blocks(kv_weight[:, :whole]),
                head_blocks(kv_weight[:, whole:]),
            ],
            axis=1,
        )
    )
    here = after(here, *beside)
    span = here.shape[2]
    kv = ring_gather(here[:, rows:].reshape(OUTER, 2, -1, span), "i")
    query = ring_gather(after(here[:, :rows], kv[-1]), "i")
    kv = ring_gather(jnp.stack(kv), "y")
    kv = after(kv, query)
    query = in_order(query, "i", 1).reshape(-1, span)
    seen = kv[-1][0, 0, 0, 0]
    return query, ring_gather(jnp.stack(kv), "c"), seen


def scatter_query(grad, *others):
    inner = lax.axis_size("i")
    blocks = grad.reshape(OUTER, inner, -1, grad.shape[1])
    blocks = from_order([blocks[:, k] for k in range(inner)], "i")
    return ring_scatter(blocks[:1] + list(after(blocks[1:], *others)), "i").astype(BF16)


def scatter_kv(kept, sent):
    mine = lax.ppermute(sent, "c", [(0, 1), (1, 0)]).astype(F32) + kept
    high, inner = lax.axis_size("y"), lax.axis_size("i")
    mine = mine.reshape(high, OUTER, inner, -1, kept.shape[-1])
    blocks = from_order([mine[k] for k in range(high)], "y")
    sent = blocks[1].astype(BF16)
    own, arrived = ring_open([blocks[0], sent] + blocks[2:], "y")
    mine = arrived.astype(F32) + own
    mine = ring_scatter(from_order([mine[:, k] for k in range(inner)], "i"), "i").astype(BF16)
    return mine, sent, arrived


def scatter_heads(query, kv, *others):
    half = kv.shape[2] // 2
    query = exchange(query)
    sent = after(kv, query, *others)
    here = exchange(sent)
    whole = [join_blocks(here[:, :, :half]), join_blocks(here[:, :, half:])]
    return join_blocks(query).astype(F32), jnp.concatenate(whole, axis=1).astype(F32), sent


def own_places():
    return jnp.stack([lax.axis_index(axis) for axis in ALL]).astype(jnp.int32)


def add_low(first, second):
    return (first.astype(F32) + second.astype(F32)).astype(BF16)


def ring_low(blocks, axis):
    travelling = blocks[1]
    for j in range(2, lax.axis_size(axis)):
        travelling = add_low(shift(travelling, axis), blocks[j])
    return add_low(shift(travelling, axis), blocks[0])


def part_low(own, other):
    return ring_low([own, other], "c")


def part_first(rows):
    half = rows.shape[2] // 2
    first, second = rows[:, :, :half], rows[:, :, half:]
    first = ring_low([first[k] for k in range(first.shape[0])], "y")
    second = ring_low([second[:, k] for k in range(second.shape[1])], "o")
    return first, second


def part_second(first, second):
    first = ring_low([first[k] for k in range(first.shape[0])], "o")
    second = ring_low([second[k] for k in range(second.shape[0])], "y")
    return jnp.concatenate([first, second])


VMEM = 56 * 1024 * 1024
ROW_STEP = 256


def nn(first, second):
    return jnp.dot(first, second, preferred_element_type=F32)


def nt(first, second):
    return lax.dot_general(first, second, (((1,), (1,)), ((), ())), preferred_element_type=F32)


def tn(first, second):
    return lax.dot_general(first, second, (((0,), (0,)), ((), ())), preferred_element_type=F32)


def as_column(row, rows):
    return jnp.broadcast_to(row, (rows, rows)).T[:, :1]


def turn(head, cosine, sine):
    return head * cosine + pltpu.roll(head, HD // 2, 1) * sine


def turn_back(head, cosine, sine):
    return head * cosine - pltpu.roll(head, HD // 2, 1) * sine


def allowed_keys(segment, length):
    keys = jnp.broadcast_to(segment, (length, length))
    row = lax.broadcasted_iota(jnp.int32, (length, length), 0)
    column = lax.broadcasted_iota(jnp.int32, (length, length), 1)
    return (keys == keys.T) & (column <= row)


def heads_nt(first, second):
    return lax.dot_general(first, second, (((2,), (2,)), ((0,), (0,))), preferred_element_type=F32)


def heads_nn(first, second):
    return lax.dot_general(first, second, (((2,), (1,)), ((0,), (0,))), preferred_element_type=F32)


def heads_tn(first, second):
    return lax.dot_general(first, second, (((1,), (1,)), ((0,), (0,))), preferred_element_type=F32)


def softmax_rows(queries, keys, allowed):
    scores = jnp.where(allowed[None], heads_nt(queries, keys) * (1.0 / math.sqrt(HD)), MASKED)
    exponent = jnp.exp(scores - jnp.max(scores, axis=-1, keepdims=True))
    return exponent / jnp.sum(exponent, axis=-1, keepdims=True)


def place_rows(places_ref, part_ref, value, length):
    count = part_ref.shape[1]
    for seq in range(count):
        slot = lax.rem(seq - places_ref[2] + count, count)
        part_ref[0, slot] = value[seq * length : (seq + 1) * length]


def arrange(places_ref, part_refs, out_ref):
    high, inner, outer, kinds, rows, span = part_refs[0].shape
    for low, part_ref in enumerate(part_refs):
        c = lax.rem(low + places_ref[1], 2)
        for first in range(high):
            y = lax.rem(first + places_ref[0], high)
            for second in range(inner):
                i = lax.rem(second + places_ref[3], inner)
                for o in range(outer):
                    start = (((y * 2 + c) * outer + o) * inner + i) * rows
                    for kind in range(kinds):
                        out_ref[
                            pl.ds(pl.multiple_of(start, 16), rows), kind * span : (kind + 1) * span
                        ] = part_ref[first, second, o, kind]


def attend_kernel(
    places_ref,
    x_ref,
    info_ref,
    cos_ref,
    sin_ref,
    query_ref,
    own_ref,
    other_ref,
    qkv_ref,
    gated_ref,
    kv_ref,
):
    @pl.when(pl.program_id(0) == 0)
    def _():
        arrange(places_ref, (own_ref, other_ref), kv_ref)

    length = cos_ref.shape[0]
    span = query_ref.shape[1]
    raw_query = nn(x_ref[...], query_ref[...])
    raw = nn(x_ref[...], kv_ref[...])
    cosine, sine = cos_ref[...], sin_ref[...]
    starts = range(0, span, HD)
    for seq in range(info_ref.shape[0]):
        rows = slice(seq * length, (seq + 1) * length)
        gate = as_column(info_ref[seq, 0:1, :], length)
        allowed = allowed_keys(info_ref[seq, 1:2, :], length)
        queries, keys, values = [], [], []
        for at in starts:
            head = raw_query[rows, at : at + HD].astype(BF16).astype(F32)
            queries.append(turn(head, cosine, sine).astype(BF16))
            keys.append(turn(raw[rows, at : at + HD], cosine, sine).astype(BF16))
            values.append(raw[rows, span + at : span + at + HD].astype(BF16))
            qkv_ref[rows, at : at + HD] = queries[-1]
            qkv_ref[rows, span + at : span + at + HD] = keys[-1]
            qkv_ref[rows, 2 * span + at : 2 * span + at + HD] = values[-1]
        probs = softmax_rows(jnp.stack(queries), jnp.stack(keys), allowed)
        gated = (heads_nn(probs.astype(BF16), jnp.stack(values)) * gate[None]).astype(BF16)
        for number, at in enumerate(starts):
            gated_ref[rows, at : at + HD] = gated[number]


def attend_back_kernel(
    places_ref,
    mid_ref,
    info_ref,
    cos_ref,
    sin_ref,
    qkv_ref,
    x_ref,
    query_ref,
    kv_ref,
    out_ref,
    d_query_ref,
    d_kv_ref,
    part_ref,
    d_gate_ref,
    d_gain_ref,
):
    del places_ref
    length = cos_ref.shape[0]
    span = out_ref.shape[0]
    scale = 1.0 / math.sqrt(HD)
    d_rows = nt(mid_ref[...], out_ref[...])
    cosine, sine = cos_ref[...], sin_ref[...]
    starts = range(0, span, HD)
    for seq in range(info_ref.shape[0]):
        rows = slice(seq * length, (seq + 1) * length)
        gate = as_column(info_ref[seq, 0:1, :], length)[None]
        allowed = allowed_keys(info_ref[seq, 1:2, :], length)
        queries = jnp.stack([qkv_ref[rows, at : at + HD] for at in starts])
        keys = jnp.stack([qkv_ref[rows, span + at : span + at + HD] for at in starts])
        values = jnp.stack([qkv_ref[rows, 2 * span + at : 2 * span + at + HD] for at in starts])
        d_heads = jnp.stack([d_rows[rows, at : at + HD] for at in starts])
        probs = softmax_rows(queries, keys, allowed)
        weighted = probs * heads_nt(d_heads.astype(BF16), values)
        sums = jnp.sum(weighted, axis=-1, keepdims=True)
        d_scores = ((weighted - probs * sums) * gate).astype(BF16)
        d_queries = heads_nn(d_scores, keys) * scale
        d_keys = heads_tn(d_scores, queries) * scale
        d_values = heads_tn(probs.astype(BF16), (d_heads * gate).astype(BF16))
        for number, at in enumerate(starts):
            cols = slice(at, at + HD)
            d_query_ref[rows, cols] = turn_back(d_queries[number], cosine, sine).astype(BF16)
            d_kv_ref[rows, cols] = turn_back(d_keys[number], cosine, sine).astype(BF16)
            d_kv_ref[rows, span + at : span + at + HD] = d_values[number].astype(BF16)
        total = jnp.broadcast_to(jnp.sum(sums, axis=0), (length, length))
        d_gate_ref[seq] = total.T[:1]
    d_input = nt(d_query_ref[...], query_ref[...]) + nt(d_kv_ref[...], kv_ref[...])

    @pl.when(pl.program_id(0) == 0)
    def _():
        d_gain_ref[...] = jnp.zeros_like(d_gain_ref)

    d_gain_ref[...] += jnp.sum(d_input * x_ref[...].astype(F32), axis=0, keepdims=True)
    part_ref[...] = d_input.astype(BF16)


def rows_kernel(parts, places_ref, *refs):
    gated_refs, down_refs, (own_ref, other_ref) = refs[:parts], refs[parts : 2 * parts], refs[2 * parts :]
    length = own_ref.shape[2]
    value = nn(gated_refs[0][...], down_refs[0][...])
    for part in range(1, parts):
        value = value + nn(gated_refs[part][...], down_refs[part][...])
    value = value.astype(BF16)
    other_first = pl.num_programs(0) // 2

    @pl.when(pl.program_id(0) < other_first)
    def _():
        place_rows(places_ref, other_ref, value, length)

    @pl.when(pl.program_id(0) >= other_first)
    def _():
        place_rows(places_ref, own_ref, value, length)


def fixed(shape):
    return pl.BlockSpec(shape, lambda step, places: (0,) * len(shape))


def rows_spec(rows, columns):
    return pl.BlockSpec((rows, columns), lambda step, places: (step, 0))


def info_spec(seqs, kinds, length):
    return pl.BlockSpec((seqs, kinds, length), lambda step, places: (step, 0, 0))


def shape(dims, dtype=BF16):
    return jax.ShapeDtypeStruct(dims, dtype)


def call(kernel, name, steps, in_specs, out_specs, out_shape, flops, moved, operands):
    return pl.pallas_call(
        kernel,
        grid_spec=pltpu.PrefetchScalarGridSpec(
            num_scalar_prefetch=1, grid=(steps,), in_specs=in_specs, out_specs=out_specs
        ),
        out_shape=out_shape,
        compiler_params=pltpu.CompilerParams(vmem_limit_bytes=VMEM),
        cost_estimate=pl.CostEstimate(flops=flops, bytes_accessed=moved, transcendentals=0),
        name=name,
    )(*operands)


def attend(places, rows, info, cosine, sine, query_mat, kv_parts):
    count, width = rows.shape
    span = query_mat.shape[1]
    length = cosine.shape[0]
    step = OUTER * length
    return call(
        attend_kernel,
        "attend",
        count // step,
        [
            rows_spec(step, width),
            info_spec(OUTER, 2, length),
            fixed(cosine.shape),
            fixed(sine.shape),
            fixed(query_mat.shape),
            *[fixed(one.shape) for one in kv_parts],
        ],
        [rows_spec(step, 3 * span), rows_spec(step, span), fixed((width, 2 * span))],
        [shape((count, 3 * span)), shape((count, span)), shape((width, 2 * span))],
        2 * count * width * 3 * span + 4 * count * length * span,
        4 * count * (width + 2 * span),
        (places, rows, info, cosine, sine, query_mat, *kv_parts),
    )


def attend_back(places, d_middle, info, cosine, sine, qkv, rows, query_mat, kv_mat, out_mat):
    count, width = d_middle.shape
    length = cosine.shape[0]
    step = OUTER * length
    span = out_mat.shape[0]
    return call(
        attend_back_kernel,
        "attend_back",
        count // step,
        [
            rows_spec(step, width),
            info_spec(OUTER, 2, length),
            fixed(cosine.shape),
            fixed(sine.shape),
            rows_spec(step, 3 * span),
            rows_spec(step, width),
            fixed(query_mat.shape),
            fixed(kv_mat.shape),
            fixed(out_mat.shape),
        ],
        [
            rows_spec(step, span),
            rows_spec(step, 2 * span),
            rows_spec(step, width),
            info_spec(OUTER, 1, length),
            fixed((1, width)),
        ],
        [
            shape((count, span)),
            shape((count, 2 * span)),
            shape((count, width)),
            shape((count // length, 1, length), F32),
            shape((1, width), F32),
        ],
        2 * count * width * 4 * span + 10 * count * length * span,
        4 * count * (2 * width + 3 * span),
        (places, d_middle, info, cosine, sine, qkv, rows, query_mat, kv_mat, out_mat),
    )


def ring_rows(places, gated, mats, length):
    count, units = gated[0].shape
    width = mats[0].shape[1]
    parts = len(mats)
    step = OUTER * length
    high = count // (2 * step)

    def pair(number, places):
        c = lax.rem(lax.div(number, high) + 1 + places[1], 2)
        return (lax.rem(lax.rem(number, high) + places[0], high) * 2 + c, 0)

    block = (1, OUTER, length, width)
    return call(
        functools.partial(rows_kernel, parts),
        "rows",
        count // step,
        [pl.BlockSpec((step, units), pair)] * parts + [fixed(one.shape) for one in mats],
        [
            pl.BlockSpec(block, lambda number, places: (lax.max(number - high, 0), 0, 0, 0)),
            pl.BlockSpec(block, lambda number, places: (lax.min(number, high - 1), 0, 0, 0)),
        ],
        [shape((high, OUTER, length, width))] * 2,
        2 * count * width * units * parts,
        4 * count * (width + units * parts),
        (places, *gated, *mats),
    )


def units_kernel(places_ref, x_ref, info_ref, d_units_ref, first_ref, second_ref, *refs):
    del places_ref
    sums_refs, (d_both_ref, gated_ref, back_ref, d_gate_ref) = refs[:-4], refs[-4:]
    length = info_ref.shape[2]
    seqs = info_ref.shape[0]
    units = first_ref.shape[0]
    rows = x_ref[...]
    gate = jnp.concatenate([as_column(info_ref[seq], length) for seq in range(seqs)], axis=0)
    gate_in = nt(rows, first_ref[...])
    up_in = nt(rows, second_ref[...])
    sigma = jax.nn.sigmoid(gate_in)
    active = gate_in * sigma
    hidden_units = active * up_in
    d_units = d_units_ref[...].astype(F32)
    d_gate = jnp.sum(hidden_units * d_units, axis=-1, keepdims=True)
    gated_ref[...] = (hidden_units * gate).astype(BF16)
    d_units = d_units * gate
    d_first = (d_units * up_in * (sigma + active * (1.0 - sigma))).astype(BF16)
    d_second = (d_units * active).astype(BF16)
    d_both_ref[:, :units] = d_first
    d_both_ref[:, units:] = d_second
    back = nn(d_first, first_ref[...]) + nn(d_second, second_ref[...])
    if sums_refs:
        back = back + sums_refs[0][...]
    back_ref[...] = back.astype(back_ref.dtype)
    for seq in range(seqs):
        column = jnp.broadcast_to(d_gate[seq * length : (seq + 1) * length], (length, length))
        d_gate_ref[seq] = column.T[:1]


def run_units(places, rows, info, d_units, first, second, sums, last):
    count, width = rows.shape
    length = info.shape[2]
    units = d_units.shape[1]
    seqs = ROW_STEP // length

    def weight_spec(block):
        return pl.BlockSpec((units, width), lambda step, places: (block, 0))

    extra = [] if sums is None else [sums]
    return call(
        units_kernel,
        "units",
        count // ROW_STEP,
        [rows_spec(ROW_STEP, width), info_spec(seqs, 1, length), rows_spec(ROW_STEP, units)]
        + [weight_spec(first[1]), weight_spec(second[1])]
        + [rows_spec(ROW_STEP, width) for _ in extra],
        [
            rows_spec(ROW_STEP, 2 * units),
            rows_spec(ROW_STEP, units),
            rows_spec(ROW_STEP, width),
            info_spec(seqs, 1, length),
        ],
        [
            shape((count, 2 * units)),
            shape((count, units)),
            shape((count, width), BF16 if last else F32),
            shape((count // length, 1, length), F32),
        ],
        0,
        0,
        (places, rows, info, d_units, first[0], second[0], *extra),
    )


def shards(
    hidden_in,
    segment_ids,
    att_route,
    mlp_route,
    norm_gain1,
    norm_gain2,
    att_router,
    mlp_router,
    kv_weight,
    query_weight,
    out_weight,
    att_bias,
    up_weight,
    down_weight,
    mlp_bias,
    cotangent,
):
    experts = lax.axis_size(EXPERT)
    inner = lax.axis_size("i")
    tokens, width = hidden_in.shape
    span = HEADS // OUTER * HD
    cosine, sine_table = rope_tables(tokens)

    places = own_places()

    down_parts = ring_gather(down_weight[0], "i")
    query_mat, kv_parts, seen = gather_heads(query_weight[0], kv_weight, down_parts[1:])
    out_parts = ring_gather(after(out_weight[0], seen), "i")
    own_up = up_weight[0].reshape(-1, width)

    residual = hidden_in.astype(F32)
    normed_one, inverse_one = norm_rows(residual, norm_gain1)
    attn_input = normed_one.astype(BF16)
    att_gate, att_onehot = pair_gates(attn_input, att_router, att_route, experts)
    info = to_experts(att_gate, att_onehot, segment_ids[0].astype(F32))
    all_attn = meet(attn_input)
    all_cot = meet(after(cotangent.astype(BF16), seen))
    qkv, gated, kv_mat = attend(
        places, all_attn, info, cosine, sine_table, query_mat, kv_parts
    )
    out_parts = out_parts[:1] + list(after(out_parts[1:], gated))
    out_mat = in_order(out_parts, "i").reshape(span, width)
    branch = part_low(*ring_rows(places, [gated], [out_mat], tokens))
    branch = part_second(*part_first(branch))

    d_units = [mm("td,fd->tf", all_cot, down).astype(BF16) for down in down_parts]
    branch = after(branch, d_units)
    middle = residual + branch.astype(F32) + att_bias
    normed_two, inverse_two = norm_rows(middle, norm_gain2)
    mlp_input = normed_two.astype(BF16)
    mlp_gate, mlp_onehot = pair_gates(mlp_input, mlp_router, mlp_route, experts)
    up_parts = ring_gather(after(own_up, gated), "i")
    all_mlp = meet(mlp_input)
    gate_m = to_experts(mlp_gate, mlp_onehot, None)
    d_both, gated_units, rows_back, d_gate_m = [], [], None, None
    for number, up in enumerate(up_parts):
        source = own_up if number == 0 else up
        found = run_units(
            places,
            all_mlp,
            gate_m,
            d_units[number],
            (source, 0),
            (source, 1),
            rows_back,
            number == inner - 1,
        )
        d_both.append(found[0])
        gated_units.append(found[1])
        rows_back = found[2]
        d_gate_m = found[3] if d_gate_m is None else d_gate_m + found[3]
    d_mlp_input = part(rows_back)
    d_mlp_gate = from_experts(d_gate_m[:, 0], mlp_onehot, experts)
    grad_up = [mm("tf,td->fd", d_here, all_mlp) for d_here in d_both]
    grad_down = [mm("tf,td->fd", here, all_cot) for here in gated_units]
    low_up = [one.astype(BF16) for one in grad_up[1:]]
    low_down = [one.astype(BF16) for one in grad_down[1:]]
    rows_out = part_low(*ring_rows(places, after(gated_units, low_down), down_parts, tokens))
    half = tokens // 2
    rows_first, rows_second = rows_out[:, :, :half], rows_out[:, :, half:]
    lower_own, lower_last = ring_open(grad_down[:1] + low_down, "i")
    upper_own, upper_last = ring_open(grad_up[:1] + low_up, "i")
    d_mlp_input = after(d_mlp_input, rows_out, low_up, lower_last)
    d_mlp_router, d_mlp_from_router = gates_back(
        mlp_gate, mlp_onehot, d_mlp_gate, mlp_input, mlp_router
    )
    d_norm_two, d_gain_two = norm_back(
        middle, inverse_two, norm_gain2, d_mlp_input.astype(F32) + d_mlp_from_router
    )
    d_middle = cotangent + d_norm_two
    sums = jnp.concatenate(
        [
            jnp.stack([d_gain_two, jnp.sum(d_middle, axis=0), jnp.sum(cotangent, axis=0)]),
            d_mlp_router,
        ]
    )

    all_mid = meet(d_middle.astype(BF16))
    rows_second = ring_low([rows_second[:, k] for k in range(OUTER)], "o")
    all_mid = after(all_mid, rows_second)
    d_heads, d_kv, rows_one, d_gate_a, d_gain_a = attend_back(
        places, all_mid, info, cosine, sine_table, qkv, all_attn, query_mat, kv_mat, out_mat
    )
    rows_first = after(rows_first, all_mid)
    rows_first = [rows_first[k] for k in range(rows_first.shape[0])]
    rows_first = ring_low(rows_first, "y")
    d_attn_input = part(rows_one)
    d_att_gate = from_experts(d_gate_a[:, 0], att_onehot, experts)
    d_kv_mat = mm("td,tf->df", all_attn, d_kv).reshape(experts // 2, 2, -1, 2 * span)
    d_kv_mat = from_order([d_kv_mat[:, 0], d_kv_mat[:, 1]], "c")
    d_kv_sent = d_kv_mat[1].astype(BF16)
    d_kv_last, kv_sent, kv_arrived = scatter_kv(d_kv_mat[0], d_kv_sent)
    d_heads, all_mid = after((d_heads, all_mid), kv_sent)
    d_att_router, d_att_from_router = gates_back(
        att_gate, att_onehot, d_att_gate, attn_input, att_router
    )
    d_gain_one = d_gain_a / norm_gain1 + jnp.sum(
        d_att_from_router * residual * inverse_one, axis=0, keepdims=True
    )
    summed = sum_over(jnp.concatenate([d_gain_one, sums, d_att_router]), ("i",))
    d_query_last = scatter_query(mm("td,tf->df", all_attn, d_heads), summed)
    d_query, d_kv_weight, heads_sent = scatter_heads(d_query_last, d_kv_last, d_attn_input)
    d_query = d_query[None]
    d_out = mm("tf,td->fd", gated, all_mid).reshape(inner, -1, width)
    d_out = from_order([d_out[k] for k in range(inner)], "i")
    d_out = d_out[:1] + list(after(d_out[1:], d_kv_last))
    d_output = ring_scatter(d_out, "i", heads_sent)[None]
    rows_out = part_second(*after((rows_first, rows_second), kv_arrived))
    layer_out = middle + rows_out.astype(F32) + mlp_bias
    d_upper = (after(upper_last, kv_sent).astype(F32) + upper_own).reshape(up_weight.shape)
    d_lower = (lower_last.astype(F32) + lower_own)[None]
    d_attn_input = after(d_attn_input, summed)
    summed = sum_over(after(summed, heads_sent), ("c", "y", "o"))
    d_norm_one, _ = norm_back(
        residual, inverse_one, norm_gain1, d_attn_input.astype(F32) + d_att_from_router
    )
    d_input = d_middle + d_norm_one
    return (
        layer_out,
        d_input,
        summed[0],
        summed[1],
        summed[4 + experts :].T,
        summed[4 : 4 + experts].T,
        d_kv_weight,
        d_query,
        d_output,
        summed[2],
        d_upper,
        d_lower,
        summed[3],
    )


def solution(mesh):
    experts, fsdp = mesh.shape["expert"], mesh.shape["fsdp"]
    fine = Mesh(mesh.devices.reshape(experts // 2, 2, OUTER, fsdp // OUTER), ALL)
    shard = ("o", "i")
    rows = P(ALL, None)
    placed = (
        rows,
        rows,
        rows,
        rows,
        P(),
        P(),
        P(),
        P(),
        rows,
        P(EXPERT, shard, None),
        P(EXPERT, shard, None),
        P(),
        P(EXPERT, None, shard, None),
        P(EXPERT, shard, None),
        P(),
        rows,
    )
    return jax.shard_map(
        shards,
        mesh=fine,
        in_specs=placed,
        out_specs=(
            rows,
            rows,
            P(),
            P(),
            P(),
            P(),
            rows,
            P(EXPERT, shard, None),
            P(EXPERT, shard, None),
            P(),
            P(EXPERT, None, shard, None),
            P(EXPERT, shard, None),
            P(),
        ),
        check_vma=False,
    )
```

```python
import functools
import math

import jax
import jax.numpy as jnp
from jax import lax
from jax.experimental import pallas as pl
from jax.experimental.pallas import tpu as pltpu
from jax.sharding import Mesh, PartitionSpec as P

HEADS = 16
HD = 128
TOP = 2


EPSILON = 1e-06
HIGHEST = lax.Precision.HIGHEST
MASKED = -1e30

GROUP = ("y", "c", "o")
EXPERT = ("y", "c")
ALL = ("y", "c", "o", "i")
OUTER = 4
F32 = jnp.float32
BF16 = jnp.bfloat16


def rope_tables(length):
    half_dim = HD // 2
    frequency = jnp.exp(jnp.arange(half_dim, dtype=F32) * (-2.0 * math.log(10000.0) / HD))
    angles = jnp.arange(length, dtype=F32)[:, None] * frequency[None, :]
    cosine, sine = jnp.cos(angles), jnp.sin(angles)
    return (
        jnp.concatenate([cosine, cosine], axis=1),
        jnp.concatenate([-sine, sine], axis=1),
    )


def norm_rows(stream, gain):
    inverse = lax.rsqrt(jnp.mean(stream * stream, axis=-1, keepdims=True) + EPSILON)
    return (stream * inverse * gain, inverse)


def norm_back(stream, inverse, gain, upstream):
    scaled = upstream * gain
    d_stream = inverse * scaled - stream * inverse**3 * jnp.mean(
        scaled * stream, axis=-1, keepdims=True
    )
    d_gain = jnp.sum(upstream * stream * inverse, axis=0)
    return (d_stream, d_gain)


def shift(value, axis):
    size = lax.axis_size(axis)
    return lax.ppermute(value, axis, [((k + 1) % size, k) for k in range(size)])


def after(value, *others):
    token, _ = lax.optimization_barrier((lax.create_token(), others))
    return lax.optimization_barrier((token, value))[1]


def ring_gather(value, axis):
    parts = [value]
    for _ in range(lax.axis_size(axis) - 1):
        parts.append(shift(parts[-1], axis))
    return parts


def ring_open(blocks, axis):
    size = lax.axis_size(axis)
    travelling = blocks[1].astype(BF16)
    for j in range(2, size):
        travelling = (shift(travelling, axis).astype(F32) + blocks[j].astype(F32)).astype(BF16)
    return blocks[0], shift(travelling, axis)


def ring_scatter(blocks, axis, *others):
    own, arrived = ring_open(blocks, axis)
    if others:
        arrived = after(arrived, *others)
    return arrived.astype(F32) + own


def in_order(parts, axis, place=0):
    if len(parts) == 2:
        first = lax.axis_index(axis) == 0
        return jnp.stack([jnp.where(first, *parts), jnp.where(first, *parts[::-1])], axis=place)
    return jnp.roll(jnp.stack(parts, axis=place), lax.axis_index(axis), axis=place)


def from_order(parts, axis):
    if len(parts) == 2:
        first = lax.axis_index(axis) == 0
        return [jnp.where(first, *parts), jnp.where(first, *parts[::-1])]
    return list(jnp.roll(jnp.stack(parts), -lax.axis_index(axis), axis=0))


def sum_over(value, axes):
    for axis in axes:
        size = lax.axis_size(axis)
        step = 1
        while step < size:
            value = value + lax.ppermute(value, axis, [(k, k ^ step) for k in range(size)])
            step *= 2
    return value


def sum_outer(value):
    one, two, three = [
        lax.ppermute(value, "o", [((k + j) % OUTER, k) for k in range(OUTER)]) for j in (1, 2, 3)
    ]
    return (value + two) + (one + three)


def pair_gates(normed, router, route, experts):
    logits = jnp.dot(normed.astype(F32), router, precision=HIGHEST)
    onehot = (route[:, :, None] == jnp.arange(experts, dtype=jnp.int32)[None, None, :]).astype(F32)
    picked = jnp.sum(logits[:, None, :] * onehot, axis=-1)
    return (jax.nn.softmax(picked, axis=-1), onehot)


def gates_back(gates, onehot, d_gates, normed, router):
    d_picked = gates * (d_gates - jnp.sum(gates * d_gates, axis=-1, keepdims=True))
    d_logits = jnp.sum(d_picked[:, :, None] * onehot, axis=1)
    d_router = jnp.dot(d_logits.T, normed.astype(F32), precision=HIGHEST)
    d_normed = jnp.dot(d_logits, router.T, precision=HIGHEST)
    return (d_router, d_normed)


def to_experts(gates, onehot, extra):
    by_expert = jnp.sum(gates[:, :, None] * onehot, axis=1).T
    rows = jnp.repeat(by_expert, OUTER, axis=0)[:, None, :]
    if extra is not None:
        rows = jnp.concatenate(
            [rows, jnp.broadcast_to(extra[None, None, :], rows.shape)], axis=1
        )
    return lax.all_to_all(rows, GROUP, split_axis=0, concat_axis=0, tiled=True)


def from_experts(d_gates, onehot, experts):
    rows = lax.all_to_all(d_gates, GROUP, split_axis=0, concat_axis=0, tiled=True)
    by_expert = jnp.sum(rows.reshape(experts, OUTER, -1), axis=1)
    return jnp.einsum("tce,et->tc", onehot, by_expert, precision=HIGHEST)


def meet(rows):
    return lax.all_gather(rows, GROUP, axis=0, tiled=True)


def part(rows):
    return lax.psum_scatter(rows, GROUP, scatter_dimension=0, tiled=True)


def mm(form, first, second):
    return jnp.einsum(form, first, second, preferred_element_type=F32)


def head_blocks(matrix):
    span = HEADS // OUTER * HD
    return jnp.stack([matrix[:, k * span : (k + 1) * span] for k in range(OUTER)])


def join_blocks(blocks):
    return jnp.concatenate([blocks[k] for k in range(OUTER)], axis=1)


def exchange(blocks):
    return lax.all_to_all(blocks, "o", split_axis=0, concat_axis=0, tiled=True)


def gather_heads(query_weight, kv_weight, beside):
    whole = HEADS * HD
    rows = query_weight.shape[0]
    here = exchange(
        jnp.concatenate(
            [
                head_blocks(query_weight),
                head_blocks(kv_weight[:, :whole]),
                head_blocks(kv_weight[:, whole:]),
            ],
            axis=1,
        )
    )
    here = after(here, *beside)
    span = here.shape[2]
    kv = ring_gather(here[:, rows:].reshape(OUTER, 2, -1, span), "i")
    query = ring_gather(after(here[:, :rows], kv[-1]), "i")
    kv = ring_gather(jnp.stack(kv), "y")
    kv = after(kv, query)
    query = in_order(query, "i", 1).reshape(-1, span)
    seen = kv[-1][0, 0, 0, 0]
    return query, ring_gather(jnp.stack(kv), "c"), seen


def scatter_query(grad, *others):
    inner = lax.axis_size("i")
    blocks = grad.reshape(OUTER, inner, -1, grad.shape[1])
    blocks = from_order([blocks[:, k] for k in range(inner)], "i")
    return ring_scatter(blocks[:1] + list(after(blocks[1:], *others)), "i").astype(BF16)


def scatter_kv(kept, sent):
    mine = lax.ppermute(sent, "c", [(0, 1), (1, 0)]).astype(F32) + kept
    high, inner = lax.axis_size("y"), lax.axis_size("i")
    mine = mine.reshape(high, OUTER, inner, -1, kept.shape[-1])
    blocks = from_order([mine[k] for k in range(high)], "y")
    sent = blocks[1].astype(BF16)
    own, arrived = ring_open([blocks[0], sent] + blocks[2:], "y")
    mine = arrived.astype(F32) + own
    mine = ring_scatter(from_order([mine[:, k] for k in range(inner)], "i"), "i").astype(BF16)
    return mine, sent, arrived


def scatter_heads(query, kv, *others):
    half = kv.shape[2] // 2
    rows, kv_rows = query.shape[1], kv.shape[1]
    sent = jnp.concatenate([query, kv[:, :, :half], kv[:, :, half:]], axis=1)
    sent = after(sent, *others)
    here = exchange(sent)
    whole = [
        join_blocks(here[:, rows + k * kv_rows : rows + (k + 1) * kv_rows]) for k in range(2)
    ]
    return join_blocks(here[:, :rows]).astype(F32), jnp.concatenate(whole, axis=1).astype(F32), sent


def own_places():
    return jnp.stack([lax.axis_index(axis) for axis in ALL]).astype(jnp.int32)


def add_low(first, second):
    return (first.astype(F32) + second.astype(F32)).astype(BF16)


def ring_low(blocks, axis):
    travelling = blocks[1]
    for j in range(2, lax.axis_size(axis)):
        travelling = add_low(shift(travelling, axis), blocks[j])
    return add_low(shift(travelling, axis), blocks[0])


def part_low(own, other):
    return ring_low([own, other], "c")


def part_first(rows):
    half = rows.shape[2] // 2
    first, second = rows[:, :, :half], rows[:, :, half:]
    first = ring_low([first[k] for k in range(first.shape[0])], "y")
    second = ring_low([second[:, k] for k in range(second.shape[1])], "o")
    return first, second


def part_second(first, second):
    first = ring_low([first[k] for k in range(first.shape[0])], "o")
    second = ring_low([second[k] for k in range(second.shape[0])], "y")
    return jnp.concatenate([first, second])


VMEM = 56 * 1024 * 1024
ROW_STEP = 256


def nn(first, second):
    return jnp.dot(first, second, preferred_element_type=F32)


def nt(first, second):
    return lax.dot_general(first, second, (((1,), (1,)), ((), ())), preferred_element_type=F32)


def tn(first, second):
    return lax.dot_general(first, second, (((0,), (0,)), ((), ())), preferred_element_type=F32)


def as_column(row, rows):
    return jnp.broadcast_to(row, (rows, rows)).T[:, :1]


def turn(head, cosine, sine):
    return head * cosine + pltpu.roll(head, HD // 2, 1) * sine


def turn_back(head, cosine, sine):
    return head * cosine - pltpu.roll(head, HD // 2, 1) * sine


def allowed_keys(segment, length):
    keys = jnp.broadcast_to(segment, (length, length))
    row = lax.broadcasted_iota(jnp.int32, (length, length), 0)
    column = lax.broadcasted_iota(jnp.int32, (length, length), 1)
    return (keys == keys.T) & (column <= row)


def heads_nt(first, second):
    return lax.dot_general(first, second, (((2,), (2,)), ((0,), (0,))), preferred_element_type=F32)


def heads_nn(first, second):
    return lax.dot_general(first, second, (((2,), (1,)), ((0,), (0,))), preferred_element_type=F32)


def heads_tn(first, second):
    return lax.dot_general(first, second, (((1,), (1,)), ((0,), (0,))), preferred_element_type=F32)


def softmax_rows(queries, keys, allowed):
    scores = jnp.where(allowed[None], heads_nt(queries, keys) * (1.0 / math.sqrt(HD)), MASKED)
    exponent = jnp.exp(scores - jnp.max(scores, axis=-1, keepdims=True))
    return exponent / jnp.sum(exponent, axis=-1, keepdims=True)


def place_rows(places_ref, part_ref, value, length):
    count = part_ref.shape[1]
    for seq in range(count):
        slot = lax.rem(seq - places_ref[2] + count, count)
        part_ref[0, slot] = value[seq * length : (seq + 1) * length]


def arrange(places_ref, part_refs, out_ref):
    high, inner, outer, kinds, rows, span = part_refs[0].shape
    for low, part_ref in enumerate(part_refs):
        c = lax.rem(low + places_ref[1], 2)
        for first in range(high):
            y = lax.rem(first + places_ref[0], high)
            for second in range(inner):
                i = lax.rem(second + places_ref[3], inner)
                for o in range(outer):
                    start = (((y * 2 + c) * outer + o) * inner + i) * rows
                    for kind in range(kinds):
                        out_ref[
                            pl.ds(pl.multiple_of(start, 16), rows), kind * span : (kind + 1) * span
                        ] = part_ref[first, second, o, kind]


def attend_kernel(
    places_ref,
    x_ref,
    info_ref,
    cos_ref,
    sin_ref,
    query_ref,
    own_ref,
    other_ref,
    qkv_ref,
    gated_ref,
    kv_ref,
):
    @pl.when(pl.program_id(0) == 0)
    def _():
        arrange(places_ref, (own_ref, other_ref), kv_ref)

    length = cos_ref.shape[0]
    span = query_ref.shape[1]
    raw_query = nn(x_ref[...], query_ref[...])
    raw = nn(x_ref[...], kv_ref[...])
    cosine, sine = cos_ref[...], sin_ref[...]
    starts = range(0, span, HD)
    for seq in range(info_ref.shape[0]):
        rows = slice(seq * length, (seq + 1) * length)
        gate = as_column(info_ref[seq, 0:1, :], length)
        allowed = allowed_keys(info_ref[seq, 1:2, :], length)
        queries, keys, values = [], [], []
        for at in starts:
            head = raw_query[rows, at : at + HD].astype(BF16).astype(F32)
            queries.append(turn(head, cosine, sine).astype(BF16))
            keys.append(turn(raw[rows, at : at + HD], cosine, sine).astype(BF16))
            values.append(raw[rows, span + at : span + at + HD].astype(BF16))
            qkv_ref[rows, at : at + HD] = queries[-1]
            qkv_ref[rows, span + at : span + at + HD] = keys[-1]
            qkv_ref[rows, 2 * span + at : 2 * span + at + HD] = values[-1]
        probs = softmax_rows(jnp.stack(queries), jnp.stack(keys), allowed)
        gated = (heads_nn(probs.astype(BF16), jnp.stack(values)) * gate[None]).astype(BF16)
        for number, at in enumerate(starts):
            gated_ref[rows, at : at + HD] = gated[number]


def attend_back_kernel(
    places_ref,
    mid_ref,
    info_ref,
    cos_ref,
    sin_ref,
    qkv_ref,
    x_ref,
    query_ref,
    kv_ref,
    out_ref,
    d_query_ref,
    d_kv_ref,
    part_ref,
    d_gate_ref,
    d_gain_ref,
):
    del places_ref
    length = cos_ref.shape[0]
    span = out_ref.shape[0]
    scale = 1.0 / math.sqrt(HD)
    d_rows = nt(mid_ref[...], out_ref[...])
    cosine, sine = cos_ref[...], sin_ref[...]
    starts = range(0, span, HD)
    for seq in range(info_ref.shape[0]):
        rows = slice(seq * length, (seq + 1) * length)
        gate = as_column(info_ref[seq, 0:1, :], length)[None]
        allowed = allowed_keys(info_ref[seq, 1:2, :], length)
        queries = jnp.stack([qkv_ref[rows, at : at + HD] for at in starts])
        keys = jnp.stack([qkv_ref[rows, span + at : span + at + HD] for at in starts])
        values = jnp.stack([qkv_ref[rows, 2 * span + at : 2 * span + at + HD] for at in starts])
        d_heads = jnp.stack([d_rows[rows, at : at + HD] for at in starts])
        probs = softmax_rows(queries, keys, allowed)
        weighted = probs * heads_nt(d_heads.astype(BF16), values)
        sums = jnp.sum(weighted, axis=-1, keepdims=True)
        d_scores = ((weighted - probs * sums) * gate).astype(BF16)
        d_queries = heads_nn(d_scores, keys) * scale
        d_keys = heads_tn(d_scores, queries) * scale
        d_values = heads_tn(probs.astype(BF16), (d_heads * gate).astype(BF16))
        for number, at in enumerate(starts):
            cols = slice(at, at + HD)
            d_query_ref[rows, cols] = turn_back(d_queries[number], cosine, sine).astype(BF16)
            d_kv_ref[rows, cols] = turn_back(d_keys[number], cosine, sine).astype(BF16)
            d_kv_ref[rows, span + at : span + at + HD] = d_values[number].astype(BF16)
        total = jnp.broadcast_to(jnp.sum(sums, axis=0), (length, length))
        d_gate_ref[seq] = total.T[:1]
    d_input = nt(d_query_ref[...], query_ref[...]) + nt(d_kv_ref[...], kv_ref[...])

    @pl.when(pl.program_id(0) == 0)
    def _():
        d_gain_ref[...] = jnp.zeros_like(d_gain_ref)

    d_gain_ref[...] += jnp.sum(d_input * x_ref[...].astype(F32), axis=0, keepdims=True)
    part_ref[...] = d_input.astype(BF16)


def rows_kernel(parts, places_ref, *refs):
    gated_refs, down_refs, (own_ref, other_ref) = refs[:parts], refs[parts : 2 * parts], refs[2 * parts :]
    length = own_ref.shape[2]
    value = nn(gated_refs[0][...], down_refs[0][...])
    for part in range(1, parts):
        value = value + nn(gated_refs[part][...], down_refs[part][...])
    value = value.astype(BF16)
    other_first = pl.num_programs(0) // 2

    @pl.when(pl.program_id(0) < other_first)
    def _():
        place_rows(places_ref, other_ref, value, length)

    @pl.when(pl.program_id(0) >= other_first)
    def _():
        place_rows(places_ref, own_ref, value, length)


def fixed(shape):
    return pl.BlockSpec(shape, lambda step, places: (0,) * len(shape))


def rows_spec(rows, columns):
    return pl.BlockSpec((rows, columns), lambda step, places: (step, 0))


def info_spec(seqs, kinds, length):
    return pl.BlockSpec((seqs, kinds, length), lambda step, places: (step, 0, 0))


def shape(dims, dtype=BF16):
    return jax.ShapeDtypeStruct(dims, dtype)


def call(kernel, name, steps, in_specs, out_specs, out_shape, flops, moved, operands):
    return pl.pallas_call(
        kernel,
        grid_spec=pltpu.PrefetchScalarGridSpec(
            num_scalar_prefetch=1, grid=(steps,), in_specs=in_specs, out_specs=out_specs
        ),
        out_shape=out_shape,
        compiler_params=pltpu.CompilerParams(vmem_limit_bytes=VMEM),
        cost_estimate=pl.CostEstimate(flops=flops, bytes_accessed=moved, transcendentals=0),
        name=name,
    )(*operands)


def attend(places, rows, info, cosine, sine, query_mat, kv_parts):
    count, width = rows.shape
    span = query_mat.shape[1]
    length = cosine.shape[0]
    step = OUTER * length
    return call(
        attend_kernel,
        "attend",
        count // step,
        [
            rows_spec(step, width),
            info_spec(OUTER, 2, length),
            fixed(cosine.shape),
            fixed(sine.shape),
            fixed(query_mat.shape),
            *[fixed(one.shape) for one in kv_parts],
        ],
        [rows_spec(step, 3 * span), rows_spec(step, span), fixed((width, 2 * span))],
        [shape((count, 3 * span)), shape((count, span)), shape((width, 2 * span))],
        2 * count * width * 3 * span + 4 * count * length * span,
        4 * count * (width + 2 * span),
        (places, rows, info, cosine, sine, query_mat, *kv_parts),
    )


def attend_back(places, d_middle, info, cosine, sine, qkv, rows, query_mat, kv_mat, out_mat):
    count, width = d_middle.shape
    length = cosine.shape[0]
    step = OUTER * length
    span = out_mat.shape[0]
    return call(
        attend_back_kernel,
        "attend_back",
        count // step,
        [
            rows_spec(step, width),
            info_spec(OUTER, 2, length),
            fixed(cosine.shape),
            fixed(sine.shape),
            rows_spec(step, 3 * span),
            rows_spec(step, width),
            fixed(query_mat.shape),
            fixed(kv_mat.shape),
            fixed(out_mat.shape),
        ],
        [
            rows_spec(step, span),
            rows_spec(step, 2 * span),
            rows_spec(step, width),
            info_spec(OUTER, 1, length),
            fixed((1, width)),
        ],
        [
            shape((count, span)),
            shape((count, 2 * span)),
            shape((count, width)),
            shape((count // length, 1, length), F32),
            shape((1, width), F32),
        ],
        2 * count * width * 4 * span + 10 * count * length * span,
        4 * count * (2 * width + 3 * span),
        (places, d_middle, info, cosine, sine, qkv, rows, query_mat, kv_mat, out_mat),
    )


def ring_rows(places, gated, mats, length):
    count, units = gated[0].shape
    width = mats[0].shape[1]
    parts = len(mats)
    step = OUTER * length
    high = count // (2 * step)

    def pair(number, places):
        c = lax.rem(lax.div(number, high) + 1 + places[1], 2)
        return (lax.rem(lax.rem(number, high) + places[0], high) * 2 + c, 0)

    block = (1, OUTER, length, width)
    return call(
        functools.partial(rows_kernel, parts),
        "rows",
        count // step,
        [pl.BlockSpec((step, units), pair)] * parts + [fixed(one.shape) for one in mats],
        [
            pl.BlockSpec(block, lambda number, places: (lax.max(number - high, 0), 0, 0, 0)),
            pl.BlockSpec(block, lambda number, places: (lax.min(number, high - 1), 0, 0, 0)),
        ],
        [shape((high, OUTER, length, width))] * 2,
        2 * count * width * units * parts,
        4 * count * (width + units * parts),
        (places, *gated, *mats),
    )


def units_kernel(places_ref, x_ref, info_ref, d_units_ref, first_ref, second_ref, *refs):
    del places_ref
    sums_refs, (d_both_ref, gated_ref, back_ref, d_gate_ref) = refs[:-4], refs[-4:]
    length = info_ref.shape[2]
    seqs = info_ref.shape[0]
    units = first_ref.shape[0]
    rows = x_ref[...]
    gate = jnp.concatenate([as_column(info_ref[seq], length) for seq in range(seqs)], axis=0)
    gate_in = nt(rows, first_ref[...])
    up_in = nt(rows, second_ref[...])
    sigma = jax.nn.sigmoid(gate_in)
    active = gate_in * sigma
    hidden_units = active * up_in
    d_units = d_units_ref[...].astype(F32)
    d_gate = jnp.sum(hidden_units * d_units, axis=-1, keepdims=True)
    gated_ref[...] = (hidden_units * gate).astype(BF16)
    d_units = d_units * gate
    d_first = (d_units * up_in * (sigma + active * (1.0 - sigma))).astype(BF16)
    d_second = (d_units * active).astype(BF16)
    d_both_ref[:, :units] = d_first
    d_both_ref[:, units:] = d_second
    back = nn(d_first, first_ref[...]) + nn(d_second, second_ref[...])
    if sums_refs:
        back = back + sums_refs[0][...]
    back_ref[...] = back.astype(back_ref.dtype)
    for seq in range(seqs):
        column = jnp.broadcast_to(d_gate[seq * length : (seq + 1) * length], (length, length))
        d_gate_ref[seq] = column.T[:1]


def run_units(places, rows, info, d_units, first, second, sums, last):
    count, width = rows.shape
    length = info.shape[2]
    units = d_units.shape[1]
    seqs = ROW_STEP // length

    def weight_spec(block):
        return pl.BlockSpec((units, width), lambda step, places: (block, 0))

    extra = [] if sums is None else [sums]
    return call(
        units_kernel,
        "units",
        count // ROW_STEP,
        [rows_spec(ROW_STEP, width), info_spec(seqs, 1, length), rows_spec(ROW_STEP, units)]
        + [weight_spec(first[1]), weight_spec(second[1])]
        + [rows_spec(ROW_STEP, width) for _ in extra],
        [
            rows_spec(ROW_STEP, 2 * units),
            rows_spec(ROW_STEP, units),
            rows_spec(ROW_STEP, width),
            info_spec(seqs, 1, length),
        ],
        [
            shape((count, 2 * units)),
            shape((count, units)),
            shape((count, width), BF16 if last else F32),
            shape((count // length, 1, length), F32),
        ],
        0,
        0,
        (places, rows, info, d_units, first[0], second[0], *extra),
    )


def shards(
    hidden_in,
    segment_ids,
    att_route,
    mlp_route,
    norm_gain1,
    norm_gain2,
    att_router,
    mlp_router,
    kv_weight,
    query_weight,
    out_weight,
    att_bias,
    up_weight,
    down_weight,
    mlp_bias,
    cotangent,
):
    experts = lax.axis_size(EXPERT)
    inner = lax.axis_size("i")
    tokens, width = hidden_in.shape
    span = HEADS // OUTER * HD
    cosine, sine_table = rope_tables(tokens)

    places = own_places()

    down_parts = ring_gather(down_weight[0], "i")
    query_mat, kv_parts, seen = gather_heads(query_weight[0], kv_weight, down_parts[1:])
    out_parts = ring_gather(after(out_weight[0], seen), "i")
    own_up = up_weight[0].reshape(-1, width)

    residual = hidden_in.astype(F32)
    normed_one, inverse_one = norm_rows(residual, norm_gain1)
    attn_input = normed_one.astype(BF16)
    att_gate, att_onehot = pair_gates(attn_input, att_router, att_route, experts)
    info = to_experts(att_gate, att_onehot, segment_ids[0].astype(F32))
    all_attn = meet(attn_input)
    all_cot = meet(after(cotangent.astype(BF16), seen))
    qkv, gated, kv_mat = attend(
        places, all_attn, info, cosine, sine_table, query_mat, kv_parts
    )
    out_parts = out_parts[:1] + list(after(out_parts[1:], gated))
    out_mat = in_order(out_parts, "i").reshape(span, width)
    branch = part_low(*ring_rows(places, [gated], [out_mat], tokens))
    branch = part_second(*part_first(branch))

    d_units = [mm("td,fd->tf", all_cot, down).astype(BF16) for down in down_parts]
    branch = after(branch, d_units)
    middle = residual + branch.astype(F32) + att_bias
    normed_two, inverse_two = norm_rows(middle, norm_gain2)
    mlp_input = normed_two.astype(BF16)
    mlp_gate, mlp_onehot = pair_gates(mlp_input, mlp_router, mlp_route, experts)
    up_parts = ring_gather(after(own_up, gated), "i")
    all_mlp = meet(mlp_input)
    gate_m = to_experts(mlp_gate, mlp_onehot, None)
    d_both, gated_units, rows_back, d_gate_m = [], [], None, None
    for number, up in enumerate(up_parts):
        source = own_up if number == 0 else up
        found = run_units(
            places,
            all_mlp,
            gate_m,
            d_units[number],
            (source, 0),
            (source, 1),
            rows_back,
            number == inner - 1,
        )
        d_both.append(found[0])
        gated_units.append(found[1])
        rows_back = found[2]
        d_gate_m = found[3] if d_gate_m is None else d_gate_m + found[3]
    d_mlp_input = part(rows_back)
    d_mlp_gate = from_experts(d_gate_m[:, 0], mlp_onehot, experts)
    grad_up = [mm("tf,td->fd", d_here, all_mlp) for d_here in d_both]
    grad_down = [mm("tf,td->fd", here, all_cot) for here in gated_units]
    low_up = [one.astype(BF16) for one in grad_up[1:]]
    low_down = [one.astype(BF16) for one in grad_down[1:]]
    rows_out = part_low(*ring_rows(places, after(gated_units, low_down), down_parts, tokens))
    half = tokens // 2
    rows_first, rows_second = rows_out[:, :, :half], rows_out[:, :, half:]
    lower_own, lower_last = ring_open(grad_down[:1] + low_down, "i")
    upper_own, upper_last = ring_open(grad_up[:1] + low_up, "i")
    d_mlp_input = after(d_mlp_input, rows_out, low_up, lower_last)
    d_mlp_router, d_mlp_from_router = gates_back(
        mlp_gate, mlp_onehot, d_mlp_gate, mlp_input, mlp_router
    )
    d_norm_two, d_gain_two = norm_back(
        middle, inverse_two, norm_gain2, d_mlp_input.astype(F32) + d_mlp_from_router
    )
    d_middle = cotangent + d_norm_two
    sums = jnp.concatenate(
        [
            jnp.stack([d_gain_two, jnp.sum(d_middle, axis=0), jnp.sum(cotangent, axis=0)]),
            d_mlp_router,
        ]
    )

    all_mid = meet(d_middle.astype(BF16))
    rows_second = ring_low([rows_second[:, k] for k in range(OUTER)], "o")
    all_mid = after(all_mid, rows_second)
    d_heads, d_kv, rows_one, d_gate_a, d_gain_a = attend_back(
        places, all_mid, info, cosine, sine_table, qkv, all_attn, query_mat, kv_mat, out_mat
    )
    rows_first = after(rows_first, all_mid)
    rows_first = [rows_first[k] for k in range(rows_first.shape[0])]
    rows_first = ring_low(rows_first, "y")
    d_attn_input = part(rows_one)
    d_att_gate = from_experts(d_gate_a[:, 0], att_onehot, experts)
    d_kv_mat = mm("td,tf->df", all_attn, d_kv).reshape(experts // 2, 2, -1, 2 * span)
    d_kv_mat = from_order([d_kv_mat[:, 0], d_kv_mat[:, 1]], "c")
    d_kv_sent = d_kv_mat[1].astype(BF16)
    d_kv_last, kv_sent, kv_arrived = scatter_kv(d_kv_mat[0], d_kv_sent)
    d_heads, all_mid = after((d_heads, all_mid), kv_sent)
    d_att_router, d_att_from_router = gates_back(
        att_gate, att_onehot, d_att_gate, attn_input, att_router
    )
    d_gain_one = d_gain_a / norm_gain1 + jnp.sum(
        d_att_from_router * residual * inverse_one, axis=0, keepdims=True
    )
    summed = sum_over(jnp.concatenate([d_gain_one, sums, d_att_router]), ("i",))
    d_query_last = scatter_query(mm("td,tf->df", all_attn, d_heads), summed)
    d_query, d_kv_weight, heads_sent = scatter_heads(d_query_last, d_kv_last, d_attn_input)
    d_query = d_query[None]
    d_out = mm("tf,td->fd", gated, all_mid).reshape(inner, -1, width)
    d_out = from_order([d_out[k] for k in range(inner)], "i")
    d_out = d_out[:1] + list(after(d_out[1:], d_kv_last))
    d_output = ring_scatter(d_out, "i", heads_sent)[None]
    rows_out = part_second(*after((rows_first, rows_second), kv_arrived))
    layer_out = middle + rows_out.astype(F32) + mlp_bias
    d_upper = (after(upper_last, kv_sent).astype(F32) + upper_own).reshape(up_weight.shape)
    d_lower = (lower_last.astype(F32) + lower_own)[None]
    d_attn_input = after(d_attn_input, summed)
    summed = sum_outer(sum_over(after(summed, heads_sent), ("c", "y")))
    d_norm_one, _ = norm_back(
        residual, inverse_one, norm_gain1, d_attn_input.astype(F32) + d_att_from_router
    )
    d_input = d_middle + d_norm_one
    return (
        layer_out,
        d_input,
        summed[0],
        summed[1],
        summed[4 + experts :].T,
        summed[4 : 4 + experts].T,
        d_kv_weight,
        d_query,
        d_output,
        summed[2],
        d_upper,
        d_lower,
        summed[3],
    )


def solution(mesh):
    experts, fsdp = mesh.shape["expert"], mesh.shape["fsdp"]
    fine = Mesh(mesh.devices.reshape(experts // 2, 2, OUTER, fsdp // OUTER), ALL)
    shard = ("o", "i")
    rows = P(ALL, None)
    placed = (
        rows,
        rows,
        rows,
        rows,
        P(),
        P(),
        P(),
        P(),
        rows,
        P(EXPERT, shard, None),
        P(EXPERT, shard, None),
        P(),
        P(EXPERT, None, shard, None),
        P(EXPERT, shard, None),
        P(),
        rows,
    )
    return jax.shard_map(
        shards,
        mesh=fine,
        in_specs=placed,
        out_specs=(
            rows,
            rows,
            P(),
            P(),
            P(),
            P(),
            rows,
            P(EXPERT, shard, None),
            P(EXPERT, shard, None),
            P(),
            P(EXPERT, None, shard, None),
            P(EXPERT, shard, None),
            P(),
        ),
        check_vma=False,
    )
```
